32 devices in a mesh: dp: 8 (over y, x, core), fsdp: 4 (over z).
Axes of the slice: x: 2, y: 2, z: 4, core: 2. Of those that a mesh axis runs over, the one named last changes fastest.
Arguments:
- tokens: bfloat16 [32, 512, 1536], P(('dp', 'fsdp')), may hold values from -50 to 50
- conv_weight: bfloat16 [5, 1536, 1536], P(None, 'fsdp'), may hold values from -0.0625 to 0.0625
- query_weight: bfloat16 [1536, 512], P('fsdp'), may hold values from -0.15625 to 0.15625
- key_weight: bfloat16 [1536, 512], P('fsdp'), may hold values from -0.15625 to 0.15625
- value_weight: bfloat16 [1536, 1536], P('fsdp'), may hold values from -0.15625 to 0.15625
- out_weight: bfloat16 [1536, 1536], P('fsdp'), may hold values from -0.875 to 0.875
- rel_weight: bfloat16 [192, 512], P(None, 'fsdp'), may hold values from -1.25 to 1.25
- up_weight: bfloat16 [1536, 3072], P('fsdp'), may hold values from -0.15625 to 0.15625
- down_weight: bfloat16 [3072, 1536], P('fsdp'), may hold values from -0.109375 to 0.109375
- gains: float32 [3, 1536], P(None, 'fsdp'), may hold values from 0.5 to 1.5
- biases: float32 [6, 1536], P(None, 'fsdp'), may hold values from -2 to 2
- up_bias: float32 [3072], P('fsdp'), may hold values from -2 to 2
- rel_bias: float32 [2, 512], P(None, 'fsdp'), may hold values from -1 to 1
- target_table: float32 [64, 1536], replicated, may hold values from -6 to 6
- clip_levels: float32 [16], replicated, may hold values from 0.5 to 8
- window_ids: int32 [32], P(('dp', 'fsdp')), may hold values from 0 to 63
- clip_index: int32 [32, 512], P(('dp', 'fsdp')), may hold values from 0 to 15
Outputs:
- mixed: bfloat16 [32, 512, 1536], P(('dp', 'fsdp'))
- tokens_grad: bfloat16 [32, 512, 1536], P(('dp', 'fsdp'))
- conv_weight_grad: float32 [5, 1536, 1536], P(None, 'fsdp')
- query_weight_grad: float32 [1536, 512], P('fsdp')
- key_weight_grad: float32 [1536, 512], P('fsdp')
- value_weight_grad: float32 [1536, 1536], P('fsdp')
- out_weight_grad: float32 [1536, 1536], P('fsdp')
- rel_weight_grad: float32 [192, 512], P(None, 'fsdp')
- up_weight_grad: float32 [1536, 3072], P('fsdp')
- down_weight_grad: float32 [3072, 1536], P('fsdp')
- gains_grad: float32 [3, 1536], P(None, 'fsdp')
- biases_grad: float32 [6, 1536], P(None, 'fsdp')
- up_bias_grad: float32 [3072], P('fsdp')
- rel_bias_grad: float32 [2, 512], P(None, 'fsdp')
The draws below stay inside these ranges and needn't reach their ends.
All inputs are finite; a program needn't handle non-finite values.
Results may differ from the reference program's by a relative error of at most 0.04.
Values may be sent and summed in bfloat16 or wider, within the bound.
A program may use at most 384 MiB of HBM per device.

```python
import math
import jax
import jax.numpy as jnp
from jax import lax

D = 1536
HEADS = 8
KEY = 64
QK = 512
FF = 3072
WIDTH = 5
NF = 192
LEN = 512
TABLE = 64
LEVELS = 16
WINDOWS = 32


def draw_tokens(key, part):
    key = jax.random.fold_in(key, 7)
    base_key, offset_key = jax.random.split(key)
    position = jnp.arange(WINDOWS, dtype=jnp.float32) / max(WINDOWS - 1, 1)
    offsets = jnp.clip(0.5 * jax.random.normal(offset_key, (D,), jnp.float32), -2.0, 2.0)
    fluctuation = jnp.clip(jax.random.normal(base_key, (WINDOWS, LEN, D), jnp.float32), -6.0, 6.0)
    scales = 8.0 ** position
    return (offsets + scales[:, None, None] * fluctuation).astype(jnp.bfloat16)


def set_ends(values, key, smallest, high):
    shape = values.shape
    index_at = [jax.random.randint(jax.random.fold_in(key, axis), (), 0, shape[axis]) for axis in range(len(shape))]
    values = values.at[tuple(index_at)].set(smallest)
    longest = shape.index(max(shape))
    index_at[longest] = (index_at[longest] + 1) % shape[longest]
    return values.at[tuple(index_at)].set(high)


def shard_levels(key, extent, cuts, low, high):
    factor_of = 1.0
    for dim, shards_of in cuts:
        heights = jax.random.uniform(jax.random.fold_in(jax.random.fold_in(key, 6), dim), (shards_of,), jnp.float32, low / len(cuts), high / len(cuts))
        factor_of = factor_of * jnp.repeat(jnp.exp(heights), extent[dim] // shards_of).reshape((-1,) + (1,) * (len(extent) - 1 - dim))
    return factor_of


def normal_values(key, extent, width, bound, cuts=(), held_as=jnp.bfloat16):
    entries = width * jax.random.normal(key, extent, jnp.float32)
    if cuts:
        entries = entries * shard_levels(key, extent, cuts, -0.22, 0.18)
    return jnp.clip(entries, -bound, bound).astype(held_as)


def setup_inputs(seed: int = 0) -> dict:
    keys = jax.random.split(jax.random.key(seed), 18)
    tokens = draw_tokens(jax.random.fold_in(keys[17], 71), 0)
    conv_weight = normal_values(keys[1], (WIDTH, D, D), (WIDTH * D) ** -0.5, 0.0625, ((1, 4),))
    query_weight = normal_values(keys[2], (D, QK), D ** -0.5, 0.15625, ((0, 4),))
    key_weight = normal_values(keys[3], (D, QK), D ** -0.5, 0.15625, ((0, 4),))
    value_weight = normal_values(keys[4], (D, D), D ** -0.5, 0.15625, ((0, 4),))
    out_weight = normal_values(keys[5], (D, D), (D // 32) ** -0.5, 0.875, ((0, 4),))
    rel_weight = normal_values(keys[6], (NF, QK), (NF // 8) ** -0.5, 1.25, ((1, 4),))
    up_weight = normal_values(keys[7], (D, FF), D ** -0.5, 0.15625, ((0, 4),))
    down_weight = normal_values(keys[8], (FF, D), FF ** -0.5, 0.109375, ((0, 4),))
    gains = jnp.clip(1.0 + 0.1 * jax.random.normal(keys[9], (3, D), jnp.float32), 0.5, 1.5)
    biases = normal_values(keys[10], (6, D), 0.3, 2.0, ((1, 4),), jnp.float32)
    up_bias = normal_values(keys[11], (FF,), 0.3, 2.0, ((0, 4),), jnp.float32)
    rel_bias = normal_values(keys[12], (2, QK), 0.15, 1.0, ((1, 4),), jnp.float32)
    target_table = normal_values(keys[13], (TABLE, D), 1.0, 6.0, (), jnp.float32)
    clip_levels = jnp.clip(jnp.exp(jax.random.uniform(keys[14], (LEVELS,), jnp.float32, math.log(0.5), math.log(8.0))), 0.5, 8.0)
    window_ids = set_ends(jax.random.randint(keys[15], (WINDOWS,), 0, TABLE), jax.random.fold_in(keys[15], 1), 0, TABLE - 1).astype(jnp.int32)
    clip_index = set_ends(jax.random.randint(keys[16], (WINDOWS, LEN), 0, LEVELS), jax.random.fold_in(keys[16], 1), 0, LEVELS - 1).astype(jnp.int32)
    return {"tokens": tokens, "conv_weight": conv_weight, "query_weight": query_weight, "key_weight": key_weight, "value_weight": value_weight, "out_weight": out_weight, "rel_weight": rel_weight, "up_weight": up_weight, "down_weight": down_weight, "gains": gains, "biases": biases, "up_bias": up_bias, "rel_bias": rel_bias, "target_table": target_table, "clip_levels": clip_levels, "window_ids": window_ids, "clip_index": clip_index}


EPSILON = 1e-05
HIGH = lax.Precision.HIGHEST

@jax.custom_vjp
def low(v):
    return lax.optimization_barrier(v.astype(jnp.bfloat16)).astype(jnp.float32)

@jax.custom_vjp
def low_back(v):
    return v

def low_keep(v):
    return (low(v), None)

def low_pass(kept, grad):
    return (grad,)

def back_keep(v):
    return (v, None)

def back_low(kept, grad):
    return (low(grad),)
low.defvjp(low_keep, low_pass)
low_back.defvjp(back_keep, back_low)

def position_table(length, features):
    basis_count = features // 6
    offsets = jnp.arange(2 * length - 1, dtype=jnp.float32) - (length - 1)
    distance = jnp.abs(offsets)[:, None]
    max_range = math.log(length) / math.log(2.0)
    half_life = 2.0 ** jnp.linspace(3.0, max_range, basis_count, dtype=jnp.float32)
    decaying = jnp.exp(-math.log(2.0) / half_life[None, :] * distance)
    widths = 2.0 ** jnp.arange(1, basis_count + 1, dtype=jnp.float32) - 1.0
    central = (widths[None, :] > distance).astype(jnp.float32)
    stddev = length / (2.0 * basis_count)
    centres = jnp.linspace(length / basis_count, length, basis_count, dtype=jnp.float32)
    shape_par = (centres / stddev) ** 2
    rate_par = centres / stddev ** 2
    safe_dist = jnp.maximum(distance, 1.0)
    log_prob = (shape_par - 1.0) * jnp.log(safe_dist) - rate_par * safe_dist
    log_prob = log_prob - lax.optimization_barrier(jnp.max(log_prob, axis=0, keepdims=True))
    gamma_feat = jnp.where(distance > 0.5, jnp.exp(log_prob), 0.0)
    symmetric = jnp.concatenate([decaying, central, gamma_feat], 1)
    sign_row = jnp.sign(offsets)[:, None]
    return jnp.concatenate([symmetric, sign_row * symmetric], 1)

def relative_shift(scores):
    row_count = scores.shape[-2]
    span_width = scores.shape[-1]
    leading = scores.shape[:-2]
    padded = jnp.pad(scores, [(0, 0)] * (scores.ndim - 1) + [(1, 0)])
    folded = padded.reshape(leading + (span_width + 1, row_count))[..., 1:, :]
    return folded.reshape(leading + (row_count, span_width))[..., :row_count]

def layer_norm(values, gain_row, bias_row):
    centred = values - lax.optimization_barrier(jnp.mean(values, -1, keepdims=True))
    spread = lax.optimization_barrier(jnp.mean(centred * centred, -1, keepdims=True))
    return centred * lax.rsqrt(spread + EPSILON) * gain_row + bias_row

def unit_forward(activated, input_win, table, params):
    conv_w, query_w, key_w, value_w, out_w, rel_w, up_w, down_w, gain_rows, bias_rows, up_offset, rel_offset = params
    length = activated.shape[0]
    tap_count = conv_w.shape[0]
    half_taps = tap_count // 2
    padded = jnp.pad(activated, ((half_taps, half_taps), (0, 0)))
    stacked = jnp.concatenate([padded[tap_index:tap_index + length] for tap_index in range(tap_count)], 1)
    conv_out = jnp.dot(stacked, conv_w.reshape(-1, conv_w.shape[2]), precision=HIGH)
    after_conv = input_win + low_back(conv_out + bias_rows[1])
    normed_one = low(layer_norm(after_conv, gain_rows[1], bias_rows[2]))
    query_raw = low_back(jnp.dot(normed_one, query_w, precision=HIGH))
    key_scale = KEY ** (-0.5)
    content_query = low(query_raw * key_scale + rel_offset[0]).reshape(length, HEADS, -1)
    position_query = low(query_raw * key_scale + rel_offset[1]).reshape(length, HEADS, -1)
    key_heads = low(low_back(jnp.dot(normed_one, key_w, precision=HIGH))).reshape(length, HEADS, -1)
    value_heads = low(low_back(jnp.dot(normed_one, value_w, precision=HIGH))).reshape(length, HEADS, -1)
    position_keys = low(low_back(jnp.dot(table, rel_w, precision=HIGH))).reshape(table.shape[0], HEADS, -1)
    content = jnp.einsum('ihk,jhk->hij', content_query, key_heads, precision=HIGH)
    relative = relative_shift(jnp.einsum('ihk,mhk->him', position_query, position_keys, precision=HIGH))
    scores = low_back(content + relative)
    attention_probs = low(jax.nn.softmax(scores, axis=-1))
    attended = jnp.einsum('hij,jhv->ihv', attention_probs, value_heads, precision=HIGH).reshape(length, -1)
    attended = low(low_back(attended))
    after_attention = after_conv + low_back(jnp.dot(attended, out_w, precision=HIGH) + bias_rows[3])
    normed_two = low(layer_norm(after_attention, gain_rows[2], bias_rows[4]))
    hidden_pre = low_back(jnp.dot(normed_two, up_w, precision=HIGH) + up_offset)
    hidden = low(jax.nn.gelu(hidden_pre))
    return low_back(after_attention + jnp.dot(hidden, down_w, precision=HIGH) + bias_rows[5])

def reference(tokens, conv_weight, query_weight, key_weight, value_weight, out_weight, rel_weight, up_weight, down_weight, gains, biases, up_bias, rel_bias, target_table, clip_levels, window_ids, clip_index):
    table = low(position_table(LEN, NF))
    params = (conv_weight.astype(jnp.float32), query_weight.astype(jnp.float32), key_weight.astype(jnp.float32), value_weight.astype(jnp.float32), out_weight.astype(jnp.float32), rel_weight.astype(jnp.float32), up_weight.astype(jnp.float32), down_weight.astype(jnp.float32), gains.astype(jnp.float32), biases.astype(jnp.float32), up_bias.astype(jnp.float32), rel_bias.astype(jnp.float32))
    inputs = tokens.astype(jnp.float32)

    def forward(inputs, params):
        gain_rows = params[8]
        bias_rows = params[9]
        centre = lax.optimization_barrier(jnp.mean(inputs, axis=(0, 1)))
        variance = lax.optimization_barrier(jnp.mean(inputs * inputs, axis=(0, 1))) - centre * centre
        normed = (inputs - centre) * lax.rsqrt(variance + EPSILON) * gain_rows[0] + bias_rows[0]
        activated = low(jax.nn.gelu(normed))

        def window(window_pair):
            return unit_forward(window_pair[0], window_pair[1], table, params)
        return lax.map(jax.checkpoint(window), (activated, inputs))
    outputs, pullback = jax.vjp(forward, inputs, params)
    targets = target_table.astype(jnp.float32)[window_ids]
    limits = clip_levels.astype(jnp.float32)[clip_index][..., None]
    cotangent = jnp.clip(outputs - targets[:, None, :], -limits, limits)
    input_grad, param_grads = pullback(cotangent)
    grad_conv, grad_query, grad_key, grad_value, grad_out, grad_rel, grad_up, grad_down, grad_gains, grad_biases, grad_up_bias, grad_rel_bias = param_grads
    return (outputs.astype(jnp.bfloat16), input_grad.astype(jnp.bfloat16), grad_conv, grad_query, grad_key, grad_value, grad_out, grad_rel, grad_up, grad_down, grad_gains, grad_biases, grad_up_bias, grad_rel_bias)
```

```python
import functools
import math

import jax
import jax.numpy as jnp
from jax import lax
from jax.experimental import pallas as pl
from jax.experimental.pallas import tpu as pltpu
from jax.sharding import PartitionSpec as P

HEADS = 8
KEY = 64
MESH = pl.DeviceIdType.MESH
PIECES = 12
AHEAD = 2
LAG = 1

def neighbours(dp):
    core = dp % 2
    along_x = dp // 2 % 2
    along_y = dp // 4 % 2
    return dp + 1 - 2 * core, dp + 2 - 4 * along_x, dp + 4 - 8 * along_y

def gather_kernel(groups, conv, query, key, value, out, rel, up, down, small,
                  full, small_full, hold, local_sem, write_sem, z_sem, x_sem, y_sem, d_sem, sib_sem, send_sem, right_send, left_send, small_send, small_recv):
    dp = lax.axis_index("dp")
    me = lax.axis_index("fsdp")
    sib, along_x, along_y = neighbours(dp)
    rows = full.shape[2]
    part = rows // 8
    others = groups - 1

    locals_ = []
    def local(src, dst, piece):
        c = pltpu.make_async_copy(src, dst, local_sem.at[len(locals_)])
        c.start()
        locals_.append((piece, c))
    for tap in range(5):
        local(conv.at[tap], hold.at[tap], tap)
    qk = query.shape[1]
    local(query, hold.at[5, :, pl.ds(0, qk)], 5)
    local(key, hold.at[5, :, pl.ds(qk, qk)], 5)
    local(rel, hold.at[5, pl.ds(0, rel.shape[0]), pl.ds(2 * qk, rel.shape[1])], 5)
    local(value, hold.at[6], 6)
    local(out, hold.at[7], 7)
    for half in range(2):
        for shard in range(groups):
            local(up.at[:, pl.ds((shard * 2 + half) * rows, rows)], hold.at[8 + half, :, pl.ds(shard * rows, rows)], 8 + half)
    for half in range(2):
        local(down.at[pl.ds(half * rows, rows)], hold.at[10 + half], 10 + half)
    local(small, small_full.at[me], 12)

    peers = [(sib, me), (along_x, me), (along_y, me)] + [(dp, (me + 1 + j) % groups) for j in range(others)]
    barrier = pltpu.get_barrier_semaphore()
    for peer in peers:
        pl.semaphore_signal(barrier, inc=1, device_id=peer, device_id_type=MESH)
    pl.semaphore_wait(barrier, len(peers))

    def remote(src, dst, ssem, rsem, dev):
        return pltpu.make_async_remote_copy(src_ref=src, dst_ref=dst, send_sem=ssem, recv_sem=rsem, device_id=dev, device_id_type=MESH)

    smalls = []
    for j in range(others):
        c = remote(small, small_full.at[me], small_send.at[j], small_recv.at[me], (dp, (me + 1 + j) % groups))
        c.start()
        smalls.append(c)

    def piece_slice(piece, shard, owner):
        return full.at[piece, shard, pl.ds(pl.multiple_of(owner % 8 * part, 16), part)]

    def copy(piece, shard, owner, rsem, dev):
        ref = piece_slice(piece, shard, owner)
        return remote(ref, ref, send_sem, rsem, dev)

    order = []
    for j in range(others):
        pick = 0
        for m in range(groups):
            near = sorted((t for t in range(groups) if t != m), key=lambda t: abs(t - m))
            pick = pick + jnp.where(me == m, near[j], 0)
        order.append(pick)

    def right_copy(piece, shard, src=None):
        dst = piece_slice(piece, shard, dp)
        return remote(dst if src is None else src, dst, right_send.at[piece, shard], z_sem.at[piece, shard], (dp, (me + 1) % groups))

    def left_copy(piece, shard, src=None):
        dst = piece_slice(piece, shard, dp)
        return remote(dst if src is None else src, dst, left_send.at[piece, shard], z_sem.at[piece, shard], (dp, (me + groups - 1) % groups))

    def z_send(piece):
        src = hold.at[piece, pl.ds(pl.multiple_of(dp % 8 * part, 16), part)]
        @pl.when(me + 1 < groups)
        def _():
            right_copy(piece, me, src).start()
        @pl.when(me > 0)
        def _():
            left_copy(piece, me, src).start()

    def route(piece, shard):
        return (piece + shard) % 2

    diag = neighbours(along_x)[2]

    def stage_a(piece):
        for shard in order:
            copy(piece, shard, dp, z_sem.at[piece, shard], (dp, me)).wait_recv()

            @pl.when(jnp.logical_and(shard < me, me + 1 < groups))
            def _():
                right_copy(piece, shard).start()

            @pl.when(jnp.logical_and(shard > me, me > 0))
            def _():
                left_copy(piece, shard).start()

            copy(piece, shard, dp, x_sem.at[piece, shard], (along_x, me)).start()
            copy(piece, shard, dp, y_sem.at[piece, shard], (along_y, me)).start()
            copy(piece, shard, dp, sib_sem, (sib, me)).start()

    def stage_b(piece):
        for shard in order:
            r = route(piece, shard)
            copy(piece, shard, along_x, x_sem.at[piece, shard], (dp, me)).wait_recv()
            copy(piece, shard, along_y, y_sem.at[piece, shard], (dp, me)).wait_recv()
            owner = r * along_x + (1 - r) * along_y
            target = r * along_y + (1 - r) * along_x
            copy(piece, shard, owner, d_sem.at[piece, shard], (target, me)).start()
            copy(piece, shard, along_x, sib_sem, (sib, me)).start()
            copy(piece, shard, along_y, sib_sem, (sib, me)).start()

    def stage_c(piece):
        for shard in order:
            copy(piece, shard, diag, d_sem.at[piece, shard], (dp, me)).wait_recv()
            copy(piece, shard, diag, sib_sem, (sib, me)).start()

    def wait_local(piece):
        for p, c in locals_:
            if p == piece:
                c.wait()
    writes = []
    for piece in range(PIECES):
        wait_local(piece)
        c = pltpu.make_async_copy(hold.at[piece], full.at[piece, me], write_sem.at[piece])
        c.start()
        writes.append(c)
        if piece < AHEAD:
            z_send(piece)

    def body(n, carry):
        @pl.when(n + AHEAD < PIECES)
        def _():
            z_send(n + AHEAD)
        @pl.when(n < PIECES)
        def _():
            stage_a(n)
        @pl.when(jnp.logical_and(n >= LAG, n < PIECES + LAG))
        def _():
            stage_b(n - LAG)
        @pl.when(n >= 2 * LAG)
        def _():
            stage_c(n - 2 * LAG)
        return carry
    lax.fori_loop(0, PIECES + 2 * LAG, body, 0)

    def drain(piece, carry):
        for shard in range(groups):
            @pl.when(jnp.logical_and(shard <= me, me + 1 < groups))
            def _():
                right_copy(piece, shard).wait_send()
            @pl.when(jnp.logical_and(shard >= me, me > 0))
            def _():
                left_copy(piece, shard).wait_send()
        return carry
    lax.fori_loop(0, PIECES, drain, 0)
    wait_local(12)
    for c in writes:
        c.wait()
    for c in smalls:
        c.wait_send()
    for j in range(others):
        shard = (me + 1 + j) % groups
        remote(small, small_full.at[shard], small_send.at[j], small_recv.at[shard], (dp, me)).wait_recv()
    got = full.at[:, pl.ds(0, others), pl.ds(0, 4 * part)]
    remote(got, got, send_sem, sib_sem, (sib, me)).wait_recv()
    sent = full.at[:, pl.ds(0, others), pl.ds(0, 7 * part)]
    remote(sent, sent, send_sem, sib_sem, (sib, me)).wait_send()


def gather(groups, *args):
    conv = args[0]
    rows, cols = conv.shape[1:]
    small = args[-1]
    any_spec = pl.BlockSpec(memory_space=pl.ANY)
    return pl.pallas_call(
        functools.partial(gather_kernel, groups),
        out_shape=(jax.ShapeDtypeStruct((PIECES, groups, rows, cols), conv.dtype),
                   jax.ShapeDtypeStruct((groups,) + small.shape, small.dtype)),
        in_specs=[any_spec] * 9,
        out_specs=(any_spec, any_spec),
        scratch_shapes=[pltpu.VMEM((PIECES, rows, cols), conv.dtype), pltpu.SemaphoreType.DMA((5 + 5 + 2 * groups + 2 + 1,)), pltpu.SemaphoreType.DMA((PIECES,))] +
          [pltpu.SemaphoreType.DMA((PIECES, groups))] * 4 +
          [pltpu.SemaphoreType.DMA(()), pltpu.SemaphoreType.DMA(()), pltpu.SemaphoreType.DMA((PIECES, groups)), pltpu.SemaphoreType.DMA((PIECES, groups)), pltpu.SemaphoreType.DMA((groups,)), pltpu.SemaphoreType.DMA((groups,))],
        compiler_params=pltpu.CompilerParams(collective_id=0, has_side_effects=True, vmem_limit_bytes=24 << 20),
        name="gather",
    )(*args)


EPSILON = 1e-05


def position_table(length, features):
    basis_count = features // 6
    offsets = jnp.arange(2 * length - 1, dtype=jnp.float32) - (length - 1)
    distance = jnp.abs(offsets)[:, None]
    max_range = math.log(length) / math.log(2.0)
    half_life = 2.0 ** jnp.linspace(3.0, max_range, basis_count, dtype=jnp.float32)
    decaying = jnp.exp(-math.log(2.0) / half_life[None, :] * distance)
    widths = 2.0 ** jnp.arange(1, basis_count + 1, dtype=jnp.float32) - 1.0
    central = (widths[None, :] > distance).astype(jnp.float32)
    stddev = length / (2.0 * basis_count)
    centres = jnp.linspace(length / basis_count, length, basis_count, dtype=jnp.float32)
    shape_par = (centres / stddev) ** 2
    rate_par = centres / stddev**2
    safe_dist = jnp.maximum(distance, 1.0)
    log_prob = (shape_par - 1.0) * jnp.log(safe_dist) - rate_par * safe_dist
    log_prob = log_prob - jnp.max(log_prob, axis=0, keepdims=True)
    gamma_feat = jnp.where(distance > 0.5, jnp.exp(log_prob), 0.0)
    symmetric = jnp.concatenate([decaying, central, gamma_feat], 1)
    sign_row = jnp.sign(offsets)[:, None]
    return jnp.concatenate([symmetric, sign_row * symmetric], 1)


def relative_shift(scores):
    row_count = scores.shape[-2]
    span_width = scores.shape[-1]
    leading = scores.shape[:-2]
    padded = jnp.pad(scores, [(0, 0)] * (scores.ndim - 1) + [(1, 0)])
    folded = padded.reshape(leading + (span_width + 1, row_count))[..., 1:, :]
    return folded.reshape(leading + (row_count, span_width))[..., :row_count]


def normalize(values):
    centred = values - jnp.mean(values, -1, keepdims=True)
    inverse = lax.rsqrt(jnp.mean(centred * centred, -1, keepdims=True) + EPSILON)
    return (centred * inverse, inverse)


def norm_back(grad_std, standard, inverse):
    return inverse * (
        grad_std
        - jnp.mean(grad_std, -1, keepdims=True)
        - standard * jnp.mean(grad_std * standard, -1, keepdims=True)
    )


def dot_leading(left_side, right_side):
    return lax.dot_general(
        left_side, right_side, (((0,), (0,)), ((), ())), preferred_element_type=jnp.float32
    )


def dot_trailing(left_side, right_side):
    return lax.dot_general(
        left_side, right_side, (((1,), (1,)), ((), ())), preferred_element_type=jnp.float32
    )


def attention_scores(content_query, key_heads, position_query, position_keys):
    content = jnp.einsum(
        "ihk,jhk->hij", content_query, key_heads, preferred_element_type=jnp.float32
    )
    relative = jnp.einsum(
        "ihk,mhk->him", position_query, position_keys, preferred_element_type=jnp.float32
    )
    return content + relative_shift(relative)


def on_device(
    tokens,
    conv_weight,
    query_weight,
    key_weight,
    value_weight,
    out_weight,
    rel_weight,
    up_weight,
    down_weight,
    gains,
    biases,
    up_bias,
    rel_bias,
    target_table,
    clip_levels,
    window_ids,
    clip_index,
):
    groups = lax.axis_size("fsdp")
    piece_rows = conv_weight.shape[1]
    small_parts = [gains, biases, up_bias, rel_bias]
    small = jnp.concatenate([part.reshape(-1) for part in small_parts])
    small = jnp.pad(small, (0, -small.shape[0] % 1024)).reshape(-1, 128)
    full, small_full = gather(
        groups,
        conv_weight,
        query_weight,
        key_weight,
        value_weight,
        out_weight,
        rel_weight,
        up_weight,
        down_weight,
        small,
    )
    pieces = full.reshape(PIECES, groups * piece_rows, conv_weight.shape[2])
    key_width = query_weight.shape[1]
    conv_full = pieces[:5]
    query_full = pieces[5, :, :key_width]
    key_full = pieces[5, :, key_width : 2 * key_width]
    rel_rows, rel_columns = rel_weight.shape
    rel_full = jnp.concatenate(
        [
            full[5, shard, :rel_rows, 2 * key_width : 2 * key_width + rel_columns]
            for shard in range(groups)
        ],
        1,
    )
    value_full = pieces[6]
    out_full = pieces[7]
    up_full = pieces[8:10]
    down_full = pieces[10:12]
    flat = small_full.reshape(groups, -1)
    taken = 0
    unpacked = []
    for part in small_parts:
        chosen = flat[:, taken : taken + part.size].reshape((groups,) + part.shape)
        unpacked.append(chosen)
        taken += part.size
    gain_rows = jnp.moveaxis(unpacked[0], 0, 1).reshape(gains.shape[0], -1)
    bias_rows = jnp.moveaxis(unpacked[1], 0, 1).reshape(biases.shape[0], -1)
    up_offset = jnp.moveaxis(unpacked[2].reshape(groups, 2, piece_rows), 0, 1).reshape(2, -1)
    rel_offset = jnp.moveaxis(unpacked[3], 0, 1).reshape(2, -1)
    inputs = tokens[0].astype(jnp.float32)
    length = inputs.shape[0]
    model_width = inputs.shape[1]
    tap_count = conv_full.shape[0]
    half_taps = tap_count // 2
    token_total = length * lax.axis_size("dp") * lax.axis_size("fsdp")
    batch_sums = lax.psum((jnp.sum(inputs, 0), jnp.sum(inputs * inputs, 0)), ("dp", "fsdp"))
    centre = batch_sums[0] / token_total
    variance = batch_sums[1] / token_total - centre * centre
    inverse = lax.rsqrt(variance + EPSILON)
    standard = (inputs - centre) * inverse
    normed = standard * gain_rows[0] + bias_rows[0]
    activated = jax.nn.gelu(normed).astype(jnp.bfloat16)
    padded = jnp.pad(activated, ((half_taps, half_taps), (0, 0)))
    stacked = jnp.concatenate(
        [padded[tap_index : tap_index + length] for tap_index in range(tap_count)], 1
    )
    after_conv = (
        inputs
        + jnp.dot(
            stacked,
            conv_full.reshape(tap_count * model_width, model_width),
            preferred_element_type=jnp.float32,
        )
        + bias_rows[1]
    )
    standard_one, inverse_one = normalize(after_conv)
    normed_one = (standard_one * gain_rows[1] + bias_rows[2]).astype(jnp.bfloat16)
    query_raw = jnp.dot(normed_one, query_full, preferred_element_type=jnp.float32)
    key_scale = KEY ** (-0.5)
    content_query = (
        (query_raw * key_scale + rel_offset[0]).astype(jnp.bfloat16).reshape(length, HEADS, -1)
    )
    position_query = (
        (query_raw * key_scale + rel_offset[1]).astype(jnp.bfloat16).reshape(length, HEADS, -1)
    )
    key_heads = (
        jnp.dot(normed_one, key_full, preferred_element_type=jnp.float32)
        .astype(jnp.bfloat16)
        .reshape(length, HEADS, -1)
    )
    value_heads = (
        jnp.dot(normed_one, value_full, preferred_element_type=jnp.float32)
        .astype(jnp.bfloat16)
        .reshape(length, HEADS, -1)
    )
    table = position_table(length, rel_full.shape[0]).astype(jnp.bfloat16)
    position_keys = (
        jnp.dot(table, rel_full, preferred_element_type=jnp.float32)
        .astype(jnp.bfloat16)
        .reshape(table.shape[0], HEADS, -1)
    )
    scores = attention_scores(content_query, key_heads, position_query, position_keys)
    row_peak = jnp.max(scores, -1, keepdims=True)
    normalizer = row_peak + jnp.log(jnp.sum(jnp.exp(scores - row_peak), -1, keepdims=True))
    attention_probs = jnp.exp(scores - normalizer)
    attended = jnp.einsum(
        "hij,jhv->ihv",
        attention_probs.astype(jnp.bfloat16),
        value_heads,
        preferred_element_type=jnp.float32,
    )
    attended = attended.reshape(length, model_width).astype(jnp.bfloat16)
    after_attention = (
        after_conv + jnp.dot(attended, out_full, preferred_element_type=jnp.float32) + bias_rows[3]
    )
    standard_two, inverse_two = normalize(after_attention)
    normed_two = (standard_two * gain_rows[2] + bias_rows[4]).astype(jnp.bfloat16)
    hidden_pre = [
        jnp.dot(normed_two, up_full[half], preferred_element_type=jnp.float32) + up_offset[half]
        for half in range(2)
    ]
    hidden = [jax.nn.gelu(half).astype(jnp.bfloat16) for half in hidden_pre]
    outputs = (
        after_attention
        + jnp.dot(hidden[0], down_full[0], preferred_element_type=jnp.float32)
        + jnp.dot(hidden[1], down_full[1], preferred_element_type=jnp.float32)
        + bias_rows[5]
    )
    target_row = lax.dynamic_index_in_dim(target_table, window_ids[0], 0, keepdims=False)
    levels = jnp.arange(clip_levels.shape[0], dtype=jnp.int32)
    selector = (clip_index[0][:, None] == levels[None, :]).astype(jnp.float32)
    limits = jnp.sum(selector * clip_levels[None, :], 1)[:, None]
    cotangent = jnp.clip(outputs - target_row, -limits, limits).astype(jnp.bfloat16)
    cot_value = cotangent.astype(jnp.float32)
    grad_down_bias = jnp.sum(cot_value, 0)
    pre_grad = []
    for half in range(2):
        hidden_grad = dot_trailing(cotangent, down_full[half])
        gelu_pull = jax.vjp(jax.nn.gelu, hidden_pre[half])[1]
        pre_grad.append(gelu_pull(hidden_grad)[0].astype(jnp.bfloat16))
    grad_up_bias = jnp.stack([jnp.sum(half.astype(jnp.float32), 0) for half in pre_grad])
    grad_up_bias = jnp.moveaxis(grad_up_bias.reshape(2, groups, piece_rows), 0, 1).reshape(-1)
    normed_two_grad = dot_trailing(pre_grad[0], up_full[0]) + dot_trailing(
        pre_grad[1], up_full[1]
    )
    grad_gain_two = jnp.sum(normed_two_grad * standard_two, 0)
    grad_bias_two = jnp.sum(normed_two_grad, 0)
    attention_grad = cot_value + norm_back(
        normed_two_grad * gain_rows[2], standard_two, inverse_two
    )
    branch_grad = attention_grad.astype(jnp.bfloat16)
    grad_out_bias = jnp.sum(branch_grad.astype(jnp.float32), 0)
    attended_grad = (
        dot_trailing(branch_grad, out_full).astype(jnp.bfloat16).reshape(length, HEADS, -1)
    )
    scores = attention_scores(content_query, key_heads, position_query, position_keys)
    attention_probs = jnp.exp(scores - normalizer)
    value_grad = jnp.einsum(
        "hij,ihv->jhv",
        attention_probs.astype(jnp.bfloat16),
        attended_grad,
        preferred_element_type=jnp.float32,
    )
    value_grad = value_grad.reshape(length, model_width).astype(jnp.bfloat16)
    prob_grad = jnp.einsum(
        "ihv,jhv->hij", attended_grad, value_heads, preferred_element_type=jnp.float32
    )
    row_dot = jnp.sum(attention_probs * prob_grad, -1, keepdims=True)
    score_grad = (attention_probs * (prob_grad - row_dot)).astype(jnp.bfloat16)
    content_grad = jnp.einsum(
        "hij,jhk->ihk", score_grad, key_heads, preferred_element_type=jnp.float32
    )
    key_grad = jnp.einsum(
        "hij,ihk->jhk", score_grad, content_query, preferred_element_type=jnp.float32
    )
    key_grad = key_grad.reshape(length, -1).astype(jnp.bfloat16)
    band_zeros = jnp.zeros((HEADS, length, position_keys.shape[0]), jnp.float32)
    shift_pull = jax.vjp(relative_shift, band_zeros)[1]
    band_grad = shift_pull(score_grad.astype(jnp.float32))[0].astype(jnp.bfloat16)
    position_grad = jnp.einsum(
        "him,mhk->ihk", band_grad, position_keys, preferred_element_type=jnp.float32
    )
    table_grad = jnp.einsum(
        "him,ihk->mhk", band_grad, position_query, preferred_element_type=jnp.float32
    )
    table_grad = table_grad.reshape(table.shape[0], -1).astype(jnp.bfloat16)
    grad_rel_bias = jnp.stack(
        [jnp.sum(content_grad, 0).reshape(-1), jnp.sum(position_grad, 0).reshape(-1)]
    )
    query_grad = (
        ((content_grad + position_grad) * key_scale).reshape(length, -1).astype(jnp.bfloat16)
    )
    normed_one_grad = (
        dot_trailing(query_grad, query_full)
        + dot_trailing(key_grad, key_full)
        + dot_trailing(value_grad, value_full)
    )
    grad_gain_one = jnp.sum(normed_one_grad * standard_one, 0)
    grad_bias_one = jnp.sum(normed_one_grad, 0)
    conv_side_grad = attention_grad + norm_back(
        normed_one_grad * gain_rows[1], standard_one, inverse_one
    )
    conv_grad = conv_side_grad.astype(jnp.bfloat16)
    grad_conv_bias = jnp.sum(conv_grad.astype(jnp.float32), 0)
    stacked_grad = dot_trailing(conv_grad, conv_full.reshape(tap_count * model_width, model_width))
    stacked_grad = stacked_grad.reshape(length, tap_count, model_width)
    padded_grad = jnp.zeros((length + 2 * half_taps, model_width), jnp.float32)
    for tap_index in range(tap_count):
        padded_grad = padded_grad.at[tap_index : tap_index + length].add(stacked_grad[:, tap_index])
    activated_grad = padded_grad[half_taps : half_taps + length]
    act_pull = jax.vjp(jax.nn.gelu, normed)[1]
    normed_grad = act_pull(activated_grad)[0]
    totals = lax.psum((jnp.sum(normed_grad * standard, 0), jnp.sum(normed_grad, 0)), ("dp", "fsdp"))
    grad_bn_gain = totals[0]
    grad_bn_bias = totals[1]
    input_grad = conv_side_grad + inverse * (
        normed_grad * gain_rows[0]
        - gain_rows[0] * (grad_bn_bias + standard * grad_bn_gain) / token_total
    )
    ln_gains = jnp.stack([grad_gain_one, grad_gain_two])
    bias_five = jnp.stack(
        [grad_conv_bias, grad_bias_one, grad_out_bias, grad_bias_two, grad_down_bias]
    )
    half_width = 2 * key_width
    projection_grad = dot_leading(normed_one, jnp.concatenate([query_grad, key_grad], 1))
    grad_rel = dot_leading(table, table_grad)
    grad_rel = jnp.moveaxis(grad_rel.reshape(rel_rows, groups, rel_columns), 0, 1)
    grad_rel = jnp.pad(
        grad_rel, ((0, 0), (0, piece_rows - rel_rows), (0, model_width - half_width - rel_columns))
    )
    mixed_grad = jnp.concatenate(
        [projection_grad, grad_rel.reshape(model_width, -1)], 1
    )
    grad_pieces = [
        dot_leading(stacked[:, tap * model_width : (tap + 1) * model_width], conv_grad)
        for tap in range(tap_count)
    ]
    grad_pieces += [
        mixed_grad,
        dot_leading(normed_one, value_grad),
        dot_leading(attended, branch_grad),
        dot_leading(normed_two, pre_grad[0]),
        dot_leading(normed_two, pre_grad[1]),
        dot_leading(hidden[0], cotangent),
        dot_leading(hidden[1], cotangent),
    ]
    grad_pieces = jnp.stack([piece.astype(jnp.bfloat16) for piece in grad_pieces])
    grad_pieces = lax.psum_scatter(grad_pieces, "fsdp", scatter_dimension=1, tiled=True)
    grad_pieces = lax.psum(grad_pieces, "dp").astype(jnp.float32)
    up_grad = jnp.moveaxis(grad_pieces[8:10].reshape(2, piece_rows, groups, piece_rows), 0, 2)
    weight_grads = (
        grad_pieces[:5],
        grad_pieces[5, :, :key_width],
        grad_pieces[5, :, key_width:half_width],
        grad_pieces[6],
        grad_pieces[7],
        grad_pieces[5, :rel_rows, half_width : half_width + rel_columns],
        up_grad.reshape(piece_rows, -1),
        grad_pieces[10:12].reshape(2 * piece_rows, -1),
    )
    parts = (
        lax.psum_scatter(
            ln_gains.astype(jnp.bfloat16), "fsdp", scatter_dimension=1, tiled=True
        ).astype(jnp.float32),
        lax.psum_scatter(
            bias_five.astype(jnp.bfloat16), "fsdp", scatter_dimension=1, tiled=True
        ).astype(jnp.float32),
        lax.psum_scatter(
            grad_up_bias.astype(jnp.bfloat16), "fsdp", scatter_dimension=0, tiled=True
        ).astype(jnp.float32),
        lax.psum_scatter(
            grad_rel_bias.astype(jnp.bfloat16), "fsdp", scatter_dimension=1, tiled=True
        ).astype(jnp.float32),
    )
    reduced = (
        lax.psum(parts[0].astype(jnp.bfloat16), "dp").astype(jnp.float32),
        lax.psum(parts[1].astype(jnp.bfloat16), "dp").astype(jnp.float32),
        lax.psum(parts[2].astype(jnp.bfloat16), "dp").astype(jnp.float32),
        lax.psum(parts[3].astype(jnp.bfloat16), "dp").astype(jnp.float32),
    )
    shard_width = gains.shape[1]
    shard_start = lax.axis_index("fsdp") * shard_width
    bn_gain_shard = lax.dynamic_slice_in_dim(grad_bn_gain, shard_start, shard_width)
    bn_bias_shard = lax.dynamic_slice_in_dim(grad_bn_bias, shard_start, shard_width)
    gains_out = jnp.concatenate([bn_gain_shard[None], reduced[0]], 0)
    biases_out = jnp.concatenate([bn_bias_shard[None], reduced[1]], 0)
    return (
        outputs.astype(jnp.bfloat16)[None],
        input_grad.astype(jnp.bfloat16)[None],
        *weight_grads,
        gains_out,
        biases_out,
        reduced[2],
        reduced[3],
    )


def solution(mesh):
    placed = (
        P(("dp", "fsdp"), None, None),
        P(None, "fsdp", None),
        P("fsdp", None),
        P("fsdp", None),
        P("fsdp", None),
        P("fsdp", None),
        P(None, "fsdp"),
        P("fsdp", None),
        P("fsdp", None),
        P(None, "fsdp"),
        P(None, "fsdp"),
        P("fsdp"),
        P(None, "fsdp"),
        P(),
        P(),
        P(("dp", "fsdp")),
        P(("dp", "fsdp"), None),
    )
    return jax.shard_map(
        on_device,
        mesh=mesh,
        in_specs=placed,
        out_specs=(
            P(("dp", "fsdp"), None, None),
            P(("dp", "fsdp"), None, None),
            P(None, "fsdp", None),
            P("fsdp", None),
            P("fsdp", None),
            P("fsdp", None),
            P("fsdp", None),
            P(None, "fsdp"),
            P("fsdp", None),
            P("fsdp", None),
            P(None, "fsdp"),
            P(None, "fsdp"),
            P("fsdp"),
            P(None, "fsdp"),
        ),
        check_vma=False,
    )
```

```python
import functools
import math

import jax
import jax.numpy as jnp
from jax import lax
from jax.experimental import pallas as pl
from jax.experimental.pallas import tpu as pltpu
from jax.sharding import PartitionSpec as P

HEADS = 8
KEY = 64
MESH = pl.DeviceIdType.MESH
AHEAD = 2


def neighbours(dp):
    core = dp % 2
    along_x = dp // 2 % 2
    along_y = dp // 4 % 2
    return dp + 1 - 2 * core, dp + 2 - 4 * along_x, dp + 4 - 8 * along_y


def remote(src, dst, send_sem, recv_sem, device):
    return pltpu.make_async_remote_copy(
        src_ref=src,
        dst_ref=dst,
        send_sem=send_sem,
        recv_sem=recv_sem,
        device_id=device,
        device_id_type=MESH,
    )


def meet(peers):
    barrier = pltpu.get_barrier_semaphore()
    for peer in peers:
        pl.semaphore_signal(barrier, inc=1, device_id=peer, device_id_type=MESH)
    pl.semaphore_wait(barrier, len(peers))


def peers_of(groups, blocks):
    dp = lax.axis_index("dp")
    me = lax.axis_index("fsdp")
    near = [(device, me) for device in neighbours(dp)]
    shards = [(dp, (me + 1 + j) % groups) for j in range(groups - 1)]
    far = [((dp + 8 * (1 + j)) % (8 * blocks), me) for j in range(blocks - 1)]
    return near, shards, far


def sum_steps(groups, blocks, vector, total, near_got, sums, shard_got, block_got, sems):
    near_send, near_recv, shard_send, shard_recv, block_send, block_recv = sems
    me = lax.axis_index("fsdp")
    block = lax.axis_index("dp") // 8
    near, shards, far = peers_of(groups, blocks)

    def near_copy(step):
        src = vector if step == 0 else sums.at[step - 1]
        return remote(
            src, near_got.at[step], near_send.at[step], near_recv.at[step], near[step]
        )

    def fold(step):
        copy = near_copy(step)
        copy.wait()
        held = vector[...] if step == 0 else sums[step - 1]
        sums[step] = held + near_got[step]

    def shard_copy(j):
        return remote(
            sums.at[2], shard_got.at[me], shard_send.at[j], shard_recv.at[me], shards[j]
        )

    def block_copy(j):
        return remote(
            sums.at[3], block_got.at[block], block_send.at[j], block_recv.at[block], far[j]
        )

    def start():
        near_copy(0).start()

    def second():
        fold(0)
        near_copy(1).start()

    def third():
        fold(1)
        near_copy(2).start()

    def fourth():
        fold(2)
        for j in range(groups - 1):
            shard_copy(j).start()
        shard_got[me] = sums[2]

    def fifth():
        for j in range(groups - 1):
            shard_copy(j).wait_send()
            other = (me + 1 + j) % groups
            remote(
                sums.at[2], shard_got.at[other], shard_send.at[j], shard_recv.at[other], shards[j]
            ).wait_recv()
        added = shard_got[0]
        for shard in range(1, groups):
            added = added + shard_got[shard]
        sums[3] = added
        for j in range(blocks - 1):
            block_copy(j).start()
        block_got[block] = added

    def sixth():
        for j in range(blocks - 1):
            block_copy(j).wait_send()
            other = (block + 1 + j) % blocks
            remote(
                sums.at[3], block_got.at[other], block_send.at[j], block_recv.at[other], far[j]
            ).wait_recv()
        added = block_got[0]
        for other in range(1, blocks):
            added = added + block_got[other]
        total[...] = added

    return [start, second, third, fourth, fifth, sixth]


def sum_scratch(groups, blocks, shape):
    return [
        pltpu.VMEM((3,) + shape, jnp.float32),
        pltpu.VMEM((4,) + shape, jnp.float32),
        pltpu.VMEM((groups,) + shape, jnp.float32),
        pltpu.VMEM((blocks,) + shape, jnp.float32),
        pltpu.SemaphoreType.DMA((3,)),
        pltpu.SemaphoreType.DMA((3,)),
        pltpu.SemaphoreType.DMA((groups,)),
        pltpu.SemaphoreType.DMA((groups,)),
        pltpu.SemaphoreType.DMA((blocks,)),
        pltpu.SemaphoreType.DMA((blocks,)),
    ]


def gather_kernel(groups, blocks, *refs):
    weights = refs[:8]
    conv, query, key, value, out, up, down, rel = weights
    small, stats = refs[8:10]
    outs = refs[10:21]
    rel_full, small_full, stat_total = outs[8:]
    hold, hold_mixed, local_sem, write_sem = refs[21:25]
    z_sem, x_sem, y_sem, d_sem, sib_sem, send_sem, right_send, left_send = refs[25:33]
    rel_send, rel_recv, small_send, small_recv = refs[33:37]
    near_got, sums, shard_got, block_got = refs[37:41]
    sum_sems = refs[41:47]
    dp = lax.axis_index("dp")
    me = lax.axis_index("fsdp")
    near, shards, far = peers_of(groups, blocks)
    sib, along_x, along_y = neighbours(dp)
    rows = conv.shape[1]
    part = rows // 8
    others = groups - 1
    pieces = [outs[0].at[tap] for tap in range(5)] + list(outs[1:8])
    count = len(pieces)
    holds = [hold.at[i] for i in range(5)] + [hold_mixed] + [hold.at[i] for i in range(5, 11)]

    pending = [[] for _ in range(count)]
    started = [0]

    def load(src, dst, piece):
        copy = pltpu.make_async_copy(src, dst, local_sem.at[started[0]])
        copy.start()
        started[0] += 1
        pending[piece].append(copy)

    for tap in range(5):
        load(conv.at[tap], holds[tap], tap)
    width = query.shape[1]
    load(query, hold_mixed.at[:, pl.ds(0, width)], 5)
    load(key, hold_mixed.at[:, pl.ds(width, width)], 5)
    load(value, holds[6], 6)
    load(out, holds[7], 7)
    for half in range(2):
        for shard in range(groups):
            load(
                up.at[:, pl.ds((shard * 2 + half) * rows, rows)],
                holds[8 + half].at[:, pl.ds(shard * rows, rows)],
                8 + half,
            )
    for half in range(2):
        load(down.at[pl.ds(half * rows, rows)], holds[10 + half], 10 + half)

    meet(near + shards + far)

    summing = sum_steps(
        groups, blocks, stats, stat_total, near_got, sums, shard_got, block_got, sum_sems
    )
    summing[0]()

    for j in range(others):
        remote(
            rel, rel_full.at[me], rel_send.at[j], rel_recv.at[me], shards[j]
        ).start()
        remote(
            small, small_full.at[me], small_send.at[j], small_recv.at[me], shards[j]
        ).start()
    rel_full[me] = rel[...]
    small_full[me] = small[...]

    def slice_of(piece, shard, owner):
        return pieces[piece].at[shard, pl.ds(pl.multiple_of(owner % 8 * part, 16), part)]

    def copy_of(piece, shard, owner, recv_sem, device):
        ref = slice_of(piece, shard, owner)
        return remote(ref, ref, send_sem.at[piece], recv_sem, (device, me))

    order = []
    for j in range(others):
        pick = 0
        for m in range(groups):
            nearest = sorted((t for t in range(groups) if t != m), key=lambda t: abs(t - m))
            pick = pick + jnp.where(me == m, nearest[j], 0)
        order.append(pick)

    def right_copy(piece, shard, src=None):
        dst = slice_of(piece, shard, dp)
        return remote(
            dst if src is None else src,
            dst,
            right_send.at[piece, shard],
            z_sem.at[piece, shard],
            (dp, (me + 1) % groups),
        )

    def left_copy(piece, shard, src=None):
        dst = slice_of(piece, shard, dp)
        return remote(
            dst if src is None else src,
            dst,
            left_send.at[piece, shard],
            z_sem.at[piece, shard],
            (dp, (me + groups - 1) % groups),
        )

    def z_send(piece):
        src = holds[piece].at[pl.ds(pl.multiple_of(dp % 8 * part, 16), part)]

        @pl.when(me + 1 < groups)
        def _():
            right_copy(piece, me, src).start()

        @pl.when(me > 0)
        def _():
            left_copy(piece, me, src).start()

    diagonal = neighbours(along_x)[2]

    def stage_a(piece):
        for shard in order:
            copy_of(piece, shard, dp, z_sem.at[piece, shard], dp).wait_recv()

            @pl.when(jnp.logical_and(shard < me, me + 1 < groups))
            def _():
                right_copy(piece, shard).start()

            @pl.when(jnp.logical_and(shard > me, me > 0))
            def _():
                left_copy(piece, shard).start()

            copy_of(piece, shard, dp, x_sem.at[piece, shard], along_x).start()
            copy_of(piece, shard, dp, y_sem.at[piece, shard], along_y).start()
            copy_of(piece, shard, dp, sib_sem.at[piece], sib).start()

    def stage_b(piece):
        for shard in order:
            route = (piece + shard) % 2
            copy_of(piece, shard, along_x, x_sem.at[piece, shard], dp).wait_recv()
            copy_of(piece, shard, along_y, y_sem.at[piece, shard], dp).wait_recv()
            owner = route * along_x + (1 - route) * along_y
            target = route * along_y + (1 - route) * along_x
            copy_of(piece, shard, owner, d_sem.at[piece, shard], target).start()
            copy_of(piece, shard, along_x, sib_sem.at[piece], sib).start()
            copy_of(piece, shard, along_y, sib_sem.at[piece], sib).start()

    def stage_c(piece):
        for shard in order:
            copy_of(piece, shard, diagonal, d_sem.at[piece, shard], dp).wait_recv()
            copy_of(piece, shard, diagonal, sib_sem.at[piece], sib).start()

    writes = []
    for piece in range(count):
        for copy in pending[piece]:
            copy.wait()
        copy = pltpu.make_async_copy(holds[piece], pieces[piece].at[me], write_sem.at[piece])
        copy.start()
        writes.append(copy)
        if piece < AHEAD:
            z_send(piece)

    for n in range(count + 2):
        if n + AHEAD < count:
            z_send(n + AHEAD)
        if n < count:
            stage_a(n)
        if 1 <= n <= count:
            stage_b(n - 1)
        if n >= 2:
            stage_c(n - 2)
        if 1 <= n < len(summing):
            summing[n]()

    for piece in range(count):
        for shard in range(groups):

            @pl.when(jnp.logical_and(shard <= me, me + 1 < groups))
            def _():
                right_copy(piece, shard).wait_send()

            @pl.when(jnp.logical_and(shard >= me, me > 0))
            def _():
                left_copy(piece, shard).wait_send()

        writes[piece].wait()
        got = pieces[piece].at[pl.ds(0, others), pl.ds(0, 4 * part)]
        remote(got, got, send_sem.at[piece], sib_sem.at[piece], (sib, me)).wait_recv()
        sent = pieces[piece].at[pl.ds(0, others), pl.ds(0, 7 * part)]
        remote(sent, sent, send_sem.at[piece], sib_sem.at[piece], (sib, me)).wait_send()
    for j in range(others):
        shard = (me + 1 + j) % groups
        remote(rel, rel_full.at[shard], rel_send.at[j], rel_recv.at[shard], shards[j]).wait()
        remote(
            small, small_full.at[shard], small_send.at[j], small_recv.at[shard], shards[j]
        ).wait()


def gather(groups, blocks, weights, small, stats):
    conv, query = weights[:2]
    rel = weights[7]
    taps, rows, columns = conv.shape
    dtype = conv.dtype
    kept = pl.BlockSpec(memory_space=pl.ANY)
    inside = pl.BlockSpec(memory_space=pltpu.VMEM)
    full = jax.ShapeDtypeStruct((groups, rows, columns), dtype)
    count = taps + 7
    grid_sems = [pltpu.SemaphoreType.DMA((count, groups))] * 4
    return pl.pallas_call(
        functools.partial(gather_kernel, groups, blocks),
        out_shape=(
            jax.ShapeDtypeStruct((taps, groups, rows, columns), dtype),
            jax.ShapeDtypeStruct((groups, rows, 2 * query.shape[1]), dtype),
            *([full] * 6),
            jax.ShapeDtypeStruct((groups,) + rel.shape, dtype),
            jax.ShapeDtypeStruct((groups,) + small.shape, jnp.float32),
            jax.ShapeDtypeStruct(stats.shape, jnp.float32),
        ),
        in_specs=[kept] * 7 + [inside] * 3,
        out_specs=[kept] * 8 + [inside] * 3,
        scratch_shapes=[
            pltpu.VMEM((count - 1, rows, columns), dtype),
            pltpu.VMEM((rows, 2 * query.shape[1]), dtype),
            pltpu.SemaphoreType.DMA((taps + 6 + 2 * groups,)),
            pltpu.SemaphoreType.DMA((count,)),
            *grid_sems,
            pltpu.SemaphoreType.DMA((count,)),
            pltpu.SemaphoreType.DMA((count,)),
            *grid_sems[:2],
            *([pltpu.SemaphoreType.DMA((groups,))] * 4),
            *sum_scratch(groups, blocks, stats.shape),
        ],
        compiler_params=pltpu.CompilerParams(
            collective_id=0, has_side_effects=True, vmem_limit_bytes=24 << 20
        ),
        name="gather",
    )(*weights, small, stats)


def reduce_kernel(groups, blocks, rel_at, *refs):
    lefts = refs[:6]
    lefts_sib = refs[6:12]
    conv_right, conv_right_sib = refs[12:14]
    rights = refs[14:21]
    rights_sib = refs[21:28]
    rel_grad, vector = refs[28:30]
    out, total = refs[30:32]
    left_hold, right_hold, grad, x_one, y_one, x_two, y_two, shard_got, block_got, partial, done = refs[32:43]
    load_sem = refs[43]
    x1s, y1s, x2s, y2s, x1r, y1r, x2r, y2r = refs[44:52]
    shard_send, shard_recv, block_send, block_recv = refs[52:56]
    write_sem, send_sem, ax, ay, ad, sib_sem = refs[56:62]
    sum_bufs = refs[62:66]
    sum_sems = refs[66:72]

    dp = lax.axis_index("dp")
    me = lax.axis_index("fsdp")
    near, shards, far = peers_of(groups, blocks)
    sib, along_x, along_y = neighbours(dp)
    core = dp % 2
    at_x = dp // 2 % 2
    at_y = dp // 4 % 2
    block = dp // 8
    slots = grad.shape[0]
    part = grad.shape[4]
    width = grad.shape[5]
    half = width // 2
    rows = 4 * part
    count = out.shape[0]
    others = groups - 1
    first = pl.ds(0, half)
    last = pl.ds(half, half)
    left_of = [0] * 5 + [1, 1, 2, 3, 3, 4, 5]

    def loads(piece, slot):
        right = conv_right.at[piece] if piece < 5 else rights[piece - 5]
        right_sib = conv_right_sib.at[piece] if piece < 5 else rights_sib[piece - 5]
        pairs = (
            (lefts[left_of[piece]], left_hold.at[slot, 0]),
            (lefts_sib[left_of[piece]], left_hold.at[slot, 1]),
            (right, right_hold.at[slot, 0]),
            (right_sib, right_hold.at[slot, 1]),
        )
        return [
            pltpu.make_async_copy(src, dst, load_sem.at[slot, i])
            for i, (src, dst) in enumerate(pairs)
        ]

    for copy in loads(0, 0):
        copy.start()

    meet(near + shards + far)

    summing = sum_steps(groups, blocks, vector, total, *sum_bufs, sum_sems)

    def one(piece):
        slot = piece % slots
        return (
            remote(
                grad.at[slot, :, :, 1 - at_x, :, first],
                x_one.at[piece],
                x1s.at[piece],
                x1r.at[piece],
                (along_x, me),
            ),
            remote(
                grad.at[slot, :, 1 - at_y, :, :, last],
                y_one.at[piece],
                y1s.at[piece],
                y1r.at[piece],
                (along_y, me),
            ),
        )

    def two(piece):
        slot = piece % slots
        return (
            remote(
                grad.at[slot, :, 1 - at_y, at_x, :, first],
                y_two.at[piece],
                y2s.at[piece],
                y2r.at[piece],
                (along_y, me),
            ),
            remote(
                grad.at[slot, :, at_y, 1 - at_x, :, last],
                x_two.at[piece],
                x2s.at[piece],
                x2r.at[piece],
                (along_x, me),
            ),
        )

    def shard_copy(piece, j):
        other = (me + 1 + j) % groups
        return remote(
            grad.at[piece % slots, other, at_y, at_x],
            shard_got.at[piece, me],
            shard_send.at[piece, j],
            shard_recv.at[piece, me],
            (dp, other),
        )

    def shard_arrival(piece, j):
        other = (me + 1 + j) % groups
        return remote(
            grad.at[piece % slots, other, at_y, at_x],
            shard_got.at[piece, other],
            shard_send.at[piece, j],
            shard_recv.at[piece, other],
            (dp, other),
        )

    def block_copy(piece, j):
        return remote(
            partial.at[piece],
            block_got.at[piece, block],
            block_send.at[piece, j],
            block_recv.at[piece, block],
            far[j],
        )

    def block_arrival(piece, j):
        other = (block + 1 + j) % blocks
        return remote(
            partial.at[piece],
            block_got.at[piece, other],
            block_send.at[piece, j],
            block_recv.at[piece, other],
            far[j],
        )

    def place(piece, owner):
        return out.at[
            piece,
            pl.ds(pl.multiple_of(owner % 8 // 2 * part, 16), part),
            pl.ds(pl.multiple_of(core * width, 128), width),
        ]

    def spread(piece, src, owner, recv_sem, device):
        return remote(src, place(piece, owner), send_sem.at[piece], recv_sem, (device, me))

    def forward(piece, owner, recv_sem, device):
        return spread(piece, place(piece, owner), owner, recv_sem, device)

    diagonal = neighbours(along_x)[2]

    def produce(piece):
        slot = piece % slots
        hold = piece % 2

        def shard_body(shard, carry):
            columns = pl.ds(pl.multiple_of(shard * rows, 128), rows)
            value = dot_leading(left_hold[hold, 0, :, columns], right_hold[hold, 0])
            value = value + dot_leading(left_hold[hold, 1, :, columns], right_hold[hold, 1])
            grad[slot, shard] = value.astype(grad.dtype).reshape(2, 2, part, width)
            return carry

        lax.fori_loop(0, groups, shard_body, 0)

        @pl.when(jnp.logical_and(piece == 5, core == 1))
        def _():
            for shard in range(groups):
                grad[slot, shard, 0, :, :, pl.ds(rel_at, rel_grad.shape[3])] = rel_grad[shard]

    def add(piece_slot, ref, columns, *index):
        ahead = grad[(piece_slot,) + index + (slice(None), columns)]
        return ahead.astype(jnp.float32) + ref.astype(jnp.float32)

    def body(n, carry):
        @pl.when(n < count)
        def _():
            @pl.when(n >= slots)
            def _():
                old = n - slots
                for copy in one(old) + two(old):
                    copy.wait_send()
                for j in range(others):
                    shard_copy(old, j).wait_send()

            for piece in range(count):

                @pl.when(n == piece)
                def _():
                    for copy in loads(piece, piece % 2):
                        copy.wait()
                    if piece + 1 < count:
                        for copy in loads(piece + 1, (piece + 1) % 2):
                            copy.start()

            produce(n)
            for copy in one(n):
                copy.start()

        @pl.when(jnp.logical_and(n >= 1, n < count + 1))
        def _():
            piece = n - 1
            slot = piece % slots
            for copy in one(piece):
                copy.wait_recv()

            def shard_body(shard, carry):
                for other in range(2):
                    value = add(slot, x_one[piece, shard, other], first, shard, other, at_x)
                    grad[slot, shard, other, at_x, :, first] = value.astype(grad.dtype)
                    value = add(slot, y_one[piece, shard, other], last, shard, at_y, other)
                    grad[slot, shard, at_y, other, :, last] = value.astype(grad.dtype)
                return carry

            lax.fori_loop(0, groups, shard_body, 0)
            for copy in two(piece):
                copy.start()

        @pl.when(jnp.logical_and(n >= 2, n < count + 2))
        def _():
            piece = n - 2
            slot = piece % slots
            for copy in two(piece):
                copy.wait_recv()

            def shard_body(shard, carry):
                value = add(slot, y_two[piece, shard], first, shard, at_y, at_x)
                grad[slot, shard, at_y, at_x, :, first] = value.astype(grad.dtype)
                value = add(slot, x_two[piece, shard], last, shard, at_y, at_x)
                grad[slot, shard, at_y, at_x, :, last] = value.astype(grad.dtype)
                return carry

            lax.fori_loop(0, groups, shard_body, 0)
            for j in range(others):
                shard_copy(piece, j).start()

        @pl.when(jnp.logical_and(n >= 3, n < count + 3))
        def _():
            piece = n - 3
            value = grad[piece % slots, me, at_y, at_x].astype(jnp.float32)
            for j in range(others):
                shard_arrival(piece, j).wait_recv()
                value = value + shard_got[piece, (me + 1 + j) % groups].astype(jnp.float32)
            if blocks > 1:
                partial[piece] = value.astype(partial.dtype)
                block_got[piece, block] = value.astype(partial.dtype)
                for j in range(blocks - 1):
                    block_copy(piece, j).start()
                for j in range(blocks - 1):
                    block_copy(piece, j).wait_send()
                    block_arrival(piece, j).wait_recv()
                value = block_got[piece, 0].astype(jnp.float32)
                for other in range(1, blocks):
                    value = value + block_got[piece, other].astype(jnp.float32)
            done[piece] = value.astype(done.dtype)
            pltpu.make_async_copy(done.at[piece], place(piece, dp), write_sem.at[piece]).start()
            spread(piece, done.at[piece], dp, ax.at[piece], along_x).start()
            spread(piece, done.at[piece], dp, ay.at[piece], along_y).start()
            spread(piece, done.at[piece], dp, sib_sem.at[piece], sib).start()

        @pl.when(jnp.logical_and(n >= 4, n < count + 4))
        def _():
            piece = n - 4
            route = piece % 2
            forward(piece, along_x, ax.at[piece], dp).wait_recv()
            forward(piece, along_y, ay.at[piece], dp).wait_recv()
            owner = route * along_x + (1 - route) * along_y
            target = route * along_y + (1 - route) * along_x
            forward(piece, owner, ad.at[piece], target).start()
            forward(piece, along_x, sib_sem.at[piece], sib).start()
            forward(piece, along_y, sib_sem.at[piece], sib).start()

        @pl.when(n >= 5)
        def _():
            piece = n - 5
            forward(piece, diagonal, ad.at[piece], dp).wait_recv()
            forward(piece, diagonal, sib_sem.at[piece], sib).start()

        for step in range(len(summing)):

            @pl.when(n == step)
            def _():
                summing[step]()

        return carry

    lax.fori_loop(0, count + 5, body, 0)

    def drain(piece, carry):
        @pl.when(piece >= count - slots)
        def _():
            for copy in one(piece) + two(piece):
                copy.wait_send()
            for j in range(others):
                shard_copy(piece, j).wait_send()

        pltpu.make_async_copy(done.at[piece], place(piece, dp), write_sem.at[piece]).wait()
        got = out.at[piece, :, pl.ds(0, width)]
        remote(got, got, send_sem.at[piece], sib_sem.at[piece], (sib, me)).wait_recv()
        sent = out.at[piece, pl.ds(0, 7 * part // 2), :]
        remote(sent, sent, send_sem.at[piece], sib_sem.at[piece], (sib, me)).wait_send()
        return carry

    lax.fori_loop(0, count, drain, 0)


def reduce(
    groups,
    blocks,
    rel_at,
    lefts,
    lefts_sib,
    conv_right,
    conv_right_sib,
    rights,
    rights_sib,
    rel_grad,
    vector,
):
    bins, columns = lefts[0].shape
    width = columns // 2
    rows = columns // groups
    part = rows // 4
    dtype = lefts[0].dtype
    taps = conv_right.shape[0]
    count = taps + len(rights)
    slots = 5
    kept = pl.BlockSpec(memory_space=pl.ANY)
    inside = pl.BlockSpec(memory_space=pltpu.VMEM)
    each = pltpu.SemaphoreType.DMA((count,))
    return pl.pallas_call(
        functools.partial(reduce_kernel, groups, blocks, rel_at),
        out_shape=(
            jax.ShapeDtypeStruct((count, rows, columns), dtype),
            jax.ShapeDtypeStruct(vector.shape, jnp.float32),
        ),
        in_specs=[kept] * 28 + [inside] * 2,
        out_specs=[kept, inside],
        scratch_shapes=[
            pltpu.VMEM((2, 2, bins, columns), dtype),
            pltpu.VMEM((2, 2, bins, width), dtype),
            pltpu.VMEM((slots, groups, 2, 2, part, width), dtype),
            pltpu.VMEM((count, groups, 2, part, width // 2), dtype),
            pltpu.VMEM((count, groups, 2, part, width // 2), dtype),
            pltpu.VMEM((count, groups, part, width // 2), dtype),
            pltpu.VMEM((count, groups, part, width // 2), dtype),
            pltpu.VMEM((count, groups, part, width), dtype),
            pltpu.VMEM((count if blocks > 1 else 1, blocks, part, width), dtype),
            pltpu.VMEM((count if blocks > 1 else 1, part, width), dtype),
            pltpu.VMEM((count, part, width), dtype),
            pltpu.SemaphoreType.DMA((2, 4)),
            *([each] * 8),
            pltpu.SemaphoreType.DMA((count, groups)),
            pltpu.SemaphoreType.DMA((count, groups)),
            pltpu.SemaphoreType.DMA((count, blocks)),
            pltpu.SemaphoreType.DMA((count, blocks)),
            *([each] * 6),
            *sum_scratch(groups, blocks, vector.shape),
        ],
        compiler_params=pltpu.CompilerParams(
            collective_id=1, has_side_effects=True, vmem_limit_bytes=60 << 20
        ),
        name="reduce",
    )(*lefts, *lefts_sib, conv_right, conv_right_sib, *rights, *rights_sib, rel_grad, vector)


EPSILON = 1e-05


def position_table(length, features):
    basis_count = features // 6
    offsets = jnp.arange(2 * length - 1, dtype=jnp.float32) - (length - 1)
    distance = jnp.abs(offsets)[:, None]
    max_range = math.log(length) / math.log(2.0)
    half_life = 2.0 ** jnp.linspace(3.0, max_range, basis_count, dtype=jnp.float32)
    decaying = jnp.exp(-math.log(2.0) / half_life[None, :] * distance)
    widths = 2.0 ** jnp.arange(1, basis_count + 1, dtype=jnp.float32) - 1.0
    central = (widths[None, :] > distance).astype(jnp.float32)
    stddev = length / (2.0 * basis_count)
    centres = jnp.linspace(length / basis_count, length, basis_count, dtype=jnp.float32)
    shape_par = (centres / stddev) ** 2
    rate_par = centres / stddev**2
    safe_dist = jnp.maximum(distance, 1.0)
    log_prob = (shape_par - 1.0) * jnp.log(safe_dist) - rate_par * safe_dist
    log_prob = log_prob - jnp.max(log_prob, axis=0, keepdims=True)
    gamma_feat = jnp.where(distance > 0.5, jnp.exp(log_prob), 0.0)
    symmetric = jnp.concatenate([decaying, central, gamma_feat], 1)
    sign_row = jnp.sign(offsets)[:, None]
    return jnp.concatenate([symmetric, sign_row * symmetric], 1)


def relative_shift(scores):
    row_count = scores.shape[-2]
    span_width = scores.shape[-1]
    leading = scores.shape[:-2]
    padded = jnp.pad(scores, [(0, 0)] * (scores.ndim - 1) + [(1, 0)])
    folded = padded.reshape(leading + (span_width + 1, row_count))[..., 1:, :]
    return folded.reshape(leading + (row_count, span_width))[..., :row_count]


def normalize(values):
    centred = values - jnp.mean(values, -1, keepdims=True)
    inverse = lax.rsqrt(jnp.mean(centred * centred, -1, keepdims=True) + EPSILON)
    return (centred * inverse, inverse)


def norm_back(grad_std, standard, inverse):
    return inverse * (
        grad_std
        - jnp.mean(grad_std, -1, keepdims=True)
        - standard * jnp.mean(grad_std * standard, -1, keepdims=True)
    )


def dot_leading(left_side, right_side):
    return lax.dot_general(
        left_side, right_side, (((0,), (0,)), ((), ())), preferred_element_type=jnp.float32
    )


def dot_trailing(left_side, right_side):
    return lax.dot_general(
        left_side, right_side, (((1,), (1,)), ((), ())), preferred_element_type=jnp.float32
    )


def attention_scores(content_query, key_heads, position_query, position_keys):
    content = jnp.einsum(
        "ihk,jhk->hij", content_query, key_heads, preferred_element_type=jnp.float32
    )
    relative = jnp.einsum(
        "ihk,mhk->him", position_query, position_keys, preferred_element_type=jnp.float32
    )
    return content + relative_shift(relative)


def on_device(
    tokens,
    conv_weight,
    query_weight,
    key_weight,
    value_weight,
    out_weight,
    rel_weight,
    up_weight,
    down_weight,
    gains,
    biases,
    up_bias,
    rel_bias,
    target_table,
    clip_levels,
    window_ids,
    clip_index,
):
    groups = lax.axis_size("fsdp")
    blocks = lax.axis_size("dp") // 8
    core = lax.axis_index("dp") % 2
    pairs = [(i, i + 1 - 2 * (i % 2)) for i in range(lax.axis_size("dp"))]
    tap_count, piece_rows, model_width = conv_weight.shape
    half_taps = tap_count // 2
    half_width = model_width // 2
    key_width = query_weight.shape[1]
    rel_rows, rel_columns = rel_weight.shape
    inputs = tokens[0].astype(jnp.float32)
    length = inputs.shape[0]
    token_total = length * lax.axis_size("dp") * lax.axis_size("fsdp")

    def exchange(array):
        return lax.ppermute(array, "dp", pairs)

    def own_half(array):
        return lax.dynamic_slice_in_dim(array, core * half_width, half_width, 1)

    def sib_half(array):
        return exchange(
            lax.dynamic_slice_in_dim(array, (1 - core) * half_width, half_width, 1)
        )

    small_parts = [gains, biases, up_bias, rel_bias]
    small = jnp.concatenate([part.reshape(-1) for part in small_parts])
    small = jnp.pad(small, (0, -small.shape[0] % 1024)).reshape(-1, 128)
    stats = jnp.concatenate([jnp.sum(inputs, 0), jnp.sum(inputs * inputs, 0)]).reshape(-1, 128)
    (
        conv_full,
        mixed_full,
        value_full,
        out_full,
        up_first,
        up_last,
        down_first,
        down_last,
        rel_full,
        small_full,
        stats,
    ) = gather(
        groups,
        blocks,
        [
            conv_weight,
            query_weight,
            key_weight,
            value_weight,
            out_weight,
            up_weight,
            down_weight,
            rel_weight,
        ],
        small,
        stats,
    )
    conv_full = conv_full.reshape(tap_count, model_width, model_width)
    mixed_full = mixed_full.reshape(model_width, -1)
    value_full = value_full.reshape(model_width, -1)
    out_full = out_full.reshape(model_width, -1)
    up_full = [up_first.reshape(model_width, -1), up_last.reshape(model_width, -1)]
    down_full = [down_first.reshape(model_width, -1), down_last.reshape(model_width, -1)]
    rel_full = jnp.concatenate([rel_full[shard] for shard in range(groups)], 1)
    flat = small_full.reshape(groups, -1)
    taken = 0
    unpacked = []
    for part in small_parts:
        chosen = flat[:, taken : taken + part.size].reshape((groups,) + part.shape)
        unpacked.append(chosen)
        taken += part.size
    gain_rows = jnp.moveaxis(unpacked[0], 0, 1).reshape(gains.shape[0], -1)
    bias_rows = jnp.moveaxis(unpacked[1], 0, 1).reshape(biases.shape[0], -1)
    up_offset = jnp.moveaxis(unpacked[2].reshape(groups, 2, piece_rows), 0, 1).reshape(2, -1)
    rel_offset = jnp.moveaxis(unpacked[3], 0, 1).reshape(2, -1)
    batch_sums = stats.reshape(2, -1)
    centre = batch_sums[0] / token_total
    variance = batch_sums[1] / token_total - centre * centre
    inverse = lax.rsqrt(variance + EPSILON)
    standard = (inputs - centre) * inverse
    normed = standard * gain_rows[0] + bias_rows[0]
    activated = jax.nn.gelu(normed).astype(jnp.bfloat16)
    padded = jnp.pad(activated, ((half_taps, half_taps), (0, 0)))
    stacked = jnp.concatenate([padded[tap : tap + length] for tap in range(tap_count)], 1)
    conv_out = jnp.dot(
        stacked, conv_full.reshape(-1, model_width), preferred_element_type=jnp.float32
    )
    after_conv = inputs + conv_out + bias_rows[1]
    standard_one, inverse_one = normalize(after_conv)
    normed_one = (standard_one * gain_rows[1] + bias_rows[2]).astype(jnp.bfloat16)
    mixed_raw = jnp.dot(normed_one, mixed_full, preferred_element_type=jnp.float32)
    query_raw = mixed_raw[:, :key_width]
    key_scale = KEY ** (-0.5)
    content_query = (
        (query_raw * key_scale + rel_offset[0]).astype(jnp.bfloat16).reshape(length, HEADS, -1)
    )
    position_query = (
        (query_raw * key_scale + rel_offset[1]).astype(jnp.bfloat16).reshape(length, HEADS, -1)
    )
    key_heads = mixed_raw[:, key_width:].astype(jnp.bfloat16).reshape(length, HEADS, -1)
    value_heads = (
        jnp.dot(normed_one, value_full, preferred_element_type=jnp.float32)
        .astype(jnp.bfloat16)
        .reshape(length, HEADS, -1)
    )
    table = position_table(length, rel_full.shape[0]).astype(jnp.bfloat16)
    position_keys = (
        jnp.dot(table, rel_full, preferred_element_type=jnp.float32)
        .astype(jnp.bfloat16)
        .reshape(table.shape[0], HEADS, -1)
    )
    scores = attention_scores(content_query, key_heads, position_query, position_keys)
    row_peak = jnp.max(scores, -1, keepdims=True)
    normalizer = row_peak + jnp.log(jnp.sum(jnp.exp(scores - row_peak), -1, keepdims=True))
    attention_probs = jnp.exp(scores - normalizer)
    attended = jnp.einsum(
        "hij,jhv->ihv",
        attention_probs.astype(jnp.bfloat16),
        value_heads,
        preferred_element_type=jnp.float32,
    )
    attended = attended.reshape(length, model_width).astype(jnp.bfloat16)
    after_attention = (
        after_conv + jnp.dot(attended, out_full, preferred_element_type=jnp.float32) + bias_rows[3]
    )
    standard_two, inverse_two = normalize(after_attention)
    normed_two = (standard_two * gain_rows[2] + bias_rows[4]).astype(jnp.bfloat16)
    hidden_pre = [
        jnp.dot(normed_two, up_full[half], preferred_element_type=jnp.float32) + up_offset[half]
        for half in range(2)
    ]
    hidden = [jax.nn.gelu(half).astype(jnp.bfloat16) for half in hidden_pre]
    outputs = (
        after_attention
        + jnp.dot(hidden[0], down_full[0], preferred_element_type=jnp.float32)
        + jnp.dot(hidden[1], down_full[1], preferred_element_type=jnp.float32)
        + bias_rows[5]
    )
    target_row = lax.dynamic_index_in_dim(target_table, window_ids[0], 0, keepdims=False)
    levels = jnp.arange(clip_levels.shape[0], dtype=jnp.int32)
    selector = (clip_index[0][:, None] == levels[None, :]).astype(jnp.float32)
    limits = jnp.sum(selector * clip_levels[None, :], 1)[:, None]
    cotangent = jnp.clip(outputs - target_row, -limits, limits).astype(jnp.bfloat16)
    cot_value = cotangent.astype(jnp.float32)
    grad_down_bias = jnp.sum(cot_value, 0)
    pre_grad = []
    for half in range(2):
        hidden_grad = dot_trailing(cotangent, down_full[half])
        gelu_pull = jax.vjp(jax.nn.gelu, hidden_pre[half])[1]
        pre_grad.append(gelu_pull(hidden_grad)[0].astype(jnp.bfloat16))
    grad_up_bias = jnp.stack([jnp.sum(half.astype(jnp.float32), 0) for half in pre_grad])
    normed_two_grad = dot_trailing(pre_grad[0], up_full[0]) + dot_trailing(
        pre_grad[1], up_full[1]
    )
    grad_gain_two = jnp.sum(normed_two_grad * standard_two, 0)
    grad_bias_two = jnp.sum(normed_two_grad, 0)
    attention_grad = cot_value + norm_back(
        normed_two_grad * gain_rows[2], standard_two, inverse_two
    )
    branch_grad = attention_grad.astype(jnp.bfloat16)
    grad_out_bias = jnp.sum(branch_grad.astype(jnp.float32), 0)
    attended_grad = (
        dot_trailing(branch_grad, out_full).astype(jnp.bfloat16).reshape(length, HEADS, -1)
    )
    scores = attention_scores(content_query, key_heads, position_query, position_keys)
    attention_probs = jnp.exp(scores - normalizer)
    value_grad = jnp.einsum(
        "hij,ihv->jhv",
        attention_probs.astype(jnp.bfloat16),
        attended_grad,
        preferred_element_type=jnp.float32,
    )
    value_grad = value_grad.reshape(length, model_width).astype(jnp.bfloat16)
    prob_grad = jnp.einsum(
        "ihv,jhv->hij", attended_grad, value_heads, preferred_element_type=jnp.float32
    )
    row_dot = jnp.sum(attention_probs * prob_grad, -1, keepdims=True)
    score_grad = (attention_probs * (prob_grad - row_dot)).astype(jnp.bfloat16)
    content_grad = jnp.einsum(
        "hij,jhk->ihk", score_grad, key_heads, preferred_element_type=jnp.float32
    )
    key_grad = jnp.einsum(
        "hij,ihk->jhk", score_grad, content_query, preferred_element_type=jnp.float32
    )
    key_grad = key_grad.reshape(length, -1).astype(jnp.bfloat16)
    band_zeros = jnp.zeros((HEADS, length, position_keys.shape[0]), jnp.float32)
    shift_pull = jax.vjp(relative_shift, band_zeros)[1]
    band_grad = shift_pull(score_grad.astype(jnp.float32))[0].astype(jnp.bfloat16)
    position_grad = jnp.einsum(
        "him,mhk->ihk", band_grad, position_keys, preferred_element_type=jnp.float32
    )
    table_grad = jnp.einsum(
        "him,ihk->mhk", band_grad, position_query, preferred_element_type=jnp.float32
    )
    table_grad = table_grad.reshape(table.shape[0], -1).astype(jnp.bfloat16)
    grad_rel_bias = jnp.stack(
        [jnp.sum(content_grad, 0).reshape(-1), jnp.sum(position_grad, 0).reshape(-1)]
    )
    query_grad = (
        ((content_grad + position_grad) * key_scale).reshape(length, -1).astype(jnp.bfloat16)
    )
    mixed_grad = jnp.concatenate([query_grad, key_grad], 1)
    normed_one_grad = (
        dot_trailing(mixed_grad, mixed_full)
        + dot_trailing(value_grad, value_full)
    )
    grad_gain_one = jnp.sum(normed_one_grad * standard_one, 0)
    grad_bias_one = jnp.sum(normed_one_grad, 0)
    conv_side_grad = attention_grad + norm_back(
        normed_one_grad * gain_rows[1], standard_one, inverse_one
    )
    conv_grad = conv_side_grad.astype(jnp.bfloat16)
    grad_conv_bias = jnp.sum(conv_grad.astype(jnp.float32), 0)
    padded = jnp.pad(conv_grad, ((half_taps, half_taps), (0, 0)))
    activated_grad = 0.0
    for tap in range(tap_count):
        moved = padded[tap_count - 1 - tap : tap_count - 1 - tap + length]
        activated_grad = activated_grad + dot_trailing(moved, conv_full[tap])
    act_pull = jax.vjp(jax.nn.gelu, normed)[1]
    normed_grad = act_pull(activated_grad)[0]
    sum_parts = [
        jnp.sum(normed_grad * standard, 0),
        grad_gain_one,
        grad_gain_two,
        jnp.sum(normed_grad, 0),
        grad_conv_bias,
        grad_bias_one,
        grad_out_bias,
        grad_bias_two,
        grad_down_bias,
        grad_up_bias[0],
        grad_up_bias[1],
        grad_rel_bias.reshape(-1),
    ]
    sums = jnp.concatenate(sum_parts)
    sums = jnp.pad(sums, (0, -sums.shape[0] % 1024)).reshape(-1, 128)
    grad_rel = dot_leading(table, table_grad).astype(jnp.bfloat16)
    grad_rel = grad_rel.astype(jnp.float32) + exchange(grad_rel).astype(jnp.float32)
    grad_rel = jnp.moveaxis(grad_rel.reshape(rel_rows, groups, rel_columns), 0, 1)
    grad_rel = grad_rel.reshape(groups, 2, rel_rows // 2, rel_columns).astype(jnp.bfloat16)
    mixed_wide = jnp.pad(mixed_grad, ((0, 0), (0, model_width - 2 * key_width)))
    lefts = [activated, normed_one, attended, normed_two, hidden[0], hidden[1]]
    rights = [mixed_wide, value_grad, branch_grad, pre_grad[0], pre_grad[1], cotangent]
    lefts_sib = [exchange(left) for left in lefts]
    rights_own = [own_half(right) for right in rights]
    rights_sib = [sib_half(right) for right in rights]

    def shifted(array):
        padded = jnp.pad(array, ((half_taps, half_taps), (0, 0)))
        return jnp.stack([padded[tap : tap + length] for tap in reversed(range(tap_count))])

    pieces, sums = reduce(
        groups,
        blocks,
        2 * key_width - half_width,
        lefts,
        lefts_sib,
        shifted(own_half(conv_grad)),
        shifted(sib_half(conv_grad)),
        rights_own + rights_own[5:],
        rights_sib + rights_sib[5:],
        grad_rel,
        sums,
    )
    flat = sums.reshape(-1)
    bn_sums = flat[: 4 * model_width].reshape(4, model_width)
    input_grad = conv_side_grad + inverse * (
        normed_grad * gain_rows[0]
        - gain_rows[0] * (bn_sums[3] + standard * bn_sums[0]) / token_total
    )
    shard = lax.axis_index("fsdp")
    by_shard = flat[: 11 * model_width].reshape(11, groups, -1)
    by_shard = lax.dynamic_index_in_dim(by_shard, shard, 1, keepdims=False)
    rel_sums = flat[11 * model_width : 11 * model_width + 2 * key_width]
    rel_sums = rel_sums.reshape(2, groups, -1)
    rel_sums = lax.dynamic_index_in_dim(rel_sums, shard, 1, keepdims=False)
    up_grad = jnp.concatenate(
        [
            pieces[8 + half, :, index * piece_rows : (index + 1) * piece_rows]
            for index in range(groups)
            for half in range(2)
        ],
        1,
    )
    mixed_sum = pieces[5].astype(jnp.float32)
    rel_at = 2 * key_width
    return (
        outputs.astype(jnp.bfloat16)[None],
        input_grad.astype(jnp.bfloat16)[None],
        pieces[:5].astype(jnp.float32),
        mixed_sum[:, :key_width],
        mixed_sum[:, key_width:rel_at],
        pieces[6].astype(jnp.float32),
        pieces[7].astype(jnp.float32),
        mixed_sum[:rel_rows, rel_at : rel_at + rel_columns],
        up_grad.astype(jnp.float32),
        pieces[10:12].reshape(2 * piece_rows, -1).astype(jnp.float32),
        by_shard[:3],
        by_shard[3:9],
        by_shard[9:11].reshape(-1),
        rel_sums,
    )


def solution(mesh):
    placed = (
        P(("dp", "fsdp"), None, None),
        P(None, "fsdp", None),
        P("fsdp", None),
        P("fsdp", None),
        P("fsdp", None),
        P("fsdp", None),
        P(None, "fsdp"),
        P("fsdp", None),
        P("fsdp", None),
        P(None, "fsdp"),
        P(None, "fsdp"),
        P("fsdp"),
        P(None, "fsdp"),
        P(),
        P(),
        P(("dp", "fsdp")),
        P(("dp", "fsdp"), None),
    )
    return jax.shard_map(
        on_device,
        mesh=mesh,
        in_specs=placed,
        out_specs=(
            P(("dp", "fsdp"), None, None),
            P(("dp", "fsdp"), None, None),
            P(None, "fsdp", None),
            P("fsdp", None),
            P("fsdp", None),
            P("fsdp", None),
            P("fsdp", None),
            P(None, "fsdp"),
            P("fsdp", None),
            P("fsdp", None),
            P(None, "fsdp"),
            P(None, "fsdp"),
            P("fsdp"),
            P(None, "fsdp"),
        ),
        check_vma=False,
    )
```

```python
import functools
import math

import jax
import jax.numpy as jnp
from jax import lax
from jax.experimental import pallas as pl
from jax.experimental.pallas import tpu as pltpu
from jax.sharding import PartitionSpec as P

HEADS = 8
KEY = 64
MESH = pl.DeviceIdType.MESH
AHEAD = 2


def neighbours(dp):
    core = dp % 2
    along_x = dp // 2 % 2
    along_y = dp // 4 % 2
    return dp + 1 - 2 * core, dp + 2 - 4 * along_x, dp + 4 - 8 * along_y


def remote(src, dst, send_sem, recv_sem, device):
    return pltpu.make_async_remote_copy(
        src_ref=src,
        dst_ref=dst,
        send_sem=send_sem,
        recv_sem=recv_sem,
        device_id=device,
        device_id_type=MESH,
    )


def meet(peers):
    barrier = pltpu.get_barrier_semaphore()
    for peer in peers:
        pl.semaphore_signal(barrier, inc=1, device_id=peer, device_id_type=MESH)
    pl.semaphore_wait(barrier, len(peers))


def peers_of(groups, blocks):
    dp = lax.axis_index("dp")
    me = lax.axis_index("fsdp")
    near = [(device, me) for device in neighbours(dp)]
    shards = [(dp, (me + 1 + j) % groups) for j in range(groups - 1)]
    far = [((dp + 8 * (1 + j)) % (8 * blocks), me) for j in range(blocks - 1)]
    return near, shards, far


def sum_steps(groups, blocks, vector, total, near_got, sums, shard_got, block_got, sems):
    near_send, near_recv, shard_send, shard_recv, block_send, block_recv = sems
    me = lax.axis_index("fsdp")
    block = lax.axis_index("dp") // 8
    near, shards, far = peers_of(groups, blocks)

    def near_copy(step):
        src = vector if step == 0 else sums.at[step - 1]
        return remote(
            src, near_got.at[step], near_send.at[step], near_recv.at[step], near[step]
        )

    def fold(step):
        copy = near_copy(step)
        copy.wait()
        held = vector[...] if step == 0 else sums[step - 1]
        sums[step] = held + near_got[step]

    def shard_copy(j):
        return remote(
            sums.at[2], shard_got.at[me], shard_send.at[j], shard_recv.at[me], shards[j]
        )

    def block_copy(j):
        return remote(
            sums.at[3], block_got.at[block], block_send.at[j], block_recv.at[block], far[j]
        )

    def start():
        near_copy(0).start()

    def second():
        fold(0)
        near_copy(1).start()

    def third():
        fold(1)
        near_copy(2).start()

    def fourth():
        fold(2)
        for j in range(groups - 1):
            shard_copy(j).start()
        shard_got[me] = sums[2]

    def fifth():
        for j in range(groups - 1):
            shard_copy(j).wait_send()
            other = (me + 1 + j) % groups
            remote(
                sums.at[2], shard_got.at[other], shard_send.at[j], shard_recv.at[other], shards[j]
            ).wait_recv()
        added = shard_got[0]
        for shard in range(1, groups):
            added = added + shard_got[shard]
        sums[3] = added
        for j in range(blocks - 1):
            block_copy(j).start()
        block_got[block] = added

    def sixth():
        for j in range(blocks - 1):
            block_copy(j).wait_send()
            other = (block + 1 + j) % blocks
            remote(
                sums.at[3], block_got.at[other], block_send.at[j], block_recv.at[other], far[j]
            ).wait_recv()
        added = block_got[0]
        for other in range(1, blocks):
            added = added + block_got[other]
        total[...] = added

    return [start, second, third, fourth, fifth, sixth]


def sum_scratch(groups, blocks, shape):
    return [
        pltpu.VMEM((3,) + shape, jnp.float32),
        pltpu.VMEM((4,) + shape, jnp.float32),
        pltpu.VMEM((groups,) + shape, jnp.float32),
        pltpu.VMEM((blocks,) + shape, jnp.float32),
        pltpu.SemaphoreType.DMA((3,)),
        pltpu.SemaphoreType.DMA((3,)),
        pltpu.SemaphoreType.DMA((groups,)),
        pltpu.SemaphoreType.DMA((groups,)),
        pltpu.SemaphoreType.DMA((blocks,)),
        pltpu.SemaphoreType.DMA((blocks,)),
    ]


def gather_kernel(groups, blocks, *refs):
    weights = refs[:8]
    conv, query, key, value, out, up, down, rel = weights
    small, stats = refs[8:10]
    outs = refs[10:21]
    rel_full, small_full, stat_total = outs[8:]
    hold, hold_mixed, local_sem, write_sem = refs[21:25]
    z_sem, x_sem, y_sem, d_sem, sib_sem, send_sem, right_send, left_send = refs[25:33]
    rel_send, rel_recv, small_send, small_recv = refs[33:37]
    near_got, sums, shard_got, block_got = refs[37:41]
    sum_sems = refs[41:47]
    dp = lax.axis_index("dp")
    me = lax.axis_index("fsdp")
    near, shards, far = peers_of(groups, blocks)
    sib, along_x, along_y = neighbours(dp)
    rows = conv.shape[1]
    part = rows // 8
    others = groups - 1
    pieces = [outs[0].at[tap] for tap in range(5)] + list(outs[1:8])
    count = len(pieces)
    holds = [hold.at[i] for i in range(5)] + [hold_mixed] + [hold.at[i] for i in range(5, 11)]

    pending = [[] for _ in range(count)]
    started = [0]

    def load(src, dst, piece):
        copy = pltpu.make_async_copy(src, dst, local_sem.at[started[0]])
        copy.start()
        started[0] += 1
        pending[piece].append(copy)

    for tap in range(5):
        load(conv.at[tap], holds[tap], tap)
    width = query.shape[1]
    load(query, hold_mixed.at[:, pl.ds(0, width)], 5)
    load(key, hold_mixed.at[:, pl.ds(width, width)], 5)
    load(value, holds[6], 6)
    load(out, holds[7], 7)
    for half in range(2):
        for shard in range(groups):
            load(
                up.at[:, pl.ds((shard * 2 + half) * rows, rows)],
                holds[8 + half].at[:, pl.ds(shard * rows, rows)],
                8 + half,
            )
    for half in range(2):
        load(down.at[pl.ds(half * rows, rows)], holds[10 + half], 10 + half)

    meet(near + shards + far)

    summing = sum_steps(
        groups, blocks, stats, stat_total, near_got, sums, shard_got, block_got, sum_sems
    )
    summing[0]()

    for j in range(others):
        remote(
            rel, rel_full.at[me], rel_send.at[j], rel_recv.at[me], shards[j]
        ).start()
        remote(
            small, small_full.at[me], small_send.at[j], small_recv.at[me], shards[j]
        ).start()
    rel_full[me] = rel[...]
    small_full[me] = small[...]

    def slice_of(piece, shard, owner):
        return pieces[piece].at[shard, pl.ds(pl.multiple_of(owner % 8 * part, 16), part)]

    def copy_of(piece, shard, owner, recv_sem, device):
        ref = slice_of(piece, shard, owner)
        return remote(ref, ref, send_sem.at[piece], recv_sem, (device, me))

    order = []
    for j in range(others):
        pick = 0
        for m in range(groups):
            nearest = sorted((t for t in range(groups) if t != m), key=lambda t: abs(t - m))
            pick = pick + jnp.where(me == m, nearest[j], 0)
        order.append(pick)

    def right_copy(piece, shard, src=None):
        dst = slice_of(piece, shard, dp)
        return remote(
            dst if src is None else src,
            dst,
            right_send.at[piece, shard],
            z_sem.at[piece, shard],
            (dp, (me + 1) % groups),
        )

    def left_copy(piece, shard, src=None):
        dst = slice_of(piece, shard, dp)
        return remote(
            dst if src is None else src,
            dst,
            left_send.at[piece, shard],
            z_sem.at[piece, shard],
            (dp, (me + groups - 1) % groups),
        )

    def z_send(piece):
        src = holds[piece].at[pl.ds(pl.multiple_of(dp % 8 * part, 16), part)]

        @pl.when(me + 1 < groups)
        def _():
            right_copy(piece, me, src).start()

        @pl.when(me > 0)
        def _():
            left_copy(piece, me, src).start()

    diagonal = neighbours(along_x)[2]

    def stage_a(piece):
        for shard in order:
            copy_of(piece, shard, dp, z_sem.at[piece, shard], dp).wait_recv()

            @pl.when(jnp.logical_and(shard < me, me + 1 < groups))
            def _():
                right_copy(piece, shard).start()

            @pl.when(jnp.logical_and(shard > me, me > 0))
            def _():
                left_copy(piece, shard).start()

            copy_of(piece, shard, dp, x_sem.at[piece, shard], along_x).start()
            copy_of(piece, shard, dp, y_sem.at[piece, shard], along_y).start()
            copy_of(piece, shard, dp, sib_sem.at[piece], sib).start()

    def stage_b(piece):
        for shard in order:
            route = (piece + shard) % 2
            copy_of(piece, shard, along_x, x_sem.at[piece, shard], dp).wait_recv()
            copy_of(piece, shard, along_y, y_sem.at[piece, shard], dp).wait_recv()
            owner = route * along_x + (1 - route) * along_y
            target = route * along_y + (1 - route) * along_x
            copy_of(piece, shard, owner, d_sem.at[piece, shard], target).start()
            copy_of(piece, shard, along_x, sib_sem.at[piece], sib).start()
            copy_of(piece, shard, along_y, sib_sem.at[piece], sib).start()

    def stage_c(piece):
        for shard in order:
            copy_of(piece, shard, diagonal, d_sem.at[piece, shard], dp).wait_recv()
            copy_of(piece, shard, diagonal, sib_sem.at[piece], sib).start()

    writes = []
    for piece in range(count):
        for copy in pending[piece]:
            copy.wait()
        copy = pltpu.make_async_copy(holds[piece], pieces[piece].at[me], write_sem.at[piece])
        copy.start()
        writes.append(copy)
        if piece < AHEAD:
            z_send(piece)

    for n in range(count + 2):
        if n + AHEAD < count:
            z_send(n + AHEAD)
        if n < count:
            stage_a(n)
        if 1 <= n <= count:
            stage_b(n - 1)
        if n >= 2:
            stage_c(n - 2)
        if 1 <= n < len(summing):
            summing[n]()

    for piece in range(count):
        for shard in range(groups):

            @pl.when(jnp.logical_and(shard <= me, me + 1 < groups))
            def _():
                right_copy(piece, shard).wait_send()

            @pl.when(jnp.logical_and(shard >= me, me > 0))
            def _():
                left_copy(piece, shard).wait_send()

        writes[piece].wait()
        got = pieces[piece].at[pl.ds(0, others), pl.ds(0, 4 * part)]
        remote(got, got, send_sem.at[piece], sib_sem.at[piece], (sib, me)).wait_recv()
        sent = pieces[piece].at[pl.ds(0, others), pl.ds(0, 7 * part)]
        remote(sent, sent, send_sem.at[piece], sib_sem.at[piece], (sib, me)).wait_send()
    for j in range(others):
        shard = (me + 1 + j) % groups
        remote(rel, rel_full.at[shard], rel_send.at[j], rel_recv.at[shard], shards[j]).wait()
        remote(
            small, small_full.at[shard], small_send.at[j], small_recv.at[shard], shards[j]
        ).wait()


def gather(groups, blocks, weights, small, stats):
    conv, query = weights[:2]
    rel = weights[7]
    taps, rows, columns = conv.shape
    dtype = conv.dtype
    kept = pl.BlockSpec(memory_space=pl.ANY)
    inside = pl.BlockSpec(memory_space=pltpu.VMEM)
    full = jax.ShapeDtypeStruct((groups, rows, columns), dtype)
    count = taps + 7
    grid_sems = [pltpu.SemaphoreType.DMA((count, groups))] * 4
    return pl.pallas_call(
        functools.partial(gather_kernel, groups, blocks),
        out_shape=(
            jax.ShapeDtypeStruct((taps, groups, rows, columns), dtype),
            jax.ShapeDtypeStruct((groups, rows, 2 * query.shape[1]), dtype),
            *([full] * 6),
            jax.ShapeDtypeStruct((groups,) + rel.shape, dtype),
            jax.ShapeDtypeStruct((groups,) + small.shape, jnp.float32),
            jax.ShapeDtypeStruct(stats.shape, jnp.float32),
        ),
        in_specs=[kept] * 7 + [inside] * 3,
        out_specs=[kept] * 8 + [inside] * 3,
        scratch_shapes=[
            pltpu.VMEM((count - 1, rows, columns), dtype),
            pltpu.VMEM((rows, 2 * query.shape[1]), dtype),
            pltpu.SemaphoreType.DMA((taps + 6 + 2 * groups,)),
            pltpu.SemaphoreType.DMA((count,)),
            *grid_sems,
            pltpu.SemaphoreType.DMA((count,)),
            pltpu.SemaphoreType.DMA((count,)),
            *grid_sems[:2],
            *([pltpu.SemaphoreType.DMA((groups,))] * 4),
            *sum_scratch(groups, blocks, stats.shape),
        ],
        compiler_params=pltpu.CompilerParams(
            collective_id=0, has_side_effects=True, vmem_limit_bytes=24 << 20
        ),
        name="gather",
    )(*weights, small, stats)


def reduce_kernel(groups, blocks, rel_at, *refs):
    lefts = refs[:6]
    rights = refs[6:13]
    rel_grad, vector = refs[13:15]
    out, total, left_got, right_got = refs[15:19]
    (
        left_hold,
        right_hold,
        grad,
        x_one,
        y_one,
        x_two,
        y_two,
        shard_got,
        block_got,
        partial,
        done,
        rel_got,
    ) = refs[19:31]
    left_send, left_recv, right_send, right_recv, rel_send, rel_recv = refs[31:37]
    refs = refs[37:]
    load_sem = refs[0]
    x1s, y1s, x2s, y2s, x1r, y1r, x2r, y2r = refs[1:9]
    shard_send, shard_recv, block_send, block_recv = refs[9:13]
    write_sem, send_sem, ax, ay, ad, sib_sem = refs[13:19]
    sum_bufs = refs[19:23]
    sum_sems = refs[23:29]

    dp = lax.axis_index("dp")
    me = lax.axis_index("fsdp")
    near, shards, far = peers_of(groups, blocks)
    sib, along_x, along_y = neighbours(dp)
    core = dp % 2
    at_x = dp // 2 % 2
    at_y = dp // 4 % 2
    block = dp // 8
    slots = grad.shape[0]
    part = grad.shape[4]
    width = grad.shape[5]
    half = width // 2
    rows = 4 * part
    count = out.shape[0]
    others = groups - 1
    first = pl.ds(0, half)
    last = pl.ds(half, half)
    taps = 5
    left_of = [0] * taps + [1, 1, 2, 3, 3, 4, 5]
    right_of = [0] * taps + [1, 2, 3, 4, 5, 6, 6]
    own_columns = pl.ds(pl.multiple_of(core * width, 128), width)
    sib_columns = pl.ds(pl.multiple_of((1 - core) * width, 128), width)

    def left_copy(index):
        return remote(
            lefts[index], left_got.at[index], left_send.at[index], left_recv.at[index], (sib, me)
        )

    def right_copy(index):
        return remote(
            rights[index].at[:, sib_columns],
            right_got.at[index],
            right_send.at[index],
            right_recv.at[index],
            (sib, me),
        )

    def rel_copy():
        return remote(rel_grad, rel_got, rel_send.at[0], rel_recv.at[0], (sib, me))

    def loads(piece, slot):
        left = left_of[piece]
        right = right_of[piece]
        pairs = (
            (lefts[left], left_hold.at[slot, 0]),
            (left_got.at[left], left_hold.at[slot, 1]),
            (rights[right].at[:, own_columns], right_hold.at[slot, 0]),
            (right_got.at[right], right_hold.at[slot, 1]),
        )
        return [
            pltpu.make_async_copy(src, dst, load_sem.at[slot, i])
            for i, (src, dst) in enumerate(pairs)
        ]

    def start_loads(piece):
        if left_of[piece] not in left_of[:piece]:
            left_copy(left_of[piece]).wait_recv()
        if right_of[piece] not in right_of[:piece]:
            right_copy(right_of[piece]).wait_recv()
        for copy in loads(piece, piece % 2):
            copy.start()

    meet(near + shards + far)

    for piece in range(count):
        if left_of[piece] not in left_of[:piece]:
            left_copy(left_of[piece]).start()
        if right_of[piece] not in right_of[:piece]:
            right_copy(right_of[piece]).start()
    rel_copy().start()
    start_loads(0)

    summing = sum_steps(groups, blocks, vector, total, *sum_bufs, sum_sems)

    def one(piece):
        slot = piece % slots
        return (
            remote(
                grad.at[slot, :, :, 1 - at_x, :, first],
                x_one.at[piece],
                x1s.at[piece],
                x1r.at[piece],
                (along_x, me),
            ),
            remote(
                grad.at[slot, :, 1 - at_y, :, :, last],
                y_one.at[piece],
                y1s.at[piece],
                y1r.at[piece],
                (along_y, me),
            ),
        )

    def two(piece):
        slot = piece % slots
        return (
            remote(
                grad.at[slot, :, 1 - at_y, at_x, :, first],
                y_two.at[piece],
                y2s.at[piece],
                y2r.at[piece],
                (along_y, me),
            ),
            remote(
                grad.at[slot, :, at_y, 1 - at_x, :, last],
                x_two.at[piece],
                x2s.at[piece],
                x2r.at[piece],
                (along_x, me),
            ),
        )

    def shard_copy(piece, j):
        other = (me + 1 + j) % groups
        return remote(
            grad.at[piece % slots, other, at_y, at_x],
            shard_got.at[piece, me],
            shard_send.at[piece, j],
            shard_recv.at[piece, me],
            (dp, other),
        )

    def shard_arrival(piece, j):
        other = (me + 1 + j) % groups
        return remote(
            grad.at[piece % slots, other, at_y, at_x],
            shard_got.at[piece, other],
            shard_send.at[piece, j],
            shard_recv.at[piece, other],
            (dp, other),
        )

    def block_copy(piece, j):
        return remote(
            partial.at[piece],
            block_got.at[piece, block],
            block_send.at[piece, j],
            block_recv.at[piece, block],
            far[j],
        )

    def block_arrival(piece, j):
        other = (block + 1 + j) % blocks
        return remote(
            partial.at[piece],
            block_got.at[piece, other],
            block_send.at[piece, j],
            block_recv.at[piece, other],
            far[j],
        )

    def place(piece, owner):
        return out.at[
            piece,
            pl.ds(pl.multiple_of(owner % 8 // 2 * part, 16), part),
            pl.ds(pl.multiple_of(core * width, 128), width),
        ]

    def spread(piece, src, owner, recv_sem, device):
        return remote(src, place(piece, owner), send_sem.at[piece], recv_sem, (device, me))

    def forward(piece, owner, recv_sem, device):
        return spread(piece, place(piece, owner), owner, recv_sem, device)

    diagonal = neighbours(along_x)[2]

    def shift(piece):
        move = piece - taps // 2
        for window in range(2):
            value = right_hold[piece % 2, window].astype(jnp.float32)
            value = pltpu.roll(value, move % value.shape[0], 0)
            row = lax.broadcasted_iota(jnp.int32, value.shape, 0)
            inside = row >= move if move > 0 else row < value.shape[0] + move
            value = jnp.where(inside, value, 0.0)
            right_hold[piece % 2, window] = value.astype(right_hold.dtype)

    def produce(piece):
        slot = piece % slots
        hold = piece % 2

        def shard_body(shard, carry):
            columns = pl.ds(pl.multiple_of(shard * rows, 128), rows)
            value = dot_leading(left_hold[hold, 0, :, columns], right_hold[hold, 0])
            value = value + dot_leading(left_hold[hold, 1, :, columns], right_hold[hold, 1])
            grad[slot, shard] = value.astype(grad.dtype).reshape(2, 2, part, width)
            return carry

        lax.fori_loop(0, groups, shard_body, 0)

        @pl.when(piece == taps)
        def _():
            rel_copy().wait()

        @pl.when(jnp.logical_and(piece == taps, core == 1))
        def _():
            for shard in range(groups):
                value = rel_grad[shard].astype(jnp.float32) + rel_got[shard].astype(jnp.float32)
                grad[slot, shard, 0, :, :, pl.ds(rel_at, rel_grad.shape[3])] = value.astype(
                    grad.dtype
                )

    def add(piece_slot, ref, columns, *index):
        ahead = grad[(piece_slot,) + index + (slice(None), columns)]
        return ahead.astype(jnp.float32) + ref.astype(jnp.float32)

    def body(n, carry):
        @pl.when(n < count)
        def _():
            @pl.when(n >= slots)
            def _():
                old = n - slots
                for copy in one(old) + two(old):
                    copy.wait_send()
                for j in range(others):
                    shard_copy(old, j).wait_send()

            for piece in range(count):

                @pl.when(n == piece)
                def _():
                    for copy in loads(piece, piece % 2):
                        copy.wait()
                    if piece + 1 < count:
                        start_loads(piece + 1)
                    if piece < taps and piece != taps // 2:
                        shift(piece)

            produce(n)
            for copy in one(n):
                copy.start()

        @pl.when(jnp.logical_and(n >= 1, n < count + 1))
        def _():
            piece = n - 1
            slot = piece % slots
            for copy in one(piece):
                copy.wait_recv()

            def shard_body(shard, carry):
                for other in range(2):
                    value = add(slot, x_one[piece, shard, other], first, shard, other, at_x)
                    grad[slot, shard, other, at_x, :, first] = value.astype(grad.dtype)
                    value = add(slot, y_one[piece, shard, other], last, shard, at_y, other)
                    grad[slot, shard, at_y, other, :, last] = value.astype(grad.dtype)
                return carry

            lax.fori_loop(0, groups, shard_body, 0)
            for copy in two(piece):
                copy.start()

        @pl.when(jnp.logical_and(n >= 2, n < count + 2))
        def _():
            piece = n - 2
            slot = piece % slots
            for copy in two(piece):
                copy.wait_recv()

            def shard_body(shard, carry):
                value = add(slot, y_two[piece, shard], first, shard, at_y, at_x)
                grad[slot, shard, at_y, at_x, :, first] = value.astype(grad.dtype)
                value = add(slot, x_two[piece, shard], last, shard, at_y, at_x)
                grad[slot, shard, at_y, at_x, :, last] = value.astype(grad.dtype)
                return carry

            lax.fori_loop(0, groups, shard_body, 0)
            for j in range(others):
                shard_copy(piece, j).start()

        @pl.when(jnp.logical_and(n >= 3, n < count + 3))
        def _():
            piece = n - 3
            value = grad[piece % slots, me, at_y, at_x].astype(jnp.float32)
            for j in range(others):
                shard_arrival(piece, j).wait_recv()
                value = value + shard_got[piece, (me + 1 + j) % groups].astype(jnp.float32)
            if blocks > 1:
                partial[piece] = value.astype(partial.dtype)
                block_got[piece, block] = value.astype(partial.dtype)
                for j in range(blocks - 1):
                    block_copy(piece, j).start()
                for j in range(blocks - 1):
                    block_copy(piece, j).wait_send()
                    block_arrival(piece, j).wait_recv()
                value = block_got[piece, 0].astype(jnp.float32)
                for other in range(1, blocks):
                    value = value + block_got[piece, other].astype(jnp.float32)
            done[piece] = value.astype(done.dtype)
            pltpu.make_async_copy(done.at[piece], place(piece, dp), write_sem.at[piece]).start()
            spread(piece, done.at[piece], dp, ax.at[piece], along_x).start()
            spread(piece, done.at[piece], dp, ay.at[piece], along_y).start()
            spread(piece, done.at[piece], dp, sib_sem.at[piece], sib).start()

        @pl.when(jnp.logical_and(n >= 4, n < count + 4))
        def _():
            piece = n - 4
            route = piece % 2
            forward(piece, along_x, ax.at[piece], dp).wait_recv()
            forward(piece, along_y, ay.at[piece], dp).wait_recv()
            owner = route * along_x + (1 - route) * along_y
            target = route * along_y + (1 - route) * along_x
            forward(piece, owner, ad.at[piece], target).start()
            forward(piece, along_x, sib_sem.at[piece], sib).start()
            forward(piece, along_y, sib_sem.at[piece], sib).start()

        @pl.when(n >= 5)
        def _():
            piece = n - 5
            forward(piece, diagonal, ad.at[piece], dp).wait_recv()
            forward(piece, diagonal, sib_sem.at[piece], sib).start()

        for step in range(len(summing)):

            @pl.when(n == step)
            def _():
                summing[step]()

        return carry

    lax.fori_loop(0, count + 5, body, 0)

    def drain(piece, carry):
        @pl.when(piece >= count - slots)
        def _():
            for copy in one(piece) + two(piece):
                copy.wait_send()
            for j in range(others):
                shard_copy(piece, j).wait_send()

        pltpu.make_async_copy(done.at[piece], place(piece, dp), write_sem.at[piece]).wait()
        got = out.at[piece, :, pl.ds(0, width)]
        remote(got, got, send_sem.at[piece], sib_sem.at[piece], (sib, me)).wait_recv()
        sent = out.at[piece, pl.ds(0, 7 * part // 2), :]
        remote(sent, sent, send_sem.at[piece], sib_sem.at[piece], (sib, me)).wait_send()
        return carry

    lax.fori_loop(0, count, drain, 0)
    for index in range(len(lefts)):
        left_copy(index).wait_send()
    for index in range(len(rights)):
        right_copy(index).wait_send()


def reduce(groups, blocks, rel_at, lefts, rights, rel_grad, vector):
    bins, columns = lefts[0].shape
    width = columns // 2
    rows = columns // groups
    part = rows // 4
    dtype = lefts[0].dtype
    count = 12
    slots = 5
    kept = pl.BlockSpec(memory_space=pl.ANY)
    inside = pl.BlockSpec(memory_space=pltpu.VMEM)
    each = pltpu.SemaphoreType.DMA((count,))
    return pl.pallas_call(
        functools.partial(reduce_kernel, groups, blocks, rel_at),
        out_shape=(
            jax.ShapeDtypeStruct((count, rows, columns), dtype),
            jax.ShapeDtypeStruct(vector.shape, jnp.float32),
            jax.ShapeDtypeStruct((len(lefts), bins, columns), dtype),
            jax.ShapeDtypeStruct((len(rights), bins, width), dtype),
        ),
        in_specs=[kept] * (len(lefts) + len(rights)) + [inside] * 2,
        out_specs=[kept, inside, kept, kept],
        scratch_shapes=[
            pltpu.VMEM((2, 2, bins, columns), dtype),
            pltpu.VMEM((2, 2, bins, width), dtype),
            pltpu.VMEM((slots, groups, 2, 2, part, width), dtype),
            pltpu.VMEM((count, groups, 2, part, width // 2), dtype),
            pltpu.VMEM((count, groups, 2, part, width // 2), dtype),
            pltpu.VMEM((count, groups, part, width // 2), dtype),
            pltpu.VMEM((count, groups, part, width // 2), dtype),
            pltpu.VMEM((count, groups, part, width), dtype),
            pltpu.VMEM((count if blocks > 1 else 1, blocks, part, width), dtype),
            pltpu.VMEM((count if blocks > 1 else 1, part, width), dtype),
            pltpu.VMEM((count, part, width), dtype),
            pltpu.VMEM(rel_grad.shape, dtype),
            pltpu.SemaphoreType.DMA((len(lefts),)),
            pltpu.SemaphoreType.DMA((len(lefts),)),
            pltpu.SemaphoreType.DMA((len(rights),)),
            pltpu.SemaphoreType.DMA((len(rights),)),
            pltpu.SemaphoreType.DMA((1,)),
            pltpu.SemaphoreType.DMA((1,)),
            pltpu.SemaphoreType.DMA((2, 4)),
            *([each] * 8),
            pltpu.SemaphoreType.DMA((count, groups)),
            pltpu.SemaphoreType.DMA((count, groups)),
            pltpu.SemaphoreType.DMA((count, blocks)),
            pltpu.SemaphoreType.DMA((count, blocks)),
            *([each] * 6),
            *sum_scratch(groups, blocks, vector.shape),
        ],
        compiler_params=pltpu.CompilerParams(
            collective_id=1, has_side_effects=True, vmem_limit_bytes=60 << 20
        ),
        name="reduce",
    )(*lefts, *rights, rel_grad, vector)


EPSILON = 1e-05


def position_table(length, features, direction):
    basis_count = features // 6
    offsets = jnp.arange(2 * length - 1, dtype=jnp.float32) - (length - 1)
    offsets = offsets * direction
    distance = jnp.abs(offsets)[:, None]
    max_range = math.log(length) / math.log(2.0)
    half_life = 2.0 ** jnp.linspace(3.0, max_range, basis_count, dtype=jnp.float32)
    decaying = jnp.exp(-math.log(2.0) / half_life[None, :] * distance)
    widths = 2.0 ** jnp.arange(1, basis_count + 1, dtype=jnp.float32) - 1.0
    central = (widths[None, :] > distance).astype(jnp.float32)
    stddev = length / (2.0 * basis_count)
    centres = jnp.linspace(length / basis_count, length, basis_count, dtype=jnp.float32)
    shape_par = (centres / stddev) ** 2
    rate_par = centres / stddev**2
    safe_dist = jnp.maximum(distance, 1.0)
    log_prob = (shape_par - 1.0) * jnp.log(safe_dist) - rate_par * safe_dist
    log_prob = log_prob - jnp.max(log_prob, axis=0, keepdims=True)
    gamma_feat = jnp.where(distance > 0.5, jnp.exp(log_prob), 0.0)
    symmetric = jnp.concatenate([decaying, central, gamma_feat], 1)
    sign_row = jnp.sign(offsets)[:, None]
    return jnp.concatenate([symmetric, sign_row * symmetric], 1)


def normalize(values):
    centred = values - jnp.mean(values, -1, keepdims=True)
    inverse = lax.rsqrt(jnp.mean(centred * centred, -1, keepdims=True) + EPSILON)
    return (centred * inverse, inverse)


def norm_back(grad_std, standard, inverse):
    return inverse * (
        grad_std
        - jnp.mean(grad_std, -1, keepdims=True)
        - standard * jnp.mean(grad_std * standard, -1, keepdims=True)
    )


def dot_leading(left_side, right_side):
    return lax.dot_general(
        left_side, right_side, (((0,), (0,)), ((), ())), preferred_element_type=jnp.float32
    )


def dot_trailing(left_side, right_side):
    return lax.dot_general(
        left_side, right_side, (((1,), (1,)), ((), ())), preferred_element_type=jnp.float32
    )


def attend_kernel(content_ref, position_ref, key_ref, value_ref, table_ref, out_ref, probs_ref):
    length = content_ref.shape[0]
    span = table_ref.shape[0]
    head_value = value_ref.shape[1] // 2
    for head in range(2):
        keys = slice(head * KEY, (head + 1) * KEY)
        values = slice(head * head_value, (head + 1) * head_value)
        band = dot_trailing(position_ref[:, keys], table_ref[:, keys])
        moved = pltpu.roll(band, span - length + 1, 1, stride=1, stride_axis=0)
        scores = dot_trailing(content_ref[:, keys], key_ref[:, keys]) + moved[:, :length]
        weight = jnp.exp(scores - jnp.max(scores, -1, keepdims=True))
        probs = (weight / jnp.sum(weight, -1, keepdims=True)).astype(jnp.bfloat16)
        probs_ref[head] = probs
        out_ref[:, values] = jnp.dot(
            probs, value_ref[:, values], preferred_element_type=jnp.float32
        ).astype(out_ref.dtype)


def attend(content, position, key, value, table):
    length = content.shape[0]
    span = table.shape[0]
    steps = HEADS // 2

    def columns(array):
        return pl.BlockSpec((array.shape[0], array.shape[1] // steps), lambda i: (0, i))

    return pl.pallas_call(
        attend_kernel,
        grid=(steps,),
        in_specs=[columns(array) for array in (content, position, key, value, table)],
        out_specs=(columns(value), pl.BlockSpec((2, length, length), lambda i: (i, 0, 0))),
        out_shape=(
            jax.ShapeDtypeStruct(value.shape, jnp.bfloat16),
            jax.ShapeDtypeStruct((HEADS, length, length), jnp.bfloat16),
        ),
        compiler_params=pltpu.CompilerParams(vmem_limit_bytes=40 << 20),
        cost_estimate=pl.CostEstimate(
            flops=2 * length * (HEADS * KEY * (length + span) + length * value.shape[1]),
            bytes_accessed=2 * HEADS * length * length,
            transcendentals=HEADS * length * length,
        ),
        name="attend",
    )(content, position, key, value, table)


def attend_back_kernel(
    probs_ref,
    out_ref,
    value_ref,
    key_ref,
    content_ref,
    position_ref,
    table_ref,
    query_grad_ref,
    key_grad_ref,
    value_grad_ref,
    table_grad_ref,
    offset_ref,
):
    length = content_ref.shape[0]
    span = table_ref.shape[0]
    head_value = value_ref.shape[1] // 2
    row = lax.broadcasted_iota(jnp.int32, (length, length), 0)
    column = lax.broadcasted_iota(jnp.int32, (length, length), 1)
    mirror = jnp.where(row + column == length - 1, 1.0, 0.0).astype(jnp.bfloat16)
    for head in range(2):
        keys = slice(head * KEY, (head + 1) * KEY)
        values = slice(head * head_value, (head + 1) * head_value)
        probs = probs_ref[head]
        out_grad = out_ref[:, values]
        value_grad_ref[:, values] = dot_leading(probs, out_grad).astype(jnp.bfloat16)
        prob_grad = dot_trailing(out_grad, value_ref[:, values])
        probs = probs.astype(jnp.float32)
        row_dot = jnp.sum(probs * prob_grad, -1, keepdims=True)
        score_grad = probs * (prob_grad - row_dot)
        rounded = score_grad.astype(jnp.bfloat16)
        key_grad_ref[:, keys] = dot_leading(rounded, content_ref[:, keys]).astype(jnp.bfloat16)
        content_grad = jnp.dot(rounded, key_ref[:, keys], preferred_element_type=jnp.float32)
        mirrored = jnp.dot(rounded, mirror, preferred_element_type=jnp.float32)
        wide = jnp.concatenate([mirrored, jnp.zeros((length, span - length), jnp.float32)], 1)
        band = pltpu.roll(wide, 0, 1, stride=1, stride_axis=0)
        band = band.astype(jnp.bfloat16)
        position_grad = jnp.dot(band, table_ref[:, keys], preferred_element_type=jnp.float32)
        table_grad_ref[:, keys] = dot_leading(band, position_ref[:, keys]).astype(jnp.bfloat16)
        query_grad_ref[:, keys] = ((content_grad + position_grad) * KEY**-0.5).astype(
            jnp.bfloat16
        )
        offset_ref[0:1, keys] = jnp.sum(content_grad, 0, keepdims=True)
        offset_ref[1:2, keys] = jnp.sum(position_grad, 0, keepdims=True)


def attend_back(probs, out_grad, value, key, content, position, table):
    length = content.shape[0]
    span = table.shape[0]
    steps = HEADS // 2

    def columns(array):
        return pl.BlockSpec((array.shape[0], array.shape[1] // steps), lambda i: (0, i))

    offsets = jax.ShapeDtypeStruct((2, key.shape[1]), jnp.float32)
    return pl.pallas_call(
        attend_back_kernel,
        grid=(steps,),
        in_specs=[pl.BlockSpec((2, length, length), lambda i: (i, 0, 0))]
        + [columns(array) for array in (out_grad, value, key, content, position, table)],
        out_specs=[columns(array) for array in (content, key, value, table, offsets)],
        out_shape=[
            jax.ShapeDtypeStruct(array.shape, jnp.bfloat16)
            for array in (content, key, value, table)
        ]
        + [offsets],
        compiler_params=pltpu.CompilerParams(vmem_limit_bytes=40 << 20),
        cost_estimate=pl.CostEstimate(
            flops=4 * length * (HEADS * KEY * (length + span) + length * value.shape[1]),
            bytes_accessed=2 * HEADS * length * length,
            transcendentals=0,
        ),
        name="attend_back",
    )(probs, out_grad, value, key, content, position, table)


def conv_back_kernel(left_ref, right_ref, out_ref):
    @pl.when(pl.program_id(0) == 0)
    def _():
        out_ref[...] = jnp.zeros_like(out_ref)

    out_ref[...] += dot_trailing(left_ref[...], right_ref[0])


def conv_back(left, right):
    length = left.shape[0]
    taps, columns = right.shape[:2]
    return pl.pallas_call(
        conv_back_kernel,
        grid=(taps,),
        in_specs=[
            pl.BlockSpec((length, columns), lambda i: (0, i)),
            pl.BlockSpec((1, columns, columns), lambda i: (i, 0, 0)),
        ],
        out_specs=pl.BlockSpec((length, columns), lambda i: (0, 0)),
        out_shape=jax.ShapeDtypeStruct((length, columns), jnp.float32),
        compiler_params=pltpu.CompilerParams(vmem_limit_bytes=40 << 20),
        cost_estimate=pl.CostEstimate(
            flops=2 * taps * length * columns * columns,
            bytes_accessed=2 * taps * columns * (columns + length),
            transcendentals=0,
        ),
        name="conv_back",
    )(left, right)


def on_device(
    tokens,
    conv_weight,
    query_weight,
    key_weight,
    value_weight,
    out_weight,
    rel_weight,
    up_weight,
    down_weight,
    gains,
    biases,
    up_bias,
    rel_bias,
    target_table,
    clip_levels,
    window_ids,
    clip_index,
):
    groups = lax.axis_size("fsdp")
    blocks = lax.axis_size("dp") // 8
    tap_count, piece_rows, model_width = conv_weight.shape
    half_taps = tap_count // 2
    half_width = model_width // 2
    key_width = query_weight.shape[1]
    rel_rows, rel_columns = rel_weight.shape
    inputs = tokens[0].astype(jnp.float32)
    length = inputs.shape[0]
    token_total = length * lax.axis_size("dp") * lax.axis_size("fsdp")

    small_parts = [gains, biases, up_bias, rel_bias]
    small = jnp.concatenate([part.reshape(-1) for part in small_parts])
    small = jnp.pad(small, (0, -small.shape[0] % 1024)).reshape(-1, 128)
    stats = jnp.concatenate([jnp.sum(inputs, 0), jnp.sum(inputs * inputs, 0)]).reshape(-1, 128)
    (
        conv_full,
        mixed_full,
        value_full,
        out_full,
        up_first,
        up_last,
        down_first,
        down_last,
        rel_full,
        small_full,
        stats,
    ) = gather(
        groups,
        blocks,
        [
            conv_weight,
            query_weight,
            key_weight,
            value_weight,
            out_weight,
            up_weight,
            down_weight,
            rel_weight,
        ],
        small,
        stats,
    )
    conv_full = conv_full.reshape(tap_count, model_width, model_width)
    mixed_full = mixed_full.reshape(model_width, -1)
    value_full = value_full.reshape(model_width, -1)
    out_full = out_full.reshape(model_width, -1)
    up_full = [up_first.reshape(model_width, -1), up_last.reshape(model_width, -1)]
    down_full = [down_first.reshape(model_width, -1), down_last.reshape(model_width, -1)]
    rel_full = jnp.concatenate([rel_full[shard] for shard in range(groups)], 1)
    flat = small_full.reshape(groups, -1)
    taken = 0
    unpacked = []
    for part in small_parts:
        chosen = flat[:, taken : taken + part.size].reshape((groups,) + part.shape)
        unpacked.append(chosen)
        taken += part.size
    gain_rows = jnp.moveaxis(unpacked[0], 0, 1).reshape(gains.shape[0], -1)
    bias_rows = jnp.moveaxis(unpacked[1], 0, 1).reshape(biases.shape[0], -1)
    up_offset = jnp.moveaxis(unpacked[2].reshape(groups, 2, piece_rows), 0, 1).reshape(2, -1)
    rel_offset = jnp.moveaxis(unpacked[3], 0, 1).reshape(2, -1)
    batch_sums = stats.reshape(2, -1)
    centre = batch_sums[0] / token_total
    variance = batch_sums[1] / token_total - centre * centre
    inverse = lax.rsqrt(variance + EPSILON)
    standard = (inputs - centre) * inverse
    normed = standard * gain_rows[0] + bias_rows[0]
    activated = jax.nn.gelu(normed).astype(jnp.bfloat16)
    padded = jnp.pad(activated, ((half_taps, half_taps), (0, 0)))
    stacked = jnp.concatenate([padded[tap : tap + length] for tap in range(tap_count)], 1)
    conv_out = jnp.dot(
        stacked, conv_full.reshape(-1, model_width), preferred_element_type=jnp.float32
    )
    after_conv = inputs + conv_out + bias_rows[1]
    standard_one, inverse_one = normalize(after_conv)
    normed_one = (standard_one * gain_rows[1] + bias_rows[2]).astype(jnp.bfloat16)
    mixed_raw = jnp.dot(normed_one, mixed_full, preferred_element_type=jnp.float32)
    query_raw = mixed_raw[:, :key_width]
    key_scale = KEY ** (-0.5)
    content_query = (query_raw * key_scale + rel_offset[0]).astype(jnp.bfloat16)
    position_query = (query_raw * key_scale + rel_offset[1]).astype(jnp.bfloat16)
    keys = mixed_raw[:, key_width:].astype(jnp.bfloat16)
    values = jnp.dot(normed_one, value_full, preferred_element_type=jnp.float32).astype(
        jnp.bfloat16
    )
    table, mirrored_table = [
        jnp.pad(position_table(length, rel_rows, direction), ((0, 1), (0, 0))).astype(jnp.bfloat16)
        for direction in (1.0, -1.0)
    ]
    position_keys, mirrored_keys = [
        jnp.dot(side, rel_full, preferred_element_type=jnp.float32).astype(jnp.bfloat16)
        for side in (table, mirrored_table)
    ]
    attended, probs = attend(content_query, position_query, keys, values, position_keys)
    after_attention = (
        after_conv + jnp.dot(attended, out_full, preferred_element_type=jnp.float32) + bias_rows[3]
    )
    standard_two, inverse_two = normalize(after_attention)
    normed_two = (standard_two * gain_rows[2] + bias_rows[4]).astype(jnp.bfloat16)
    hidden_pre = [
        jnp.dot(normed_two, up_full[half], preferred_element_type=jnp.float32) + up_offset[half]
        for half in range(2)
    ]
    hidden = [jax.nn.gelu(half).astype(jnp.bfloat16) for half in hidden_pre]
    outputs = (
        after_attention
        + jnp.dot(hidden[0], down_full[0], preferred_element_type=jnp.float32)
        + jnp.dot(hidden[1], down_full[1], preferred_element_type=jnp.float32)
        + bias_rows[5]
    )
    target_row = lax.dynamic_index_in_dim(target_table, window_ids[0], 0, keepdims=False)
    levels = jnp.arange(clip_levels.shape[0], dtype=jnp.int32)
    selector = (clip_index[0][:, None] == levels[None, :]).astype(jnp.float32)
    limits = jnp.sum(selector * clip_levels[None, :], 1)[:, None]
    cotangent = jnp.clip(outputs - target_row, -limits, limits).astype(jnp.bfloat16)
    cot_value = cotangent.astype(jnp.float32)
    grad_down_bias = jnp.sum(cot_value, 0)
    pre_grad = []
    for half in range(2):
        hidden_grad = dot_trailing(cotangent, down_full[half])
        gelu_pull = jax.vjp(jax.nn.gelu, hidden_pre[half])[1]
        pre_grad.append(gelu_pull(hidden_grad)[0].astype(jnp.bfloat16))
    grad_up_bias = jnp.stack([jnp.sum(half.astype(jnp.float32), 0) for half in pre_grad])
    normed_two_grad = dot_trailing(pre_grad[0], up_full[0]) + dot_trailing(
        pre_grad[1], up_full[1]
    )
    grad_gain_two = jnp.sum(normed_two_grad * standard_two, 0)
    grad_bias_two = jnp.sum(normed_two_grad, 0)
    attention_grad = cot_value + norm_back(
        normed_two_grad * gain_rows[2], standard_two, inverse_two
    )
    branch_grad = attention_grad.astype(jnp.bfloat16)
    grad_out_bias = jnp.sum(branch_grad.astype(jnp.float32), 0)
    attended_grad = dot_trailing(branch_grad, out_full).astype(jnp.bfloat16)
    query_grad, key_grad, value_grad, table_grad, grad_rel_bias = attend_back(
        probs, attended_grad, values, keys, content_query, position_query, mirrored_keys
    )
    mixed_grad = jnp.concatenate([query_grad, key_grad], 1)
    normed_one_grad = (
        dot_trailing(mixed_grad, mixed_full)
        + dot_trailing(value_grad, value_full)
    )
    grad_gain_one = jnp.sum(normed_one_grad * standard_one, 0)
    grad_bias_one = jnp.sum(normed_one_grad, 0)
    conv_side_grad = attention_grad + norm_back(
        normed_one_grad * gain_rows[1], standard_one, inverse_one
    )
    conv_grad = conv_side_grad.astype(jnp.bfloat16)
    grad_conv_bias = jnp.sum(conv_grad.astype(jnp.float32), 0)
    padded = jnp.pad(conv_grad, ((half_taps, half_taps), (0, 0)))
    stacked_grad = jnp.concatenate(
        [padded[tap : tap + length] for tap in reversed(range(tap_count))], 1
    )
    activated_grad = conv_back(stacked_grad, conv_full)
    act_pull = jax.vjp(jax.nn.gelu, normed)[1]
    normed_grad = act_pull(activated_grad)[0]
    sum_parts = [
        jnp.sum(normed_grad * standard, 0),
        grad_gain_one,
        grad_gain_two,
        jnp.sum(normed_grad, 0),
        grad_conv_bias,
        grad_bias_one,
        grad_out_bias,
        grad_bias_two,
        grad_down_bias,
        grad_up_bias[0],
        grad_up_bias[1],
        grad_rel_bias.reshape(-1),
    ]
    sums = jnp.concatenate(sum_parts)
    sums = jnp.pad(sums, (0, -sums.shape[0] % 1024)).reshape(-1, 128)
    grad_rel = dot_leading(mirrored_table, table_grad).astype(jnp.bfloat16)
    grad_rel = jnp.moveaxis(grad_rel.reshape(rel_rows, groups, rel_columns), 0, 1)
    grad_rel = grad_rel.reshape(groups, 2, rel_rows // 2, rel_columns)
    mixed_wide = jnp.pad(mixed_grad, ((0, 0), (0, model_width - 2 * key_width)))
    lefts = [activated, normed_one, attended, normed_two, hidden[0], hidden[1]]
    rights = [
        conv_grad,
        mixed_wide,
        value_grad,
        branch_grad,
        pre_grad[0],
        pre_grad[1],
        cotangent,
    ]
    pieces, sums, _, _ = reduce(
        groups, blocks, 2 * key_width - half_width, lefts, rights, grad_rel, sums
    )
    flat = sums.reshape(-1)
    bn_sums = flat[: 4 * model_width].reshape(4, model_width)
    input_grad = conv_side_grad + inverse * (
        normed_grad * gain_rows[0]
        - gain_rows[0] * (bn_sums[3] + standard * bn_sums[0]) / token_total
    )
    shard = lax.axis_index("fsdp")
    by_shard = flat[: 11 * model_width].reshape(11, groups, -1)
    by_shard = lax.dynamic_index_in_dim(by_shard, shard, 1, keepdims=False)
    rel_sums = flat[11 * model_width : 11 * model_width + 2 * key_width]
    rel_sums = rel_sums.reshape(2, groups, -1)
    rel_sums = lax.dynamic_index_in_dim(rel_sums, shard, 1, keepdims=False)
    up_grad = jnp.concatenate(
        [
            pieces[8 + half, :, index * piece_rows : (index + 1) * piece_rows]
            for index in range(groups)
            for half in range(2)
        ],
        1,
    )
    mixed_sum = pieces[5].astype(jnp.float32)
    rel_at = 2 * key_width
    return (
        outputs.astype(jnp.bfloat16)[None],
        input_grad.astype(jnp.bfloat16)[None],
        pieces[:5].astype(jnp.float32),
        mixed_sum[:, :key_width],
        mixed_sum[:, key_width:rel_at],
        pieces[6].astype(jnp.float32),
        pieces[7].astype(jnp.float32),
        mixed_sum[:rel_rows, rel_at : rel_at + rel_columns],
        up_grad.astype(jnp.float32),
        pieces[10:12].reshape(2 * piece_rows, -1).astype(jnp.float32),
        by_shard[:3],
        by_shard[3:9],
        by_shard[9:11].reshape(-1),
        rel_sums,
    )


def solution(mesh):
    placed = (
        P(("dp", "fsdp"), None, None),
        P(None, "fsdp", None),
        P("fsdp", None),
        P("fsdp", None),
        P("fsdp", None),
        P("fsdp", None),
        P(None, "fsdp"),
        P("fsdp", None),
        P("fsdp", None),
        P(None, "fsdp"),
        P(None, "fsdp"),
        P("fsdp"),
        P(None, "fsdp"),
        P(),
        P(),
        P(("dp", "fsdp")),
        P(("dp", "fsdp"), None),
    )
    return jax.shard_map(
        on_device,
        mesh=mesh,
        in_specs=placed,
        out_specs=(
            P(("dp", "fsdp"), None, None),
            P(("dp", "fsdp"), None, None),
            P(None, "fsdp", None),
            P("fsdp", None),
            P("fsdp", None),
            P("fsdp", None),
            P("fsdp", None),
            P(None, "fsdp"),
            P("fsdp", None),
            P("fsdp", None),
            P(None, "fsdp"),
            P(None, "fsdp"),
            P("fsdp"),
            P(None, "fsdp"),
        ),
        check_vma=False,
    )
```

```python
import functools
import math

import jax
import jax.numpy as jnp
from jax import lax
from jax.experimental import pallas as pl
from jax.experimental.pallas import tpu as pltpu
from jax.sharding import PartitionSpec as P

HEADS = 8
KEY = 64
MESH = pl.DeviceIdType.MESH
AHEAD = 2


def neighbours(dp):
    core = dp % 2
    along_x = dp // 2 % 2
    along_y = dp // 4 % 2
    return dp + 1 - 2 * core, dp + 2 - 4 * along_x, dp + 4 - 8 * along_y


def remote(src, dst, send_sem, recv_sem, device):
    return pltpu.make_async_remote_copy(
        src_ref=src,
        dst_ref=dst,
        send_sem=send_sem,
        recv_sem=recv_sem,
        device_id=device,
        device_id_type=MESH,
    )


def meet(peers):
    barrier = pltpu.get_barrier_semaphore()
    for peer in peers:
        pl.semaphore_signal(barrier, inc=1, device_id=peer, device_id_type=MESH)
    pl.semaphore_wait(barrier, len(peers))


def peers_of(groups, blocks):
    dp = lax.axis_index("dp")
    me = lax.axis_index("fsdp")
    near = [(device, me) for device in neighbours(dp)]
    shards = [(dp, (me + 1 + j) % groups) for j in range(groups - 1)]
    far = [((dp + 8 * (1 + j)) % (8 * blocks), me) for j in range(blocks - 1)]
    return near, shards, far


def sum_steps(groups, blocks, vector, total, near_got, sums, shard_got, block_got, sems):
    near_send, near_recv, shard_send, shard_recv, block_send, block_recv = sems
    me = lax.axis_index("fsdp")
    block = lax.axis_index("dp") // 8
    near, shards, far = peers_of(groups, blocks)

    def near_copy(step):
        src = vector if step == 0 else sums.at[step - 1]
        return remote(
            src, near_got.at[step], near_send.at[step], near_recv.at[step], near[step]
        )

    def fold(step):
        copy = near_copy(step)
        copy.wait()
        held = vector[...] if step == 0 else sums[step - 1]
        sums[step] = held + near_got[step]

    def shard_copy(j):
        return remote(
            sums.at[2], shard_got.at[me], shard_send.at[j], shard_recv.at[me], shards[j]
        )

    def block_copy(j):
        return remote(
            sums.at[3], block_got.at[block], block_send.at[j], block_recv.at[block], far[j]
        )

    def start():
        near_copy(0).start()

    def second():
        fold(0)
        near_copy(1).start()

    def third():
        fold(1)
        near_copy(2).start()

    def fourth():
        fold(2)
        for j in range(groups - 1):
            shard_copy(j).start()
        shard_got[me] = sums[2]

    def fifth():
        for j in range(groups - 1):
            shard_copy(j).wait_send()
            other = (me + 1 + j) % groups
            remote(
                sums.at[2], shard_got.at[other], shard_send.at[j], shard_recv.at[other], shards[j]
            ).wait_recv()
        added = shard_got[0]
        for shard in range(1, groups):
            added = added + shard_got[shard]
        sums[3] = added
        for j in range(blocks - 1):
            block_copy(j).start()
        block_got[block] = added

    def sixth():
        for j in range(blocks - 1):
            block_copy(j).wait_send()
            other = (block + 1 + j) % blocks
            remote(
                sums.at[3], block_got.at[other], block_send.at[j], block_recv.at[other], far[j]
            ).wait_recv()
        added = block_got[0]
        for other in range(1, blocks):
            added = added + block_got[other]
        total[...] = added

    return [start, second, third, fourth, fifth, sixth]


def sum_scratch(groups, blocks, shape):
    return [
        pltpu.VMEM((3,) + shape, jnp.float32),
        pltpu.VMEM((4,) + shape, jnp.float32),
        pltpu.VMEM((groups,) + shape, jnp.float32),
        pltpu.VMEM((blocks,) + shape, jnp.float32),
        pltpu.SemaphoreType.DMA((3,)),
        pltpu.SemaphoreType.DMA((3,)),
        pltpu.SemaphoreType.DMA((groups,)),
        pltpu.SemaphoreType.DMA((groups,)),
        pltpu.SemaphoreType.DMA((blocks,)),
        pltpu.SemaphoreType.DMA((blocks,)),
    ]


def gather_kernel(groups, blocks, *refs):
    weights = refs[:8]
    conv, query, key, value, out, up, down, rel = weights
    small, stats, inputs, tables = refs[8:12]
    outs = refs[12:21]
    conv_out, mixed_out, value_out, out_out, up_out, down_out = outs[:6]
    rel_full, small_full, stat_total = outs[6:]
    results = refs[21:33]
    hold, hold_mixed, local_sem, write_sem = refs[33:37]
    z_sem, x_sem, y_sem, d_sem, sib_sem, send_sem, right_send, left_send = refs[37:45]
    rel_send, rel_recv, small_send, small_recv = refs[45:49]
    near_got, sums, shard_got, block_got = refs[49:53]
    sum_sems = refs[53:59]
    weight_hold, weight_sem, result_sem = refs[59:62]
    params, shifted_ref, total_ref = refs[62:65]
    act_ref, norm_ref, content_ref, position_ref, key_ref, value_ref = refs[65:71]
    table_ref, probs_ref, attended_ref = refs[71:74]
    dp = lax.axis_index("dp")
    me = lax.axis_index("fsdp")
    near, shards, far = peers_of(groups, blocks)
    sib, along_x, along_y = neighbours(dp)
    rows = conv.shape[1]
    part = rows // 8
    others = groups - 1
    columns = conv.shape[2]
    pieces = [conv_out.at[tap] for tap in range(5)] + [mixed_out, value_out, out_out]
    pieces += [up_out.at[:, :, pl.ds(half * columns, columns)] for half in range(2)]
    pieces += [down_out.at[:, pl.ds(half * rows, rows)] for half in range(2)]
    count = len(pieces)
    holds = [hold.at[i] for i in range(5)] + [hold_mixed] + [hold.at[i] for i in range(5, 11)]

    pending = [[] for _ in range(count)]
    started = [0]

    def load(src, dst, piece):
        copy = pltpu.make_async_copy(src, dst, local_sem.at[started[0]])
        copy.start()
        started[0] += 1
        pending[piece].append(copy)

    for tap in range(5):
        load(conv.at[tap], holds[tap], tap)
    width = query.shape[1]
    load(query, hold_mixed.at[:, pl.ds(0, width)], 5)
    load(key, hold_mixed.at[:, pl.ds(width, width)], 5)
    load(value, holds[6], 6)
    load(out, holds[7], 7)
    for half in range(2):
        load(up.at[:, pl.ds(half * columns, columns)], holds[8 + half], 8 + half)
    for half in range(2):
        load(down.at[pl.ds(half * rows, rows)], holds[10 + half], 10 + half)

    meet(near + shards + far)

    summing = sum_steps(
        groups, blocks, stats, stat_total, near_got, sums, shard_got, block_got, sum_sems
    )
    summing[0]()

    for j in range(others):
        remote(
            rel, rel_full.at[me], rel_send.at[j], rel_recv.at[me], shards[j]
        ).start()
        remote(
            small, small_full.at[me], small_send.at[j], small_recv.at[me], shards[j]
        ).start()
    rel_full[me] = rel[...]
    small_full[me] = small[...]

    def slice_of(piece, shard, owner):
        return pieces[piece].at[shard, pl.ds(pl.multiple_of(owner % 8 * part, 16), part)]

    def copy_of(piece, shard, owner, recv_sem, device):
        ref = slice_of(piece, shard, owner)
        return remote(ref, ref, send_sem.at[piece], recv_sem, (device, me))

    order = []
    for j in range(others):
        pick = 0
        for m in range(groups):
            nearest = sorted((t for t in range(groups) if t != m), key=lambda t: abs(t - m))
            pick = pick + jnp.where(me == m, nearest[j], 0)
        order.append(pick)

    def right_copy(piece, shard, src=None):
        dst = slice_of(piece, shard, dp)
        return remote(
            dst if src is None else src,
            dst,
            right_send.at[piece, shard],
            z_sem.at[piece, shard],
            (dp, (me + 1) % groups),
        )

    def left_copy(piece, shard, src=None):
        dst = slice_of(piece, shard, dp)
        return remote(
            dst if src is None else src,
            dst,
            left_send.at[piece, shard],
            z_sem.at[piece, shard],
            (dp, (me + groups - 1) % groups),
        )

    def z_send(piece):
        src = holds[piece].at[pl.ds(pl.multiple_of(dp % 8 * part, 16), part)]

        @pl.when(me + 1 < groups)
        def _():
            right_copy(piece, me, src).start()

        @pl.when(me > 0)
        def _():
            left_copy(piece, me, src).start()

    diagonal = neighbours(along_x)[2]

    def stage_a(piece, shards_now):
        for shard in shards_now:
            copy_of(piece, shard, dp, z_sem.at[piece, shard], dp).wait_recv()

            @pl.when(jnp.logical_and(shard < me, me + 1 < groups))
            def _():
                right_copy(piece, shard).start()

            @pl.when(jnp.logical_and(shard > me, me > 0))
            def _():
                left_copy(piece, shard).start()

            copy_of(piece, shard, dp, x_sem.at[piece, shard], along_x).start()
            copy_of(piece, shard, dp, y_sem.at[piece, shard], along_y).start()
            copy_of(piece, shard, dp, sib_sem.at[piece], sib).start()

    def stage_b(piece, shards_now):
        for shard in shards_now:
            route = (piece + shard) % 2
            copy_of(piece, shard, along_x, x_sem.at[piece, shard], dp).wait_recv()
            copy_of(piece, shard, along_y, y_sem.at[piece, shard], dp).wait_recv()
            owner = route * along_x + (1 - route) * along_y
            target = route * along_y + (1 - route) * along_x
            copy_of(piece, shard, owner, d_sem.at[piece, shard], target).start()
            copy_of(piece, shard, along_x, sib_sem.at[piece], sib).start()
            copy_of(piece, shard, along_y, sib_sem.at[piece], sib).start()

    def stage_c(piece, shards_now):
        for shard in shards_now:
            copy_of(piece, shard, diagonal, d_sem.at[piece, shard], dp).wait_recv()
            copy_of(piece, shard, diagonal, sib_sem.at[piece], sib).start()

    writes = []
    for piece in range(count):
        for copy in pending[piece]:
            copy.wait()
        copy = pltpu.make_async_copy(holds[piece], pieces[piece].at[me], write_sem.at[piece])
        copy.start()
        writes.append(copy)
        if piece < AHEAD:
            z_send(piece)

    def complete(piece):
        writes[piece].wait()
        got = pieces[piece].at[pl.ds(0, others), pl.ds(0, 4 * part)]
        remote(got, got, send_sem.at[piece], sib_sem.at[piece], (sib, me)).wait_recv()

    def weight_loads(piece):
        width = pieces[piece].shape[2]
        return [
            pltpu.make_async_copy(
                pieces[piece].at[shard],
                weight_hold.at[piece % 2, pl.ds(shard * rows, rows), pl.ds(0, width)],
                weight_sem.at[piece % 2, shard],
            )
            for shard in range(groups)
        ]

    def start_weight(piece):
        for copy in weight_loads(piece):
            copy.start()

    def wait_weight(piece):
        for copy in weight_loads(piece):
            copy.wait()

    def wait_smalls():
        for j in range(others):
            shard = (me + 1 + j) % groups
            remote(
                rel, rel_full.at[shard], rel_send.at[j], rel_recv.at[shard], shards[j]
            ).wait()
            remote(
                small, small_full.at[shard], small_send.at[j], small_recv.at[shard], shards[j]
            ).wait()

    length = inputs.shape[0]
    block_rows = 128
    tile = 512
    per_row = rows // 128
    token_total = length * 8 * blocks * groups

    def by_rows(fn):
        def row_body(i, carry):
            fn(pl.ds(pl.multiple_of(i * block_rows, block_rows), block_rows))
            return carry

        lax.fori_loop(0, length // block_rows, row_body, 0)

    def unpack():
        for row in range(9):
            for shard in range(groups):
                for j in range(per_row):
                    at = shard * rows + j * 128
                    source = row * per_row + j
                    params[row : row + 1, at : at + 128] = small_full[
                        shard, source : source + 1, :
                    ]
        lanes = columns // 128
        for j in range(lanes):
            centre = stat_total[j : j + 1, :] / token_total
            square = stat_total[lanes + j : lanes + j + 1, :] / token_total
            params[9:10, j * 128 : (j + 1) * 128] = centre
            params[10:11, j * 128 : (j + 1) * 128] = lax.rsqrt(
                square - centre * centre + EPSILON
            )
        taken = (9 * rows + 2 * rows) // 128
        for side in range(2):
            for shard in range(groups):
                params[11 + side : 12 + side, shard * 128 : (shard + 1) * 128] = small_full[
                    shard, taken + side : taken + side + 1, :
                ]

    def activate():
        def rows_fn(at):
            standard = (inputs[at, :].astype(jnp.float32) - params[9:10, :]) * params[10:11, :]
            act_ref[at, :] = jax.nn.gelu(standard * params[0:1, :] + params[3:4, :]).astype(
                act_ref.dtype
            )

        by_rows(rows_fn)

    result_of = [
        act_ref,
        total_ref,
        norm_ref,
        content_ref,
        position_ref,
        key_ref,
        value_ref,
        table_ref.at[1],
        probs_ref,
        attended_ref,
        total_ref,
        norm_ref,
    ]

    def write_result(index):
        return pltpu.make_async_copy(result_of[index], results[index], result_sem.at[index])

    def shift_tap(tap):
        move = tap - 2

        def column_body(i, carry):
            at = pl.ds(pl.multiple_of(i * rows, 128), rows)
            value = act_ref[:, at].astype(jnp.float32)
            value = pltpu.roll(value, -move % length, 0)
            row = lax.broadcasted_iota(jnp.int32, value.shape, 0)
            inside = row < length - move if move > 0 else row >= -move
            shifted_ref[:, at] = jnp.where(inside, value, 0.0).astype(shifted_ref.dtype)
            return carry

        lax.fori_loop(0, columns // rows, column_body, 0)

    def conv_tap(tap, i):
        at = pl.ds(i * tile, tile)
        left = act_ref if tap == 2 else shifted_ref
        value = jnp.dot(
            left[...], weight_hold[tap % 2, :, at], preferred_element_type=jnp.float32
        )
        if tap == 0:
            value = value + (inputs[:, at].astype(jnp.float32) + params[4:5, at])
        else:
            value = value + total_ref[:, at]
        total_ref[:, at] = value

    def norm_step(gain, bias):
        def rows_fn(at):
            standard, _ = normalize(total_ref[at, :])
            norm_ref[at, :] = (
                standard * params[gain : gain + 1, :] + params[bias : bias + 1, :]
            ).astype(norm_ref.dtype)

        by_rows(rows_fn)

    def query_step():
        raw = jnp.dot(
            norm_ref[...], weight_hold[1, :, 0:width], preferred_element_type=jnp.float32
        )
        raw = raw * KEY**-0.5
        content_ref[...] = (raw + params[11:12, 0:width]).astype(content_ref.dtype)
        position_ref[...] = (raw + params[12:13, 0:width]).astype(position_ref.dtype)

    def key_step():
        key_ref[...] = jnp.dot(
            norm_ref[...], weight_hold[1, :, width : 2 * width], preferred_element_type=jnp.float32
        ).astype(key_ref.dtype)

    def table_step():
        for side in range(2):
            for shard in range(groups):
                table_ref[side, :, shard * 128 : (shard + 1) * 128] = jnp.dot(
                    tables[side], rel_full[shard], preferred_element_type=jnp.float32
                ).astype(table_ref.dtype)

    def value_step(i):
        at = pl.ds(i * tile, tile)
        value_ref[:, at] = jnp.dot(
            norm_ref[...], weight_hold[0, :, at], preferred_element_type=jnp.float32
        ).astype(value_ref.dtype)

    def head_step(head):
        head_value = columns // HEADS
        span = tables.shape[1]
        pair = slice(head // 2 * 2 * KEY, (head // 2 + 1) * 2 * KEY)
        value_pair = slice(head // 2 * 2 * head_value, (head // 2 + 1) * 2 * head_value)
        keys = slice(head % 2 * KEY, (head % 2 + 1) * KEY)
        band = dot_trailing(position_ref[:, pair][:, keys], table_ref[0, :, pair][:, keys])
        moved = pltpu.roll(band, span - length + 1, 1, stride=1, stride_axis=0)
        scores = dot_trailing(content_ref[:, pair][:, keys], key_ref[:, pair][:, keys])
        scores = scores + moved[:, :length]
        weight = jnp.exp(scores - jnp.max(scores, -1, keepdims=True))
        probs = (weight / jnp.sum(weight, -1, keepdims=True)).astype(probs_ref.dtype)
        probs_ref[head] = probs
        chosen = value_ref[:, value_pair][
            :, head % 2 * head_value : (head % 2 + 1) * head_value
        ]
        return jnp.dot(probs, chosen, preferred_element_type=jnp.float32)

    def pair_step(index):
        both = [head_step(2 * index + side).astype(attended_ref.dtype) for side in range(2)]
        wide = 2 * columns // HEADS
        attended_ref[:, index * wide : (index + 1) * wide] = jnp.concatenate(both, 1)

    def out_step(i):
        at = pl.ds(i * tile, tile)
        value = jnp.dot(
            attended_ref[...], weight_hold[1, :, at], preferred_element_type=jnp.float32
        )
        total_ref[:, at] = total_ref[:, at] + value + params[6:7, at]

    tiles = range(columns // tile)

    def compute_list(n):
        if n == 2:
            return [wait_smalls, unpack, activate, lambda: write_result(0).start()]
        piece = n - 4
        if 0 <= piece < 5:
            work = [functools.partial(wait_weight, piece)]
            if piece != 2:
                work.append(functools.partial(shift_tap, piece))
            work += [functools.partial(conv_tap, piece, i) for i in tiles]
            return work
        if piece == 5:
            return [
                lambda: write_result(1).start(),
                functools.partial(norm_step, 1, 5),
                lambda: write_result(2).start(),
                table_step,
                lambda: write_result(7).start(),
                functools.partial(wait_weight, piece),
                query_step,
                key_step,
                lambda: [write_result(i).start() for i in (3, 4, 5)],
            ]
        if piece == 6:
            work = [functools.partial(wait_weight, piece)]
            work += [functools.partial(value_step, i) for i in tiles]
            work += [lambda: write_result(6).start(), functools.partial(pair_step, 0)]
            return work + [functools.partial(pair_step, 1)]
        if piece == 7:
            work = [functools.partial(pair_step, 2), functools.partial(pair_step, 3)]
            work += [lambda: [write_result(i).start() for i in (8, 9)]]
            work += [functools.partial(wait_weight, piece), lambda: write_result(1).wait()]
            work += [functools.partial(out_step, i) for i in tiles]
            work += [lambda: write_result(10).start(), lambda: write_result(2).wait()]
            return work + [
                functools.partial(norm_step, 2, 7),
                lambda: write_result(11).start(),
            ]
        return []

    def send_list(n):
        work = []
        if n + AHEAD < count:
            work.append(functools.partial(z_send, n + AHEAD))
        for shard in order:
            if n < count:
                work.append(functools.partial(stage_a, n, [shard]))
            if 1 <= n <= count:
                work.append(functools.partial(stage_b, n - 1, [shard]))
            if 2 <= n < count + 2:
                work.append(functools.partial(stage_c, n - 2, [shard]))
        return work

    for step in summing[1:4]:
        step()

    for n in range(count + 3):
        sends = send_list(n)
        work = compute_list(n)
        if 0 <= n - 3 < count:
            complete(n - 3)
            if n - 3 < 8:
                start_weight(n - 3)
        slots = max(len(work), 1)
        for i in range(slots):
            for send in sends[len(sends) * i // slots : len(sends) * (i + 1) // slots]:
                send()
            if i < len(work):
                work[i]()
        if n < 2:
            summing[4 + n]()

    for index in range(len(results)):
        if index not in (1, 2):
            write_result(index).wait()

    for piece in range(count):
        for shard in range(groups):

            @pl.when(jnp.logical_and(shard <= me, me + 1 < groups))
            def _():
                right_copy(piece, shard).wait_send()

            @pl.when(jnp.logical_and(shard >= me, me > 0))
            def _():
                left_copy(piece, shard).wait_send()

        sent = pieces[piece].at[pl.ds(0, others), pl.ds(0, 7 * part)]
        remote(sent, sent, send_sem.at[piece], sib_sem.at[piece], (sib, me)).wait_send()


def gather(groups, blocks, weights, small, stats, inputs, tables):
    conv, query = weights[:2]
    rel = weights[7]
    taps, rows, columns = conv.shape
    width = query.shape[1]
    length = inputs.shape[0]
    span = tables.shape[1]
    dtype = conv.dtype
    kept = pl.BlockSpec(memory_space=pl.ANY)
    inside = pl.BlockSpec(memory_space=pltpu.VMEM)
    full = jax.ShapeDtypeStruct((groups, rows, columns), dtype)
    count = taps + 7
    grid_sems = [pltpu.SemaphoreType.DMA((count, groups))] * 4
    wide = (length, columns)
    narrow = (length, width)
    made = [
        jax.ShapeDtypeStruct(wide, dtype),
        jax.ShapeDtypeStruct(wide, jnp.float32),
        jax.ShapeDtypeStruct(wide, dtype),
        jax.ShapeDtypeStruct(narrow, dtype),
        jax.ShapeDtypeStruct(narrow, dtype),
        jax.ShapeDtypeStruct(narrow, dtype),
        jax.ShapeDtypeStruct(wide, dtype),
        jax.ShapeDtypeStruct((span, width), dtype),
        jax.ShapeDtypeStruct((HEADS, length, length), dtype),
        jax.ShapeDtypeStruct(wide, dtype),
        jax.ShapeDtypeStruct(wide, jnp.float32),
        jax.ShapeDtypeStruct(wide, dtype),
    ]
    return pl.pallas_call(
        functools.partial(gather_kernel, groups, blocks),
        out_shape=(
            jax.ShapeDtypeStruct((taps, groups, rows, columns), dtype),
            jax.ShapeDtypeStruct((groups, rows, 2 * width), dtype),
            full,
            full,
            jax.ShapeDtypeStruct((groups, rows, 2 * columns), dtype),
            jax.ShapeDtypeStruct((groups, 2 * rows, columns), dtype),
            jax.ShapeDtypeStruct((groups,) + rel.shape, dtype),
            jax.ShapeDtypeStruct((groups,) + small.shape, jnp.float32),
            jax.ShapeDtypeStruct(stats.shape, jnp.float32),
            *made,
        ),
        in_specs=[kept] * 7 + [inside] * 5,
        out_specs=[kept] * 6 + [inside] * 3 + [kept] * len(made),
        scratch_shapes=[
            pltpu.VMEM((count - 1, rows, columns), dtype),
            pltpu.VMEM((rows, 2 * width), dtype),
            pltpu.SemaphoreType.DMA((taps + 8,)),
            pltpu.SemaphoreType.DMA((count,)),
            *grid_sems,
            pltpu.SemaphoreType.DMA((count,)),
            pltpu.SemaphoreType.DMA((count,)),
            *grid_sems[:2],
            *([pltpu.SemaphoreType.DMA((groups,))] * 4),
            *sum_scratch(groups, blocks, stats.shape),
            pltpu.VMEM((2, columns, columns), dtype),
            pltpu.SemaphoreType.DMA((2, groups)),
            pltpu.SemaphoreType.DMA((len(made),)),
            pltpu.VMEM((16, columns), jnp.float32),
            pltpu.VMEM(wide, dtype),
            pltpu.VMEM(wide, jnp.float32),
            pltpu.VMEM(wide, dtype),
            pltpu.VMEM(wide, dtype),
            pltpu.VMEM(narrow, dtype),
            pltpu.VMEM(narrow, dtype),
            pltpu.VMEM(narrow, dtype),
            pltpu.VMEM(wide, dtype),
            pltpu.VMEM((2, span, width), dtype),
            pltpu.VMEM((HEADS, length, length), dtype),
            pltpu.VMEM(wide, dtype),
        ],
        compiler_params=pltpu.CompilerParams(
            collective_id=0, has_side_effects=True, vmem_limit_bytes=60 << 20
        ),
        name="gather",
    )(*weights, small, stats, inputs, tables)


def reduce_kernel(groups, blocks, rel_at, *refs):
    lefts = refs[:5]
    rights = list(refs[5:11])
    rel_grad, vector = refs[11:13]
    out, total, left_got, wide_got, right_got = refs[13:18]
    (
        left_hold,
        right_hold,
        grad,
        x_one,
        y_one,
        x_two,
        y_two,
        shard_got,
        block_got,
        partial,
        done,
        rel_got,
    ) = refs[18:30]
    left_send, left_recv, right_send, right_recv, rel_send, rel_recv = refs[30:36]
    refs = refs[36:]
    load_sem = refs[0]
    x1s, y1s, x2s, y2s, x1r, y1r, x2r, y2r = refs[1:9]
    shard_send, shard_recv, block_send, block_recv = refs[9:13]
    write_sem, send_sem, ax, ay, ad, sib_sem = refs[13:19]
    sum_bufs = refs[19:23]
    sum_sems = refs[23:29]

    dp = lax.axis_index("dp")
    me = lax.axis_index("fsdp")
    near, shards, far = peers_of(groups, blocks)
    sib, along_x, along_y = neighbours(dp)
    core = dp % 2
    at_x = dp // 2 % 2
    at_y = dp // 4 % 2
    block = dp // 8
    slots = grad.shape[0]
    part = grad.shape[4]
    width = grad.shape[5]
    half = width // 2
    rows = 4 * part
    count = out.shape[0]
    others = groups - 1
    first = pl.ds(0, half)
    last = pl.ds(half, half)
    taps = 5
    up_right = rights[4]
    rights[4:5] = [up_right.at[:, pl.ds(side * 2 * width, 2 * width)] for side in range(2)]
    lefts_got = [left_got.at[index] for index in range(4)] + [wide_got]
    left_of = [0] * taps + [1, 1, 2, 3, 3, 4, 4]
    right_of = [0] * taps + [1, 2, 3, 4, 5, 6, 6]
    own_columns = pl.ds(pl.multiple_of(core * width, 128), width)
    sib_columns = pl.ds(pl.multiple_of((1 - core) * width, 128), width)

    def left_copy(index):
        return remote(
            lefts[index], lefts_got[index], left_send.at[index], left_recv.at[index], (sib, me)
        )

    def right_copy(index):
        return remote(
            rights[index].at[:, sib_columns],
            right_got.at[index],
            right_send.at[index],
            right_recv.at[index],
            (sib, me),
        )

    def rel_copy():
        return remote(rel_grad, rel_got, rel_send.at[0], rel_recv.at[0], (sib, me))

    def loads(piece, slot):
        left = left_of[piece]
        right = right_of[piece]
        pairs = [
            (rights[right].at[:, own_columns], right_hold.at[slot, 0]),
            (right_got.at[right], right_hold.at[slot, 1]),
        ]
        if left < 4:
            pairs.append((lefts[left], left_hold.at[slot, 0]))
            pairs.append((lefts_got[left], left_hold.at[slot, 1]))
        else:
            for shard in range(groups):
                source = pl.ds((2 * shard + piece % 2) * rows, rows)
                target = pl.ds(shard * rows, rows)
                pairs.append((lefts[left].at[:, source], left_hold.at[slot, 0, :, target]))
                pairs.append((lefts_got[left].at[:, source], left_hold.at[slot, 1, :, target]))
        return [
            pltpu.make_async_copy(src, dst, load_sem.at[slot, i])
            for i, (src, dst) in enumerate(pairs)
        ]

    def start_loads(piece):
        if left_of[piece] not in left_of[:piece]:
            left_copy(left_of[piece]).wait_recv()
        if right_of[piece] not in right_of[:piece]:
            right_copy(right_of[piece]).wait_recv()
        for copy in loads(piece, piece % 2):
            copy.start()

    meet(near + shards + far)

    for piece in range(count):
        if left_of[piece] not in left_of[:piece]:
            left_copy(left_of[piece]).start()
        if right_of[piece] not in right_of[:piece]:
            right_copy(right_of[piece]).start()
    rel_copy().start()
    start_loads(0)

    summing = sum_steps(groups, blocks, vector, total, *sum_bufs, sum_sems)

    def one(piece):
        slot = piece % slots
        return (
            remote(
                grad.at[slot, :, :, 1 - at_x, :, first],
                x_one.at[piece],
                x1s.at[piece],
                x1r.at[piece],
                (along_x, me),
            ),
            remote(
                grad.at[slot, :, 1 - at_y, :, :, last],
                y_one.at[piece],
                y1s.at[piece],
                y1r.at[piece],
                (along_y, me),
            ),
        )

    def two(piece):
        slot = piece % slots
        return (
            remote(
                grad.at[slot, :, 1 - at_y, at_x, :, first],
                y_two.at[piece],
                y2s.at[piece],
                y2r.at[piece],
                (along_y, me),
            ),
            remote(
                grad.at[slot, :, at_y, 1 - at_x, :, last],
                x_two.at[piece],
                x2s.at[piece],
                x2r.at[piece],
                (along_x, me),
            ),
        )

    def shard_copy(piece, j):
        other = (me + 1 + j) % groups
        return remote(
            grad.at[piece % slots, other, at_y, at_x],
            shard_got.at[piece, me],
            shard_send.at[piece, j],
            shard_recv.at[piece, me],
            (dp, other),
        )

    def shard_arrival(piece, j):
        other = (me + 1 + j) % groups
        return remote(
            grad.at[piece % slots, other, at_y, at_x],
            shard_got.at[piece, other],
            shard_send.at[piece, j],
            shard_recv.at[piece, other],
            (dp, other),
        )

    def block_copy(piece, j):
        return remote(
            partial.at[piece],
            block_got.at[piece, block],
            block_send.at[piece, j],
            block_recv.at[piece, block],
            far[j],
        )

    def block_arrival(piece, j):
        other = (block + 1 + j) % blocks
        return remote(
            partial.at[piece],
            block_got.at[piece, other],
            block_send.at[piece, j],
            block_recv.at[piece, other],
            far[j],
        )

    def place(piece, owner):
        return out.at[
            piece,
            pl.ds(pl.multiple_of(owner % 8 // 2 * part, 16), part),
            pl.ds(pl.multiple_of(core * width, 128), width),
        ]

    def spread(piece, src, owner, recv_sem, device):
        return remote(src, place(piece, owner), send_sem.at[piece], recv_sem, (device, me))

    def forward(piece, owner, recv_sem, device):
        return spread(piece, place(piece, owner), owner, recv_sem, device)

    diagonal = neighbours(along_x)[2]

    def shift(piece):
        move = piece - taps // 2
        for window in range(2):
            value = right_hold[piece % 2, window].astype(jnp.float32)
            value = pltpu.roll(value, move % value.shape[0], 0)
            row = lax.broadcasted_iota(jnp.int32, value.shape, 0)
            inside = row >= move if move > 0 else row < value.shape[0] + move
            value = jnp.where(inside, value, 0.0)
            right_hold[piece % 2, window] = value.astype(right_hold.dtype)

    def produce(piece):
        slot = piece % slots
        hold = piece % 2

        def shard_body(shard, carry):
            columns = pl.ds(pl.multiple_of(shard * rows, 128), rows)
            value = dot_leading(left_hold[hold, 0, :, columns], right_hold[hold, 0])
            value = value + dot_leading(left_hold[hold, 1, :, columns], right_hold[hold, 1])
            grad[slot, shard] = value.astype(grad.dtype).reshape(2, 2, part, width)
            return carry

        lax.fori_loop(0, groups, shard_body, 0)

        @pl.when(piece == taps)
        def _():
            rel_copy().wait()

        @pl.when(jnp.logical_and(piece == taps, core == 1))
        def _():
            for shard in range(groups):
                value = rel_grad[shard].astype(jnp.float32) + rel_got[shard].astype(jnp.float32)
                grad[slot, shard, 0, :, :, pl.ds(rel_at, rel_grad.shape[3])] = value.astype(
                    grad.dtype
                )

    def add(piece_slot, ref, columns, *index):
        ahead = grad[(piece_slot,) + index + (slice(None), columns)]
        return ahead.astype(jnp.float32) + ref.astype(jnp.float32)

    def body(n, carry):
        @pl.when(n < count)
        def _():
            @pl.when(n >= slots)
            def _():
                old = n - slots
                for copy in one(old) + two(old):
                    copy.wait_send()
                for j in range(others):
                    shard_copy(old, j).wait_send()

            for piece in range(count):

                @pl.when(n == piece)
                def _():
                    for copy in loads(piece, piece % 2):
                        copy.wait()
                    if piece + 1 < count:
                        start_loads(piece + 1)
                    if piece < taps and piece != taps // 2:
                        shift(piece)

            produce(n)
            for copy in one(n):
                copy.start()

        @pl.when(jnp.logical_and(n >= 1, n < count + 1))
        def _():
            piece = n - 1
            slot = piece % slots
            for copy in one(piece):
                copy.wait_recv()

            def shard_body(shard, carry):
                for other in range(2):
                    value = add(slot, x_one[piece, shard, other], first, shard, other, at_x)
                    grad[slot, shard, other, at_x, :, first] = value.astype(grad.dtype)
                    value = add(slot, y_one[piece, shard, other], last, shard, at_y, other)
                    grad[slot, shard, at_y, other, :, last] = value.astype(grad.dtype)
                return carry

            lax.fori_loop(0, groups, shard_body, 0)
            for copy in two(piece):
                copy.start()

        @pl.when(jnp.logical_and(n >= 2, n < count + 2))
        def _():
            piece = n - 2
            slot = piece % slots
            for copy in two(piece):
                copy.wait_recv()

            def shard_body(shard, carry):
                value = add(slot, y_two[piece, shard], first, shard, at_y, at_x)
                grad[slot, shard, at_y, at_x, :, first] = value.astype(grad.dtype)
                value = add(slot, x_two[piece, shard], last, shard, at_y, at_x)
                grad[slot, shard, at_y, at_x, :, last] = value.astype(grad.dtype)
                return carry

            lax.fori_loop(0, groups, shard_body, 0)
            for j in range(others):
                shard_copy(piece, j).start()

        @pl.when(jnp.logical_and(n >= 3, n < count + 3))
        def _():
            piece = n - 3
            value = grad[piece % slots, me, at_y, at_x].astype(jnp.float32)
            for j in range(others):
                shard_arrival(piece, j).wait_recv()
                value = value + shard_got[piece, (me + 1 + j) % groups].astype(jnp.float32)
            if blocks > 1:
                partial[piece] = value.astype(partial.dtype)
                block_got[piece, block] = value.astype(partial.dtype)
                for j in range(blocks - 1):
                    block_copy(piece, j).start()
                for j in range(blocks - 1):
                    block_copy(piece, j).wait_send()
                    block_arrival(piece, j).wait_recv()
                value = block_got[piece, 0].astype(jnp.float32)
                for other in range(1, blocks):
                    value = value + block_got[piece, other].astype(jnp.float32)
            done[piece] = value.astype(done.dtype)
            pltpu.make_async_copy(done.at[piece], place(piece, dp), write_sem.at[piece]).start()
            spread(piece, done.at[piece], dp, ax.at[piece], along_x).start()
            spread(piece, done.at[piece], dp, ay.at[piece], along_y).start()
            spread(piece, done.at[piece], dp, sib_sem.at[piece], sib).start()

        @pl.when(jnp.logical_and(n >= 4, n < count + 4))
        def _():
            piece = n - 4
            route = piece % 2
            forward(piece, along_x, ax.at[piece], dp).wait_recv()
            forward(piece, along_y, ay.at[piece], dp).wait_recv()
            owner = route * along_x + (1 - route) * along_y
            target = route * along_y + (1 - route) * along_x
            forward(piece, owner, ad.at[piece], target).start()
            forward(piece, along_x, sib_sem.at[piece], sib).start()
            forward(piece, along_y, sib_sem.at[piece], sib).start()

        @pl.when(n >= 5)
        def _():
            piece = n - 5
            forward(piece, diagonal, ad.at[piece], dp).wait_recv()
            forward(piece, diagonal, sib_sem.at[piece], sib).start()

        for step in range(len(summing)):

            @pl.when(n == step)
            def _():
                summing[step]()

        return carry

    lax.fori_loop(0, count + 5, body, 0)

    def drain(piece, carry):
        @pl.when(piece >= count - slots)
        def _():
            for copy in one(piece) + two(piece):
                copy.wait_send()
            for j in range(others):
                shard_copy(piece, j).wait_send()

        pltpu.make_async_copy(done.at[piece], place(piece, dp), write_sem.at[piece]).wait()
        got = out.at[piece, :, pl.ds(0, width)]
        remote(got, got, send_sem.at[piece], sib_sem.at[piece], (sib, me)).wait_recv()
        sent = out.at[piece, pl.ds(0, 7 * part // 2), :]
        remote(sent, sent, send_sem.at[piece], sib_sem.at[piece], (sib, me)).wait_send()
        return carry

    lax.fori_loop(0, count, drain, 0)
    for index in range(len(lefts)):
        left_copy(index).wait_send()
    for index in range(len(rights)):
        right_copy(index).wait_send()


def reduce(groups, blocks, rel_at, lefts, rights, rel_grad, vector):
    bins, columns = lefts[0].shape
    width = columns // 2
    rows = columns // groups
    part = rows // 4
    dtype = lefts[0].dtype
    count = 12
    slots = 5
    kept = pl.BlockSpec(memory_space=pl.ANY)
    inside = pl.BlockSpec(memory_space=pltpu.VMEM)
    each = pltpu.SemaphoreType.DMA((count,))
    return pl.pallas_call(
        functools.partial(reduce_kernel, groups, blocks, rel_at),
        out_shape=(
            jax.ShapeDtypeStruct((count, rows, columns), dtype),
            jax.ShapeDtypeStruct(vector.shape, jnp.float32),
            jax.ShapeDtypeStruct((4, bins, columns), dtype),
            jax.ShapeDtypeStruct(lefts[4].shape, dtype),
            jax.ShapeDtypeStruct((len(rights) + 1, bins, width), dtype),
        ),
        in_specs=[kept] * (len(lefts) + len(rights)) + [inside] * 2,
        out_specs=[kept, inside, kept, kept, kept],
        scratch_shapes=[
            pltpu.VMEM((2, 2, bins, columns), dtype),
            pltpu.VMEM((2, 2, bins, width), dtype),
            pltpu.VMEM((slots, groups, 2, 2, part, width), dtype),
            pltpu.VMEM((count, groups, 2, part, width // 2), dtype),
            pltpu.VMEM((count, groups, 2, part, width // 2), dtype),
            pltpu.VMEM((count, groups, part, width // 2), dtype),
            pltpu.VMEM((count, groups, part, width // 2), dtype),
            pltpu.VMEM((count, groups, part, width), dtype),
            pltpu.VMEM((count if blocks > 1 else 1, blocks, part, width), dtype),
            pltpu.VMEM((count if blocks > 1 else 1, part, width), dtype),
            pltpu.VMEM((count, part, width), dtype),
            pltpu.VMEM(rel_grad.shape, dtype),
            pltpu.SemaphoreType.DMA((len(lefts),)),
            pltpu.SemaphoreType.DMA((len(lefts),)),
            pltpu.SemaphoreType.DMA((len(rights) + 1,)),
            pltpu.SemaphoreType.DMA((len(rights) + 1,)),
            pltpu.SemaphoreType.DMA((1,)),
            pltpu.SemaphoreType.DMA((1,)),
            pltpu.SemaphoreType.DMA((2, 2 + 2 * groups)),
            *([each] * 8),
            pltpu.SemaphoreType.DMA((count, groups)),
            pltpu.SemaphoreType.DMA((count, groups)),
            pltpu.SemaphoreType.DMA((count, blocks)),
            pltpu.SemaphoreType.DMA((count, blocks)),
            *([each] * 6),
            *sum_scratch(groups, blocks, vector.shape),
        ],
        compiler_params=pltpu.CompilerParams(
            collective_id=1, has_side_effects=True, vmem_limit_bytes=60 << 20
        ),
        name="reduce",
    )(*lefts, *rights, rel_grad, vector)


EPSILON = 1e-05


def position_table(length, features, direction):
    basis_count = features // 6
    offsets = jnp.arange(2 * length - 1, dtype=jnp.float32) - (length - 1)
    offsets = offsets * direction
    distance = jnp.abs(offsets)[:, None]
    max_range = math.log(length) / math.log(2.0)
    half_life = 2.0 ** jnp.linspace(3.0, max_range, basis_count, dtype=jnp.float32)
    decaying = jnp.exp(-math.log(2.0) / half_life[None, :] * distance)
    widths = 2.0 ** jnp.arange(1, basis_count + 1, dtype=jnp.float32) - 1.0
    central = (widths[None, :] > distance).astype(jnp.float32)
    stddev = length / (2.0 * basis_count)
    centres = jnp.linspace(length / basis_count, length, basis_count, dtype=jnp.float32)
    shape_par = (centres / stddev) ** 2
    rate_par = centres / stddev**2
    safe_dist = jnp.maximum(distance, 1.0)
    log_prob = (shape_par - 1.0) * jnp.log(safe_dist) - rate_par * safe_dist
    log_prob = log_prob - jnp.max(log_prob, axis=0, keepdims=True)
    gamma_feat = jnp.where(distance > 0.5, jnp.exp(log_prob), 0.0)
    symmetric = jnp.concatenate([decaying, central, gamma_feat], 1)
    sign_row = jnp.sign(offsets)[:, None]
    return jnp.concatenate([symmetric, sign_row * symmetric], 1)


def normalize(values):
    centred = values - jnp.mean(values, -1, keepdims=True)
    inverse = lax.rsqrt(jnp.mean(centred * centred, -1, keepdims=True) + EPSILON)
    return (centred * inverse, inverse)


def norm_back(grad_std, standard, inverse):
    return inverse * (
        grad_std
        - jnp.mean(grad_std, -1, keepdims=True)
        - standard * jnp.mean(grad_std * standard, -1, keepdims=True)
    )


def dot_leading(left_side, right_side):
    return lax.dot_general(
        left_side, right_side, (((0,), (0,)), ((), ())), preferred_element_type=jnp.float32
    )


def dot_trailing(left_side, right_side):
    return lax.dot_general(
        left_side, right_side, (((1,), (1,)), ((), ())), preferred_element_type=jnp.float32
    )


def attend_back_kernel(
    probs_ref,
    out_ref,
    value_ref,
    key_ref,
    content_ref,
    position_ref,
    table_ref,
    query_grad_ref,
    key_grad_ref,
    value_grad_ref,
    table_grad_ref,
    offset_ref,
):
    length = content_ref.shape[0]
    span = table_ref.shape[0]
    head_value = value_ref.shape[1] // 2
    row = lax.broadcasted_iota(jnp.int32, (length, length), 0)
    column = lax.broadcasted_iota(jnp.int32, (length, length), 1)
    mirror = jnp.where(row + column == length - 1, 1.0, 0.0).astype(jnp.bfloat16)
    for head in range(2):
        keys = slice(head * KEY, (head + 1) * KEY)
        values = slice(head * head_value, (head + 1) * head_value)
        probs = probs_ref[head]
        out_grad = out_ref[:, values]
        value_grad_ref[:, values] = dot_leading(probs, out_grad).astype(jnp.bfloat16)
        prob_grad = dot_trailing(out_grad, value_ref[:, values])
        probs = probs.astype(jnp.float32)
        row_dot = jnp.sum(probs * prob_grad, -1, keepdims=True)
        score_grad = probs * (prob_grad - row_dot)
        rounded = score_grad.astype(jnp.bfloat16)
        key_grad_ref[:, keys] = dot_leading(rounded, content_ref[:, keys]).astype(jnp.bfloat16)
        content_grad = jnp.dot(rounded, key_ref[:, keys], preferred_element_type=jnp.float32)
        mirrored = jnp.dot(rounded, mirror, preferred_element_type=jnp.float32)
        wide = jnp.concatenate([mirrored, jnp.zeros((length, span - length), jnp.float32)], 1)
        band = pltpu.roll(wide, 0, 1, stride=1, stride_axis=0)
        band = band.astype(jnp.bfloat16)
        position_grad = jnp.dot(band, table_ref[:, keys], preferred_element_type=jnp.float32)
        table_grad_ref[:, keys] = dot_leading(band, position_ref[:, keys]).astype(jnp.bfloat16)
        query_grad_ref[:, keys] = ((content_grad + position_grad) * KEY**-0.5).astype(
            jnp.bfloat16
        )
        offset_ref[0:1, keys] = jnp.sum(content_grad, 0, keepdims=True)
        offset_ref[1:2, keys] = jnp.sum(position_grad, 0, keepdims=True)


def attend_back(probs, out_grad, value, key, content, position, table):
    length = content.shape[0]
    span = table.shape[0]
    steps = HEADS // 2

    def columns(array):
        return pl.BlockSpec((array.shape[0], array.shape[1] // steps), lambda i: (0, i))

    offsets = jax.ShapeDtypeStruct((2, key.shape[1]), jnp.float32)
    return pl.pallas_call(
        attend_back_kernel,
        grid=(steps,),
        in_specs=[pl.BlockSpec((2, length, length), lambda i: (i, 0, 0))]
        + [columns(array) for array in (out_grad, value, key, content, position, table)],
        out_specs=[columns(array) for array in (content, key, value, table, offsets)],
        out_shape=[
            jax.ShapeDtypeStruct(array.shape, jnp.bfloat16)
            for array in (content, key, value, table)
        ]
        + [offsets],
        compiler_params=pltpu.CompilerParams(vmem_limit_bytes=40 << 20),
        cost_estimate=pl.CostEstimate(
            flops=4 * length * (HEADS * KEY * (length + span) + length * value.shape[1]),
            bytes_accessed=2 * HEADS * length * length,
            transcendentals=0,
        ),
        name="attend_back",
    )(probs, out_grad, value, key, content, position, table)


def conv_back_kernel(left_ref, right_ref, out_ref):
    @pl.when(pl.program_id(0) == 0)
    def _():
        out_ref[...] = jnp.zeros_like(out_ref)

    out_ref[...] += dot_trailing(left_ref[...], right_ref[0])


def conv_back(left, right):
    length = left.shape[0]
    taps, columns = right.shape[:2]
    return pl.pallas_call(
        conv_back_kernel,
        grid=(taps,),
        in_specs=[
            pl.BlockSpec((length, columns), lambda i: (0, i)),
            pl.BlockSpec((1, columns, columns), lambda i: (i, 0, 0)),
        ],
        out_specs=pl.BlockSpec((length, columns), lambda i: (0, 0)),
        out_shape=jax.ShapeDtypeStruct((length, columns), jnp.float32),
        compiler_params=pltpu.CompilerParams(vmem_limit_bytes=40 << 20),
        cost_estimate=pl.CostEstimate(
            flops=2 * taps * length * columns * columns,
            bytes_accessed=2 * taps * columns * (columns + length),
            transcendentals=0,
        ),
        name="conv_back",
    )(left, right)


def on_device(
    tokens,
    conv_weight,
    query_weight,
    key_weight,
    value_weight,
    out_weight,
    rel_weight,
    up_weight,
    down_weight,
    gains,
    biases,
    up_bias,
    rel_bias,
    target_table,
    clip_levels,
    window_ids,
    clip_index,
):
    groups = lax.axis_size("fsdp")
    blocks = lax.axis_size("dp") // 8
    tap_count, piece_rows, model_width = conv_weight.shape
    half_taps = tap_count // 2
    half_width = model_width // 2
    key_width = query_weight.shape[1]
    rel_rows, rel_columns = rel_weight.shape
    inputs = tokens[0].astype(jnp.float32)
    length = inputs.shape[0]
    token_total = length * lax.axis_size("dp") * lax.axis_size("fsdp")

    small_parts = [gains, biases, up_bias, rel_bias]
    small = jnp.concatenate([part.reshape(-1) for part in small_parts])
    small = jnp.pad(small, (0, -small.shape[0] % 1024)).reshape(-1, 128)
    stats = jnp.concatenate([jnp.sum(inputs, 0), jnp.sum(inputs * inputs, 0)]).reshape(-1, 128)
    tables = jnp.stack(
        [
            jnp.pad(position_table(length, rel_rows, direction), ((0, 1), (0, 0)))
            for direction in (1.0, -1.0)
        ]
    ).astype(jnp.bfloat16)
    (
        conv_full,
        mixed_full,
        value_full,
        out_full,
        up_full,
        down_full,
        _,
        small_full,
        stats,
        activated,
        after_conv,
        normed_one,
        content_query,
        position_query,
        keys,
        values,
        mirrored_keys,
        probs,
        attended,
        after_attention,
        normed_two,
    ) = gather(
        groups,
        blocks,
        [
            conv_weight,
            query_weight,
            key_weight,
            value_weight,
            out_weight,
            up_weight,
            down_weight,
            rel_weight,
        ],
        small,
        stats,
        tokens[0],
        tables,
    )
    conv_full = conv_full.reshape(tap_count, model_width, model_width)
    mixed_full = mixed_full.reshape(model_width, -1)
    value_full = value_full.reshape(model_width, -1)
    out_full = out_full.reshape(model_width, -1)
    up_full = up_full.reshape(model_width, -1)
    down_full = down_full.reshape(-1, model_width)
    flat = small_full.reshape(groups, -1)
    taken = 0
    unpacked = []
    for part in small_parts:
        chosen = flat[:, taken : taken + part.size].reshape((groups,) + part.shape)
        unpacked.append(chosen)
        taken += part.size
    gain_rows = jnp.moveaxis(unpacked[0], 0, 1).reshape(gains.shape[0], -1)
    bias_rows = jnp.moveaxis(unpacked[1], 0, 1).reshape(biases.shape[0], -1)
    up_offset = unpacked[2].reshape(-1)
    batch_sums = stats.reshape(2, -1)
    centre = batch_sums[0] / token_total
    variance = batch_sums[1] / token_total - centre * centre
    inverse = lax.rsqrt(variance + EPSILON)
    standard = (inputs - centre) * inverse
    normed = standard * gain_rows[0] + bias_rows[0]
    standard_one, inverse_one = normalize(after_conv)
    standard_two, inverse_two = normalize(after_attention)
    hidden_pre = jnp.dot(normed_two, up_full, preferred_element_type=jnp.float32) + up_offset
    hidden = jax.nn.gelu(hidden_pre).astype(jnp.bfloat16)
    outputs = (
        after_attention
        + jnp.dot(hidden, down_full, preferred_element_type=jnp.float32)
        + bias_rows[5]
    )
    target_row = lax.dynamic_index_in_dim(target_table, window_ids[0], 0, keepdims=False)
    levels = jnp.arange(clip_levels.shape[0], dtype=jnp.int32)
    selector = (clip_index[0][:, None] == levels[None, :]).astype(jnp.float32)
    limits = jnp.sum(selector * clip_levels[None, :], 1)[:, None]
    cotangent = jnp.clip(outputs - target_row, -limits, limits).astype(jnp.bfloat16)
    cot_value = cotangent.astype(jnp.float32)
    grad_down_bias = jnp.sum(cot_value, 0)
    hidden_grad = dot_trailing(cotangent, down_full)
    gelu_pull = jax.vjp(jax.nn.gelu, hidden_pre)[1]
    pre_grad = gelu_pull(hidden_grad)[0].astype(jnp.bfloat16)
    grad_up_bias = jnp.sum(pre_grad.astype(jnp.float32), 0)
    normed_two_grad = dot_trailing(pre_grad, up_full)
    grad_gain_two = jnp.sum(normed_two_grad * standard_two, 0)
    grad_bias_two = jnp.sum(normed_two_grad, 0)
    attention_grad = cot_value + norm_back(
        normed_two_grad * gain_rows[2], standard_two, inverse_two
    )
    branch_grad = attention_grad.astype(jnp.bfloat16)
    grad_out_bias = jnp.sum(branch_grad.astype(jnp.float32), 0)
    attended_grad = dot_trailing(branch_grad, out_full).astype(jnp.bfloat16)
    query_grad, key_grad, value_grad, table_grad, grad_rel_bias = attend_back(
        probs, attended_grad, values, keys, content_query, position_query, mirrored_keys
    )
    mixed_grad = jnp.concatenate([query_grad, key_grad], 1)
    normed_one_grad = (
        dot_trailing(mixed_grad, mixed_full)
        + dot_trailing(value_grad, value_full)
    )
    grad_gain_one = jnp.sum(normed_one_grad * standard_one, 0)
    grad_bias_one = jnp.sum(normed_one_grad, 0)
    conv_side_grad = attention_grad + norm_back(
        normed_one_grad * gain_rows[1], standard_one, inverse_one
    )
    conv_grad = conv_side_grad.astype(jnp.bfloat16)
    grad_conv_bias = jnp.sum(conv_grad.astype(jnp.float32), 0)
    padded = jnp.pad(conv_grad, ((half_taps, half_taps), (0, 0)))
    stacked_grad = jnp.concatenate(
        [padded[tap : tap + length] for tap in reversed(range(tap_count))], 1
    )
    activated_grad = conv_back(stacked_grad, conv_full)
    act_pull = jax.vjp(jax.nn.gelu, normed)[1]
    normed_grad = act_pull(activated_grad)[0]
    sum_parts = [
        jnp.sum(normed_grad * standard, 0),
        grad_gain_one,
        grad_gain_two,
        jnp.sum(normed_grad, 0),
        grad_conv_bias,
        grad_bias_one,
        grad_out_bias,
        grad_bias_two,
        grad_down_bias,
        grad_up_bias,
        grad_rel_bias.reshape(-1),
    ]
    sums = jnp.concatenate(sum_parts)
    sums = jnp.pad(sums, (0, -sums.shape[0] % 1024)).reshape(-1, 128)
    grad_rel = dot_leading(tables[1], table_grad).astype(jnp.bfloat16)
    grad_rel = jnp.moveaxis(grad_rel.reshape(rel_rows, groups, rel_columns), 0, 1)
    grad_rel = grad_rel.reshape(groups, 2, rel_rows // 2, rel_columns)
    mixed_wide = jnp.pad(mixed_grad, ((0, 0), (0, model_width - 2 * key_width)))
    lefts = [activated, normed_one, attended, normed_two, hidden]
    rights = [
        conv_grad,
        mixed_wide,
        value_grad,
        branch_grad,
        pre_grad,
        cotangent,
    ]
    pieces, sums, _, _, _ = reduce(
        groups, blocks, 2 * key_width - half_width, lefts, rights, grad_rel, sums
    )
    flat = sums.reshape(-1)
    bn_sums = flat[: 4 * model_width].reshape(4, model_width)
    input_grad = conv_side_grad + inverse * (
        normed_grad * gain_rows[0]
        - gain_rows[0] * (bn_sums[3] + standard * bn_sums[0]) / token_total
    )
    shard = lax.axis_index("fsdp")
    by_shard = flat[: 9 * model_width].reshape(9, groups, -1)
    by_shard = lax.dynamic_index_in_dim(by_shard, shard, 1, keepdims=False)
    up_sums = flat[9 * model_width : 11 * model_width].reshape(groups, -1)
    up_sums = lax.dynamic_index_in_dim(up_sums, shard, 0, keepdims=False)
    rel_sums = flat[11 * model_width : 11 * model_width + 2 * key_width]
    rel_sums = rel_sums.reshape(2, groups, -1)
    rel_sums = lax.dynamic_index_in_dim(rel_sums, shard, 1, keepdims=False)
    up_grad = jnp.concatenate([pieces[8], pieces[9]], 1)
    mixed_sum = pieces[5].astype(jnp.float32)
    rel_at = 2 * key_width
    return (
        outputs.astype(jnp.bfloat16)[None],
        input_grad.astype(jnp.bfloat16)[None],
        pieces[:5].astype(jnp.float32),
        mixed_sum[:, :key_width],
        mixed_sum[:, key_width:rel_at],
        pieces[6].astype(jnp.float32),
        pieces[7].astype(jnp.float32),
        mixed_sum[:rel_rows, rel_at : rel_at + rel_columns],
        up_grad.astype(jnp.float32),
        pieces[10:12].reshape(2 * piece_rows, -1).astype(jnp.float32),
        by_shard[:3],
        by_shard[3:9],
        up_sums,
        rel_sums,
    )


def solution(mesh):
    placed = (
        P(("dp", "fsdp"), None, None),
        P(None, "fsdp", None),
        P("fsdp", None),
        P("fsdp", None),
        P("fsdp", None),
        P("fsdp", None),
        P(None, "fsdp"),
        P("fsdp", None),
        P("fsdp", None),
        P(None, "fsdp"),
        P(None, "fsdp"),
        P("fsdp"),
        P(None, "fsdp"),
        P(),
        P(),
        P(("dp", "fsdp")),
        P(("dp", "fsdp"), None),
    )
    return jax.shard_map(
        on_device,
        mesh=mesh,
        in_specs=placed,
        out_specs=(
            P(("dp", "fsdp"), None, None),
            P(("dp", "fsdp"), None, None),
            P(None, "fsdp", None),
            P("fsdp", None),
            P("fsdp", None),
            P("fsdp", None),
            P("fsdp", None),
            P(None, "fsdp"),
            P("fsdp", None),
            P("fsdp", None),
            P(None, "fsdp"),
            P(None, "fsdp"),
            P("fsdp"),
            P(None, "fsdp"),
        ),
        check_vma=False,
    )
```

```python
import functools
import math

import jax
import jax.numpy as jnp
from jax import lax
from jax.experimental import pallas as pl
from jax.experimental.pallas import tpu as pltpu
from jax.sharding import PartitionSpec as P

HEADS = 8
KEY = 64
MESH = pl.DeviceIdType.MESH
AHEAD = 2
GELU = 0.7978845608028654
VMEM_LIMIT = 62 << 20


def neighbours(dp):
    core = dp % 2
    along_x = dp // 2 % 2
    along_y = dp // 4 % 2
    return dp + 1 - 2 * core, dp + 2 - 4 * along_x, dp + 4 - 8 * along_y


def remote(src, dst, send_sem, recv_sem, device):
    return pltpu.make_async_remote_copy(
        src_ref=src,
        dst_ref=dst,
        send_sem=send_sem,
        recv_sem=recv_sem,
        device_id=device,
        device_id_type=MESH,
    )


def meet(peers):
    barrier = pltpu.get_barrier_semaphore()
    for peer in peers:
        pl.semaphore_signal(barrier, inc=1, device_id=peer, device_id_type=MESH)
    pl.semaphore_wait(barrier, len(peers))


def peers_of(groups, blocks):
    dp = lax.axis_index("dp")
    me = lax.axis_index("fsdp")
    near = [(device, me) for device in neighbours(dp)]
    shards = [(dp, (me + 1 + j) % groups) for j in range(groups - 1)]
    far = [((dp + 8 * (1 + j)) % (8 * blocks), me) for j in range(blocks - 1)]
    return near, shards, far


def sum_steps(groups, blocks, vector, total, near_got, sums, shard_got, block_got, sems):
    near_send, near_recv, shard_send, shard_recv, block_send, block_recv = sems
    me = lax.axis_index("fsdp")
    block = lax.axis_index("dp") // 8
    near, shards, far = peers_of(groups, blocks)

    def near_copy(step):
        src = vector if step == 0 else sums.at[step - 1]
        return remote(
            src, near_got.at[step], near_send.at[step], near_recv.at[step], near[step]
        )

    def fold(step):
        copy = near_copy(step)
        copy.wait()
        held = vector[...] if step == 0 else sums[step - 1]
        sums[step] = held + near_got[step]

    def shard_copy(j):
        return remote(
            sums.at[2], shard_got.at[me], shard_send.at[j], shard_recv.at[me], shards[j]
        )

    def block_copy(j):
        return remote(
            sums.at[3], block_got.at[block], block_send.at[j], block_recv.at[block], far[j]
        )

    def start():
        near_copy(0).start()

    def second():
        fold(0)
        near_copy(1).start()

    def third():
        fold(1)
        near_copy(2).start()

    def fourth():
        fold(2)
        for j in range(groups - 1):
            shard_copy(j).start()
        shard_got[me] = sums[2]

    def fifth():
        for j in range(groups - 1):
            shard_copy(j).wait_send()
            other = (me + 1 + j) % groups
            remote(
                sums.at[2], shard_got.at[other], shard_send.at[j], shard_recv.at[other], shards[j]
            ).wait_recv()
        added = shard_got[0]
        for shard in range(1, groups):
            added = added + shard_got[shard]
        sums[3] = added
        for j in range(blocks - 1):
            block_copy(j).start()
        block_got[block] = added

    def sixth():
        for j in range(blocks - 1):
            block_copy(j).wait_send()
            other = (block + 1 + j) % blocks
            remote(
                sums.at[3], block_got.at[other], block_send.at[j], block_recv.at[other], far[j]
            ).wait_recv()
        added = block_got[0]
        for other in range(1, blocks):
            added = added + block_got[other]
        total[...] = added

    return [start, second, third, fourth, fifth, sixth]


def sum_scratch(groups, blocks, shape):
    return [
        pltpu.VMEM((3,) + shape, jnp.float32),
        pltpu.VMEM((4,) + shape, jnp.float32),
        pltpu.VMEM((groups,) + shape, jnp.float32),
        pltpu.VMEM((blocks,) + shape, jnp.float32),
        pltpu.SemaphoreType.DMA((3,)),
        pltpu.SemaphoreType.DMA((3,)),
        pltpu.SemaphoreType.DMA((groups,)),
        pltpu.SemaphoreType.DMA((groups,)),
        pltpu.SemaphoreType.DMA((blocks,)),
        pltpu.SemaphoreType.DMA((blocks,)),
    ]


def gather_kernel(groups, blocks, *refs):
    weights = refs[:8]
    conv, query, key, value, out, up, down, rel = weights
    small, stats, inputs, tables = refs[8:12]
    outs = refs[12:21]
    conv_out, mixed_out, value_out, out_out, up_out, down_out = outs[:6]
    rel_full, small_full, stat_total = outs[6:]
    results = refs[21:33]
    hold, hold_mixed, local_sem, write_sem = refs[33:37]
    z_sem, x_sem, y_sem, d_sem, sib_sem, send_sem, right_send, left_send = refs[37:45]
    rel_send, rel_recv, small_send, small_recv = refs[45:49]
    near_got, sums, shard_got, block_got = refs[49:53]
    sum_sems = refs[53:59]
    weight_hold, weight_sem, result_sem = refs[59:62]
    params, shifted_ref, total_ref = refs[62:65]
    act_ref, norm_ref, content_ref, position_ref, key_ref, value_ref = refs[65:71]
    table_ref, probs_ref, attended_ref = refs[71:74]
    dp = lax.axis_index("dp")
    me = lax.axis_index("fsdp")
    near, shards, far = peers_of(groups, blocks)
    sib, along_x, along_y = neighbours(dp)
    rows = conv.shape[1]
    part = rows // 8
    others = groups - 1
    columns = conv.shape[2]
    pieces = [conv_out.at[tap] for tap in range(5)] + [mixed_out, value_out, out_out]
    pieces += [up_out.at[:, :, pl.ds(half * columns, columns)] for half in range(2)]
    pieces += [down_out.at[:, pl.ds(half * rows, rows)] for half in range(2)]
    count = len(pieces)
    holds = [hold.at[i] for i in range(5)] + [hold_mixed] + [hold.at[i] for i in range(5, 11)]

    pending = [[] for _ in range(count)]
    started = [0]

    def load(src, dst, piece):
        copy = pltpu.make_async_copy(src, dst, local_sem.at[started[0]])
        copy.start()
        started[0] += 1
        pending[piece].append(copy)

    for tap in range(5):
        load(conv.at[tap], holds[tap], tap)
    width = query.shape[1]
    load(query, hold_mixed.at[:, pl.ds(0, width)], 5)
    load(key, hold_mixed.at[:, pl.ds(width, width)], 5)
    load(value, holds[6], 6)
    load(out, holds[7], 7)
    for half in range(2):
        load(up.at[:, pl.ds(half * columns, columns)], holds[8 + half], 8 + half)
    for half in range(2):
        load(down.at[pl.ds(half * rows, rows)], holds[10 + half], 10 + half)

    meet(near + shards + far)

    summing = sum_steps(
        groups, blocks, stats, stat_total, near_got, sums, shard_got, block_got, sum_sems
    )
    summing[0]()

    for j in range(others):
        remote(
            rel, rel_full.at[me], rel_send.at[j], rel_recv.at[me], shards[j]
        ).start()
        remote(
            small, small_full.at[me], small_send.at[j], small_recv.at[me], shards[j]
        ).start()
    rel_full[me] = rel[...]
    small_full[me] = small[...]

    def slice_of(piece, shard, owner):
        return pieces[piece].at[shard, pl.ds(pl.multiple_of(owner % 8 * part, 16), part)]

    def copy_of(piece, shard, owner, recv_sem, device):
        ref = slice_of(piece, shard, owner)
        return remote(ref, ref, send_sem.at[piece], recv_sem, (device, me))

    order = []
    for j in range(others):
        pick = 0
        for m in range(groups):
            nearest = sorted((t for t in range(groups) if t != m), key=lambda t: abs(t - m))
            pick = pick + jnp.where(me == m, nearest[j], 0)
        order.append(pick)

    def right_copy(piece, shard, src=None):
        dst = slice_of(piece, shard, dp)
        return remote(
            dst if src is None else src,
            dst,
            right_send.at[piece, shard],
            z_sem.at[piece, shard],
            (dp, (me + 1) % groups),
        )

    def left_copy(piece, shard, src=None):
        dst = slice_of(piece, shard, dp)
        return remote(
            dst if src is None else src,
            dst,
            left_send.at[piece, shard],
            z_sem.at[piece, shard],
            (dp, (me + groups - 1) % groups),
        )

    def z_send(piece):
        src = holds[piece].at[pl.ds(pl.multiple_of(dp % 8 * part, 16), part)]

        @pl.when(me + 1 < groups)
        def _():
            right_copy(piece, me, src).start()

        @pl.when(me > 0)
        def _():
            left_copy(piece, me, src).start()

    diagonal = neighbours(along_x)[2]

    def stage_a(piece, shards_now):
        for shard in shards_now:
            copy_of(piece, shard, dp, z_sem.at[piece, shard], dp).wait_recv()

            @pl.when(jnp.logical_and(shard < me, me + 1 < groups))
            def _():
                right_copy(piece, shard).start()

            @pl.when(jnp.logical_and(shard > me, me > 0))
            def _():
                left_copy(piece, shard).start()

            copy_of(piece, shard, dp, x_sem.at[piece, shard], along_x).start()
            copy_of(piece, shard, dp, y_sem.at[piece, shard], along_y).start()
            copy_of(piece, shard, dp, sib_sem.at[piece], sib).start()

    def stage_b(piece, shards_now):
        for shard in shards_now:
            route = (piece + shard) % 2
            copy_of(piece, shard, along_x, x_sem.at[piece, shard], dp).wait_recv()
            copy_of(piece, shard, along_y, y_sem.at[piece, shard], dp).wait_recv()
            owner = route * along_x + (1 - route) * along_y
            target = route * along_y + (1 - route) * along_x
            copy_of(piece, shard, owner, d_sem.at[piece, shard], target).start()
            copy_of(piece, shard, along_x, sib_sem.at[piece], sib).start()
            copy_of(piece, shard, along_y, sib_sem.at[piece], sib).start()

    def stage_c(piece, shards_now):
        for shard in shards_now:
            copy_of(piece, shard, diagonal, d_sem.at[piece, shard], dp).wait_recv()
            copy_of(piece, shard, diagonal, sib_sem.at[piece], sib).start()

    writes = []
    for piece in range(count):
        for copy in pending[piece]:
            copy.wait()
        copy = pltpu.make_async_copy(holds[piece], pieces[piece].at[me], write_sem.at[piece])
        copy.start()
        writes.append(copy)
        if piece < AHEAD:
            z_send(piece)

    def complete(piece):
        writes[piece].wait()
        got = pieces[piece].at[pl.ds(0, others), pl.ds(0, 4 * part)]
        remote(got, got, send_sem.at[piece], sib_sem.at[piece], (sib, me)).wait_recv()

    def weight_loads(piece):
        width = pieces[piece].shape[2]
        return [
            pltpu.make_async_copy(
                pieces[piece].at[shard],
                weight_hold.at[piece % 2, pl.ds(shard * rows, rows), pl.ds(0, width)],
                weight_sem.at[piece % 2, shard],
            )
            for shard in range(groups)
        ]

    def start_weight(piece):
        for copy in weight_loads(piece):
            copy.start()

    def wait_weight(piece):
        for copy in weight_loads(piece):
            copy.wait()

    def wait_smalls():
        for j in range(others):
            shard = (me + 1 + j) % groups
            remote(
                rel, rel_full.at[shard], rel_send.at[j], rel_recv.at[shard], shards[j]
            ).wait()
            remote(
                small, small_full.at[shard], small_send.at[j], small_recv.at[shard], shards[j]
            ).wait()

    length = inputs.shape[0]
    block_rows = 128
    tile = 512
    per_row = rows // 128
    token_total = length * 8 * blocks * groups

    def by_rows(fn):
        def row_body(i, carry):
            fn(pl.ds(pl.multiple_of(i * block_rows, block_rows), block_rows))
            return carry

        lax.fori_loop(0, length // block_rows, row_body, 0)

    def unpack():
        for row in range(9):
            for shard in range(groups):
                for j in range(per_row):
                    at = shard * rows + j * 128
                    source = row * per_row + j
                    params[row : row + 1, at : at + 128] = small_full[
                        shard, source : source + 1, :
                    ]
        lanes = columns // 128
        for j in range(lanes):
            centre = stat_total[j : j + 1, :] / token_total
            square = stat_total[lanes + j : lanes + j + 1, :] / token_total
            params[9:10, j * 128 : (j + 1) * 128] = centre
            params[10:11, j * 128 : (j + 1) * 128] = lax.rsqrt(
                square - centre * centre + EPSILON
            )
        taken = (9 * rows + 2 * rows) // 128
        for side in range(2):
            for shard in range(groups):
                params[11 + side : 12 + side, shard * 128 : (shard + 1) * 128] = small_full[
                    shard, taken + side : taken + side + 1, :
                ]

    def activate():
        def rows_fn(at):
            standard = (inputs[at, :].astype(jnp.float32) - params[9:10, :]) * params[10:11, :]
            act_ref[at, :] = jax.nn.gelu(standard * params[0:1, :] + params[3:4, :]).astype(
                act_ref.dtype
            )

        by_rows(rows_fn)

    result_of = [
        act_ref,
        total_ref,
        norm_ref,
        content_ref,
        position_ref,
        key_ref,
        value_ref,
        table_ref.at[1],
        probs_ref,
        attended_ref,
        total_ref,
        norm_ref,
    ]

    def write_result(index):
        return pltpu.make_async_copy(result_of[index], results[index], result_sem.at[index])

    def shift_tap(tap):
        move = tap - 2

        def column_body(i, carry):
            at = pl.ds(pl.multiple_of(i * rows, 128), rows)
            value = act_ref[:, at].astype(jnp.float32)
            value = pltpu.roll(value, -move % length, 0)
            row = lax.broadcasted_iota(jnp.int32, value.shape, 0)
            inside = row < length - move if move > 0 else row >= -move
            shifted_ref[:, at] = jnp.where(inside, value, 0.0).astype(shifted_ref.dtype)
            return carry

        lax.fori_loop(0, columns // rows, column_body, 0)

    def conv_tap(tap, i):
        at = pl.ds(i * tile, tile)
        left = act_ref if tap == 2 else shifted_ref
        value = jnp.dot(
            left[...], weight_hold[tap % 2, :, at], preferred_element_type=jnp.float32
        )
        if tap == 0:
            value = value + (inputs[:, at].astype(jnp.float32) + params[4:5, at])
        else:
            value = value + total_ref[:, at]
        total_ref[:, at] = value

    def norm_step(gain, bias):
        def rows_fn(at):
            standard, _ = normalize(total_ref[at, :])
            norm_ref[at, :] = (
                standard * params[gain : gain + 1, :] + params[bias : bias + 1, :]
            ).astype(norm_ref.dtype)

        by_rows(rows_fn)

    def query_step():
        raw = jnp.dot(
            norm_ref[...], weight_hold[1, :, 0:width], preferred_element_type=jnp.float32
        )
        raw = raw * KEY**-0.5
        content_ref[...] = (raw + params[11:12, 0:width]).astype(content_ref.dtype)
        position_ref[...] = (raw + params[12:13, 0:width]).astype(position_ref.dtype)

    def key_step():
        key_ref[...] = jnp.dot(
            norm_ref[...], weight_hold[1, :, width : 2 * width], preferred_element_type=jnp.float32
        ).astype(key_ref.dtype)

    def table_step():
        for side in range(2):
            for shard in range(groups):
                table_ref[side, :, shard * 128 : (shard + 1) * 128] = jnp.dot(
                    tables[side], rel_full[shard], preferred_element_type=jnp.float32
                ).astype(table_ref.dtype)

    def value_step(i):
        at = pl.ds(i * tile, tile)
        value_ref[:, at] = jnp.dot(
            norm_ref[...], weight_hold[0, :, at], preferred_element_type=jnp.float32
        ).astype(value_ref.dtype)

    def head_step(head):
        head_value = columns // HEADS
        span = tables.shape[1]
        pair = slice(head // 2 * 2 * KEY, (head // 2 + 1) * 2 * KEY)
        value_pair = slice(head // 2 * 2 * head_value, (head // 2 + 1) * 2 * head_value)
        keys = slice(head % 2 * KEY, (head % 2 + 1) * KEY)
        band = dot_trailing(position_ref[:, pair][:, keys], table_ref[0, :, pair][:, keys])
        moved = pltpu.roll(band, span - length + 1, 1, stride=1, stride_axis=0)
        scores = dot_trailing(content_ref[:, pair][:, keys], key_ref[:, pair][:, keys])
        scores = scores + moved[:, :length]
        weight = jnp.exp(scores - jnp.max(scores, -1, keepdims=True))
        probs = (weight / jnp.sum(weight, -1, keepdims=True)).astype(probs_ref.dtype)
        probs_ref[head] = probs
        chosen = value_ref[:, value_pair][
            :, head % 2 * head_value : (head % 2 + 1) * head_value
        ]
        return jnp.dot(probs, chosen, preferred_element_type=jnp.float32)

    def pair_step(index):
        both = [head_step(2 * index + side).astype(attended_ref.dtype) for side in range(2)]
        wide = 2 * columns // HEADS
        attended_ref[:, index * wide : (index + 1) * wide] = jnp.concatenate(both, 1)

    def out_step(i):
        at = pl.ds(i * tile, tile)
        value = jnp.dot(
            attended_ref[...], weight_hold[1, :, at], preferred_element_type=jnp.float32
        )
        total_ref[:, at] = total_ref[:, at] + value + params[6:7, at]

    tiles = range(columns // tile)

    def compute_list(n):
        if n == 2:
            return [wait_smalls, unpack, activate, lambda: write_result(0).start()]
        piece = n - 4
        if 0 <= piece < 5:
            work = [functools.partial(wait_weight, piece)]
            if piece != 2:
                work.append(functools.partial(shift_tap, piece))
            work += [functools.partial(conv_tap, piece, i) for i in tiles]
            return work
        if piece == 5:
            return [
                lambda: write_result(1).start(),
                functools.partial(norm_step, 1, 5),
                lambda: write_result(2).start(),
                table_step,
                lambda: write_result(7).start(),
                functools.partial(wait_weight, piece),
                query_step,
                key_step,
                lambda: [write_result(i).start() for i in (3, 4, 5)],
            ]
        if piece == 6:
            work = [functools.partial(wait_weight, piece)]
            work += [functools.partial(value_step, i) for i in tiles]
            work += [lambda: write_result(6).start(), functools.partial(pair_step, 0)]
            return work + [functools.partial(pair_step, 1)]
        if piece == 7:
            work = [functools.partial(pair_step, 2), functools.partial(pair_step, 3)]
            work += [lambda: [write_result(i).start() for i in (8, 9)]]
            work += [functools.partial(wait_weight, piece), lambda: write_result(1).wait()]
            work += [functools.partial(out_step, i) for i in tiles]
            work += [lambda: write_result(10).start(), lambda: write_result(2).wait()]
            return work + [
                functools.partial(norm_step, 2, 7),
                lambda: write_result(11).start(),
            ]
        return []

    def send_list(n):
        work = []
        if n + AHEAD < count:
            work.append(functools.partial(z_send, n + AHEAD))
        for shard in order:
            if n < count:
                work.append(functools.partial(stage_a, n, [shard]))
            if 1 <= n <= count:
                work.append(functools.partial(stage_b, n - 1, [shard]))
            if 2 <= n < count + 2:
                work.append(functools.partial(stage_c, n - 2, [shard]))
        return work

    for step in summing[1:4]:
        step()

    for n in range(count + 3):
        sends = send_list(n)
        work = compute_list(n)
        if 0 <= n - 3 < count:
            complete(n - 3)
            if n - 3 < 8:
                start_weight(n - 3)
        slots = max(len(work), 1)
        for i in range(slots):
            for send in sends[len(sends) * i // slots : len(sends) * (i + 1) // slots]:
                send()
            if i < len(work):
                work[i]()
        if n < 2:
            summing[4 + n]()

    for index in range(len(results)):
        if index not in (1, 2):
            write_result(index).wait()

    for piece in range(count):
        for shard in range(groups):

            @pl.when(jnp.logical_and(shard <= me, me + 1 < groups))
            def _():
                right_copy(piece, shard).wait_send()

            @pl.when(jnp.logical_and(shard >= me, me > 0))
            def _():
                left_copy(piece, shard).wait_send()

        sent = pieces[piece].at[pl.ds(0, others), pl.ds(0, 7 * part)]
        remote(sent, sent, send_sem.at[piece], sib_sem.at[piece], (sib, me)).wait_send()


def gather(groups, blocks, weights, small, stats, inputs, tables):
    conv, query = weights[:2]
    rel = weights[7]
    taps, rows, columns = conv.shape
    width = query.shape[1]
    length = inputs.shape[0]
    span = tables.shape[1]
    dtype = conv.dtype
    kept = pl.BlockSpec(memory_space=pl.ANY)
    inside = pl.BlockSpec(memory_space=pltpu.VMEM)
    full = jax.ShapeDtypeStruct((groups, rows, columns), dtype)
    count = taps + 7
    grid_sems = [pltpu.SemaphoreType.DMA((count, groups))] * 4
    wide = (length, columns)
    narrow = (length, width)
    made = [
        jax.ShapeDtypeStruct(wide, dtype),
        jax.ShapeDtypeStruct(wide, jnp.float32),
        jax.ShapeDtypeStruct(wide, dtype),
        jax.ShapeDtypeStruct(narrow, dtype),
        jax.ShapeDtypeStruct(narrow, dtype),
        jax.ShapeDtypeStruct(narrow, dtype),
        jax.ShapeDtypeStruct(wide, dtype),
        jax.ShapeDtypeStruct((span, width), dtype),
        jax.ShapeDtypeStruct((HEADS, length, length), dtype),
        jax.ShapeDtypeStruct(wide, dtype),
        jax.ShapeDtypeStruct(wide, jnp.float32),
        jax.ShapeDtypeStruct(wide, dtype),
    ]
    return pl.pallas_call(
        functools.partial(gather_kernel, groups, blocks),
        out_shape=(
            jax.ShapeDtypeStruct((taps, groups, rows, columns), dtype),
            jax.ShapeDtypeStruct((groups, rows, 2 * width), dtype),
            full,
            full,
            jax.ShapeDtypeStruct((groups, rows, 2 * columns), dtype),
            jax.ShapeDtypeStruct((groups, 2 * rows, columns), dtype),
            jax.ShapeDtypeStruct((groups,) + rel.shape, dtype),
            jax.ShapeDtypeStruct((groups,) + small.shape, jnp.float32),
            jax.ShapeDtypeStruct(stats.shape, jnp.float32),
            *made,
        ),
        in_specs=[kept] * 7 + [inside] * 5,
        out_specs=[kept] * 6 + [inside] * 3 + [kept] * len(made),
        scratch_shapes=[
            pltpu.VMEM((count - 1, rows, columns), dtype),
            pltpu.VMEM((rows, 2 * width), dtype),
            pltpu.SemaphoreType.DMA((taps + 8,)),
            pltpu.SemaphoreType.DMA((count,)),
            *grid_sems,
            pltpu.SemaphoreType.DMA((count,)),
            pltpu.SemaphoreType.DMA((count,)),
            *grid_sems[:2],
            *([pltpu.SemaphoreType.DMA((groups,))] * 4),
            *sum_scratch(groups, blocks, stats.shape),
            pltpu.VMEM((2, columns, columns), dtype),
            pltpu.SemaphoreType.DMA((2, groups)),
            pltpu.SemaphoreType.DMA((len(made),)),
            pltpu.VMEM((16, columns), jnp.float32),
            pltpu.VMEM(wide, dtype),
            pltpu.VMEM(wide, jnp.float32),
            pltpu.VMEM(wide, dtype),
            pltpu.VMEM(wide, dtype),
            pltpu.VMEM(narrow, dtype),
            pltpu.VMEM(narrow, dtype),
            pltpu.VMEM(narrow, dtype),
            pltpu.VMEM(wide, dtype),
            pltpu.VMEM((2, span, width), dtype),
            pltpu.VMEM((HEADS, length, length), dtype),
            pltpu.VMEM(wide, dtype),
        ],
        compiler_params=pltpu.CompilerParams(
            collective_id=0, has_side_effects=True, vmem_limit_bytes=60 << 20
        ),
        name="gather",
    )(*weights, small, stats, inputs, tables)


def gelu_slope(value):
    inner = GELU * (value + 0.044715 * value * value * value)
    curve = jnp.tanh(inner)
    slope = GELU * (1.0 + 3 * 0.044715 * value * value)
    return 0.5 * (1.0 + curve) + 0.5 * value * (1.0 - curve * curve) * slope


def reduce_kernel(groups, blocks, rel_at, *refs):
    lefts = refs[:5]
    cotangent, hidden_pre, after_attention, after_conv, tokens = refs[5:10]
    down_full, up_full, out_full, value_full, mixed_full, conv_full = refs[10:16]
    probs, values, keys, contents, positions, mirrored_keys = refs[16:22]
    params, table = refs[22:24]
    out, total, part_grad = refs[24:27]
    made = refs[27:32]
    hidden_got, left_got, right_got = refs[32:35]
    rights = [cotangent, *made]
    (
        left_hold,
        right_hold,
        grad,
        x_one,
        y_one,
        x_two,
        y_two,
        shard_got,
        block_got,
        done,
        rel_grad,
        rel_got,
        vector,
    ) = refs[35:48]
    left_send, left_recv, right_send, right_recv, rel_send, rel_recv = refs[48:54]
    load_sem = refs[54]
    x1s, y1s, x2s, y2s, x1r, y1r, x2r, y2r = refs[55:63]
    shard_send, shard_recv, block_send, block_recv = refs[63:67]
    write_sem, send_sem, ax, ay, ad, sib_sem = refs[67:73]
    sum_bufs = refs[73:77]
    sum_sems = refs[77:83]
    credit, shard_credit = refs[83:85]
    (
        attn_grad,
        total_ref,
        kept_ref,
        weight_hold,
        wide_hold,
        right_ref,
        value_grad_ref,
        mixed_ref,
        key_ref,
        content_ref,
        position_ref,
        table_ref,
        table_grad_ref,
        probs_ref,
    ) = refs[85:99]
    tile_sem, host_sem, probs_sem, kept_sem = refs[99:103]

    dp = lax.axis_index("dp")
    me = lax.axis_index("fsdp")
    near, shards, far = peers_of(groups, blocks)
    sib, along_x, along_y = neighbours(dp)
    core = dp % 2
    at_x = dp // 2 % 2
    at_y = dp // 4 % 2
    block = dp // 8
    slots = grad.shape[0]
    part = grad.shape[4]
    width = grad.shape[5]
    half = width // 2
    rows = 4 * part
    count = out.shape[0]
    others = groups - 1
    first = pl.ds(0, half)
    last = pl.ds(half, half)
    taps = 5
    up_right = rights[1]
    rights[1:2] = [up_right.at[:, pl.ds(side * 2 * width, 2 * width)] for side in range(2)]
    lefts_got = [hidden_got] + [left_got.at[index] for index in range(4)]
    left_of = [0, 0, 1, 1, 2, 3, 3] + [4] * taps
    right_of = [0, 0, 1, 2, 3, 4, 5] + [6] * taps
    mixed_piece = 6
    first_tap = 7
    own_columns = pl.ds(pl.multiple_of(core * width, 128), width)
    sib_columns = pl.ds(pl.multiple_of((1 - core) * width, 128), width)

    def left_copy(index):
        return remote(
            lefts[index], lefts_got[index], left_send.at[index], left_recv.at[index], (sib, me)
        )

    def right_copy(index):
        return remote(
            rights[index].at[:, sib_columns],
            right_got.at[index],
            right_send.at[index],
            right_recv.at[index],
            (sib, me),
        )

    def rel_copy():
        return remote(rel_grad, rel_got, rel_send.at[0], rel_recv.at[0], (sib, me))

    def loads(piece, slot):
        left = left_of[piece]
        right = right_of[piece]
        pairs = [
            (rights[right].at[:, own_columns], right_hold.at[slot, 0]),
            (right_got.at[right], right_hold.at[slot, 1]),
        ]
        if left > 0:
            pairs.append((lefts[left], left_hold.at[slot, 0]))
            pairs.append((lefts_got[left], left_hold.at[slot, 1]))
        else:
            for shard in range(groups):
                source = pl.ds((2 * shard + piece % 2) * rows, rows)
                target = pl.ds(shard * rows, rows)
                pairs.append((lefts[left].at[:, source], left_hold.at[slot, 0, :, target]))
                pairs.append((lefts_got[left].at[:, source], left_hold.at[slot, 1, :, target]))
        return [
            pltpu.make_async_copy(src, dst, load_sem.at[slot, i])
            for i, (src, dst) in enumerate(pairs)
        ]

    def start_loads(piece):
        if left_of[piece] not in left_of[:piece]:
            left_copy(left_of[piece]).wait_recv()
        if right_of[piece] not in right_of[:piece]:
            right_copy(right_of[piece]).wait_recv()
        for copy in loads(piece, piece % 2):
            copy.start()

    meet(near + shards + far)

    for index in range(len(lefts)):
        left_copy(index).start()
        if index == 0:
            right_copy(0).start()
    start_loads(0)

    summing = sum_steps(groups, blocks, vector, total, *sum_bufs, sum_sems)

    ring = x_one.shape[0]

    def pay(piece, index, device):
        @pl.when(piece < count - ring)
        def _():
            pl.semaphore_signal(
                credit.at[index], inc=1, device_id=(device, me), device_id_type=MESH
            )

    def claim(piece, index):
        @pl.when(piece >= ring)
        def _():
            pl.semaphore_wait(credit.at[index], 1)

    def one(piece):
        slot = piece % slots
        return (
            remote(
                grad.at[slot, :, :, 1 - at_x, :, first],
                x_one.at[piece % ring],
                x1s.at[piece],
                x1r.at[piece],
                (along_x, me),
            ),
            remote(
                grad.at[slot, :, 1 - at_y, :, :, last],
                y_one.at[piece % ring],
                y1s.at[piece],
                y1r.at[piece],
                (along_y, me),
            ),
        )

    def two(piece):
        slot = piece % slots
        return (
            remote(
                grad.at[slot, :, 1 - at_y, at_x, :, first],
                y_two.at[piece % ring],
                y2s.at[piece],
                y2r.at[piece],
                (along_y, me),
            ),
            remote(
                grad.at[slot, :, at_y, 1 - at_x, :, last],
                x_two.at[piece % ring],
                x2s.at[piece],
                x2r.at[piece],
                (along_x, me),
            ),
        )

    def shard_copy(piece, j):
        other = (me + 1 + j) % groups
        return remote(
            grad.at[piece % slots, other, at_y, at_x],
            shard_got.at[piece % ring, me],
            shard_send.at[piece, j],
            shard_recv.at[piece, me],
            (dp, other),
        )

    def shard_arrival(piece, j):
        other = (me + 1 + j) % groups
        return remote(
            grad.at[piece % slots, other, at_y, at_x],
            shard_got.at[piece % ring, other],
            shard_send.at[piece, j],
            shard_recv.at[piece, other],
            (dp, other),
        )

    def block_copy(piece, j):
        return remote(
            done.at[piece],
            block_got.at[piece, block],
            block_send.at[piece, j],
            block_recv.at[piece, block],
            far[j],
        )

    def block_arrival(piece, j):
        other = (block + 1 + j) % blocks
        return remote(
            done.at[piece],
            block_got.at[piece, other],
            block_send.at[piece, j],
            block_recv.at[piece, other],
            far[j],
        )

    def place(piece, owner):
        return out.at[
            piece,
            pl.ds(pl.multiple_of(owner % 8 // 2 * part, 16), part),
            pl.ds(pl.multiple_of(core * width, 128), width),
        ]

    def spread(piece, src, owner, recv_sem, device):
        return remote(src, place(piece, owner), send_sem.at[piece], recv_sem, (device, me))

    def forward(piece, owner, recv_sem, device):
        return spread(piece, place(piece, owner), owner, recv_sem, device)

    diagonal = neighbours(along_x)[2]

    def shift(piece):
        move = piece - first_tap - taps // 2
        for window in range(2):
            value = right_hold[piece % 2, window].astype(jnp.float32)
            value = pltpu.roll(value, move % value.shape[0], 0)
            row = lax.broadcasted_iota(jnp.int32, value.shape, 0)
            inside = row >= move if move > 0 else row < value.shape[0] + move
            value = jnp.where(inside, value, 0.0)
            right_hold[piece % 2, window] = value.astype(right_hold.dtype)

    def produce(piece):
        slot = piece % slots
        hold = piece % 2

        def shard_body(shard, carry):
            columns = pl.ds(pl.multiple_of(shard * rows, 128), rows)
            value = dot_leading(left_hold[hold, 0, :, columns], right_hold[hold, 0])
            value = value + dot_leading(left_hold[hold, 1, :, columns], right_hold[hold, 1])
            grad[slot, shard] = value.astype(grad.dtype).reshape(2, 2, part, width)
            return carry

        lax.fori_loop(0, groups, shard_body, 0)

        @pl.when(piece == mixed_piece)
        def _():
            rel_copy().wait()

        @pl.when(jnp.logical_and(piece == mixed_piece, core == 1))
        def _():
            for shard in range(groups):
                value = rel_grad[shard].astype(jnp.float32) + rel_got[shard].astype(jnp.float32)
                grad[slot, shard, 0, :, :, pl.ds(rel_at, rel_grad.shape[3])] = value.astype(
                    grad.dtype
                )

    def add(piece_slot, ref, columns, *index):
        ahead = grad[(piece_slot,) + index + (slice(None), columns)]
        return ahead.astype(jnp.float32) + ref.astype(jnp.float32)

    length = tokens.shape[0]
    columns = 2 * width
    tile = 512
    block_rows = 128
    head_value = columns // HEADS
    tiles = columns // tile
    hidden_tiles = hidden_pre.shape[1] // tile

    def tile_of(phase, i):
        at = pl.ds(pl.multiple_of(i * tile, tile), tile)
        if phase == 0:
            return down_full.at[at]
        if phase == 1:
            at = pl.ds(pl.multiple_of(i // 2 * tile, tile), tile)
            return up_full.at[at, pl.ds(pl.multiple_of(i % 2 * columns, columns), columns)]
        if phase == 5:
            at = pl.ds(pl.multiple_of(i % tiles * tile, tile), tile)
            return conv_full.at[i // tiles, at]
        return (out_full, mixed_full, value_full)[phase - 2].at[at]

    lengths = [hidden_tiles, 2 * tiles, tiles, tiles, tiles, taps * tiles]
    widths = [columns, columns, columns, mixed_full.shape[1], columns, columns]

    def tile_load(phase, i):
        slot = (sum(lengths[:phase]) + i) % 2
        return pltpu.make_async_copy(
            tile_of(phase, i),
            weight_hold.at[slot, :, pl.ds(0, widths[phase])],
            tile_sem.at[slot],
        )

    def next_tile(phase, i):
        tile_load(phase, i).wait()

        @pl.when(i + 1 < lengths[phase])
        def _():
            tile_load(phase, i + 1).start()

        if phase + 1 < len(lengths):

            @pl.when(i + 1 == lengths[phase])
            def _():
                tile_load(phase + 1, 0).start()

        slot = (sum(lengths[:phase]) + i) % 2
        return weight_hold[slot, :, 0 : widths[phase]]

    def over(count, fn):
        def step_body(i, carry):
            fn(i)
            return carry

        lax.fori_loop(0, count, step_body, 0)

    def columns_at(i, wide, offset=0):
        return pl.ds(pl.multiple_of(offset + i * wide, 128), wide)

    def host_load(index):
        pairs = [
            (cotangent, right_ref),
            (after_attention, kept_ref),
            (after_conv, kept_ref),
            (values, wide_hold.at[:, pl.ds(columns, columns)]),
            (keys, key_ref),
            (contents, content_ref),
            (positions, position_ref),
            (mirrored_keys, table_ref),
            (tokens, wide_hold.at[:, pl.ds(columns, columns)]),
            (wide_hold, made[0]),
            (right_ref, made[1]),
            (value_grad_ref, made[2]),
            (mixed_ref, made[3]),
            (right_ref, made[4]),
        ]
        return pltpu.make_async_copy(*pairs[index], host_sem.at[index])

    def load(*indices):
        def thunk():
            for index in indices:
                host_load(index).start()

        return thunk

    def ready(*indices):
        def thunk():
            for index in indices:
                host_load(index).wait()

        return thunk

    def send_right(*indices):
        def thunk():
            for index in indices:
                right_copy(index).start()

        return thunk

    def pre_load(i):
        return pltpu.make_async_copy(
            hidden_pre.at[:, columns_at(i, tile)],
            kept_ref.at[:, columns_at(i % 3, tile)],
            kept_sem.at[i],
        )

    def write_part():
        return pltpu.make_async_copy(attn_grad, part_grad, kept_sem.at[hidden_tiles])

    def by_rows(fn):
        def row_body(i, carry):
            fn(pl.ds(pl.multiple_of(i * block_rows, block_rows), block_rows))
            return carry

        lax.fori_loop(0, length // block_rows, row_body, 0)

    def put(row, value):
        vector[row : row + 1, :] += jnp.sum(value, 0, keepdims=True)

    def clear_total():
        def rows_fn(at):
            total_ref[at, :] = jnp.zeros((block_rows, columns), jnp.float32)

        by_rows(rows_fn)

    def begin():
        vector[...] = jnp.zeros_like(vector)
        mixed_ref[...] = jnp.zeros_like(mixed_ref)
        tile_load(0, 0).start()
        for i in range(3):
            pre_load(i).start()
        clear_total()

    def hidden_step(i):
        value = dot_trailing(right_ref[...], next_tile(0, i))
        pre_load(i).wait()
        value = value * gelu_slope(kept_ref[:, columns_at(i % 3, tile)])

        @pl.when(i + 3 < hidden_tiles)
        def _():
            pre_load(i + 3).start()

        rounded = value.astype(wide_hold.dtype)
        wide_hold[:, columns_at(i, tile)] = rounded
        sums_here = jnp.sum(rounded.astype(jnp.float32), 0, keepdims=True)
        for side in range(2):

            @pl.when(i // tiles == side)
            def _():
                vector[9 + side : 10 + side, columns_at(i % tiles, tile)] = sums_here

    def norm_two_step(i):
        left = wide_hold[:, columns_at(i % 2, columns)]
        total_ref[:, columns_at(i // 2, tile)] += dot_trailing(left, next_tile(1, i))

    def norm_two_back():
        def rows_fn(at):
            standard, inverse = normalize(kept_ref[at, :])
            value = total_ref[at, :]
            put(2, value * standard)
            put(7, value)
            cot = right_ref[at, :].astype(jnp.float32)
            put(8, cot)
            value = cot + norm_back(value * params[2:3, :], standard, inverse)
            attn_grad[at, :] = value
            rounded = value.astype(right_ref.dtype)
            right_ref[at, :] = rounded
            put(6, rounded.astype(jnp.float32))

        by_rows(rows_fn)

    def attended_step(i):
        value = dot_trailing(right_ref[...], next_tile(2, i))
        wide_hold[:, columns_at(i, tile)] = value.astype(wide_hold.dtype)

    def probs_load(head):
        return pltpu.make_async_copy(
            probs.at[head], probs_ref.at[head % 2], probs_sem.at[head % 2]
        )

    def pair_step(index):
        span = table_ref.shape[0]
        row = lax.broadcasted_iota(jnp.int32, (length, length), 0)
        column = lax.broadcasted_iota(jnp.int32, (length, length), 1)
        mirror = jnp.where(row + column == length - 1, 1.0, 0.0).astype(jnp.bfloat16)
        pair = columns_at(index, 2 * KEY)
        key_pair = columns_at(index, 2 * KEY, key_ref.shape[1])
        value_pair = columns_at(index, 2 * head_value)
        far_pair = columns_at(index, 2 * head_value, columns)
        made_here = [[], [], [], [], [], []]
        for side in range(2):
            head = 2 * index + side
            probs_load(head).wait()
            keys_at = slice(side * KEY, (side + 1) * KEY)
            values_at = slice(side * head_value, (side + 1) * head_value)
            prob = probs_ref[side]
            out_grad = wide_hold[:, value_pair][:, values_at]
            made_here[0].append(dot_leading(prob, out_grad).astype(jnp.bfloat16))
            prob_grad = dot_trailing(out_grad, wide_hold[:, far_pair][:, values_at])
            prob = prob.astype(jnp.float32)
            row_dot = jnp.sum(prob * prob_grad, -1, keepdims=True)
            rounded = (prob * (prob_grad - row_dot)).astype(jnp.bfloat16)
            content = content_ref[:, pair][:, keys_at]
            made_here[1].append(dot_leading(rounded, content).astype(jnp.bfloat16))
            content_grad = jnp.dot(
                rounded, key_ref[:, pair][:, keys_at], preferred_element_type=jnp.float32
            )
            mirrored = jnp.dot(rounded, mirror, preferred_element_type=jnp.float32)
            wide = jnp.concatenate([mirrored, jnp.zeros((length, span - length), jnp.float32)], 1)
            band = pltpu.roll(wide, 0, 1, stride=1, stride_axis=0).astype(jnp.bfloat16)
            position_grad = jnp.dot(
                band, table_ref[:, pair][:, keys_at], preferred_element_type=jnp.float32
            )
            position = position_ref[:, pair][:, keys_at]
            made_here[2].append(dot_leading(band, position).astype(jnp.bfloat16))
            made_here[3].append(((content_grad + position_grad) * KEY**-0.5).astype(jnp.bfloat16))
            made_here[4].append(jnp.sum(content_grad, 0, keepdims=True))
            made_here[5].append(jnp.sum(position_grad, 0, keepdims=True))
        value_grad_ref[:, value_pair] = jnp.concatenate(made_here[0], 1)
        mixed_ref[:, key_pair] = jnp.concatenate(made_here[1], 1)
        table_grad_ref[:, pair] = jnp.concatenate(made_here[2], 1)
        mixed_ref[:, pair] = jnp.concatenate(made_here[3], 1)
        vector[11:12, pair] = jnp.concatenate(made_here[4], 1)
        vector[11:12, key_pair] = jnp.concatenate(made_here[5], 1)

        @pl.when(index + 1 < HEADS // 2)
        def _():
            for side in range(2):
                probs_load(2 * index + 2 + side).start()

    def rel_step():
        for shard in range(groups):
            value = dot_leading(table[...], table_grad_ref[:, shard * 128 : (shard + 1) * 128])
            rel_grad[shard] = value.astype(rel_grad.dtype).reshape(rel_grad.shape[1:])
        rel_copy().start()

    def mixed_step(i):
        left = mixed_ref[:, 0 : mixed_full.shape[1]]
        total_ref[:, columns_at(i, tile)] = dot_trailing(left, next_tile(3, i))

    def value_step(i):
        total_ref[:, columns_at(i, tile)] += dot_trailing(value_grad_ref[...], next_tile(4, i))

    def norm_one_back():
        def rows_fn(at):
            standard, inverse = normalize(kept_ref[at, :])
            value = total_ref[at, :]
            put(1, value * standard)
            put(5, value)
            value = attn_grad[at, :] + norm_back(value * params[1:2, :], standard, inverse)
            attn_grad[at, :] = value
            rounded = value.astype(right_ref.dtype)
            right_ref[at, :] = rounded
            put(4, rounded.astype(jnp.float32))

        by_rows(rows_fn)

    def conv_shift(tap):
        move = tap - taps // 2

        def column_body(i, carry):
            at = columns_at(i, rows)
            value = right_ref[:, at].astype(jnp.float32)
            value = pltpu.roll(value, (move + length) % length, 0)
            row = lax.broadcasted_iota(jnp.int32, value.shape, 0) - move
            inside = jnp.logical_and(row >= 0, row < length)
            wide_hold[:, at] = jnp.where(inside, value, 0.0).astype(wide_hold.dtype)
            return carry

        lax.fori_loop(0, columns // rows, column_body, 0)

    def conv_step(i):
        left = wide_hold[:, 0:columns]
        total_ref[:, columns_at(i % tiles, tile)] += dot_trailing(left, next_tile(5, i))

    def batch_back():
        def rows_fn(at):
            value = wide_hold[at, columns : 2 * columns].astype(jnp.float32)
            standard = (value - params[4:5, :]) * params[5:6, :]
            normed = standard * params[0:1, :] + params[3:4, :]
            value = total_ref[at, :] * gelu_slope(normed)
            put(0, value * standard)
            put(3, value)
            attn_grad[at, :] += params[5:6, :] * params[0:1, :] * value

        by_rows(rows_fn)

    def start_probs():
        for head in range(2):
            probs_load(head).start()

    def step_zero():
        begin()
        ready(0)()
        over(hidden_tiles, hidden_step)
        load(9, 1)()
        ready(9)()
        send_right(1, 2)()

    def step_one():
        over(2 * tiles, norm_two_step)
        load(3)()
        ready(1)()
        norm_two_back()
        load(10, 2)()
        start_probs()

    def step_two():
        over(tiles, attended_step)
        ready(10)()
        send_right(3)()
        ready(3, 4, 5, 6, 7)()

    def step_three():
        load(11, 12, 8)()
        rel_step()
        ready(11, 12)()
        send_right(4, 5)()

    def step_four():
        over(tiles, mixed_step)
        over(tiles, value_step)
        ready(2)()
        norm_one_back()
        load(13)()
        ready(13)()
        send_right(6)()
        clear_total()

    def step_last():
        ready(8)()
        batch_back()
        write_part().start()

    pairs_each = HEADS // 4

    for copy in (0, 4, 5, 6, 7):
        host_load(copy).start()

    def host(n):
        pl.when(n == 0)(step_zero)
        pl.when(n == 1)(step_one)
        pl.when(n == 2)(step_two)

        @pl.when(jnp.logical_and(n >= 2, n < 4))
        def _():
            over(pairs_each, lambda i: pair_step((n - 2) * pairs_each + i))

        pl.when(n == 3)(step_three)
        pl.when(n == 4)(step_four)

        @pl.when(jnp.logical_and(n >= 5, n < 5 + taps))
        def _():
            conv_shift(n - 5)
            over(tiles, lambda i: conv_step((n - 5) * tiles + i))

        pl.when(n == 4 + taps)(step_last)

    def body(n, carry):
        @pl.when(n < count)
        def _():
            @pl.when(n >= slots)
            def _():
                old = n - slots
                for copy in one(old) + two(old):
                    copy.wait_send()
                for j in range(others):
                    shard_copy(old, j).wait_send()

            for piece in range(count):

                @pl.when(n == piece)
                def _():
                    for copy in loads(piece, piece % 2):
                        copy.wait()
                    if piece + 1 < count:
                        start_loads(piece + 1)
                    if piece >= first_tap and piece != first_tap + taps // 2:
                        shift(piece)

            produce(n)
            claim(n, 0)
            claim(n, 1)
            for copy in one(n):
                copy.start()

        host(n)

        @pl.when(jnp.logical_and(n >= 1, n < count + 1))
        def _():
            piece = n - 1
            slot = piece % slots
            for copy in one(piece):
                copy.wait_recv()

            def shard_body(shard, carry):
                for other in range(2):
                    value = add(slot, x_one[piece % ring, shard, other], first, shard, other, at_x)
                    grad[slot, shard, other, at_x, :, first] = value.astype(grad.dtype)
                    value = add(slot, y_one[piece % ring, shard, other], last, shard, at_y, other)
                    grad[slot, shard, at_y, other, :, last] = value.astype(grad.dtype)
                return carry

            lax.fori_loop(0, groups, shard_body, 0)
            pay(piece, 0, along_x)
            pay(piece, 1, along_y)
            claim(piece, 2)
            claim(piece, 3)
            for copy in two(piece):
                copy.start()

        @pl.when(jnp.logical_and(n >= 2, n < count + 2))
        def _():
            piece = n - 2
            slot = piece % slots
            for copy in two(piece):
                copy.wait_recv()

            def shard_body(shard, carry):
                value = add(slot, y_two[piece % ring, shard], first, shard, at_y, at_x)
                grad[slot, shard, at_y, at_x, :, first] = value.astype(grad.dtype)
                value = add(slot, x_two[piece % ring, shard], last, shard, at_y, at_x)
                grad[slot, shard, at_y, at_x, :, last] = value.astype(grad.dtype)
                return carry

            lax.fori_loop(0, groups, shard_body, 0)
            pay(piece, 2, along_y)
            pay(piece, 3, along_x)
            for j in range(others):

                @pl.when(piece >= ring)
                def _():
                    pl.semaphore_wait(shard_credit.at[(me + 1 + j) % groups], 1)

                shard_copy(piece, j).start()

        @pl.when(jnp.logical_and(n >= 3, n < count + 3))
        def _():
            piece = n - 3
            value = grad[piece % slots, me, at_y, at_x].astype(jnp.float32)
            for j in range(others):
                shard_arrival(piece, j).wait_recv()
                value = value + shard_got[piece % ring, (me + 1 + j) % groups].astype(jnp.float32)

            @pl.when(piece < count - ring)
            def _():
                for j in range(others):
                    pl.semaphore_signal(
                        shard_credit.at[me], inc=1, device_id=shards[j], device_id_type=MESH
                    )

            if blocks > 1:
                done[piece] = value.astype(done.dtype)
                block_got[piece, block] = value.astype(done.dtype)
                for j in range(blocks - 1):
                    block_copy(piece, j).start()
                for j in range(blocks - 1):
                    block_copy(piece, j).wait_send()
                    block_arrival(piece, j).wait_recv()
                value = block_got[piece, 0].astype(jnp.float32)
                for other in range(1, blocks):
                    value = value + block_got[piece, other].astype(jnp.float32)
            done[piece] = value.astype(done.dtype)
            pltpu.make_async_copy(done.at[piece], place(piece, dp), write_sem.at[piece]).start()
            spread(piece, done.at[piece], dp, ax.at[piece], along_x).start()
            spread(piece, done.at[piece], dp, ay.at[piece], along_y).start()
            spread(piece, done.at[piece], dp, sib_sem.at[piece], sib).start()

        @pl.when(jnp.logical_and(n >= 4, n < count + 4))
        def _():
            piece = n - 4
            route = piece % 2
            forward(piece, along_x, ax.at[piece], dp).wait_recv()
            forward(piece, along_y, ay.at[piece], dp).wait_recv()
            owner = route * along_x + (1 - route) * along_y
            target = route * along_y + (1 - route) * along_x
            forward(piece, owner, ad.at[piece], target).start()
            forward(piece, along_x, sib_sem.at[piece], sib).start()
            forward(piece, along_y, sib_sem.at[piece], sib).start()

        @pl.when(n >= 5)
        def _():
            piece = n - 5
            forward(piece, diagonal, ad.at[piece], dp).wait_recv()
            forward(piece, diagonal, sib_sem.at[piece], sib).start()

        for step in range(len(summing)):

            @pl.when(n == count + step - 1)
            def _():
                summing[step]()

        return carry

    lax.fori_loop(0, count + 5, body, 0)
    write_part().wait()

    def drain(piece, carry):
        @pl.when(piece >= count - slots)
        def _():
            for copy in one(piece) + two(piece):
                copy.wait_send()
            for j in range(others):
                shard_copy(piece, j).wait_send()

        pltpu.make_async_copy(done.at[piece], place(piece, dp), write_sem.at[piece]).wait()
        got = out.at[piece, :, pl.ds(0, width)]
        remote(got, got, send_sem.at[piece], sib_sem.at[piece], (sib, me)).wait_recv()
        sent = out.at[piece, pl.ds(0, 7 * part // 2), :]
        remote(sent, sent, send_sem.at[piece], sib_sem.at[piece], (sib, me)).wait_send()
        return carry

    lax.fori_loop(0, count, drain, 0)
    for index in range(len(lefts)):
        left_copy(index).wait_send()
    for index in range(len(rights)):
        right_copy(index).wait_send()


def reduce(groups, blocks, rel_at, lefts, saved, weights, heads, params, table):
    hidden, _, _, _, activated = lefts
    length, columns = activated.shape
    width = columns // 2
    rows = columns // groups
    part = rows // 4
    dtype = activated.dtype
    count = 12
    slots = 4
    ring = 3 if blocks == 1 else 2
    narrow = heads[2].shape
    span = table.shape[0]
    kept = pl.BlockSpec(memory_space=pl.ANY)
    inside = pl.BlockSpec(memory_space=pltpu.VMEM)
    each = pltpu.SemaphoreType.DMA((count,))
    wide = (length, columns)
    rel_shape = (groups, 2, table.shape[1] // 2, 128)
    sums = (16, columns)
    inputs = [*lefts, *saved, *weights, *heads]
    half_got = (ring, groups, part, width // 2)
    two_got = (ring, groups, 2, part, width // 2)
    return pl.pallas_call(
        functools.partial(reduce_kernel, groups, blocks, rel_at),
        out_shape=(
            jax.ShapeDtypeStruct((count, rows, columns), dtype),
            jax.ShapeDtypeStruct(sums, jnp.float32),
            jax.ShapeDtypeStruct(wide, jnp.float32),
            jax.ShapeDtypeStruct(hidden.shape, dtype),
            jax.ShapeDtypeStruct(wide, dtype),
            jax.ShapeDtypeStruct(wide, dtype),
            jax.ShapeDtypeStruct(wide, dtype),
            jax.ShapeDtypeStruct(wide, dtype),
            jax.ShapeDtypeStruct(hidden.shape, dtype),
            jax.ShapeDtypeStruct((4,) + wide, dtype),
            jax.ShapeDtypeStruct((7, length, width), dtype),
        ),
        in_specs=[kept] * len(inputs) + [inside] * 2,
        out_specs=[kept, inside] + [kept] * 9,
        scratch_shapes=[
            pltpu.VMEM((2, 2) + wide, dtype),
            pltpu.VMEM((2, 2, length, width), dtype),
            pltpu.VMEM((slots, groups, 2, 2, part, width), dtype),
            pltpu.VMEM(two_got, dtype),
            pltpu.VMEM(two_got, dtype),
            pltpu.VMEM(half_got, dtype),
            pltpu.VMEM(half_got, dtype),
            pltpu.VMEM((ring, groups, part, width), dtype),
            pltpu.VMEM((count if blocks > 1 else 1, blocks, part, width), dtype),
            pltpu.VMEM((count, part, width), dtype),
            pltpu.VMEM(rel_shape, dtype),
            pltpu.VMEM(rel_shape, dtype),
            pltpu.VMEM(sums, jnp.float32),
            *([pltpu.SemaphoreType.DMA((5,))] * 2),
            *([pltpu.SemaphoreType.DMA((7,))] * 2),
            *([pltpu.SemaphoreType.DMA((1,))] * 2),
            pltpu.SemaphoreType.DMA((2, 2 + 2 * groups)),
            *([each] * 8),
            *([pltpu.SemaphoreType.DMA((count, groups))] * 2),
            *([pltpu.SemaphoreType.DMA((count, blocks))] * 2),
            *([each] * 6),
            *sum_scratch(groups, blocks, sums),
            pltpu.SemaphoreType.REGULAR((4,)),
            pltpu.SemaphoreType.REGULAR((groups,)),
            pltpu.VMEM(wide, jnp.float32),
            pltpu.VMEM(wide, jnp.float32),
            pltpu.VMEM(wide, jnp.float32),
            pltpu.VMEM((2, 512, columns), dtype),
            pltpu.VMEM(hidden.shape, dtype),
            pltpu.VMEM(wide, dtype),
            pltpu.VMEM(wide, dtype),
            pltpu.VMEM(wide, dtype),
            *([pltpu.VMEM(narrow, dtype)] * 3),
            pltpu.VMEM((span, narrow[1]), dtype),
            pltpu.VMEM((span, narrow[1]), dtype),
            pltpu.VMEM((2, length, length), dtype),
            pltpu.SemaphoreType.DMA((2,)),
            pltpu.SemaphoreType.DMA((14,)),
            pltpu.SemaphoreType.DMA((2,)),
            pltpu.SemaphoreType.DMA((hidden.shape[1] // 512 + 1,)),
        ],
        compiler_params=pltpu.CompilerParams(
            collective_id=1, has_side_effects=True, vmem_limit_bytes=VMEM_LIMIT
        ),
        name="reduce",
    )(*inputs, params, table)


EPSILON = 1e-05


def position_table(length, features, direction):
    basis_count = features // 6
    offsets = jnp.arange(2 * length - 1, dtype=jnp.float32) - (length - 1)
    offsets = offsets * direction
    distance = jnp.abs(offsets)[:, None]
    max_range = math.log(length) / math.log(2.0)
    half_life = 2.0 ** jnp.linspace(3.0, max_range, basis_count, dtype=jnp.float32)
    decaying = jnp.exp(-math.log(2.0) / half_life[None, :] * distance)
    widths = 2.0 ** jnp.arange(1, basis_count + 1, dtype=jnp.float32) - 1.0
    central = (widths[None, :] > distance).astype(jnp.float32)
    stddev = length / (2.0 * basis_count)
    centres = jnp.linspace(length / basis_count, length, basis_count, dtype=jnp.float32)
    shape_par = (centres / stddev) ** 2
    rate_par = centres / stddev**2
    safe_dist = jnp.maximum(distance, 1.0)
    log_prob = (shape_par - 1.0) * jnp.log(safe_dist) - rate_par * safe_dist
    log_prob = log_prob - jnp.max(log_prob, axis=0, keepdims=True)
    gamma_feat = jnp.where(distance > 0.5, jnp.exp(log_prob), 0.0)
    symmetric = jnp.concatenate([decaying, central, gamma_feat], 1)
    sign_row = jnp.sign(offsets)[:, None]
    return jnp.concatenate([symmetric, sign_row * symmetric], 1)


def normalize(values):
    centred = values - jnp.mean(values, -1, keepdims=True)
    inverse = lax.rsqrt(jnp.mean(centred * centred, -1, keepdims=True) + EPSILON)
    return (centred * inverse, inverse)


def norm_back(grad_std, standard, inverse):
    return inverse * (
        grad_std
        - jnp.mean(grad_std, -1, keepdims=True)
        - standard * jnp.mean(grad_std * standard, -1, keepdims=True)
    )


def dot_leading(left_side, right_side):
    return lax.dot_general(
        left_side, right_side, (((0,), (0,)), ((), ())), preferred_element_type=jnp.float32
    )


def dot_trailing(left_side, right_side):
    return lax.dot_general(
        left_side, right_side, (((1,), (1,)), ((), ())), preferred_element_type=jnp.float32
    )


def on_device(
    tokens,
    conv_weight,
    query_weight,
    key_weight,
    value_weight,
    out_weight,
    rel_weight,
    up_weight,
    down_weight,
    gains,
    biases,
    up_bias,
    rel_bias,
    target_table,
    clip_levels,
    window_ids,
    clip_index,
):
    groups = lax.axis_size("fsdp")
    blocks = lax.axis_size("dp") // 8
    tap_count, piece_rows, model_width = conv_weight.shape
    half_taps = tap_count // 2
    half_width = model_width // 2
    key_width = query_weight.shape[1]
    rel_rows, rel_columns = rel_weight.shape
    inputs = tokens[0].astype(jnp.float32)
    length = inputs.shape[0]
    token_total = length * lax.axis_size("dp") * lax.axis_size("fsdp")

    small_parts = [gains, biases, up_bias, rel_bias]
    small = jnp.concatenate([part.reshape(-1) for part in small_parts])
    small = jnp.pad(small, (0, -small.shape[0] % 1024)).reshape(-1, 128)
    stats = jnp.concatenate([jnp.sum(inputs, 0), jnp.sum(inputs * inputs, 0)]).reshape(-1, 128)
    tables = jnp.stack(
        [
            jnp.pad(position_table(length, rel_rows, direction), ((0, 1), (0, 0)))
            for direction in (1.0, -1.0)
        ]
    ).astype(jnp.bfloat16)
    (
        conv_full,
        mixed_full,
        value_full,
        out_full,
        up_full,
        down_full,
        _,
        small_full,
        stats,
        activated,
        after_conv,
        normed_one,
        content_query,
        position_query,
        keys,
        values,
        mirrored_keys,
        probs,
        attended,
        after_attention,
        normed_two,
    ) = gather(
        groups,
        blocks,
        [
            conv_weight,
            query_weight,
            key_weight,
            value_weight,
            out_weight,
            up_weight,
            down_weight,
            rel_weight,
        ],
        small,
        stats,
        tokens[0],
        tables,
    )
    conv_full = conv_full.reshape(tap_count, model_width, model_width)
    mixed_full = mixed_full.reshape(model_width, -1)
    value_full = value_full.reshape(model_width, -1)
    out_full = out_full.reshape(model_width, -1)
    up_full = up_full.reshape(model_width, -1)
    down_full = down_full.reshape(-1, model_width)
    flat = small_full.reshape(groups, -1)
    taken = 0
    unpacked = []
    for part in small_parts:
        chosen = flat[:, taken : taken + part.size].reshape((groups,) + part.shape)
        unpacked.append(chosen)
        taken += part.size
    gain_rows = jnp.moveaxis(unpacked[0], 0, 1).reshape(gains.shape[0], -1)
    bias_rows = jnp.moveaxis(unpacked[1], 0, 1).reshape(biases.shape[0], -1)
    up_offset = unpacked[2].reshape(-1)
    batch_sums = stats.reshape(2, -1)
    centre = batch_sums[0] / token_total
    variance = batch_sums[1] / token_total - centre * centre
    inverse = lax.rsqrt(variance + EPSILON)
    standard = (inputs - centre) * inverse
    hidden_pre = jnp.dot(normed_two, up_full, preferred_element_type=jnp.float32) + up_offset
    hidden = jax.nn.gelu(hidden_pre).astype(jnp.bfloat16)
    outputs = (
        after_attention
        + jnp.dot(hidden, down_full, preferred_element_type=jnp.float32)
        + bias_rows[5]
    )
    target_row = lax.dynamic_index_in_dim(target_table, window_ids[0], 0, keepdims=False)
    levels = jnp.arange(clip_levels.shape[0], dtype=jnp.int32)
    selector = (clip_index[0][:, None] == levels[None, :]).astype(jnp.float32)
    limits = jnp.sum(selector * clip_levels[None, :], 1)[:, None]
    cotangent = jnp.clip(outputs - target_row, -limits, limits).astype(jnp.bfloat16)
    params = jnp.concatenate([gain_rows, bias_rows[:1], centre[None], inverse[None]], 0)
    params = jnp.pad(params, ((0, 2), (0, 0)))
    pieces, sums, part_grad, *_ = reduce(
        groups,
        blocks,
        2 * key_width - half_width,
        [hidden, normed_two, attended, normed_one, activated],
        [cotangent, hidden_pre, after_attention, after_conv, tokens[0]],
        [down_full, up_full, out_full, value_full, mixed_full, conv_full],
        [probs, values, keys, content_query, position_query, mirrored_keys],
        params,
        tables[1],
    )
    input_grad = part_grad - inverse * gain_rows[0] * (
        sums[3] + standard * sums[0]
    ) / token_total
    shard = lax.axis_index("fsdp")
    by_shard = sums[:9].reshape(9, groups, -1)
    by_shard = lax.dynamic_index_in_dim(by_shard, shard, 1, keepdims=False)
    up_sums = sums[9:11].reshape(groups, -1)
    up_sums = lax.dynamic_index_in_dim(up_sums, shard, 0, keepdims=False)
    rel_sums = sums[11, : 2 * key_width].reshape(2, groups, -1)
    rel_sums = lax.dynamic_index_in_dim(rel_sums, shard, 1, keepdims=False)
    up_grad = jnp.concatenate([pieces[2], pieces[3]], 1)
    mixed_sum = pieces[6].astype(jnp.float32)
    rel_at = 2 * key_width
    return (
        outputs.astype(jnp.bfloat16)[None],
        input_grad.astype(jnp.bfloat16)[None],
        pieces[7:12].astype(jnp.float32),
        mixed_sum[:, :key_width],
        mixed_sum[:, key_width:rel_at],
        pieces[5].astype(jnp.float32),
        pieces[4].astype(jnp.float32),
        mixed_sum[:rel_rows, rel_at : rel_at + rel_columns],
        up_grad.astype(jnp.float32),
        pieces[:2].reshape(2 * piece_rows, -1).astype(jnp.float32),
        by_shard[:3],
        by_shard[3:9],
        up_sums,
        rel_sums,
    )


def solution(mesh):
    placed = (
        P(("dp", "fsdp"), None, None),
        P(None, "fsdp", None),
        P("fsdp", None),
        P("fsdp", None),
        P("fsdp", None),
        P("fsdp", None),
        P(None, "fsdp"),
        P("fsdp", None),
        P("fsdp", None),
        P(None, "fsdp"),
        P(None, "fsdp"),
        P("fsdp"),
        P(None, "fsdp"),
        P(),
        P(),
        P(("dp", "fsdp")),
        P(("dp", "fsdp"), None),
    )
    return jax.shard_map(
        on_device,
        mesh=mesh,
        in_specs=placed,
        out_specs=(
            P(("dp", "fsdp"), None, None),
            P(("dp", "fsdp"), None, None),
            P(None, "fsdp", None),
            P("fsdp", None),
            P("fsdp", None),
            P("fsdp", None),
            P("fsdp", None),
            P(None, "fsdp"),
            P("fsdp", None),
            P("fsdp", None),
            P(None, "fsdp"),
            P(None, "fsdp"),
            P("fsdp"),
            P(None, "fsdp"),
        ),
        check_vma=False,
    )
```

```python
import functools
import math

import jax
import jax.numpy as jnp
from jax import lax
from jax.experimental import pallas as pl
from jax.experimental.pallas import tpu as pltpu
from jax.sharding import PartitionSpec as P

HEADS = 8
KEY = 64
MESH = pl.DeviceIdType.MESH
AHEAD = 2
GELU = 0.7978845608028654
VMEM_LIMIT = 62 << 20


def neighbours(dp):
    core = dp % 2
    along_x = dp // 2 % 2
    along_y = dp // 4 % 2
    return dp + 1 - 2 * core, dp + 2 - 4 * along_x, dp + 4 - 8 * along_y


def remote(src, dst, send_sem, recv_sem, device):
    return pltpu.make_async_remote_copy(
        src_ref=src,
        dst_ref=dst,
        send_sem=send_sem,
        recv_sem=recv_sem,
        device_id=device,
        device_id_type=MESH,
    )


def meet(peers):
    barrier = pltpu.get_barrier_semaphore()
    for peer in peers:
        pl.semaphore_signal(barrier, inc=1, device_id=peer, device_id_type=MESH)
    pl.semaphore_wait(barrier, len(peers))


def peers_of(groups, blocks):
    dp = lax.axis_index("dp")
    me = lax.axis_index("fsdp")
    near = [(device, me) for device in neighbours(dp)]
    shards = [(dp, (me + 1 + j) % groups) for j in range(groups - 1)]
    far = [((dp + 8 * (1 + j)) % (8 * blocks), me) for j in range(blocks - 1)]
    return near, shards, far


def sum_steps(groups, blocks, vector, total, near_got, sums, shard_got, block_got, sems):
    near_send, near_recv, shard_send, shard_recv, block_send, block_recv = sems
    me = lax.axis_index("fsdp")
    block = lax.axis_index("dp") // 8
    near, shards, far = peers_of(groups, blocks)

    def near_copy(step):
        src = vector if step == 0 else sums.at[step - 1]
        return remote(
            src, near_got.at[step], near_send.at[step], near_recv.at[step], near[step]
        )

    def fold(step):
        copy = near_copy(step)
        copy.wait()
        held = vector[...] if step == 0 else sums[step - 1]
        sums[step] = held + near_got[step]

    def shard_copy(j):
        return remote(
            sums.at[2], shard_got.at[me], shard_send.at[j], shard_recv.at[me], shards[j]
        )

    def block_copy(j):
        return remote(
            sums.at[3], block_got.at[block], block_send.at[j], block_recv.at[block], far[j]
        )

    def start():
        near_copy(0).start()

    def second():
        fold(0)
        near_copy(1).start()

    def third():
        fold(1)
        near_copy(2).start()

    def fourth():
        fold(2)
        for j in range(groups - 1):
            shard_copy(j).start()
        shard_got[me] = sums[2]

    def fifth():
        for j in range(groups - 1):
            shard_copy(j).wait_send()
            other = (me + 1 + j) % groups
            remote(
                sums.at[2], shard_got.at[other], shard_send.at[j], shard_recv.at[other], shards[j]
            ).wait_recv()
        added = shard_got[0]
        for shard in range(1, groups):
            added = added + shard_got[shard]
        sums[3] = added
        for j in range(blocks - 1):
            block_copy(j).start()
        block_got[block] = added

    def sixth():
        for j in range(blocks - 1):
            block_copy(j).wait_send()
            other = (block + 1 + j) % blocks
            remote(
                sums.at[3], block_got.at[other], block_send.at[j], block_recv.at[other], far[j]
            ).wait_recv()
        added = block_got[0]
        for other in range(1, blocks):
            added = added + block_got[other]
        total[...] = added

    return [start, second, third, fourth, fifth, sixth]


def sum_scratch(groups, blocks, shape):
    return [
        pltpu.VMEM((3,) + shape, jnp.float32),
        pltpu.VMEM((4,) + shape, jnp.float32),
        pltpu.VMEM((groups,) + shape, jnp.float32),
        pltpu.VMEM((blocks,) + shape, jnp.float32),
        pltpu.SemaphoreType.DMA((3,)),
        pltpu.SemaphoreType.DMA((3,)),
        pltpu.SemaphoreType.DMA((groups,)),
        pltpu.SemaphoreType.DMA((groups,)),
        pltpu.SemaphoreType.DMA((blocks,)),
        pltpu.SemaphoreType.DMA((blocks,)),
    ]


def gather_kernel(groups, blocks, *refs):
    weights = refs[:8]
    conv, query, key, value, out, up, down, rel = weights
    small, inputs, target, limits = refs[8:12]
    outs = refs[12:21]
    conv_out, mixed_out, value_out, out_out, up_out, down_out = outs[:6]
    rel_full, small_full, stat_total = outs[6:]
    results = list(refs[21:37])
    pre_out = results.pop(12)
    hidden_out = results.pop(12)
    results[12:12] = [
        hidden_out.at[:, pl.ds(side * conv.shape[2], conv.shape[2])] for side in range(2)
    ]
    tables = refs[37]
    refs = refs[38:]
    hold, hold_mixed, local_sem, write_sem = refs[:4]
    z_sem, x_sem, y_sem, d_sem, sib_sem, send_sem, right_send, left_send = refs[4:12]
    rel_send, rel_recv, small_send, small_recv = refs[12:16]
    near_got, sums, shard_got, block_got = refs[16:20]
    sum_sems = refs[20:26]
    weight_hold, weight_sem, result_sem = refs[26:29]
    params, shifted_ref, total_ref = refs[29:32]
    act_ref, norm_ref, content_ref, position_ref, key_ref, value_ref = refs[32:38]
    table_ref, probs_ref, attended_ref = refs[38:41]
    stats, loss_ref, part_sem, part_right, part_left = refs[41:46]
    dp = lax.axis_index("dp")
    me = lax.axis_index("fsdp")
    near, shards, far = peers_of(groups, blocks)
    sib, along_x, along_y = neighbours(dp)
    rows = conv.shape[1]
    part = rows // 8
    others = groups - 1
    columns = conv.shape[2]
    pieces = [conv_out.at[tap] for tap in range(5)] + [mixed_out, value_out, out_out]
    pieces += [up_out.at[:, :, pl.ds(half * columns, columns)] for half in range(2)]
    pieces += [down_out.at[:, pl.ds(half * rows, rows)] for half in range(2)]
    count = len(pieces)
    holds = [hold.at[i] for i in range(5)] + [hold_mixed] + [hold.at[i] for i in range(5, 11)]

    pending = [[] for _ in range(count)]
    started = [0]

    def load(src, dst, piece):
        copy = pltpu.make_async_copy(src, dst, local_sem.at[started[0]])
        copy.start()
        started[0] += 1
        pending[piece].append(copy)

    for tap in range(5):
        load(conv.at[tap], holds[tap], tap)
    width = query.shape[1]
    load(query, hold_mixed.at[:, pl.ds(0, width)], 5)
    load(key, hold_mixed.at[:, pl.ds(width, width)], 5)
    load(value, holds[6], 6)
    load(out, holds[7], 7)
    for half in range(2):
        load(up.at[:, pl.ds(half * columns, columns)], holds[8 + half], 8 + half)
    for half in range(2):
        load(down.at[pl.ds(half * rows, rows)], holds[10 + half], 10 + half)

    meet(near + shards + far)

    summing = sum_steps(
        groups, blocks, stats, stat_total, near_got, sums, shard_got, block_got, sum_sems
    )
    for j in range(others):
        remote(
            rel, rel_full.at[me], rel_send.at[j], rel_recv.at[me], shards[j]
        ).start()
        remote(
            small, small_full.at[me], small_send.at[j], small_recv.at[me], shards[j]
        ).start()
    rel_full[me] = rel[...]
    small_full[me] = small[...]

    def slice_of(piece, shard, owner):
        return pieces[piece].at[shard, pl.ds(pl.multiple_of(owner % 8 * part, 16), part)]

    def copy_of(piece, shard, owner, recv_sem, device):
        ref = slice_of(piece, shard, owner)
        return remote(ref, ref, send_sem.at[piece], recv_sem, (device, me))

    order = []
    for j in range(others):
        pick = 0
        for m in range(groups):
            nearest = sorted((t for t in range(groups) if t != m), key=lambda t: abs(t - m))
            pick = pick + jnp.where(me == m, nearest[j], 0)
        order.append(pick)

    def right_copy(piece, shard, src=None):
        dst = slice_of(piece, shard, dp)
        return remote(
            dst if src is None else src,
            dst,
            right_send.at[piece, shard],
            z_sem.at[piece, shard],
            (dp, (me + 1) % groups),
        )

    def left_copy(piece, shard, src=None):
        dst = slice_of(piece, shard, dp)
        return remote(
            dst if src is None else src,
            dst,
            left_send.at[piece, shard],
            z_sem.at[piece, shard],
            (dp, (me + groups - 1) % groups),
        )

    last = count - 1

    def part_copy(step, shard, device, sems, src=None):
        dst = slice_of(last, shard, 2 * step + dp % 2)
        return remote(
            dst if src is None else src,
            dst,
            sems.at[step, shard],
            part_sem.at[step, shard],
            (dp, device),
        )

    def part_send(step):
        at = pl.ds(pl.multiple_of((2 * step + dp % 2) * part, 16), part)
        src = holds[last].at[at]

        @pl.when(me + 1 < groups)
        def _():
            part_copy(step, me, (me + 1) % groups, part_right, src).start()

        @pl.when(me > 0)
        def _():
            part_copy(step, me, (me + groups - 1) % groups, part_left, src).start()

    def part_stage(step, shard):
        part_copy(step, shard, me, part_right).wait_recv()

        @pl.when(jnp.logical_and(shard < me, me + 1 < groups))
        def _():
            part_copy(step, shard, (me + 1) % groups, part_right).start()

        @pl.when(jnp.logical_and(shard > me, me > 0))
        def _():
            part_copy(step, shard, (me + groups - 1) % groups, part_left).start()

        ref = slice_of(last, shard, 2 * step + dp % 2)
        remote(ref, ref, send_sem.at[last], sib_sem.at[last], (sib, me)).start()

    def z_send(piece):
        src = holds[piece].at[pl.ds(pl.multiple_of(dp % 8 * part, 16), part)]

        @pl.when(me + 1 < groups)
        def _():
            right_copy(piece, me, src).start()

        @pl.when(me > 0)
        def _():
            left_copy(piece, me, src).start()

    diagonal = neighbours(along_x)[2]

    def stage_a(piece, shards_now):
        for shard in shards_now:
            copy_of(piece, shard, dp, z_sem.at[piece, shard], dp).wait_recv()

            @pl.when(jnp.logical_and(shard < me, me + 1 < groups))
            def _():
                right_copy(piece, shard).start()

            @pl.when(jnp.logical_and(shard > me, me > 0))
            def _():
                left_copy(piece, shard).start()

            copy_of(piece, shard, dp, x_sem.at[piece, shard], along_x).start()
            copy_of(piece, shard, dp, y_sem.at[piece, shard], along_y).start()
            copy_of(piece, shard, dp, sib_sem.at[piece], sib).start()

    def stage_b(piece, shards_now):
        for shard in shards_now:
            route = (piece + shard) % 2
            copy_of(piece, shard, along_x, x_sem.at[piece, shard], dp).wait_recv()
            copy_of(piece, shard, along_y, y_sem.at[piece, shard], dp).wait_recv()
            owner = route * along_x + (1 - route) * along_y
            target = route * along_y + (1 - route) * along_x
            copy_of(piece, shard, owner, d_sem.at[piece, shard], target).start()
            copy_of(piece, shard, along_x, sib_sem.at[piece], sib).start()
            copy_of(piece, shard, along_y, sib_sem.at[piece], sib).start()

    def stage_c(piece, shards_now):
        for shard in shards_now:
            copy_of(piece, shard, diagonal, d_sem.at[piece, shard], dp).wait_recv()
            copy_of(piece, shard, diagonal, sib_sem.at[piece], sib).start()

    writes = []
    for piece in range(count):
        for copy in pending[piece]:
            copy.wait()
        copy = pltpu.make_async_copy(holds[piece], pieces[piece].at[me], write_sem.at[piece])
        copy.start()
        writes.append(copy)
        if piece < AHEAD:
            z_send(piece)

    def complete(piece):
        writes[piece].wait()
        got = pieces[piece].at[pl.ds(0, others), pl.ds(0, 4 * part)]
        remote(got, got, send_sem.at[piece], sib_sem.at[piece], (sib, me)).wait_recv()

    def weight_loads(piece):
        width = pieces[piece].shape[2]
        return [
            pltpu.make_async_copy(
                pieces[piece].at[shard],
                weight_hold.at[piece % 2, pl.ds(shard * rows, rows), pl.ds(0, width)],
                weight_sem.at[piece % 2, shard],
            )
            for shard in range(groups)
        ]

    def start_weight(piece):
        for copy in weight_loads(piece):
            copy.start()

    def wait_weight(piece):
        for copy in weight_loads(piece):
            copy.wait()

    def wait_smalls():
        for j in range(others):
            shard = (me + 1 + j) % groups
            remote(
                rel, rel_full.at[shard], rel_send.at[j], rel_recv.at[shard], shards[j]
            ).wait()
            remote(
                small, small_full.at[shard], small_send.at[j], small_recv.at[shard], shards[j]
            ).wait()

    length = inputs.shape[0]
    block_rows = 128
    tile = 256
    per_row = rows // 128
    token_total = length * 8 * blocks * groups

    def by_rows(fn):
        def row_body(i, carry):
            fn(pl.ds(pl.multiple_of(i * block_rows, block_rows), block_rows))
            return carry

        lax.fori_loop(0, length // block_rows, row_body, 0)

    def local_sums():
        stats[...] = jnp.zeros_like(stats)
        lanes = columns // 128

        def rows_fn(at):
            value = inputs[at, :].astype(jnp.float32)
            total = jnp.sum(value, 0, keepdims=True)
            square = jnp.sum(value * value, 0, keepdims=True)
            for j in range(lanes):
                stats[j : j + 1, :] += total[:, j * 128 : (j + 1) * 128]
                stats[lanes + j : lanes + j + 1, :] += square[:, j * 128 : (j + 1) * 128]

        by_rows(rows_fn)

    def unpack():
        for row in range(9):
            for shard in range(groups):
                for j in range(per_row):
                    at = shard * rows + j * 128
                    source = row * per_row + j
                    params[row : row + 1, at : at + 128] = small_full[
                        shard, source : source + 1, :
                    ]
        lanes = columns // 128
        for j in range(lanes):
            centre = stat_total[j : j + 1, :] / token_total
            square = stat_total[lanes + j : lanes + j + 1, :] / token_total
            params[9:10, j * 128 : (j + 1) * 128] = centre
            params[10:11, j * 128 : (j + 1) * 128] = lax.rsqrt(
                square - centre * centre + EPSILON
            )
        for shard in range(groups):
            for j in range(2 * per_row):
                source = 9 * per_row + j
                at = (shard * 2 * per_row + j) * 128
                params[13 + at // columns : 14 + at // columns, at % columns : at % columns + 128] = (
                    small_full[shard, source : source + 1, :]
                )
        taken = (9 * rows + 2 * rows) // 128
        for side in range(2):
            for shard in range(groups):
                params[11 + side : 12 + side, shard * 128 : (shard + 1) * 128] = small_full[
                    shard, taken + side : taken + side + 1, :
                ]

    def activate():
        def rows_fn(at):
            standard = (inputs[at, :].astype(jnp.float32) - params[9:10, :]) * params[10:11, :]
            act_ref[at, :] = jax.nn.gelu(standard * params[0:1, :] + params[3:4, :]).astype(
                act_ref.dtype
            )

        by_rows(rows_fn)

    result_of = [
        act_ref,
        total_ref,
        norm_ref,
        content_ref,
        position_ref,
        key_ref,
        value_ref,
        table_ref.at[1],
        probs_ref,
        attended_ref,
        total_ref,
        norm_ref,
        shifted_ref,
        act_ref,
        attended_ref,
        norm_ref,
    ]

    def write_result(index):
        return pltpu.make_async_copy(result_of[index], results[index], result_sem.at[index])

    def write_pre(half):
        at = pl.ds(half * columns, columns)
        return pltpu.make_async_copy(loss_ref, pre_out.at[:, at], result_sem.at[16 + half])

    def shift_tap(tap):
        move = tap - 2

        def column_body(i, carry):
            at = pl.ds(pl.multiple_of(i * rows, 128), rows)
            value = act_ref[:, at].astype(jnp.float32)
            value = pltpu.roll(value, -move % length, 0)
            row = lax.broadcasted_iota(jnp.int32, value.shape, 0)
            inside = row < length - move if move > 0 else row >= -move
            shifted_ref[:, at] = jnp.where(inside, value, 0.0).astype(shifted_ref.dtype)
            return carry

        lax.fori_loop(0, columns // rows, column_body, 0)

    def conv_tap(tap, i):
        at = pl.ds(pl.multiple_of(i * tile, 128), tile)
        left = act_ref if tap == 2 else shifted_ref
        value = jnp.dot(
            left[...], weight_hold[tap % 2, :, at], preferred_element_type=jnp.float32
        )
        if tap == 0:
            value = value + (inputs[:, at].astype(jnp.float32) + params[4:5, at])
        else:
            value = value + total_ref[:, at]
        total_ref[:, at] = value

    def norm_step(gain, bias):
        def rows_fn(at):
            standard, _ = normalize(total_ref[at, :])
            norm_ref[at, :] = (
                standard * params[gain : gain + 1, :] + params[bias : bias + 1, :]
            ).astype(norm_ref.dtype)

        by_rows(rows_fn)

    def query_step():
        raw = jnp.dot(
            norm_ref[...], weight_hold[1, :, 0:width], preferred_element_type=jnp.float32
        )
        raw = raw * KEY**-0.5
        content_ref[...] = (raw + params[11:12, 0:width]).astype(content_ref.dtype)
        position_ref[...] = (raw + params[12:13, 0:width]).astype(position_ref.dtype)

    def key_step():
        key_ref[...] = jnp.dot(
            norm_ref[...], weight_hold[1, :, width : 2 * width], preferred_element_type=jnp.float32
        ).astype(key_ref.dtype)

    def table_step():
        for side in range(2):
            for shard in range(groups):
                table_ref[side, :, shard * 128 : (shard + 1) * 128] = jnp.dot(
                    tables[side], rel_full[shard], preferred_element_type=jnp.float32
                ).astype(table_ref.dtype)

    def value_step(i):
        at = pl.ds(pl.multiple_of(i * tile, 128), tile)
        value_ref[:, at] = jnp.dot(
            norm_ref[...], weight_hold[0, :, at], preferred_element_type=jnp.float32
        ).astype(value_ref.dtype)

    def head_step(index, side):
        head_value = columns // HEADS
        span = tables.shape[1]
        pair = pl.ds(pl.multiple_of(index * 2 * KEY, 128), 2 * KEY)
        value_pair = pl.ds(pl.multiple_of(index * 2 * head_value, 128), 2 * head_value)
        keys = slice(side * KEY, (side + 1) * KEY)
        band = dot_trailing(position_ref[:, pair][:, keys], table_ref[0, :, pair][:, keys])
        moved = pltpu.roll(band, span - length + 1, 1, stride=1, stride_axis=0)
        scores = dot_trailing(content_ref[:, pair][:, keys], key_ref[:, pair][:, keys])
        scores = scores + moved[:, :length]
        weight = jnp.exp(scores - jnp.max(scores, -1, keepdims=True))
        probs = (weight / jnp.sum(weight, -1, keepdims=True)).astype(probs_ref.dtype)
        probs_ref[2 * index + side] = probs
        chosen = value_ref[:, value_pair][:, side * head_value : (side + 1) * head_value]
        return jnp.dot(probs, chosen, preferred_element_type=jnp.float32)

    def pair_step(index):
        both = [head_step(index, side).astype(attended_ref.dtype) for side in range(2)]
        wide = 2 * columns // HEADS
        attended_ref[:, pl.ds(pl.multiple_of(index * wide, 128), wide)] = jnp.concatenate(both, 1)

    def out_step(i):
        at = pl.ds(pl.multiple_of(i * tile, 128), tile)
        value = jnp.dot(
            attended_ref[...], weight_hold[1, :, at], preferred_element_type=jnp.float32
        )
        total_ref[:, at] = total_ref[:, at] + value + params[6:7, at]

    def make_tables():
        features = rel.shape[0]
        basis = features // 6
        span = tables.shape[1]
        row = lax.broadcasted_iota(jnp.int32, (span, features), 0)
        column = lax.broadcasted_iota(jnp.int32, (span, features), 1)
        offset = row - (length - 1)
        whole = jnp.abs(offset)
        distance = whole.astype(jnp.float32)
        order_at = column % basis
        index = order_at.astype(jnp.float32)
        ratio = index / (basis - 1)
        half_life = jnp.exp2(3.0 + (math.log2(length) - 3.0) * ratio)
        decaying = jnp.exp(-math.log(2.0) / half_life * distance)
        limit = lax.shift_left(jnp.ones_like(order_at), jnp.minimum(order_at + 1, 16)) - 1
        central = jnp.where(limit > whole, 1.0, 0.0)
        stddev = length / (2.0 * basis)
        centres = length / basis + (length - length / basis) * ratio
        shape_par = (centres / stddev) * (centres / stddev)
        rate_par = centres / (stddev * stddev)
        safe = jnp.maximum(distance, 1.0)
        score = (shape_par - 1.0) * jnp.log(safe) - rate_par * safe
        peak = jnp.max(jnp.where(whole < length, score, -jnp.inf), 0, keepdims=True)
        gamma = jnp.where(whole > 0, jnp.exp(score - peak), 0.0)
        kind = column // basis % 3
        value = jnp.where(kind == 0, decaying, jnp.where(kind == 1, central, gamma))
        value = jnp.where(whole < length, value, 0.0)
        flipped = column >= 3 * basis
        for side in range(2):
            signed = offset if side == 0 else -offset
            sign = jnp.where(signed > 0, 1.0, jnp.where(signed < 0, -1.0, 0.0))
            tables[side] = jnp.where(flipped, value * sign, value).astype(tables.dtype)

    halves = [shifted_ref, act_ref]

    def up_step(half, i):
        at = pl.ds(pl.multiple_of(i * tile, 128), tile)
        value = jnp.dot(
            norm_ref[...], weight_hold[half, :, at], preferred_element_type=jnp.float32
        )
        value = value + params[13 + half : 14 + half, at]
        loss_ref[:, at] = value
        halves[half][:, at] = jax.nn.gelu(value).astype(act_ref.dtype)

    def down_step(half, i):
        at = pl.ds(pl.multiple_of(i * tile, 128), tile)
        value = total_ref[:, at]
        for shard in range(groups):
            source = (2 * shard + half) * rows
            left = halves[source // columns][:, source % columns : source % columns + rows]
            value = value + jnp.dot(
                left,
                weight_hold[half, shard * rows : (shard + 1) * rows, at],
                preferred_element_type=jnp.float32,
            )
        if half == 0:
            total_ref[:, at] = value + params[8:9, at]
        else:
            attended_ref[:, at] = value.astype(attended_ref.dtype)
            limit = limits[:, 0:1]
            norm_ref[:, at] = jnp.clip(value - target[0:1, at], -limit, limit).astype(
                norm_ref.dtype
            )

    def over_tiles(fn):
        def tile_body(i, carry):
            fn(i)
            return carry

        lax.fori_loop(0, columns // tile, tile_body, 0)

    def over_pairs(first):
        def pair_body(i, carry):
            pair_step(i)
            return carry

        lax.fori_loop(first, first + 2, pair_body, 0)


    def compute_list(n):
        if n == 2:
            return [wait_smalls, unpack, activate, make_tables, lambda: write_result(0).start()]
        piece = n - 4
        if 0 <= piece < 5:
            work = [functools.partial(wait_weight, piece)]
            if piece != 2:
                work.append(functools.partial(shift_tap, piece))
            work += [functools.partial(over_tiles, functools.partial(conv_tap, piece))]
            return work
        if piece == 5:
            return [
                lambda: write_result(1).start(),
                functools.partial(norm_step, 1, 5),
                lambda: write_result(2).start(),
                table_step,
                lambda: write_result(7).start(),
                functools.partial(wait_weight, piece),
                query_step,
                key_step,
                lambda: [write_result(i).start() for i in (3, 4, 5)],
            ]
        if piece == 6:
            work = [functools.partial(wait_weight, piece)]
            work += [functools.partial(over_tiles, value_step)]
            return work + [lambda: write_result(6).start(), functools.partial(over_pairs, 0)]
        if piece == 7:
            work = [functools.partial(over_pairs, 2)]
            work += [lambda: [write_result(i).start() for i in (8, 9)]]
            work += [functools.partial(wait_weight, piece), lambda: write_result(1).wait()]
            work += [functools.partial(over_tiles, out_step)]
            work += [lambda: write_result(10).start(), lambda: write_result(2).wait()]
            return work + [
                functools.partial(norm_step, 2, 7),
                lambda: write_result(11).start(),
                lambda: write_result(0).wait(),
            ]
        if piece in (8, 9):
            half = piece - 8
            work = [functools.partial(wait_weight, piece)]
            if half == 1:
                work.append(lambda: write_pre(0).wait())
            work += [functools.partial(over_tiles, functools.partial(up_step, half))]
            work.append(lambda: [write_pre(half).start(), write_result(12 + half).start()])
            return work
        if piece in (10, 11):
            half = piece - 10
            work = [functools.partial(wait_weight, piece)]
            if half == 0:
                work.append(lambda: write_result(10).wait())
            else:
                work.append(lambda: [write_result(i).wait() for i in (9, 11)])
            work += [functools.partial(over_tiles, functools.partial(down_step, half))]
            if half == 1:
                work.append(lambda: [write_result(i).start() for i in (14, 15)])
            return work
        return []

    def send_list(n):
        work = []
        if n + AHEAD < last:
            work.append(functools.partial(z_send, n + AHEAD))
        if n in (0, 2, 4, 6):
            work.append(functools.partial(part_send, n // 2))
        for shard in order:
            if n < last:
                work.append(functools.partial(stage_a, n, [shard]))
            if 1 <= n <= last:
                work.append(functools.partial(stage_b, n - 1, [shard]))
            if 2 <= n < last + 2:
                work.append(functools.partial(stage_c, n - 2, [shard]))
            if n in (2, 4, 6, 8):
                work.append(functools.partial(part_stage, n // 2 - 1, shard))
        return work

    local_sums()
    for step in summing[:4]:
        step()

    for n in range(count + 4):
        sends = send_list(n)
        work = compute_list(n)
        if 0 <= n - 3 < count:
            complete(n - 3)
            start_weight(n - 3)
        slots = max(len(work), 1)
        for i in range(slots):
            for send in sends[len(sends) * i // slots : len(sends) * (i + 1) // slots]:
                send()
            if i < len(work):
                work[i]()
        if n < 2:
            summing[4 + n]()

    for index in (3, 4, 5, 6, 7, 8, 12, 13, 14, 15):
        write_result(index).wait()
    write_pre(1).wait()

    for step in range(4):
        for shard in range(groups):

            @pl.when(jnp.logical_and(shard <= me, me + 1 < groups))
            def _():
                part_copy(step, shard, (me + 1) % groups, part_right).wait_send()

            @pl.when(jnp.logical_and(shard >= me, me > 0))
            def _():
                part_copy(step, shard, (me + groups - 1) % groups, part_left).wait_send()

    sent = pieces[last].at[pl.ds(0, others), pl.ds(0, 4 * part)]
    remote(sent, sent, send_sem.at[last], sib_sem.at[last], (sib, me)).wait_send()
    for piece in range(last):
        for shard in range(groups):

            @pl.when(jnp.logical_and(shard <= me, me + 1 < groups))
            def _():
                right_copy(piece, shard).wait_send()

            @pl.when(jnp.logical_and(shard >= me, me > 0))
            def _():
                left_copy(piece, shard).wait_send()

        sent = pieces[piece].at[pl.ds(0, others), pl.ds(0, 7 * part)]
        remote(sent, sent, send_sem.at[piece], sib_sem.at[piece], (sib, me)).wait_send()


def gather(groups, blocks, weights, small, inputs, target, limits):
    conv, query = weights[:2]
    rel = weights[7]
    taps, rows, columns = conv.shape
    width = query.shape[1]
    length = inputs.shape[0]
    span = 2 * length
    stats_shape = (2 * columns // 128, 128)
    dtype = conv.dtype
    kept = pl.BlockSpec(memory_space=pl.ANY)
    inside = pl.BlockSpec(memory_space=pltpu.VMEM)
    full = jax.ShapeDtypeStruct((groups, rows, columns), dtype)
    count = taps + 7
    grid_sems = [pltpu.SemaphoreType.DMA((count, groups))] * 4
    wide = (length, columns)
    narrow = (length, width)
    made = [
        jax.ShapeDtypeStruct(wide, dtype),
        jax.ShapeDtypeStruct(wide, jnp.float32),
        jax.ShapeDtypeStruct(wide, dtype),
        jax.ShapeDtypeStruct(narrow, dtype),
        jax.ShapeDtypeStruct(narrow, dtype),
        jax.ShapeDtypeStruct(narrow, dtype),
        jax.ShapeDtypeStruct(wide, dtype),
        jax.ShapeDtypeStruct((span, width), dtype),
        jax.ShapeDtypeStruct((HEADS, length, length), dtype),
        jax.ShapeDtypeStruct(wide, dtype),
        jax.ShapeDtypeStruct(wide, jnp.float32),
        jax.ShapeDtypeStruct(wide, dtype),
        jax.ShapeDtypeStruct((length, 2 * columns), jnp.float32),
        jax.ShapeDtypeStruct((length, 2 * columns), dtype),
        jax.ShapeDtypeStruct(wide, dtype),
        jax.ShapeDtypeStruct(wide, dtype),
    ]
    return pl.pallas_call(
        functools.partial(gather_kernel, groups, blocks),
        out_shape=(
            jax.ShapeDtypeStruct((taps, groups, rows, columns), dtype),
            jax.ShapeDtypeStruct((groups, rows, 2 * width), dtype),
            full,
            full,
            jax.ShapeDtypeStruct((groups, rows, 2 * columns), dtype),
            jax.ShapeDtypeStruct((groups, 2 * rows, columns), dtype),
            jax.ShapeDtypeStruct((groups,) + rel.shape, dtype),
            jax.ShapeDtypeStruct((groups,) + small.shape, jnp.float32),
            jax.ShapeDtypeStruct(stats_shape, jnp.float32),
            *made,
            jax.ShapeDtypeStruct((2, span, rel.shape[0]), dtype),
        ),
        in_specs=[kept] * 7 + [inside] * 5,
        out_specs=[kept] * 6 + [inside] * 3 + [kept] * len(made) + [inside],
        scratch_shapes=[
            pltpu.VMEM((count - 1, rows, columns), dtype),
            pltpu.VMEM((rows, 2 * width), dtype),
            pltpu.SemaphoreType.DMA((taps + 8,)),
            pltpu.SemaphoreType.DMA((count,)),
            *grid_sems,
            pltpu.SemaphoreType.DMA((count,)),
            pltpu.SemaphoreType.DMA((count,)),
            *grid_sems[:2],
            *([pltpu.SemaphoreType.DMA((groups,))] * 4),
            *sum_scratch(groups, blocks, stats_shape),
            pltpu.VMEM((2, columns, columns), dtype),
            pltpu.SemaphoreType.DMA((2, groups)),
            pltpu.SemaphoreType.DMA((len(made) + 2,)),
            pltpu.VMEM((16, columns), jnp.float32),
            pltpu.VMEM(wide, dtype),
            pltpu.VMEM(wide, jnp.float32),
            pltpu.VMEM(wide, dtype),
            pltpu.VMEM(wide, dtype),
            pltpu.VMEM(narrow, dtype),
            pltpu.VMEM(narrow, dtype),
            pltpu.VMEM(narrow, dtype),
            pltpu.VMEM(wide, dtype),
            pltpu.VMEM((2, span, width), dtype),
            pltpu.VMEM((HEADS, length, length), dtype),
            pltpu.VMEM(wide, dtype),
            pltpu.VMEM(stats_shape, jnp.float32),
            pltpu.VMEM(wide, jnp.float32),
            *([pltpu.SemaphoreType.DMA((4, groups))] * 3),
        ],
        compiler_params=pltpu.CompilerParams(
            collective_id=0, has_side_effects=True, vmem_limit_bytes=60 << 20
        ),
        name="gather",
    )(*weights, small, inputs, target, limits)


def gelu_slope(value):
    inner = GELU * (value + 0.044715 * value * value * value)
    curve = jnp.tanh(inner)
    slope = GELU * (1.0 + 3 * 0.044715 * value * value)
    return 0.5 * (1.0 + curve) + 0.5 * value * (1.0 - curve * curve) * slope


def reduce_kernel(groups, blocks, rel_at, *refs):
    lefts = refs[:5]
    cotangent, hidden_pre, after_attention, after_conv, tokens = refs[5:10]
    down_full, up_full, out_full, value_full, mixed_full, conv_full = refs[10:16]
    probs, values, keys, contents, positions, mirrored_keys = refs[16:22]
    params, table = refs[22:24]
    out, total, part_grad = refs[24:27]
    made = refs[27:32]
    hidden_got, left_got, right_got = refs[32:35]
    rights = [cotangent, *made]
    (
        left_hold,
        right_hold,
        grad,
        x_one,
        y_one,
        x_two,
        y_two,
        shard_got,
        block_got,
        done,
        rel_grad,
        rel_got,
        vector,
    ) = refs[35:48]
    left_send, left_recv, right_send, right_recv, rel_send, rel_recv = refs[48:54]
    load_sem = refs[54]
    x1s, y1s, x2s, y2s, x1r, y1r, x2r, y2r = refs[55:63]
    shard_send, shard_recv, block_send, block_recv = refs[63:67]
    write_sem, send_sem, ax, ay, ad, sib_sem = refs[67:73]
    sum_bufs = refs[73:77]
    sum_sems = refs[77:83]
    credit, shard_credit = refs[83:85]
    (
        attn_grad,
        total_ref,
        kept_ref,
        weight_hold,
        wide_hold,
        right_ref,
        value_grad_ref,
        mixed_ref,
        key_ref,
        content_ref,
        position_ref,
        table_ref,
        table_grad_ref,
        probs_ref,
    ) = refs[85:99]
    tile_sem, host_sem, probs_sem, kept_sem = refs[99:103]
    slab, slab_got, x_slab, y_slab, x_part, y_part, slab_credit = refs[103:110]

    dp = lax.axis_index("dp")
    me = lax.axis_index("fsdp")
    near, shards, far = peers_of(groups, blocks)
    sib, along_x, along_y = neighbours(dp)
    core = dp % 2
    at_x = dp // 2 % 2
    at_y = dp // 4 % 2
    block = dp // 8
    slots = grad.shape[0]
    part = grad.shape[4]
    width = grad.shape[5]
    half = width // 2
    rows = 4 * part
    count = out.shape[0]
    others = groups - 1
    first = pl.ds(0, half)
    last = pl.ds(half, half)
    taps = 5
    up_right = rights[1]
    rights[1:2] = [up_right.at[:, pl.ds(side * 2 * width, 2 * width)] for side in range(2)]
    lefts_got = [hidden_got] + [left_got.at[index] for index in range(4)]
    left_of = [0, 1, 1, 2, 3, 3, 4, 4, 4, 4, 0, 4]
    right_of = [0, 1, 2, 3, 4, 5, 6, 6, 6, 6, 0, 6]
    tap_of = {6: 0, 7: 1, 8: 2, 9: 3, 11: 4}
    mixed_piece = 5
    normal = 10
    extra_at = {0: 10, 6: 11}
    own_columns = pl.ds(pl.multiple_of(core * width, 128), width)
    sib_columns = pl.ds(pl.multiple_of((1 - core) * width, 128), width)

    def left_copy(index):
        return remote(
            lefts[index], lefts_got[index], left_send.at[index], left_recv.at[index], (sib, me)
        )

    def right_copy(index):
        return remote(
            rights[index].at[:, sib_columns],
            right_got.at[index],
            right_send.at[index],
            right_recv.at[index],
            (sib, me),
        )

    def rel_copy():
        return remote(rel_grad, rel_got, rel_send.at[0], rel_recv.at[0], (sib, me))

    def loads(piece):
        left = left_of[piece]
        right = right_of[piece]
        pairs = [
            (rights[right].at[:, own_columns], right_hold.at[0]),
            (right_got.at[right], right_hold.at[1]),
        ]
        if left > 0:
            pairs.append((lefts[left], left_hold.at[0]))
            pairs.append((lefts_got[left], left_hold.at[1]))
        else:
            for shard in range(groups):
                source = pl.ds((2 * shard + piece // normal) * rows, rows)
                target = pl.ds(shard * rows, rows)
                pairs.append((lefts[left].at[:, source], left_hold.at[0, :, target]))
                pairs.append((lefts_got[left].at[:, source], left_hold.at[1, :, target]))
        return [
            pltpu.make_async_copy(src, dst, load_sem.at[i]) for i, (src, dst) in enumerate(pairs)
        ]

    def start_loads(piece):
        if left_of[piece] not in left_of[:piece]:
            left_copy(left_of[piece]).wait_recv()
        if right_of[piece] not in right_of[:piece]:
            right_copy(right_of[piece]).wait_recv()
        for copy in loads(piece):
            copy.start()

    def wait_loads(piece):
        for copy in loads(piece):
            copy.wait()
        if tap_of.get(piece, 2) != 2:
            shift(tap_of[piece] - taps // 2)

    meet(near + shards + far)

    for index in range(len(lefts)):
        left_copy(index).start()
        if index == 0:
            right_copy(0).start()
    start_loads(0)

    summing = sum_steps(groups, blocks, vector, total, *sum_bufs, sum_sems)

    ring = x_one.shape[0]

    def pay(piece, index, device):
        @pl.when(piece < normal - ring)
        def _():
            pl.semaphore_signal(
                credit.at[index], inc=1, device_id=(device, me), device_id_type=MESH
            )

    def claim(piece, index):
        @pl.when(piece >= ring)
        def _():
            pl.semaphore_wait(credit.at[index], 1)

    def one(piece):
        slot = piece % slots
        return (
            remote(
                grad.at[slot, :, :, 1 - at_x, :, first],
                x_one.at[piece % ring],
                x1s.at[piece],
                x1r.at[piece],
                (along_x, me),
            ),
            remote(
                grad.at[slot, :, 1 - at_y, :, :, last],
                y_one.at[piece % ring],
                y1s.at[piece],
                y1r.at[piece],
                (along_y, me),
            ),
        )

    def two(piece):
        slot = piece % slots
        return (
            remote(
                grad.at[slot, :, 1 - at_y, at_x, :, first],
                y_two.at[piece % ring],
                y2s.at[piece],
                y2r.at[piece],
                (along_y, me),
            ),
            remote(
                grad.at[slot, :, at_y, 1 - at_x, :, last],
                x_two.at[piece % ring],
                x2s.at[piece],
                x2r.at[piece],
                (along_x, me),
            ),
        )

    def shard_copy(piece, j):
        other = (me + 1 + j) % groups
        return remote(
            grad.at[piece % slots, other, at_y, at_x],
            shard_got.at[piece % ring, me],
            shard_send.at[piece, j],
            shard_recv.at[piece, me],
            (dp, other),
        )

    def shard_arrival(piece, j):
        other = (me + 1 + j) % groups
        return remote(
            grad.at[piece % slots, other, at_y, at_x],
            shard_got.at[piece % ring, other],
            shard_send.at[piece, j],
            shard_recv.at[piece, other],
            (dp, other),
        )

    def block_copy(piece, j):
        return remote(
            done.at[piece],
            block_got.at[piece, block],
            block_send.at[piece, j],
            block_recv.at[piece, block],
            far[j],
        )

    def block_arrival(piece, j):
        other = (block + 1 + j) % blocks
        return remote(
            done.at[piece],
            block_got.at[piece, other],
            block_send.at[piece, j],
            block_recv.at[piece, other],
            far[j],
        )

    def place(piece, owner):
        return out.at[
            piece,
            pl.ds(pl.multiple_of(owner % 8 // 2 * part, 16), part),
            pl.ds(pl.multiple_of(core * width, 128), width),
        ]

    def spread(piece, src, owner, recv_sem, device):
        return remote(src, place(piece, owner), send_sem.at[piece], recv_sem, (device, me))

    def forward(piece, owner, recv_sem, device):
        return spread(piece, place(piece, owner), owner, recv_sem, device)

    diagonal = neighbours(along_x)[2]

    def shift(move):
        for window in range(2):
            value = right_hold[window].astype(jnp.float32)
            value = pltpu.roll(value, move % value.shape[0], 0)
            row = lax.broadcasted_iota(jnp.int32, value.shape, 0)
            inside = row >= move if move > 0 else row < value.shape[0] + move
            value = jnp.where(inside, value, 0.0)
            right_hold[window] = value.astype(right_hold.dtype)

    def product(shard):
        at = pl.ds(pl.multiple_of(shard * rows, 128), rows)
        value = dot_leading(left_hold[0, :, at], right_hold[0])
        value = value + dot_leading(left_hold[1, :, at], right_hold[1])
        return value.astype(grad.dtype).reshape(2, 2, part, width)

    def produce(piece):
        slot = piece % slots

        def shard_body(shard, carry):
            grad[slot, shard] = product(shard)
            return carry

        lax.fori_loop(0, groups, shard_body, 0)

        @pl.when(piece == mixed_piece)
        def _():
            rel_copy().wait()

        @pl.when(jnp.logical_and(piece == mixed_piece, core == 1))
        def _():
            for shard in range(groups):
                value = rel_grad[shard].astype(jnp.float32) + rel_got[shard].astype(jnp.float32)
                grad[slot, shard, 0, :, :, pl.ds(rel_at, rel_grad.shape[3])] = value.astype(
                    grad.dtype
                )

    def slab_copy(piece, j, arriving=False):
        other = (me + 1 + j) % groups
        at = j if arriving else groups - 2 - j
        return remote(
            slab.at[other],
            slab_got.at[at],
            shard_send.at[piece, j],
            shard_recv.at[piece, at],
            (dp, other),
        )

    def slab_one(piece, e):
        return (
            remote(
                slab.at[me, :, 1 - at_x, :, first],
                x_slab.at[e],
                x1s.at[piece],
                x1r.at[piece],
                (along_x, me),
            ),
            remote(
                slab.at[me, 1 - at_y, :, :, last],
                y_slab.at[e],
                y1s.at[piece],
                y1r.at[piece],
                (along_y, me),
            ),
        )

    def slab_two(piece, e):
        return (
            remote(
                slab.at[me, 1 - at_y, at_x, :, first],
                y_part.at[e],
                y2s.at[piece],
                y2r.at[piece],
                (along_y, me),
            ),
            remote(
                slab.at[me, at_y, 1 - at_x, :, last],
                x_part.at[e],
                x2s.at[piece],
                x2r.at[piece],
                (along_x, me),
            ),
        )

    def slab_sent(piece, e):
        for j in range(others):
            slab_copy(piece, j).wait_send()
        for copy in slab_one(piece, e) + slab_two(piece, e):
            copy.wait_send()

    def extra_start(piece, e):
        for copy in loads(piece):
            copy.start()
        if e > 0:
            slab_sent(piece - 1, e - 1)
        wait_loads(piece)

        def shard_body(shard, carry):
            slab[shard] = product(shard)
            return carry

        lax.fori_loop(0, groups, shard_body, 0)
        for j in range(others):
            if e > 0:
                pl.semaphore_wait(slab_credit.at[(me + 1 + j) % groups], 1)
            slab_copy(piece, j).start()

    def extra_sum(piece, e):
        for j in range(others):
            slab_copy(piece, j, True).wait_recv()
        for y in range(2):
            for x in range(2):
                value = slab[me, y, x].astype(jnp.float32)
                for j in range(others):
                    value = value + slab_got[j, y, x].astype(jnp.float32)
                slab[me, y, x] = value.astype(slab.dtype)
        if e == 0:
            for j in range(others):
                pl.semaphore_signal(
                    slab_credit.at[me], inc=1, device_id=shards[j], device_id_type=MESH
                )
        for copy in slab_one(piece, e):
            copy.start()

    def extra_fold(piece, e):
        for copy in slab_one(piece, e):
            copy.wait_recv()
        for other in range(2):
            value = slab[me, other, at_x, :, first].astype(jnp.float32)
            value = value + x_slab[e, other].astype(jnp.float32)
            slab[me, other, at_x, :, first] = value.astype(slab.dtype)
            value = slab[me, at_y, other, :, last].astype(jnp.float32)
            value = value + y_slab[e, other].astype(jnp.float32)
            slab[me, at_y, other, :, last] = value.astype(slab.dtype)
        for copy in slab_two(piece, e):
            copy.start()

    def extra_done(piece, e):
        for copy in slab_two(piece, e):
            copy.wait_recv()
        low = slab[me, at_y, at_x, :, first].astype(jnp.float32)
        high = slab[me, at_y, at_x, :, last].astype(jnp.float32)
        low = low + y_part[e].astype(jnp.float32)
        high = high + x_part[e].astype(jnp.float32)
        finish(piece, jnp.concatenate([low, high], 1))

    def finish(piece, value):
        if blocks > 1:
            done[piece] = value.astype(done.dtype)
            block_got[piece, block] = value.astype(done.dtype)
            for j in range(blocks - 1):
                block_copy(piece, j).start()
            for j in range(blocks - 1):
                block_copy(piece, j).wait_send()
                block_arrival(piece, j).wait_recv()
            value = block_got[piece, 0].astype(jnp.float32)
            for other in range(1, blocks):
                value = value + block_got[piece, other].astype(jnp.float32)
        done[piece] = value.astype(done.dtype)
        pltpu.make_async_copy(done.at[piece], place(piece, dp), write_sem.at[piece]).start()
        spread(piece, done.at[piece], dp, ax.at[piece], along_x).start()
        spread(piece, done.at[piece], dp, ay.at[piece], along_y).start()
        spread(piece, done.at[piece], dp, sib_sem.at[piece], sib).start()

    def cross(piece):
        route = piece % 2
        forward(piece, along_x, ax.at[piece], dp).wait_recv()
        forward(piece, along_y, ay.at[piece], dp).wait_recv()
        owner = route * along_x + (1 - route) * along_y
        target = route * along_y + (1 - route) * along_x
        forward(piece, owner, ad.at[piece], target).start()
        forward(piece, along_x, sib_sem.at[piece], sib).start()
        forward(piece, along_y, sib_sem.at[piece], sib).start()

    def close(piece):
        forward(piece, diagonal, ad.at[piece], dp).wait_recv()
        forward(piece, diagonal, sib_sem.at[piece], sib).start()

    def add(piece_slot, ref, columns, *index):
        ahead = grad[(piece_slot,) + index + (slice(None), columns)]
        return ahead.astype(jnp.float32) + ref.astype(jnp.float32)

    length = tokens.shape[0]
    columns = 2 * width
    tile = 512
    block_rows = 128
    head_value = columns // HEADS
    tiles = columns // tile
    hidden_tiles = hidden_pre.shape[1] // tile

    def tile_of(phase, i):
        at = pl.ds(pl.multiple_of(i * tile, tile), tile)
        if phase == 0:
            return down_full.at[at]
        if phase == 1:
            at = pl.ds(pl.multiple_of(i // 2 * tile, tile), tile)
            return up_full.at[at, pl.ds(pl.multiple_of(i % 2 * columns, columns), columns)]
        if phase == 5:
            at = pl.ds(pl.multiple_of(i % tiles * tile, tile), tile)
            return conv_full.at[i // tiles, at]
        return (out_full, mixed_full, value_full)[phase - 2].at[at]

    lengths = [hidden_tiles, 2 * tiles, tiles, tiles, tiles, taps * tiles]
    widths = [columns, columns, columns, mixed_full.shape[1], columns, columns]

    def tile_load(phase, i):
        slot = (sum(lengths[:phase]) + i) % 2
        return pltpu.make_async_copy(
            tile_of(phase, i),
            weight_hold.at[slot, :, pl.ds(0, widths[phase])],
            tile_sem.at[slot],
        )

    def next_tile(phase, i):
        tile_load(phase, i).wait()

        @pl.when(i + 1 < lengths[phase])
        def _():
            tile_load(phase, i + 1).start()

        if phase + 1 < len(lengths):

            @pl.when(i + 1 == lengths[phase])
            def _():
                tile_load(phase + 1, 0).start()

        slot = (sum(lengths[:phase]) + i) % 2
        return weight_hold[slot, :, 0 : widths[phase]]

    def over(count, fn):
        def step_body(i, carry):
            fn(i)
            return carry

        lax.fori_loop(0, count, step_body, 0)

    def columns_at(i, wide, offset=0):
        return pl.ds(pl.multiple_of(offset + i * wide, 128), wide)

    def host_load(index):
        pairs = [
            (cotangent, right_ref),
            (after_attention, kept_ref),
            (after_conv, kept_ref),
            (values, wide_hold.at[:, pl.ds(columns, columns)]),
            (keys, key_ref),
            (contents, content_ref),
            (positions, position_ref),
            (mirrored_keys, table_ref),
            (tokens, wide_hold.at[:, pl.ds(columns, columns)]),
            (wide_hold, made[0]),
            (right_ref, made[1]),
            (value_grad_ref, made[2]),
            (mixed_ref, made[3]),
            (right_ref, made[4]),
        ]
        return pltpu.make_async_copy(*pairs[index], host_sem.at[index])

    def load(*indices):
        def thunk():
            for index in indices:
                host_load(index).start()

        return thunk

    def ready(*indices):
        def thunk():
            for index in indices:
                host_load(index).wait()

        return thunk

    def send_right(*indices):
        def thunk():
            for index in indices:
                right_copy(index).start()

        return thunk

    def pre_load(i):
        return pltpu.make_async_copy(
            hidden_pre.at[:, columns_at(i, tile)],
            kept_ref.at[:, columns_at(i % 3, tile)],
            kept_sem.at[i],
        )

    def write_part():
        return pltpu.make_async_copy(attn_grad, part_grad, kept_sem.at[hidden_tiles])

    def by_rows(fn):
        def row_body(i, carry):
            fn(pl.ds(pl.multiple_of(i * block_rows, block_rows), block_rows))
            return carry

        lax.fori_loop(0, length // block_rows, row_body, 0)

    def put(row, value):
        vector[row : row + 1, :] += jnp.sum(value, 0, keepdims=True)

    def clear_total():
        def rows_fn(at):
            total_ref[at, :] = jnp.zeros((block_rows, columns), jnp.float32)

        by_rows(rows_fn)

    def begin():
        vector[...] = jnp.zeros_like(vector)
        mixed_ref[...] = jnp.zeros_like(mixed_ref)
        tile_load(0, 0).start()
        for i in range(3):
            pre_load(i).start()
        clear_total()

    def hidden_step(i):
        value = dot_trailing(right_ref[...], next_tile(0, i))
        pre_load(i).wait()
        value = value * gelu_slope(kept_ref[:, columns_at(i % 3, tile)])

        @pl.when(i + 3 < hidden_tiles)
        def _():
            pre_load(i + 3).start()

        rounded = value.astype(wide_hold.dtype)
        wide_hold[:, columns_at(i, tile)] = rounded
        sums_here = jnp.sum(rounded.astype(jnp.float32), 0, keepdims=True)
        for side in range(2):

            @pl.when(i // tiles == side)
            def _():
                vector[9 + side : 10 + side, columns_at(i % tiles, tile)] = sums_here

    def norm_two_step(i):
        left = wide_hold[:, columns_at(i % 2, columns)]
        total_ref[:, columns_at(i // 2, tile)] += dot_trailing(left, next_tile(1, i))

    def norm_two_back():
        def rows_fn(at):
            standard, inverse = normalize(kept_ref[at, :])
            value = total_ref[at, :]
            put(2, value * standard)
            put(7, value)
            cot = right_ref[at, :].astype(jnp.float32)
            put(8, cot)
            value = cot + norm_back(value * params[2:3, :], standard, inverse)
            attn_grad[at, :] = value
            rounded = value.astype(right_ref.dtype)
            right_ref[at, :] = rounded
            put(6, rounded.astype(jnp.float32))

        by_rows(rows_fn)

    def attended_step(i):
        value = dot_trailing(right_ref[...], next_tile(2, i))
        wide_hold[:, columns_at(i, tile)] = value.astype(wide_hold.dtype)

    def probs_load(head):
        return pltpu.make_async_copy(
            probs.at[head], probs_ref.at[head % 2], probs_sem.at[head % 2]
        )

    def pair_step(index):
        span = table_ref.shape[0]
        row = lax.broadcasted_iota(jnp.int32, (length, length), 0)
        column = lax.broadcasted_iota(jnp.int32, (length, length), 1)
        mirror = jnp.where(row + column == length - 1, 1.0, 0.0).astype(jnp.bfloat16)
        pair = columns_at(index, 2 * KEY)
        key_pair = columns_at(index, 2 * KEY, key_ref.shape[1])
        value_pair = columns_at(index, 2 * head_value)
        far_pair = columns_at(index, 2 * head_value, columns)
        made_here = [[], [], [], [], [], []]
        for side in range(2):
            head = 2 * index + side
            probs_load(head).wait()
            keys_at = slice(side * KEY, (side + 1) * KEY)
            values_at = slice(side * head_value, (side + 1) * head_value)
            prob = probs_ref[side]
            out_grad = wide_hold[:, value_pair][:, values_at]
            made_here[0].append(dot_leading(prob, out_grad).astype(jnp.bfloat16))
            prob_grad = dot_trailing(out_grad, wide_hold[:, far_pair][:, values_at])
            prob = prob.astype(jnp.float32)
            row_dot = jnp.sum(prob * prob_grad, -1, keepdims=True)
            rounded = (prob * (prob_grad - row_dot)).astype(jnp.bfloat16)
            content = content_ref[:, pair][:, keys_at]
            made_here[1].append(dot_leading(rounded, content).astype(jnp.bfloat16))
            content_grad = jnp.dot(
                rounded, key_ref[:, pair][:, keys_at], preferred_element_type=jnp.float32
            )
            mirrored = jnp.dot(rounded, mirror, preferred_element_type=jnp.float32)
            wide = jnp.concatenate([mirrored, jnp.zeros((length, span - length), jnp.float32)], 1)
            band = pltpu.roll(wide, 0, 1, stride=1, stride_axis=0).astype(jnp.bfloat16)
            position_grad = jnp.dot(
                band, table_ref[:, pair][:, keys_at], preferred_element_type=jnp.float32
            )
            position = position_ref[:, pair][:, keys_at]
            made_here[2].append(dot_leading(band, position).astype(jnp.bfloat16))
            made_here[3].append(((content_grad + position_grad) * KEY**-0.5).astype(jnp.bfloat16))
            made_here[4].append(jnp.sum(content_grad, 0, keepdims=True))
            made_here[5].append(jnp.sum(position_grad, 0, keepdims=True))
        value_grad_ref[:, value_pair] = jnp.concatenate(made_here[0], 1)
        mixed_ref[:, key_pair] = jnp.concatenate(made_here[1], 1)
        table_grad_ref[:, pair] = jnp.concatenate(made_here[2], 1)
        mixed_ref[:, pair] = jnp.concatenate(made_here[3], 1)
        vector[11:12, pair] = jnp.concatenate(made_here[4], 1)
        vector[11:12, key_pair] = jnp.concatenate(made_here[5], 1)

        @pl.when(index + 1 < HEADS // 2)
        def _():
            for side in range(2):
                probs_load(2 * index + 2 + side).start()

    def rel_step():
        for shard in range(groups):
            value = dot_leading(table[...], table_grad_ref[:, shard * 128 : (shard + 1) * 128])
            rel_grad[shard] = value.astype(rel_grad.dtype).reshape(rel_grad.shape[1:])
        rel_copy().start()

    def mixed_step(i):
        left = mixed_ref[:, 0 : mixed_full.shape[1]]
        total_ref[:, columns_at(i, tile)] = dot_trailing(left, next_tile(3, i))

    def value_step(i):
        total_ref[:, columns_at(i, tile)] += dot_trailing(value_grad_ref[...], next_tile(4, i))

    def norm_one_back():
        def rows_fn(at):
            standard, inverse = normalize(kept_ref[at, :])
            value = total_ref[at, :]
            put(1, value * standard)
            put(5, value)
            value = attn_grad[at, :] + norm_back(value * params[1:2, :], standard, inverse)
            attn_grad[at, :] = value
            rounded = value.astype(right_ref.dtype)
            right_ref[at, :] = rounded
            put(4, rounded.astype(jnp.float32))

        by_rows(rows_fn)

    def conv_shift(tap):
        move = tap - taps // 2

        def column_body(i, carry):
            at = columns_at(i, rows)
            value = right_ref[:, at].astype(jnp.float32)
            value = pltpu.roll(value, (move + length) % length, 0)
            row = lax.broadcasted_iota(jnp.int32, value.shape, 0) - move
            inside = jnp.logical_and(row >= 0, row < length)
            wide_hold[:, at] = jnp.where(inside, value, 0.0).astype(wide_hold.dtype)
            return carry

        lax.fori_loop(0, columns // rows, column_body, 0)

    def conv_step(i):
        left = wide_hold[:, 0:columns]
        total_ref[:, columns_at(i % tiles, tile)] += dot_trailing(left, next_tile(5, i))

    def batch_back():
        def rows_fn(at):
            value = wide_hold[at, columns : 2 * columns].astype(jnp.float32)
            standard = (value - params[4:5, :]) * params[5:6, :]
            normed = standard * params[0:1, :] + params[3:4, :]
            value = total_ref[at, :] * gelu_slope(normed)
            put(0, value * standard)
            put(3, value)
            attn_grad[at, :] += params[5:6, :] * params[0:1, :] * value

        by_rows(rows_fn)

    def start_probs():
        for head in range(2):
            probs_load(head).start()

    def step_zero():
        begin()
        ready(0)()
        over(hidden_tiles, hidden_step)
        load(9, 1)()
        ready(9)()
        send_right(1, 2)()

    def step_one():
        over(2 * tiles, norm_two_step)
        load(3)()
        ready(1)()
        norm_two_back()
        load(10, 2)()
        start_probs()

    def step_two():
        over(tiles, attended_step)
        ready(10)()
        send_right(3)()
        ready(3, 4, 5, 6, 7)()

    def step_three():
        load(11, 12, 8)()
        rel_step()
        ready(11, 12)()
        send_right(4, 5)()

    def step_four():
        over(tiles, mixed_step)
        over(tiles, value_step)
        ready(2)()
        norm_one_back()
        load(13)()
        ready(13)()
        send_right(6)()
        clear_total()

    def step_last():
        ready(8)()
        batch_back()
        write_part().start()

    pairs_each = HEADS // 4

    for copy in (0, 4, 5, 6, 7):
        host_load(copy).start()

    def host(n):
        pl.when(n == 0)(step_zero)
        pl.when(n == 1)(step_one)
        pl.when(n == 2)(step_two)

        @pl.when(jnp.logical_and(n >= 2, n < 4))
        def _():
            over(pairs_each, lambda i: pair_step((n - 2) * pairs_each + i))

        pl.when(n == 3)(step_three)
        pl.when(n == 4)(step_four)

        @pl.when(jnp.logical_and(n >= 5, n < 5 + taps))
        def _():
            conv_shift(n - 5)
            over(tiles, lambda i: conv_step((n - 5) * tiles + i))

        pl.when(n == 4 + taps)(step_last)

    def body(n, carry):
        @pl.when(n < normal)
        def _():
            @pl.when(n >= slots)
            def _():
                old = n - slots
                for copy in one(old) + two(old):
                    copy.wait_send()
                for j in range(others):
                    shard_copy(old, j).wait_send()

            for piece in range(normal):

                @pl.when(n == piece)
                def _():
                    wait_loads(piece)

            produce(n)
            claim(n, 0)
            claim(n, 1)
            for copy in one(n):
                copy.start()

        for e, (at, piece) in enumerate(extra_at.items()):

            @pl.when(n == at)
            def _():
                extra_start(piece, e)

        host(n)
        for piece in range(1, normal):

            @pl.when(n == piece - 1)
            def _():
                start_loads(piece)

        @pl.when(jnp.logical_and(n >= 1, n < normal + 1))
        def _():
            piece = n - 1
            slot = piece % slots
            for copy in one(piece):
                copy.wait_recv()

            def shard_body(shard, carry):
                for other in range(2):
                    value = add(slot, x_one[piece % ring, shard, other], first, shard, other, at_x)
                    grad[slot, shard, other, at_x, :, first] = value.astype(grad.dtype)
                    value = add(slot, y_one[piece % ring, shard, other], last, shard, at_y, other)
                    grad[slot, shard, at_y, other, :, last] = value.astype(grad.dtype)
                return carry

            lax.fori_loop(0, groups, shard_body, 0)
            pay(piece, 0, along_x)
            pay(piece, 1, along_y)
            claim(piece, 2)
            claim(piece, 3)
            for copy in two(piece):
                copy.start()

        @pl.when(jnp.logical_and(n >= 2, n < normal + 2))
        def _():
            piece = n - 2
            slot = piece % slots
            for copy in two(piece):
                copy.wait_recv()

            def shard_body(shard, carry):
                value = add(slot, y_two[piece % ring, shard], first, shard, at_y, at_x)
                grad[slot, shard, at_y, at_x, :, first] = value.astype(grad.dtype)
                value = add(slot, x_two[piece % ring, shard], last, shard, at_y, at_x)
                grad[slot, shard, at_y, at_x, :, last] = value.astype(grad.dtype)
                return carry

            lax.fori_loop(0, groups, shard_body, 0)
            pay(piece, 2, along_y)
            pay(piece, 3, along_x)
            for j in range(others):

                @pl.when(piece >= ring)
                def _():
                    pl.semaphore_wait(shard_credit.at[(me + 1 + j) % groups], 1)

                shard_copy(piece, j).start()

        @pl.when(jnp.logical_and(n >= 3, n < normal + 3))
        def _():
            piece = n - 3
            value = grad[piece % slots, me, at_y, at_x].astype(jnp.float32)
            for j in range(others):
                shard_arrival(piece, j).wait_recv()
                value = value + shard_got[piece % ring, (me + 1 + j) % groups].astype(jnp.float32)

            @pl.when(piece < normal - ring)
            def _():
                for j in range(others):
                    pl.semaphore_signal(
                        shard_credit.at[me], inc=1, device_id=shards[j], device_id_type=MESH
                    )

            finish(piece, value)

        @pl.when(jnp.logical_and(n >= 4, n < normal + 4))
        def _():
            cross(n - 4)

        @pl.when(n >= 5)
        def _():
            close(n - 5)

        for e, (at, piece) in enumerate(extra_at.items()):
            for later, action in (
                (3, functools.partial(extra_sum, piece, e)),
                (4, functools.partial(extra_fold, piece, e)),
                (5, functools.partial(extra_done, piece, e)),
                (6, functools.partial(cross, piece)),
                (7, functools.partial(close, piece)),
            ):
                pl.when(n == at + later)(action)

        for step in range(len(summing)):

            @pl.when(n == normal + step - 1)
            def _():
                summing[step]()

        return carry

    lax.fori_loop(0, normal + 5, body, 0)
    slab_sent(11, 1)
    write_part().wait()

    def drain(piece, carry):
        @pl.when(jnp.logical_and(piece >= normal - slots, piece < normal))
        def _():
            for copy in one(piece) + two(piece):
                copy.wait_send()
            for j in range(others):
                shard_copy(piece, j).wait_send()

        pltpu.make_async_copy(done.at[piece], place(piece, dp), write_sem.at[piece]).wait()
        got = out.at[piece, :, pl.ds(0, width)]
        remote(got, got, send_sem.at[piece], sib_sem.at[piece], (sib, me)).wait_recv()
        sent = out.at[piece, pl.ds(0, 7 * part // 2), :]
        remote(sent, sent, send_sem.at[piece], sib_sem.at[piece], (sib, me)).wait_send()
        return carry

    lax.fori_loop(0, count, drain, 0)
    for index in range(len(lefts)):
        left_copy(index).wait_send()
    for index in range(len(rights)):
        right_copy(index).wait_send()


def reduce(groups, blocks, rel_at, lefts, saved, weights, heads, params, table):
    hidden, _, _, _, activated = lefts
    length, columns = activated.shape
    width = columns // 2
    rows = columns // groups
    part = rows // 4
    dtype = activated.dtype
    count = 12
    slots = 4
    ring = 3 if blocks == 1 else 2
    narrow = heads[2].shape
    span = table.shape[0]
    kept = pl.BlockSpec(memory_space=pl.ANY)
    inside = pl.BlockSpec(memory_space=pltpu.VMEM)
    each = pltpu.SemaphoreType.DMA((count,))
    wide = (length, columns)
    rel_shape = (groups, 2, table.shape[1] // 2, 128)
    sums = (16, columns)
    inputs = [*lefts, *saved, *weights, *heads]
    half_got = (ring, groups, part, width // 2)
    two_got = (ring, groups, 2, part, width // 2)
    return pl.pallas_call(
        functools.partial(reduce_kernel, groups, blocks, rel_at),
        out_shape=(
            jax.ShapeDtypeStruct((count, rows, columns), dtype),
            jax.ShapeDtypeStruct(sums, jnp.float32),
            jax.ShapeDtypeStruct(wide, jnp.float32),
            jax.ShapeDtypeStruct(hidden.shape, dtype),
            jax.ShapeDtypeStruct(wide, dtype),
            jax.ShapeDtypeStruct(wide, dtype),
            jax.ShapeDtypeStruct(wide, dtype),
            jax.ShapeDtypeStruct(wide, dtype),
            jax.ShapeDtypeStruct(hidden.shape, dtype),
            jax.ShapeDtypeStruct((4,) + wide, dtype),
            jax.ShapeDtypeStruct((7, length, width), dtype),
        ),
        in_specs=[kept] * len(inputs) + [inside] * 2,
        out_specs=[kept, inside] + [kept] * 9,
        scratch_shapes=[
            pltpu.VMEM((2,) + wide, dtype),
            pltpu.VMEM((2, length, width), dtype),
            pltpu.VMEM((slots, groups, 2, 2, part, width), dtype),
            pltpu.VMEM(two_got, dtype),
            pltpu.VMEM(two_got, dtype),
            pltpu.VMEM(half_got, dtype),
            pltpu.VMEM(half_got, dtype),
            pltpu.VMEM((ring, groups, part, width), dtype),
            pltpu.VMEM((count if blocks > 1 else 1, blocks, part, width), dtype),
            pltpu.VMEM((count, part, width), dtype),
            pltpu.VMEM(rel_shape, dtype),
            pltpu.VMEM(rel_shape, dtype),
            pltpu.VMEM(sums, jnp.float32),
            *([pltpu.SemaphoreType.DMA((5,))] * 2),
            *([pltpu.SemaphoreType.DMA((7,))] * 2),
            *([pltpu.SemaphoreType.DMA((1,))] * 2),
            pltpu.SemaphoreType.DMA((2 + 2 * groups,)),
            *([each] * 8),
            *([pltpu.SemaphoreType.DMA((count, groups))] * 2),
            *([pltpu.SemaphoreType.DMA((count, blocks))] * 2),
            *([each] * 6),
            *sum_scratch(groups, blocks, sums),
            pltpu.SemaphoreType.REGULAR((4,)),
            pltpu.SemaphoreType.REGULAR((groups,)),
            pltpu.VMEM(wide, jnp.float32),
            pltpu.VMEM(wide, jnp.float32),
            pltpu.VMEM(wide, jnp.float32),
            pltpu.VMEM((2, 512, columns), dtype),
            pltpu.VMEM(hidden.shape, dtype),
            pltpu.VMEM(wide, dtype),
            pltpu.VMEM(wide, dtype),
            pltpu.VMEM(wide, dtype),
            *([pltpu.VMEM(narrow, dtype)] * 3),
            pltpu.VMEM((span, narrow[1]), dtype),
            pltpu.VMEM((span, narrow[1]), dtype),
            pltpu.VMEM((2, length, length), dtype),
            pltpu.SemaphoreType.DMA((2,)),
            pltpu.SemaphoreType.DMA((14,)),
            pltpu.SemaphoreType.DMA((2,)),
            pltpu.SemaphoreType.DMA((hidden.shape[1] // 512 + 1,)),
            pltpu.VMEM((groups, 2, 2, part, width), dtype),
            pltpu.VMEM((groups - 1, 2, 2, part, width), dtype),
            pltpu.VMEM((2, 2, part, width // 2), dtype),
            pltpu.VMEM((2, 2, part, width // 2), dtype),
            pltpu.VMEM((2, part, width // 2), dtype),
            pltpu.VMEM((2, part, width // 2), dtype),
            pltpu.SemaphoreType.REGULAR((groups,)),
        ],
        compiler_params=pltpu.CompilerParams(
            collective_id=1, has_side_effects=True, vmem_limit_bytes=VMEM_LIMIT
        ),
        name="reduce",
    )(*inputs, params, table)


EPSILON = 1e-05


def normalize(values):
    centred = values - jnp.mean(values, -1, keepdims=True)
    inverse = lax.rsqrt(jnp.mean(centred * centred, -1, keepdims=True) + EPSILON)
    return (centred * inverse, inverse)


def norm_back(grad_std, standard, inverse):
    return inverse * (
        grad_std
        - jnp.mean(grad_std, -1, keepdims=True)
        - standard * jnp.mean(grad_std * standard, -1, keepdims=True)
    )


def dot_leading(left_side, right_side):
    return lax.dot_general(
        left_side, right_side, (((0,), (0,)), ((), ())), preferred_element_type=jnp.float32
    )


def dot_trailing(left_side, right_side):
    return lax.dot_general(
        left_side, right_side, (((1,), (1,)), ((), ())), preferred_element_type=jnp.float32
    )


def on_device(
    tokens,
    conv_weight,
    query_weight,
    key_weight,
    value_weight,
    out_weight,
    rel_weight,
    up_weight,
    down_weight,
    gains,
    biases,
    up_bias,
    rel_bias,
    target_table,
    clip_levels,
    window_ids,
    clip_index,
):
    groups = lax.axis_size("fsdp")
    blocks = lax.axis_size("dp") // 8
    tap_count, piece_rows, model_width = conv_weight.shape
    half_taps = tap_count // 2
    half_width = model_width // 2
    key_width = query_weight.shape[1]
    rel_rows, rel_columns = rel_weight.shape
    inputs = tokens[0].astype(jnp.float32)
    length = inputs.shape[0]
    token_total = length * lax.axis_size("dp") * lax.axis_size("fsdp")

    small_parts = [gains, biases, up_bias, rel_bias]
    small = jnp.concatenate([part.reshape(-1) for part in small_parts])
    small = jnp.pad(small, (0, -small.shape[0] % 1024)).reshape(-1, 128)
    target_row = lax.dynamic_index_in_dim(target_table, window_ids[0], 0, keepdims=True)
    levels = jnp.arange(clip_levels.shape[0], dtype=jnp.int32)
    selector = (clip_index[0][:, None] == levels[None, :]).astype(jnp.float32)
    limits = jnp.sum(selector * clip_levels[None, :], 1)[:, None]
    limits = jnp.broadcast_to(limits, (length, 128))
    (
        conv_full,
        mixed_full,
        value_full,
        out_full,
        up_full,
        down_full,
        _,
        small_full,
        stats,
        activated,
        after_conv,
        normed_one,
        content_query,
        position_query,
        keys,
        values,
        mirrored_keys,
        probs,
        attended,
        after_attention,
        normed_two,
        hidden_pre,
        hidden,
        outputs,
        cotangent,
        tables,
    ) = gather(
        groups,
        blocks,
        [
            conv_weight,
            query_weight,
            key_weight,
            value_weight,
            out_weight,
            up_weight,
            down_weight,
            rel_weight,
        ],
        small,
        tokens[0],
        target_row,
        limits,
    )
    conv_full = conv_full.reshape(tap_count, model_width, model_width)
    mixed_full = mixed_full.reshape(model_width, -1)
    value_full = value_full.reshape(model_width, -1)
    out_full = out_full.reshape(model_width, -1)
    up_full = up_full.reshape(model_width, -1)
    down_full = down_full.reshape(-1, model_width)
    flat = small_full.reshape(groups, -1)
    taken = 0
    unpacked = []
    for part in small_parts:
        chosen = flat[:, taken : taken + part.size].reshape((groups,) + part.shape)
        unpacked.append(chosen)
        taken += part.size
    gain_rows = jnp.moveaxis(unpacked[0], 0, 1).reshape(gains.shape[0], -1)
    bias_rows = jnp.moveaxis(unpacked[1], 0, 1).reshape(biases.shape[0], -1)
    batch_sums = stats.reshape(2, -1)
    centre = batch_sums[0] / token_total
    variance = batch_sums[1] / token_total - centre * centre
    inverse = lax.rsqrt(variance + EPSILON)
    standard = (inputs - centre) * inverse
    params = jnp.concatenate([gain_rows, bias_rows[:1], centre[None], inverse[None]], 0)
    params = jnp.pad(params, ((0, 2), (0, 0)))
    pieces, sums, part_grad, *_ = reduce(
        groups,
        blocks,
        2 * key_width - half_width,
        [hidden, normed_two, attended, normed_one, activated],
        [cotangent, hidden_pre, after_attention, after_conv, tokens[0]],
        [down_full, up_full, out_full, value_full, mixed_full, conv_full],
        [probs, values, keys, content_query, position_query, mirrored_keys],
        params,
        tables[1],
    )
    input_grad = part_grad - inverse * gain_rows[0] * (
        sums[3] + standard * sums[0]
    ) / token_total
    shard = lax.axis_index("fsdp")
    by_shard = sums[:9].reshape(9, groups, -1)
    by_shard = lax.dynamic_index_in_dim(by_shard, shard, 1, keepdims=False)
    up_sums = sums[9:11].reshape(groups, -1)
    up_sums = lax.dynamic_index_in_dim(up_sums, shard, 0, keepdims=False)
    rel_sums = sums[11, : 2 * key_width].reshape(2, groups, -1)
    rel_sums = lax.dynamic_index_in_dim(rel_sums, shard, 1, keepdims=False)
    up_grad = jnp.concatenate([pieces[1], pieces[2]], 1)
    mixed_sum = pieces[5].astype(jnp.float32)
    rel_at = 2 * key_width
    return (
        outputs[None],
        input_grad.astype(jnp.bfloat16)[None],
        jnp.concatenate([pieces[6:10], pieces[11:12]], 0).astype(jnp.float32),
        mixed_sum[:, :key_width],
        mixed_sum[:, key_width:rel_at],
        pieces[4].astype(jnp.float32),
        pieces[3].astype(jnp.float32),
        mixed_sum[:rel_rows, rel_at : rel_at + rel_columns],
        up_grad.astype(jnp.float32),
        jnp.concatenate([pieces[0], pieces[10]], 0).astype(jnp.float32),
        by_shard[:3],
        by_shard[3:9],
        up_sums,
        rel_sums,
    )


def solution(mesh):
    placed = (
        P(("dp", "fsdp"), None, None),
        P(None, "fsdp", None),
        P("fsdp", None),
        P("fsdp", None),
        P("fsdp", None),
        P("fsdp", None),
        P(None, "fsdp"),
        P("fsdp", None),
        P("fsdp", None),
        P(None, "fsdp"),
        P(None, "fsdp"),
        P("fsdp"),
        P(None, "fsdp"),
        P(),
        P(),
        P(("dp", "fsdp")),
        P(("dp", "fsdp"), None),
    )
    return jax.shard_map(
        on_device,
        mesh=mesh,
        in_specs=placed,
        out_specs=(
            P(("dp", "fsdp"), None, None),
            P(("dp", "fsdp"), None, None),
            P(None, "fsdp", None),
            P("fsdp", None),
            P("fsdp", None),
            P("fsdp", None),
            P("fsdp", None),
            P(None, "fsdp"),
            P("fsdp", None),
            P("fsdp", None),
            P(None, "fsdp"),
            P(None, "fsdp"),
            P("fsdp"),
            P(None, "fsdp"),
        ),
        check_vma=False,
    )
```

```python
import functools
import math

import jax
import jax.numpy as jnp
from jax import lax
from jax.experimental import pallas as pl
from jax.experimental.pallas import tpu as pltpu
from jax.sharding import PartitionSpec as P

HEADS = 8
KEY = 64
MESH = pl.DeviceIdType.MESH
AHEAD = 2
GELU = 0.7978845608028654
VMEM_LIMIT = 62 << 20


def neighbours(dp):
    core = dp % 2
    along_x = dp // 2 % 2
    along_y = dp // 4 % 2
    return dp + 1 - 2 * core, dp + 2 - 4 * along_x, dp + 4 - 8 * along_y


def remote(src, dst, send_sem, recv_sem, device):
    return pltpu.make_async_remote_copy(
        src_ref=src,
        dst_ref=dst,
        send_sem=send_sem,
        recv_sem=recv_sem,
        device_id=device,
        device_id_type=MESH,
    )


def meet(peers):
    barrier = pltpu.get_barrier_semaphore()
    for peer in peers:
        pl.semaphore_signal(barrier, inc=1, device_id=peer, device_id_type=MESH)
    pl.semaphore_wait(barrier, len(peers))


def peers_of(groups, blocks):
    dp = lax.axis_index("dp")
    me = lax.axis_index("fsdp")
    near = [(device, me) for device in neighbours(dp)]
    shards = [(dp, (me + 1 + j) % groups) for j in range(groups - 1)]
    far = [((dp + 8 * (1 + j)) % (8 * blocks), me) for j in range(blocks - 1)]
    return near, shards, far


def sum_steps(groups, blocks, vector, total, near_got, sums, shard_got, block_got, sems):
    near_send, near_recv, shard_send, shard_recv, block_send, block_recv = sems
    me = lax.axis_index("fsdp")
    block = lax.axis_index("dp") // 8
    near, shards, far = peers_of(groups, blocks)

    def near_copy(step):
        src = vector if step == 0 else sums.at[step - 1]
        return remote(
            src, near_got.at[step], near_send.at[step], near_recv.at[step], near[step]
        )

    def fold(step):
        copy = near_copy(step)
        copy.wait()
        held = vector[...] if step == 0 else sums[step - 1]
        sums[step] = held + near_got[step]

    def shard_copy(j):
        return remote(
            sums.at[2], shard_got.at[me], shard_send.at[j], shard_recv.at[me], shards[j]
        )

    def block_copy(j):
        return remote(
            sums.at[3], block_got.at[block], block_send.at[j], block_recv.at[block], far[j]
        )

    def start():
        near_copy(0).start()

    def second():
        fold(0)
        near_copy(1).start()

    def third():
        fold(1)
        near_copy(2).start()

    def fourth():
        fold(2)
        for j in range(groups - 1):
            shard_copy(j).start()
        shard_got[me] = sums[2]

    def fifth():
        for j in range(groups - 1):
            shard_copy(j).wait_send()
            other = (me + 1 + j) % groups
            remote(
                sums.at[2], shard_got.at[other], shard_send.at[j], shard_recv.at[other], shards[j]
            ).wait_recv()
        added = shard_got[0]
        for shard in range(1, groups):
            added = added + shard_got[shard]
        sums[3] = added
        for j in range(blocks - 1):
            block_copy(j).start()
        block_got[block] = added

    def sixth():
        for j in range(blocks - 1):
            block_copy(j).wait_send()
            other = (block + 1 + j) % blocks
            remote(
                sums.at[3], block_got.at[other], block_send.at[j], block_recv.at[other], far[j]
            ).wait_recv()
        added = block_got[0]
        for other in range(1, blocks):
            added = added + block_got[other]
        total[...] = added

    return [start, second, third, fourth, fifth, sixth]


def sum_scratch(groups, blocks, shape):
    return [
        pltpu.VMEM((3,) + shape, jnp.float32),
        pltpu.VMEM((4,) + shape, jnp.float32),
        pltpu.VMEM((groups,) + shape, jnp.float32),
        pltpu.VMEM((blocks,) + shape, jnp.float32),
        pltpu.SemaphoreType.DMA((3,)),
        pltpu.SemaphoreType.DMA((3,)),
        pltpu.SemaphoreType.DMA((groups,)),
        pltpu.SemaphoreType.DMA((groups,)),
        pltpu.SemaphoreType.DMA((blocks,)),
        pltpu.SemaphoreType.DMA((blocks,)),
    ]


def gather_kernel(groups, blocks, *refs):
    weights = refs[:8]
    conv, query, key, value, out, up, down, rel = weights
    small, inputs, target, limits = refs[8:12]
    outs = refs[12:21]
    conv_out, mixed_out, value_out, out_out, up_out, down_out = outs[:6]
    rel_full, small_full, stat_total = outs[6:]
    results = list(refs[21:37])
    pre_out = results.pop(12)
    hidden_out = results.pop(12)
    results[12:12] = [
        hidden_out.at[:, pl.ds(side * conv.shape[2], conv.shape[2])] for side in range(2)
    ]
    tables, params = refs[37:39]
    refs = refs[39:]
    hold, hold_mixed, local_sem, write_sem = refs[:4]
    z_sem, x_sem, y_sem, d_sem, sib_sem, send_sem, right_send, left_send = refs[4:12]
    rel_send, rel_recv, small_send, small_recv = refs[12:16]
    near_got, sums, shard_got, block_got = refs[16:20]
    sum_sems = refs[20:26]
    weight_hold, weight_sem, result_sem = refs[26:29]
    shifted_ref, total_ref = refs[29:31]
    act_ref, norm_ref, content_ref, position_ref, key_ref, value_ref = refs[31:37]
    table_ref, probs_ref, attended_ref = refs[37:40]
    stats, loss_ref, part_sem, part_right, part_left = refs[40:45]
    dp = lax.axis_index("dp")
    me = lax.axis_index("fsdp")
    near, shards, far = peers_of(groups, blocks)
    sib, along_x, along_y = neighbours(dp)
    rows = conv.shape[1]
    part = rows // 8
    others = groups - 1
    columns = conv.shape[2]
    pieces = [conv_out.at[tap] for tap in range(5)] + [mixed_out, value_out, out_out]
    pieces += [up_out.at[:, :, pl.ds(half * columns, columns)] for half in range(2)]
    pieces += [down_out.at[:, pl.ds(half * rows, rows)] for half in range(2)]
    count = len(pieces)
    holds = [hold.at[i] for i in range(5)] + [hold_mixed] + [hold.at[i] for i in range(5, 11)]

    pending = [[] for _ in range(count)]
    started = [0]

    def load(src, dst, piece):
        copy = pltpu.make_async_copy(src, dst, local_sem.at[started[0]])
        copy.start()
        started[0] += 1
        pending[piece].append(copy)

    for tap in range(5):
        load(conv.at[tap], holds[tap], tap)
    width = query.shape[1]
    load(query, hold_mixed.at[:, pl.ds(0, width)], 5)
    load(key, hold_mixed.at[:, pl.ds(width, width)], 5)
    load(value, holds[6], 6)
    load(out, holds[7], 7)
    for half in range(2):
        load(up.at[:, pl.ds(half * columns, columns)], holds[8 + half], 8 + half)
    for half in range(2):
        load(down.at[pl.ds(half * rows, rows)], holds[10 + half], 10 + half)

    meet(near + shards + far)

    summing = sum_steps(
        groups, blocks, stats, stat_total, near_got, sums, shard_got, block_got, sum_sems
    )
    for j in range(others):
        remote(
            rel, rel_full.at[me], rel_send.at[j], rel_recv.at[me], shards[j]
        ).start()
        remote(
            small, small_full.at[me], small_send.at[j], small_recv.at[me], shards[j]
        ).start()
    rel_full[me] = rel[...]
    small_full[me] = small[...]

    def slice_of(piece, shard, owner):
        return pieces[piece].at[shard, pl.ds(pl.multiple_of(owner % 8 * part, 16), part)]

    def copy_of(piece, shard, owner, recv_sem, device):
        ref = slice_of(piece, shard, owner)
        return remote(ref, ref, send_sem.at[piece], recv_sem, (device, me))

    order = []
    for j in range(others):
        pick = 0
        for m in range(groups):
            nearest = sorted((t for t in range(groups) if t != m), key=lambda t: abs(t - m))
            pick = pick + jnp.where(me == m, nearest[j], 0)
        order.append(pick)

    def right_copy(piece, shard, src=None):
        dst = slice_of(piece, shard, dp)
        return remote(
            dst if src is None else src,
            dst,
            right_send.at[piece, shard],
            z_sem.at[piece, shard],
            (dp, (me + 1) % groups),
        )

    def left_copy(piece, shard, src=None):
        dst = slice_of(piece, shard, dp)
        return remote(
            dst if src is None else src,
            dst,
            left_send.at[piece, shard],
            z_sem.at[piece, shard],
            (dp, (me + groups - 1) % groups),
        )

    alone = count - 2
    waves = [piece for piece in range(count) if piece != alone]
    wave_count = len(waves)

    def part_copy(step, shard, device, sems, src=None):
        dst = slice_of(alone, shard, 2 * step + dp % 2)
        return remote(
            dst if src is None else src,
            dst,
            sems.at[step, shard],
            part_sem.at[step, shard],
            (dp, device),
        )

    def part_send(step):
        at = pl.ds(pl.multiple_of((2 * step + dp % 2) * part, 16), part)
        src = holds[alone].at[at]

        @pl.when(me + 1 < groups)
        def _():
            part_copy(step, me, (me + 1) % groups, part_right, src).start()

        @pl.when(me > 0)
        def _():
            part_copy(step, me, (me + groups - 1) % groups, part_left, src).start()

    def part_stage(step, shard):
        part_copy(step, shard, me, part_right).wait_recv()

        @pl.when(jnp.logical_and(shard < me, me + 1 < groups))
        def _():
            part_copy(step, shard, (me + 1) % groups, part_right).start()

        @pl.when(jnp.logical_and(shard > me, me > 0))
        def _():
            part_copy(step, shard, (me + groups - 1) % groups, part_left).start()

        ref = slice_of(alone, shard, 2 * step + dp % 2)
        remote(ref, ref, send_sem.at[alone], sib_sem.at[alone], (sib, me)).start()

    def z_send(piece):
        src = holds[piece].at[pl.ds(pl.multiple_of(dp % 8 * part, 16), part)]

        @pl.when(me + 1 < groups)
        def _():
            right_copy(piece, me, src).start()

        @pl.when(me > 0)
        def _():
            left_copy(piece, me, src).start()

    diagonal = neighbours(along_x)[2]

    def stage_a(piece, shards_now):
        for shard in shards_now:
            copy_of(piece, shard, dp, z_sem.at[piece, shard], dp).wait_recv()

            @pl.when(jnp.logical_and(shard < me, me + 1 < groups))
            def _():
                right_copy(piece, shard).start()

            @pl.when(jnp.logical_and(shard > me, me > 0))
            def _():
                left_copy(piece, shard).start()

            copy_of(piece, shard, dp, x_sem.at[piece, shard], along_x).start()
            copy_of(piece, shard, dp, y_sem.at[piece, shard], along_y).start()
            copy_of(piece, shard, dp, sib_sem.at[piece], sib).start()

    def stage_b(piece, shards_now):
        for shard in shards_now:
            route = (piece + shard) % 2
            copy_of(piece, shard, along_x, x_sem.at[piece, shard], dp).wait_recv()
            copy_of(piece, shard, along_y, y_sem.at[piece, shard], dp).wait_recv()
            owner = route * along_x + (1 - route) * along_y
            target = route * along_y + (1 - route) * along_x
            copy_of(piece, shard, owner, d_sem.at[piece, shard], target).start()
            copy_of(piece, shard, along_x, sib_sem.at[piece], sib).start()
            copy_of(piece, shard, along_y, sib_sem.at[piece], sib).start()

    def stage_c(piece, shards_now):
        for shard in shards_now:
            copy_of(piece, shard, diagonal, d_sem.at[piece, shard], dp).wait_recv()
            copy_of(piece, shard, diagonal, sib_sem.at[piece], sib).start()

    writes = []
    for piece in range(count):
        for copy in pending[piece]:
            copy.wait()
        copy = pltpu.make_async_copy(holds[piece], pieces[piece].at[me], write_sem.at[piece])
        copy.start()
        writes.append(copy)
        if piece < AHEAD:
            z_send(piece)

    def complete(piece):
        writes[piece].wait()
        got = pieces[piece].at[pl.ds(0, others), pl.ds(0, 4 * part)]
        remote(got, got, send_sem.at[piece], sib_sem.at[piece], (sib, me)).wait_recv()

    def weight_loads(piece):
        width = pieces[piece].shape[2]
        return [
            pltpu.make_async_copy(
                pieces[piece].at[shard],
                weight_hold.at[piece % 2, pl.ds(shard * rows, rows), pl.ds(0, width)],
                weight_sem.at[piece % 2, shard],
            )
            for shard in range(groups)
        ]

    def start_weight(piece):
        for copy in weight_loads(piece):
            copy.start()

    def wait_weight(piece):
        for copy in weight_loads(piece):
            copy.wait()

    def wait_smalls():
        for j in range(others):
            shard = (me + 1 + j) % groups
            remote(
                rel, rel_full.at[shard], rel_send.at[j], rel_recv.at[shard], shards[j]
            ).wait()
            remote(
                small, small_full.at[shard], small_send.at[j], small_recv.at[shard], shards[j]
            ).wait()

    length = inputs.shape[0]
    block_rows = 128
    tile = 256
    per_row = rows // 128
    token_total = length * 8 * blocks * groups

    def by_rows(fn):
        def row_body(i, carry):
            fn(pl.ds(pl.multiple_of(i * block_rows, block_rows), block_rows))
            return carry

        lax.fori_loop(0, length // block_rows, row_body, 0)

    def local_sums():
        stats[...] = jnp.zeros_like(stats)
        lanes = columns // 128

        def rows_fn(at):
            value = inputs[at, :].astype(jnp.float32)
            total = jnp.sum(value, 0, keepdims=True)
            square = jnp.sum(value * value, 0, keepdims=True)
            for j in range(lanes):
                stats[j : j + 1, :] += total[:, j * 128 : (j + 1) * 128]
                stats[lanes + j : lanes + j + 1, :] += square[:, j * 128 : (j + 1) * 128]

        by_rows(rows_fn)

    def unpack():
        for row in range(9):
            for shard in range(groups):
                for j in range(per_row):
                    at = shard * rows + j * 128
                    source = row * per_row + j
                    params[row : row + 1, at : at + 128] = small_full[
                        shard, source : source + 1, :
                    ]
        lanes = columns // 128
        for j in range(lanes):
            centre = stat_total[j : j + 1, :] / token_total
            square = stat_total[lanes + j : lanes + j + 1, :] / token_total
            params[9:10, j * 128 : (j + 1) * 128] = centre
            params[10:11, j * 128 : (j + 1) * 128] = lax.rsqrt(
                square - centre * centre + EPSILON
            )
        for shard in range(groups):
            for j in range(2 * per_row):
                source = 9 * per_row + j
                at = (shard * 2 * per_row + j) * 128
                params[13 + at // columns : 14 + at // columns, at % columns : at % columns + 128] = (
                    small_full[shard, source : source + 1, :]
                )
        taken = (9 * rows + 2 * rows) // 128
        for side in range(2):
            for shard in range(groups):
                params[11 + side : 12 + side, shard * 128 : (shard + 1) * 128] = small_full[
                    shard, taken + side : taken + side + 1, :
                ]

    def activate():
        def rows_fn(at):
            standard = (inputs[at, :].astype(jnp.float32) - params[9:10, :]) * params[10:11, :]
            act_ref[at, :] = jax.nn.gelu(standard * params[0:1, :] + params[3:4, :]).astype(
                act_ref.dtype
            )

        by_rows(rows_fn)

    result_of = [
        act_ref,
        total_ref,
        norm_ref,
        content_ref,
        position_ref,
        key_ref,
        value_ref,
        table_ref.at[1],
        probs_ref,
        attended_ref,
        total_ref,
        norm_ref,
        shifted_ref,
        act_ref,
        attended_ref,
        norm_ref,
    ]

    def write_result(index):
        return pltpu.make_async_copy(result_of[index], results[index], result_sem.at[index])

    def write_pre(half):
        at = pl.ds(half * columns, columns)
        return pltpu.make_async_copy(loss_ref, pre_out.at[:, at], result_sem.at[16 + half])

    def shift_tap(tap):
        move = tap - 2

        def column_body(i, carry):
            at = pl.ds(pl.multiple_of(i * rows, 128), rows)
            value = act_ref[:, at].astype(jnp.float32)
            value = pltpu.roll(value, -move % length, 0)
            row = lax.broadcasted_iota(jnp.int32, value.shape, 0)
            inside = row < length - move if move > 0 else row >= -move
            shifted_ref[:, at] = jnp.where(inside, value, 0.0).astype(shifted_ref.dtype)
            return carry

        lax.fori_loop(0, columns // rows, column_body, 0)

    def conv_tap(tap, i):
        at = pl.ds(pl.multiple_of(i * tile, 128), tile)
        left = act_ref if tap == 2 else shifted_ref
        value = jnp.dot(
            left[...], weight_hold[tap % 2, :, at], preferred_element_type=jnp.float32
        )
        if tap == 0:
            value = value + (inputs[:, at].astype(jnp.float32) + params[4:5, at])
        else:
            value = value + total_ref[:, at]
        total_ref[:, at] = value

    def norm_step(gain, bias):
        def rows_fn(at):
            standard, _ = normalize(total_ref[at, :])
            norm_ref[at, :] = (
                standard * params[gain : gain + 1, :] + params[bias : bias + 1, :]
            ).astype(norm_ref.dtype)

        by_rows(rows_fn)

    def query_step():
        raw = jnp.dot(
            norm_ref[...], weight_hold[1, :, 0:width], preferred_element_type=jnp.float32
        )
        raw = raw * KEY**-0.5
        content_ref[...] = (raw + params[11:12, 0:width]).astype(content_ref.dtype)
        position_ref[...] = (raw + params[12:13, 0:width]).astype(position_ref.dtype)

    def key_step():
        key_ref[...] = jnp.dot(
            norm_ref[...], weight_hold[1, :, width : 2 * width], preferred_element_type=jnp.float32
        ).astype(key_ref.dtype)

    def table_step():
        for side in range(2):
            for shard in range(groups):
                table_ref[side, :, shard * 128 : (shard + 1) * 128] = jnp.dot(
                    tables[side], rel_full[shard], preferred_element_type=jnp.float32
                ).astype(table_ref.dtype)

    def value_step(i):
        at = pl.ds(pl.multiple_of(i * tile, 128), tile)
        value_ref[:, at] = jnp.dot(
            norm_ref[...], weight_hold[0, :, at], preferred_element_type=jnp.float32
        ).astype(value_ref.dtype)

    def head_step(index, side):
        head_value = columns // HEADS
        span = tables.shape[1]
        pair = pl.ds(pl.multiple_of(index * 2 * KEY, 128), 2 * KEY)
        value_pair = pl.ds(pl.multiple_of(index * 2 * head_value, 128), 2 * head_value)
        keys = slice(side * KEY, (side + 1) * KEY)
        band = dot_trailing(position_ref[:, pair][:, keys], table_ref[0, :, pair][:, keys])
        moved = pltpu.roll(band, span - length + 1, 1, stride=1, stride_axis=0)
        scores = dot_trailing(content_ref[:, pair][:, keys], key_ref[:, pair][:, keys])
        scores = scores + moved[:, :length]
        weight = jnp.exp(scores - jnp.max(scores, -1, keepdims=True))
        probs = (weight / jnp.sum(weight, -1, keepdims=True)).astype(probs_ref.dtype)
        probs_ref[2 * index + side] = probs
        chosen = value_ref[:, value_pair][:, side * head_value : (side + 1) * head_value]
        return jnp.dot(probs, chosen, preferred_element_type=jnp.float32)

    def pair_step(index):
        both = [head_step(index, side).astype(attended_ref.dtype) for side in range(2)]
        wide = 2 * columns // HEADS
        attended_ref[:, pl.ds(pl.multiple_of(index * wide, 128), wide)] = jnp.concatenate(both, 1)

    def out_step(i):
        at = pl.ds(pl.multiple_of(i * tile, 128), tile)
        value = jnp.dot(
            attended_ref[...], weight_hold[1, :, at], preferred_element_type=jnp.float32
        )
        total_ref[:, at] = total_ref[:, at] + value + params[6:7, at]

    def make_tables():
        features = rel.shape[0]
        basis = features // 6
        span = tables.shape[1]
        row = lax.broadcasted_iota(jnp.int32, (span, features), 0)
        column = lax.broadcasted_iota(jnp.int32, (span, features), 1)
        offset = row - (length - 1)
        whole = jnp.abs(offset)
        distance = whole.astype(jnp.float32)
        order_at = column % basis
        index = order_at.astype(jnp.float32)
        ratio = index / (basis - 1)
        half_life = jnp.exp2(3.0 + (math.log2(length) - 3.0) * ratio)
        decaying = jnp.exp(-math.log(2.0) / half_life * distance)
        limit = lax.shift_left(jnp.ones_like(order_at), jnp.minimum(order_at + 1, 16)) - 1
        central = jnp.where(limit > whole, 1.0, 0.0)
        stddev = length / (2.0 * basis)
        centres = length / basis + (length - length / basis) * ratio
        shape_par = (centres / stddev) * (centres / stddev)
        rate_par = centres / (stddev * stddev)
        safe = jnp.maximum(distance, 1.0)
        score = (shape_par - 1.0) * jnp.log(safe) - rate_par * safe
        peak = jnp.max(jnp.where(whole < length, score, -jnp.inf), 0, keepdims=True)
        gamma = jnp.where(whole > 0, jnp.exp(score - peak), 0.0)
        kind = column // basis % 3
        value = jnp.where(kind == 0, decaying, jnp.where(kind == 1, central, gamma))
        value = jnp.where(whole < length, value, 0.0)
        flipped = column >= 3 * basis
        for side in range(2):
            signed = offset if side == 0 else -offset
            sign = jnp.where(signed > 0, 1.0, jnp.where(signed < 0, -1.0, 0.0))
            tables[side] = jnp.where(flipped, value * sign, value).astype(tables.dtype)

    halves = [shifted_ref, act_ref]

    def up_step(half, i):
        at = pl.ds(pl.multiple_of(i * tile, 128), tile)
        value = jnp.dot(
            norm_ref[...], weight_hold[half, :, at], preferred_element_type=jnp.float32
        )
        value = value + params[13 + half : 14 + half, at]
        loss_ref[:, at] = value
        halves[half][:, at] = jax.nn.gelu(value).astype(act_ref.dtype)

    def down_step(half, i):
        at = pl.ds(pl.multiple_of(i * tile, 128), tile)
        value = total_ref[:, at]
        for shard in range(groups):
            source = (2 * shard + half) * rows
            left = halves[source // columns][:, source % columns : source % columns + rows]
            value = value + jnp.dot(
                left,
                weight_hold[half, shard * rows : (shard + 1) * rows, at],
                preferred_element_type=jnp.float32,
            )
        if half == 0:
            total_ref[:, at] = value + params[8:9, at]
        else:
            attended_ref[:, at] = value.astype(attended_ref.dtype)
            limit = limits[:, 0:1]
            norm_ref[:, at] = jnp.clip(value - target[0:1, at], -limit, limit).astype(
                norm_ref.dtype
            )

    def over_tiles(fn):
        def tile_body(i, carry):
            fn(i)
            return carry

        lax.fori_loop(0, columns // tile, tile_body, 0)

    def over_pairs(first):
        def pair_body(i, carry):
            pair_step(i)
            return carry

        lax.fori_loop(first, first + 2, pair_body, 0)


    def compute_list(n):
        if n == 2:
            return [wait_smalls, unpack, activate, make_tables, lambda: write_result(0).start()]
        piece = n - 3
        if 0 <= piece < 5:
            work = [functools.partial(wait_weight, piece)]
            if piece != 2:
                work.append(functools.partial(shift_tap, piece))
            work += [functools.partial(over_tiles, functools.partial(conv_tap, piece))]
            return work
        if piece == 5:
            return [
                lambda: write_result(1).start(),
                functools.partial(norm_step, 1, 5),
                lambda: write_result(2).start(),
                table_step,
                lambda: write_result(7).start(),
                functools.partial(wait_weight, piece),
                query_step,
                key_step,
                lambda: [write_result(i).start() for i in (3, 4, 5)],
            ]
        if piece == 6:
            work = [functools.partial(wait_weight, piece)]
            work += [functools.partial(over_tiles, value_step)]
            return work + [lambda: write_result(6).start(), functools.partial(over_pairs, 0)]
        if piece == 7:
            work = [functools.partial(over_pairs, 2)]
            work += [lambda: [write_result(i).start() for i in (8, 9)]]
            work += [functools.partial(wait_weight, piece), lambda: write_result(1).wait()]
            work += [functools.partial(over_tiles, out_step)]
            work += [lambda: write_result(10).start(), lambda: write_result(2).wait()]
            return work + [
                functools.partial(norm_step, 2, 7),
                lambda: write_result(11).start(),
                lambda: write_result(0).wait(),
            ]
        if piece in (8, 9):
            half = piece - 8
            work = [functools.partial(wait_weight, piece)]
            if half == 1:
                work.append(lambda: write_pre(0).wait())
            work += [functools.partial(over_tiles, functools.partial(up_step, half))]
            work.append(lambda: [write_pre(half).start(), write_result(12 + half).start()])
            return work
        if piece in (10, 11):
            half = piece - 10
            work = [functools.partial(wait_weight, piece)]
            if half == 0:
                work.append(lambda: write_result(10).wait())
            else:
                work.append(lambda: [write_result(i).wait() for i in (9, 11)])
            work += [functools.partial(over_tiles, functools.partial(down_step, half))]
            if half == 1:
                work.append(lambda: [write_result(i).start() for i in (14, 15)])
            return work
        return []

    def send_list(n):
        work = []
        if n + AHEAD < wave_count:
            work.append(functools.partial(z_send, waves[n + AHEAD]))
        if n in (0, 2, 4, 6):
            work.append(functools.partial(part_send, n // 2))
        for shard in order:
            if n < wave_count:
                work.append(functools.partial(stage_a, waves[n], [shard]))
            if 1 <= n <= wave_count:
                work.append(functools.partial(stage_b, waves[n - 1], [shard]))
            if 2 <= n < wave_count + 2:
                work.append(functools.partial(stage_c, waves[n - 2], [shard]))
            if n in (2, 4, 6, 8):
                work.append(functools.partial(part_stage, n // 2 - 1, shard))
        return work

    local_sums()
    for step in summing[:4]:
        step()

    for n in range(count):
        sends = send_list(n)
        work = compute_list(n)
        if 0 <= n - 3 < wave_count - 2:
            complete(waves[n - 3])
            start_weight(waves[n - 3])
        slots = max(len(work), 1)
        for i in range(slots):
            for send in sends[len(sends) * i // slots : len(sends) * (i + 1) // slots]:
                send()
            if i < len(work):
                work[i]()
        if n < 2:
            summing[4 + n]()
    for piece in (alone - 1, alone):
        complete(piece)
        start_weight(piece)
    for work in compute_list(alone + 2) + send_list(count) + compute_list(alone + 3):
        work()
    complete(count - 1)
    start_weight(count - 1)
    for work in compute_list(count + 2):
        work()

    for index in (3, 4, 5, 6, 7, 8, 12, 13, 14, 15):
        write_result(index).wait()
    write_pre(1).wait()

    for step in range(4):
        for shard in range(groups):

            @pl.when(jnp.logical_and(shard <= me, me + 1 < groups))
            def _():
                part_copy(step, shard, (me + 1) % groups, part_right).wait_send()

            @pl.when(jnp.logical_and(shard >= me, me > 0))
            def _():
                part_copy(step, shard, (me + groups - 1) % groups, part_left).wait_send()

    sent = pieces[alone].at[pl.ds(0, others), pl.ds(0, 4 * part)]
    remote(sent, sent, send_sem.at[alone], sib_sem.at[alone], (sib, me)).wait_send()
    for piece in waves:
        for shard in range(groups):

            @pl.when(jnp.logical_and(shard <= me, me + 1 < groups))
            def _():
                right_copy(piece, shard).wait_send()

            @pl.when(jnp.logical_and(shard >= me, me > 0))
            def _():
                left_copy(piece, shard).wait_send()

        sent = pieces[piece].at[pl.ds(0, others), pl.ds(0, 7 * part)]
        remote(sent, sent, send_sem.at[piece], sib_sem.at[piece], (sib, me)).wait_send()


def gather(groups, blocks, weights, small, inputs, target, limits):
    conv, query = weights[:2]
    rel = weights[7]
    taps, rows, columns = conv.shape
    width = query.shape[1]
    length = inputs.shape[0]
    span = 2 * length
    stats_shape = (2 * columns // 128, 128)
    dtype = conv.dtype
    kept = pl.BlockSpec(memory_space=pl.ANY)
    inside = pl.BlockSpec(memory_space=pltpu.VMEM)
    full = jax.ShapeDtypeStruct((groups, rows, columns), dtype)
    count = taps + 7
    grid_sems = [pltpu.SemaphoreType.DMA((count, groups))] * 4
    wide = (length, columns)
    narrow = (length, width)
    made = [
        jax.ShapeDtypeStruct(wide, dtype),
        jax.ShapeDtypeStruct(wide, jnp.float32),
        jax.ShapeDtypeStruct(wide, dtype),
        jax.ShapeDtypeStruct(narrow, dtype),
        jax.ShapeDtypeStruct(narrow, dtype),
        jax.ShapeDtypeStruct(narrow, dtype),
        jax.ShapeDtypeStruct(wide, dtype),
        jax.ShapeDtypeStruct((span, width), dtype),
        jax.ShapeDtypeStruct((HEADS, length, length), dtype),
        jax.ShapeDtypeStruct(wide, dtype),
        jax.ShapeDtypeStruct(wide, jnp.float32),
        jax.ShapeDtypeStruct(wide, dtype),
        jax.ShapeDtypeStruct((length, 2 * columns), jnp.float32),
        jax.ShapeDtypeStruct((length, 2 * columns), dtype),
        jax.ShapeDtypeStruct(wide, dtype),
        jax.ShapeDtypeStruct(wide, dtype),
    ]
    return pl.pallas_call(
        functools.partial(gather_kernel, groups, blocks),
        out_shape=(
            jax.ShapeDtypeStruct((taps, groups, rows, columns), dtype),
            jax.ShapeDtypeStruct((groups, rows, 2 * width), dtype),
            full,
            full,
            jax.ShapeDtypeStruct((groups, rows, 2 * columns), dtype),
            jax.ShapeDtypeStruct((groups, 2 * rows, columns), dtype),
            jax.ShapeDtypeStruct((groups,) + rel.shape, dtype),
            jax.ShapeDtypeStruct((groups,) + small.shape, jnp.float32),
            jax.ShapeDtypeStruct(stats_shape, jnp.float32),
            *made,
            jax.ShapeDtypeStruct((2, span, rel.shape[0]), dtype),
            jax.ShapeDtypeStruct((16, columns), jnp.float32),
        ),
        in_specs=[kept] * 7 + [inside] * 5,
        out_specs=[kept] * 6 + [inside] * 3 + [kept] * len(made) + [inside] * 2,
        scratch_shapes=[
            pltpu.VMEM((count - 1, rows, columns), dtype),
            pltpu.VMEM((rows, 2 * width), dtype),
            pltpu.SemaphoreType.DMA((taps + 8,)),
            pltpu.SemaphoreType.DMA((count,)),
            *grid_sems,
            pltpu.SemaphoreType.DMA((count,)),
            pltpu.SemaphoreType.DMA((count,)),
            *grid_sems[:2],
            *([pltpu.SemaphoreType.DMA((groups,))] * 4),
            *sum_scratch(groups, blocks, stats_shape),
            pltpu.VMEM((2, columns, columns), dtype),
            pltpu.SemaphoreType.DMA((2, groups)),
            pltpu.SemaphoreType.DMA((len(made) + 2,)),
            pltpu.VMEM(wide, dtype),
            pltpu.VMEM(wide, jnp.float32),
            pltpu.VMEM(wide, dtype),
            pltpu.VMEM(wide, dtype),
            pltpu.VMEM(narrow, dtype),
            pltpu.VMEM(narrow, dtype),
            pltpu.VMEM(narrow, dtype),
            pltpu.VMEM(wide, dtype),
            pltpu.VMEM((2, span, width), dtype),
            pltpu.VMEM((HEADS, length, length), dtype),
            pltpu.VMEM(wide, dtype),
            pltpu.VMEM(stats_shape, jnp.float32),
            pltpu.VMEM(wide, jnp.float32),
            *([pltpu.SemaphoreType.DMA((4, groups))] * 3),
        ],
        compiler_params=pltpu.CompilerParams(
            collective_id=0, has_side_effects=True, vmem_limit_bytes=60 << 20
        ),
        name="gather",
    )(*weights, small, inputs, target, limits)


def gelu_slope(value):
    inner = GELU * (value + 0.044715 * value * value * value)
    curve = jnp.tanh(inner)
    slope = GELU * (1.0 + 3 * 0.044715 * value * value)
    return 0.5 * (1.0 + curve) + 0.5 * value * (1.0 - curve * curve) * slope


def reduce_kernel(groups, blocks, rel_at, *refs):
    lefts = refs[:5]
    cotangent, hidden_pre, after_attention, after_conv, tokens = refs[5:10]
    down_full, up_full, out_full, value_full, mixed_full, conv_full = refs[10:16]
    probs, values, keys, contents, positions, mirrored_keys = refs[16:22]
    params, table = refs[22:24]
    out, total, part_grad = refs[24:27]
    made = refs[27:32]
    hidden_got, left_got, right_got = refs[32:35]
    rights = [cotangent, *made]
    (
        left_hold,
        right_hold,
        grad,
        x_one,
        y_one,
        x_two,
        y_two,
        shard_got,
        block_got,
        done,
        rel_grad,
        rel_got,
        vector,
    ) = refs[35:48]
    left_send, left_recv, right_send, right_recv, rel_send, rel_recv = refs[48:54]
    load_sem = refs[54]
    x1s, y1s, x2s, y2s, x1r, y1r, x2r, y2r = refs[55:63]
    shard_send, shard_recv, block_send, block_recv = refs[63:67]
    write_sem, send_sem, ax, ay, ad, sib_sem = refs[67:73]
    sum_bufs = refs[73:77]
    sum_sems = refs[77:83]
    credit, shard_credit = refs[83:85]
    (
        attn_grad,
        total_ref,
        kept_ref,
        weight_hold,
        wide_hold,
        right_ref,
        value_grad_ref,
        mixed_ref,
        key_ref,
        content_ref,
        position_ref,
        table_ref,
        table_grad_ref,
        probs_ref,
    ) = refs[85:99]
    tile_sem, host_sem, probs_sem, kept_sem = refs[99:103]
    slab, slab_got, x_slab, y_slab, x_part, y_part, slab_credit = refs[103:110]

    dp = lax.axis_index("dp")
    me = lax.axis_index("fsdp")
    near, shards, far = peers_of(groups, blocks)
    sib, along_x, along_y = neighbours(dp)
    core = dp % 2
    at_x = dp // 2 % 2
    at_y = dp // 4 % 2
    block = dp // 8
    slots = grad.shape[0]
    part = grad.shape[4]
    width = grad.shape[5]
    half = width // 2
    rows = 4 * part
    count = out.shape[0]
    others = groups - 1
    first = pl.ds(0, half)
    last = pl.ds(half, half)
    taps = 5
    up_right = rights[1]
    rights[1:2] = [up_right.at[:, pl.ds(side * 2 * width, 2 * width)] for side in range(2)]
    lefts_got = [hidden_got] + [left_got.at[index] for index in range(4)]
    left_of = [0, 1, 1, 2, 3, 3, 4, 4, 4, 4, 0, 4]
    right_of = [0, 1, 2, 3, 4, 5, 6, 6, 6, 6, 0, 6]
    sequence = [0, 10, 1, 2, 3, 4, 5, 6, 11, 7, 8, 9]
    tap_of = {6: 0, 7: 1, 8: 2, 9: 3, 11: 4}
    mixed_piece = 5
    normal = 10
    extra_at = {0: 10, 6: 11}
    own_columns = pl.ds(pl.multiple_of(core * width, 128), width)
    sib_columns = pl.ds(pl.multiple_of((1 - core) * width, 128), width)

    def left_copy(index):
        return remote(
            lefts[index], lefts_got[index], left_send.at[index], left_recv.at[index], (sib, me)
        )

    def right_copy(index):
        return remote(
            rights[index].at[:, sib_columns],
            right_got.at[index],
            right_send.at[index],
            right_recv.at[index],
            (sib, me),
        )

    def rel_copy():
        return remote(rel_grad, rel_got, rel_send.at[0], rel_recv.at[0], (sib, me))

    def loads(piece):
        left = left_of[piece]
        right = right_of[piece]
        pairs = [
            (rights[right].at[:, own_columns], right_hold.at[0]),
            (right_got.at[right], right_hold.at[1]),
        ]
        if left > 0:
            pairs.append((lefts[left], left_hold.at[0]))
            pairs.append((lefts_got[left], left_hold.at[1]))
        else:
            for shard in range(groups):
                source = pl.ds((2 * shard + piece // normal) * rows, rows)
                target = pl.ds(shard * rows, rows)
                pairs.append((lefts[left].at[:, source], left_hold.at[0, :, target]))
                pairs.append((lefts_got[left].at[:, source], left_hold.at[1, :, target]))
        return [
            pltpu.make_async_copy(src, dst, load_sem.at[i]) for i, (src, dst) in enumerate(pairs)
        ]

    def start_loads(piece):
        before = sequence[: sequence.index(piece)]
        if left_of[piece] not in [left_of[other] for other in before]:
            left_copy(left_of[piece]).wait_recv()
        if right_of[piece] not in [right_of[other] for other in before]:
            right_copy(right_of[piece]).wait_recv()
        for copy in loads(piece):
            copy.start()

    def wait_loads(piece):
        for copy in loads(piece):
            copy.wait()
        if tap_of.get(piece, 2) != 2:
            shift(tap_of[piece] - taps // 2)

    meet(near + shards + far)

    for index in range(len(lefts)):
        left_copy(index).start()
        if index == 0:
            right_copy(0).start()
    start_loads(0)

    summing = sum_steps(groups, blocks, vector, total, *sum_bufs, sum_sems)

    ring = x_one.shape[0]

    def pay(piece, index, device):
        @pl.when(piece < normal - ring)
        def _():
            pl.semaphore_signal(
                credit.at[index], inc=1, device_id=(device, me), device_id_type=MESH
            )

    def claim(piece, index):
        @pl.when(piece >= ring)
        def _():
            pl.semaphore_wait(credit.at[index], 1)

    def one(piece):
        slot = piece % slots
        return (
            remote(
                grad.at[slot, :, :, 1 - at_x, :, first],
                x_one.at[piece % ring],
                x1s.at[piece],
                x1r.at[piece],
                (along_x, me),
            ),
            remote(
                grad.at[slot, :, 1 - at_y, :, :, last],
                y_one.at[piece % ring],
                y1s.at[piece],
                y1r.at[piece],
                (along_y, me),
            ),
        )

    def two(piece):
        slot = piece % slots
        return (
            remote(
                grad.at[slot, :, 1 - at_y, at_x, :, first],
                y_two.at[piece % ring],
                y2s.at[piece],
                y2r.at[piece],
                (along_y, me),
            ),
            remote(
                grad.at[slot, :, at_y, 1 - at_x, :, last],
                x_two.at[piece % ring],
                x2s.at[piece],
                x2r.at[piece],
                (along_x, me),
            ),
        )

    def shard_copy(piece, j):
        other = (me + 1 + j) % groups
        return remote(
            grad.at[piece % slots, other, at_y, at_x],
            shard_got.at[piece % ring, me],
            shard_send.at[piece, j],
            shard_recv.at[piece, me],
            (dp, other),
        )

    def shard_arrival(piece, j):
        other = (me + 1 + j) % groups
        return remote(
            grad.at[piece % slots, other, at_y, at_x],
            shard_got.at[piece % ring, other],
            shard_send.at[piece, j],
            shard_recv.at[piece, other],
            (dp, other),
        )

    def block_copy(piece, j):
        return remote(
            done.at[piece],
            block_got.at[piece, block],
            block_send.at[piece, j],
            block_recv.at[piece, block],
            far[j],
        )

    def block_arrival(piece, j):
        other = (block + 1 + j) % blocks
        return remote(
            done.at[piece],
            block_got.at[piece, other],
            block_send.at[piece, j],
            block_recv.at[piece, other],
            far[j],
        )

    def place(piece, owner):
        return out.at[
            piece,
            pl.ds(pl.multiple_of(owner % 8 // 2 * part, 16), part),
            pl.ds(pl.multiple_of(core * width, 128), width),
        ]

    def spread(piece, src, owner, recv_sem, device):
        return remote(src, place(piece, owner), send_sem.at[piece], recv_sem, (device, me))

    def forward(piece, owner, recv_sem, device):
        return spread(piece, place(piece, owner), owner, recv_sem, device)

    diagonal = neighbours(along_x)[2]

    def shift(move):
        for window in range(2):
            value = right_hold[window].astype(jnp.float32)
            value = pltpu.roll(value, move % value.shape[0], 0)
            row = lax.broadcasted_iota(jnp.int32, value.shape, 0)
            inside = row >= move if move > 0 else row < value.shape[0] + move
            value = jnp.where(inside, value, 0.0)
            right_hold[window] = value.astype(right_hold.dtype)

    def product(shard):
        at = pl.ds(pl.multiple_of(shard * rows, 128), rows)
        value = dot_leading(left_hold[0, :, at], right_hold[0])
        value = value + dot_leading(left_hold[1, :, at], right_hold[1])
        return value.astype(grad.dtype).reshape(2, 2, part, width)

    def produce(piece):
        slot = piece % slots

        def shard_body(shard, carry):
            grad[slot, shard] = product(shard)
            return carry

        lax.fori_loop(0, groups, shard_body, 0)

        @pl.when(piece == mixed_piece)
        def _():
            rel_copy().wait()

        @pl.when(jnp.logical_and(piece == mixed_piece, core == 1))
        def _():
            for shard in range(groups):
                value = rel_grad[shard].astype(jnp.float32) + rel_got[shard].astype(jnp.float32)
                grad[slot, shard, 0, :, :, pl.ds(rel_at, rel_grad.shape[3])] = value.astype(
                    grad.dtype
                )

    def slab_copy(piece, j, arriving=False):
        other = (me + 1 + j) % groups
        at = j if arriving else groups - 2 - j
        return remote(
            slab.at[other],
            slab_got.at[at],
            shard_send.at[piece, j],
            shard_recv.at[piece, at],
            (dp, other),
        )

    def slab_one(piece, e):
        return (
            remote(
                slab.at[me, :, 1 - at_x, :, first],
                x_slab.at[e],
                x1s.at[piece],
                x1r.at[piece],
                (along_x, me),
            ),
            remote(
                slab.at[me, 1 - at_y, :, :, last],
                y_slab.at[e],
                y1s.at[piece],
                y1r.at[piece],
                (along_y, me),
            ),
        )

    def slab_two(piece, e):
        return (
            remote(
                slab.at[me, 1 - at_y, at_x, :, first],
                y_part.at[e],
                y2s.at[piece],
                y2r.at[piece],
                (along_y, me),
            ),
            remote(
                slab.at[me, at_y, 1 - at_x, :, last],
                x_part.at[e],
                x2s.at[piece],
                x2r.at[piece],
                (along_x, me),
            ),
        )

    def slab_sent(piece, e):
        for j in range(others):
            slab_copy(piece, j).wait_send()
        for copy in slab_one(piece, e) + slab_two(piece, e):
            copy.wait_send()

    def extra_start(piece, e):
        start_loads(piece)
        if e > 0:
            slab_sent(piece - 1, e - 1)
        wait_loads(piece)

        def shard_body(shard, carry):
            slab[shard] = product(shard)
            return carry

        lax.fori_loop(0, groups, shard_body, 0)
        for j in range(others):
            if e > 0:
                pl.semaphore_wait(slab_credit.at[(me + 1 + j) % groups], 1)
            slab_copy(piece, j).start()

    def extra_sum(piece, e):
        for j in range(others):
            slab_copy(piece, j, True).wait_recv()
        for y in range(2):
            for x in range(2):
                value = slab[me, y, x].astype(jnp.float32)
                for j in range(others):
                    value = value + slab_got[j, y, x].astype(jnp.float32)
                slab[me, y, x] = value.astype(slab.dtype)
        if e == 0:
            for j in range(others):
                pl.semaphore_signal(
                    slab_credit.at[me], inc=1, device_id=shards[j], device_id_type=MESH
                )
        for copy in slab_one(piece, e):
            copy.start()

    def extra_fold(piece, e):
        for copy in slab_one(piece, e):
            copy.wait_recv()
        for other in range(2):
            value = slab[me, other, at_x, :, first].astype(jnp.float32)
            value = value + x_slab[e, other].astype(jnp.float32)
            slab[me, other, at_x, :, first] = value.astype(slab.dtype)
            value = slab[me, at_y, other, :, last].astype(jnp.float32)
            value = value + y_slab[e, other].astype(jnp.float32)
            slab[me, at_y, other, :, last] = value.astype(slab.dtype)
        for copy in slab_two(piece, e):
            copy.start()

    def extra_done(piece, e):
        for copy in slab_two(piece, e):
            copy.wait_recv()
        low = slab[me, at_y, at_x, :, first].astype(jnp.float32)
        high = slab[me, at_y, at_x, :, last].astype(jnp.float32)
        low = low + y_part[e].astype(jnp.float32)
        high = high + x_part[e].astype(jnp.float32)
        finish(piece, jnp.concatenate([low, high], 1))

    def finish(piece, value):
        if blocks > 1:
            done[piece] = value.astype(done.dtype)
            block_got[piece, block] = value.astype(done.dtype)
            for j in range(blocks - 1):
                block_copy(piece, j).start()
            for j in range(blocks - 1):
                block_copy(piece, j).wait_send()
                block_arrival(piece, j).wait_recv()
            value = block_got[piece, 0].astype(jnp.float32)
            for other in range(1, blocks):
                value = value + block_got[piece, other].astype(jnp.float32)
        done[piece] = value.astype(done.dtype)
        pltpu.make_async_copy(done.at[piece], place(piece, dp), write_sem.at[piece]).start()
        spread(piece, done.at[piece], dp, ax.at[piece], along_x).start()
        spread(piece, done.at[piece], dp, ay.at[piece], along_y).start()
        spread(piece, done.at[piece], dp, sib_sem.at[piece], sib).start()

    def cross(piece):
        route = piece % 2
        forward(piece, along_x, ax.at[piece], dp).wait_recv()
        forward(piece, along_y, ay.at[piece], dp).wait_recv()
        owner = route * along_x + (1 - route) * along_y
        target = route * along_y + (1 - route) * along_x
        forward(piece, owner, ad.at[piece], target).start()
        forward(piece, along_x, sib_sem.at[piece], sib).start()
        forward(piece, along_y, sib_sem.at[piece], sib).start()

    def close(piece):
        forward(piece, diagonal, ad.at[piece], dp).wait_recv()
        forward(piece, diagonal, sib_sem.at[piece], sib).start()

    def add(piece_slot, ref, columns, *index):
        ahead = grad[(piece_slot,) + index + (slice(None), columns)]
        return ahead.astype(jnp.float32) + ref.astype(jnp.float32)

    length = tokens.shape[0]
    columns = 2 * width
    tile = 512
    block_rows = 128
    head_value = columns // HEADS
    tiles = columns // tile
    hidden_tiles = hidden_pre.shape[1] // tile

    def tile_of(phase, i):
        at = pl.ds(pl.multiple_of(i * tile, tile), tile)
        if phase == 0:
            return down_full.at[at]
        if phase == 1:
            at = pl.ds(pl.multiple_of(i // 2 * tile, tile), tile)
            return up_full.at[at, pl.ds(pl.multiple_of(i % 2 * columns, columns), columns)]
        if phase == 5:
            at = pl.ds(pl.multiple_of(i % tiles * tile, tile), tile)
            return conv_full.at[i // tiles, at]
        return (out_full, mixed_full, value_full)[phase - 2].at[at]

    lengths = [hidden_tiles, 2 * tiles, tiles, tiles, tiles, taps * tiles]
    widths = [columns, columns, columns, mixed_full.shape[1], columns, columns]

    def tile_load(phase, i):
        slot = (sum(lengths[:phase]) + i) % 2
        return pltpu.make_async_copy(
            tile_of(phase, i),
            weight_hold.at[slot, :, pl.ds(0, widths[phase])],
            tile_sem.at[slot],
        )

    def next_tile(phase, i):
        tile_load(phase, i).wait()

        @pl.when(i + 1 < lengths[phase])
        def _():
            tile_load(phase, i + 1).start()

        if phase + 1 < len(lengths):

            @pl.when(i + 1 == lengths[phase])
            def _():
                tile_load(phase + 1, 0).start()

        slot = (sum(lengths[:phase]) + i) % 2
        return weight_hold[slot, :, 0 : widths[phase]]

    def over(count, fn):
        def step_body(i, carry):
            fn(i)
            return carry

        lax.fori_loop(0, count, step_body, 0)

    def columns_at(i, wide, offset=0):
        return pl.ds(pl.multiple_of(offset + i * wide, 128), wide)

    def host_load(index):
        pairs = [
            (cotangent, right_ref),
            (after_attention, kept_ref),
            (after_conv, kept_ref),
            (values, wide_hold.at[:, pl.ds(columns, columns)]),
            (keys, key_ref),
            (contents, content_ref),
            (positions, position_ref),
            (mirrored_keys, table_ref),
            (tokens, wide_hold.at[:, pl.ds(columns, columns)]),
            (wide_hold, made[0]),
            (right_ref, made[1]),
            (value_grad_ref, made[2]),
            (mixed_ref, made[3]),
            (right_ref, made[4]),
        ]
        return pltpu.make_async_copy(*pairs[index], host_sem.at[index])

    def load(*indices):
        def thunk():
            for index in indices:
                host_load(index).start()

        return thunk

    def ready(*indices):
        def thunk():
            for index in indices:
                host_load(index).wait()

        return thunk

    def send_right(*indices):
        def thunk():
            for index in indices:
                right_copy(index).start()

        return thunk

    def pre_load(i):
        return pltpu.make_async_copy(
            hidden_pre.at[:, columns_at(i, tile)],
            kept_ref.at[:, columns_at(i % 3, tile)],
            kept_sem.at[i],
        )

    def write_part():
        return pltpu.make_async_copy(attn_grad, part_grad, kept_sem.at[hidden_tiles])

    def by_rows(fn):
        def row_body(i, carry):
            fn(pl.ds(pl.multiple_of(i * block_rows, block_rows), block_rows))
            return carry

        lax.fori_loop(0, length // block_rows, row_body, 0)

    def put(row, value):
        vector[row : row + 1, :] += jnp.sum(value, 0, keepdims=True)

    def clear_total():
        def rows_fn(at):
            total_ref[at, :] = jnp.zeros((block_rows, columns), jnp.float32)

        by_rows(rows_fn)

    def begin():
        vector[...] = jnp.zeros_like(vector)
        mixed_ref[...] = jnp.zeros_like(mixed_ref)
        tile_load(0, 0).start()
        for i in range(3):
            pre_load(i).start()
        clear_total()

    def hidden_step(i):
        value = dot_trailing(right_ref[...], next_tile(0, i))
        pre_load(i).wait()
        value = value * gelu_slope(kept_ref[:, columns_at(i % 3, tile)])

        @pl.when(i + 3 < hidden_tiles)
        def _():
            pre_load(i + 3).start()

        rounded = value.astype(wide_hold.dtype)
        wide_hold[:, columns_at(i, tile)] = rounded
        sums_here = jnp.sum(rounded.astype(jnp.float32), 0, keepdims=True)
        for side in range(2):

            @pl.when(i // tiles == side)
            def _():
                vector[9 + side : 10 + side, columns_at(i % tiles, tile)] = sums_here

    def norm_two_step(i):
        left = wide_hold[:, columns_at(i % 2, columns)]
        total_ref[:, columns_at(i // 2, tile)] += dot_trailing(left, next_tile(1, i))

    def norm_two_back():
        def rows_fn(at):
            standard, inverse = normalize(kept_ref[at, :])
            value = total_ref[at, :]
            put(2, value * standard)
            put(7, value)
            cot = right_ref[at, :].astype(jnp.float32)
            put(8, cot)
            value = cot + norm_back(value * params[2:3, :], standard, inverse)
            attn_grad[at, :] = value
            rounded = value.astype(right_ref.dtype)
            right_ref[at, :] = rounded
            put(6, rounded.astype(jnp.float32))

        by_rows(rows_fn)

    def attended_step(i):
        value = dot_trailing(right_ref[...], next_tile(2, i))
        wide_hold[:, columns_at(i, tile)] = value.astype(wide_hold.dtype)

    def probs_load(head):
        return pltpu.make_async_copy(
            probs.at[head], probs_ref.at[head % 2], probs_sem.at[head % 2]
        )

    def pair_step(index):
        span = table_ref.shape[0]
        row = lax.broadcasted_iota(jnp.int32, (length, length), 0)
        column = lax.broadcasted_iota(jnp.int32, (length, length), 1)
        mirror = jnp.where(row + column == length - 1, 1.0, 0.0).astype(jnp.bfloat16)
        pair = columns_at(index, 2 * KEY)
        key_pair = columns_at(index, 2 * KEY, key_ref.shape[1])
        value_pair = columns_at(index, 2 * head_value)
        far_pair = columns_at(index, 2 * head_value, columns)
        made_here = [[], [], [], [], [], []]
        for side in range(2):
            head = 2 * index + side
            probs_load(head).wait()
            keys_at = slice(side * KEY, (side + 1) * KEY)
            values_at = slice(side * head_value, (side + 1) * head_value)
            prob = probs_ref[side]
            out_grad = wide_hold[:, value_pair][:, values_at]
            made_here[0].append(dot_leading(prob, out_grad).astype(jnp.bfloat16))
            prob_grad = dot_trailing(out_grad, wide_hold[:, far_pair][:, values_at])
            prob = prob.astype(jnp.float32)
            row_dot = jnp.sum(prob * prob_grad, -1, keepdims=True)
            rounded = (prob * (prob_grad - row_dot)).astype(jnp.bfloat16)
            content = content_ref[:, pair][:, keys_at]
            made_here[1].append(dot_leading(rounded, content).astype(jnp.bfloat16))
            content_grad = jnp.dot(
                rounded, key_ref[:, pair][:, keys_at], preferred_element_type=jnp.float32
            )
            mirrored = jnp.dot(rounded, mirror, preferred_element_type=jnp.float32)
            wide = jnp.concatenate([mirrored, jnp.zeros((length, span - length), jnp.float32)], 1)
            band = pltpu.roll(wide, 0, 1, stride=1, stride_axis=0).astype(jnp.bfloat16)
            position_grad = jnp.dot(
                band, table_ref[:, pair][:, keys_at], preferred_element_type=jnp.float32
            )
            position = position_ref[:, pair][:, keys_at]
            made_here[2].append(dot_leading(band, position).astype(jnp.bfloat16))
            made_here[3].append(((content_grad + position_grad) * KEY**-0.5).astype(jnp.bfloat16))
            made_here[4].append(jnp.sum(content_grad, 0, keepdims=True))
            made_here[5].append(jnp.sum(position_grad, 0, keepdims=True))
        value_grad_ref[:, value_pair] = jnp.concatenate(made_here[0], 1)
        mixed_ref[:, key_pair] = jnp.concatenate(made_here[1], 1)
        table_grad_ref[:, pair] = jnp.concatenate(made_here[2], 1)
        mixed_ref[:, pair] = jnp.concatenate(made_here[3], 1)
        vector[11:12, pair] = jnp.concatenate(made_here[4], 1)
        vector[11:12, key_pair] = jnp.concatenate(made_here[5], 1)

        @pl.when(index + 1 < HEADS // 2)
        def _():
            for side in range(2):
                probs_load(2 * index + 2 + side).start()

    def rel_step():
        for shard in range(groups):
            value = dot_leading(table[1], table_grad_ref[:, shard * 128 : (shard + 1) * 128])
            rel_grad[shard] = value.astype(rel_grad.dtype).reshape(rel_grad.shape[1:])
        rel_copy().start()

    def mixed_step(i):
        left = mixed_ref[:, 0 : mixed_full.shape[1]]
        total_ref[:, columns_at(i, tile)] = dot_trailing(left, next_tile(3, i))

    def value_step(i):
        total_ref[:, columns_at(i, tile)] += dot_trailing(value_grad_ref[...], next_tile(4, i))

    def norm_one_back():
        def rows_fn(at):
            standard, inverse = normalize(kept_ref[at, :])
            value = total_ref[at, :]
            put(1, value * standard)
            put(5, value)
            value = attn_grad[at, :] + norm_back(value * params[1:2, :], standard, inverse)
            attn_grad[at, :] = value
            rounded = value.astype(right_ref.dtype)
            right_ref[at, :] = rounded
            put(4, rounded.astype(jnp.float32))

        by_rows(rows_fn)

    def conv_shift(tap):
        move = tap - taps // 2

        def column_body(i, carry):
            at = columns_at(i, rows)
            value = right_ref[:, at].astype(jnp.float32)
            value = pltpu.roll(value, (move + length) % length, 0)
            row = lax.broadcasted_iota(jnp.int32, value.shape, 0) - move
            inside = jnp.logical_and(row >= 0, row < length)
            wide_hold[:, at] = jnp.where(inside, value, 0.0).astype(wide_hold.dtype)
            return carry

        lax.fori_loop(0, columns // rows, column_body, 0)

    def conv_step(i):
        left = wide_hold[:, 0:columns]
        total_ref[:, columns_at(i % tiles, tile)] += dot_trailing(left, next_tile(5, i))

    def batch_back():
        def rows_fn(at):
            value = wide_hold[at, columns : 2 * columns].astype(jnp.float32)
            standard = (value - params[9:10, :]) * params[10:11, :]
            normed = standard * params[0:1, :] + params[3:4, :]
            value = total_ref[at, :] * gelu_slope(normed)
            put(0, value * standard)
            put(3, value)
            attn_grad[at, :] += params[10:11, :] * params[0:1, :] * value

        by_rows(rows_fn)

    def start_probs():
        for head in range(2):
            probs_load(head).start()

    def step_zero():
        begin()
        ready(0)()
        over(hidden_tiles, hidden_step)
        load(9, 1)()
        ready(9)()
        send_right(1, 2)()

    def step_one():
        over(2 * tiles, norm_two_step)
        load(3)()
        ready(1)()
        norm_two_back()
        load(10, 2)()
        start_probs()

    def step_two():
        over(tiles, attended_step)
        ready(10)()
        send_right(3)()
        ready(3, 4, 5, 6, 7)()

    def step_three():
        load(11, 12, 8)()
        rel_step()
        ready(11, 12)()
        send_right(4, 5)()

    def step_four():
        over(tiles, mixed_step)
        over(tiles, value_step)
        ready(2)()
        norm_one_back()
        load(13)()
        ready(13)()
        send_right(6)()
        clear_total()

    def step_last():
        ready(8)()
        batch_back()
        write_part().start()

    pairs_each = HEADS // 4

    for copy in (0, 4, 5, 6, 7):
        host_load(copy).start()

    def host(n):
        pl.when(n == 0)(step_zero)
        pl.when(n == 1)(step_one)
        pl.when(n == 2)(step_two)

        @pl.when(jnp.logical_and(n >= 2, n < 4))
        def _():
            over(pairs_each, lambda i: pair_step((n - 2) * pairs_each + i))

        pl.when(n == 3)(step_three)
        pl.when(n == 4)(step_four)

        @pl.when(jnp.logical_and(n >= 5, n < 5 + taps))
        def _():
            conv_shift(n - 5)
            over(tiles, lambda i: conv_step((n - 5) * tiles + i))

        pl.when(n == 4 + taps)(step_last)

    def body(n, carry):
        @pl.when(n < normal)
        def _():
            @pl.when(n >= slots)
            def _():
                old = n - slots
                for copy in one(old) + two(old):
                    copy.wait_send()
                for j in range(others):
                    shard_copy(old, j).wait_send()

            for piece in range(normal):

                @pl.when(n == piece)
                def _():
                    wait_loads(piece)

            produce(n)
            claim(n, 0)
            claim(n, 1)
            for copy in one(n):
                copy.start()

        for e, (at, piece) in enumerate(extra_at.items()):

            @pl.when(n == at)
            def _():
                extra_start(piece, e)

        host(n)
        for piece in range(1, normal):

            @pl.when(n == piece - 1)
            def _():
                start_loads(piece)

        @pl.when(jnp.logical_and(n >= 1, n < normal + 1))
        def _():
            piece = n - 1
            slot = piece % slots
            for copy in one(piece):
                copy.wait_recv()

            def shard_body(shard, carry):
                for other in range(2):
                    value = add(slot, x_one[piece % ring, shard, other], first, shard, other, at_x)
                    grad[slot, shard, other, at_x, :, first] = value.astype(grad.dtype)
                    value = add(slot, y_one[piece % ring, shard, other], last, shard, at_y, other)
                    grad[slot, shard, at_y, other, :, last] = value.astype(grad.dtype)
                return carry

            lax.fori_loop(0, groups, shard_body, 0)
            pay(piece, 0, along_x)
            pay(piece, 1, along_y)
            claim(piece, 2)
            claim(piece, 3)
            for copy in two(piece):
                copy.start()

        @pl.when(jnp.logical_and(n >= 2, n < normal + 2))
        def _():
            piece = n - 2
            slot = piece % slots
            for copy in two(piece):
                copy.wait_recv()

            def shard_body(shard, carry):
                value = add(slot, y_two[piece % ring, shard], first, shard, at_y, at_x)
                grad[slot, shard, at_y, at_x, :, first] = value.astype(grad.dtype)
                value = add(slot, x_two[piece % ring, shard], last, shard, at_y, at_x)
                grad[slot, shard, at_y, at_x, :, last] = value.astype(grad.dtype)
                return carry

            lax.fori_loop(0, groups, shard_body, 0)
            pay(piece, 2, along_y)
            pay(piece, 3, along_x)
            for j in range(others):

                @pl.when(piece >= ring)
                def _():
                    pl.semaphore_wait(shard_credit.at[(me + 1 + j) % groups], 1)

                shard_copy(piece, j).start()

        @pl.when(jnp.logical_and(n >= 3, n < normal + 3))
        def _():
            piece = n - 3
            value = grad[piece % slots, me, at_y, at_x].astype(jnp.float32)
            for j in range(others):
                shard_arrival(piece, j).wait_recv()
                value = value + shard_got[piece % ring, (me + 1 + j) % groups].astype(jnp.float32)

            @pl.when(piece < normal - ring)
            def _():
                for j in range(others):
                    pl.semaphore_signal(
                        shard_credit.at[me], inc=1, device_id=shards[j], device_id_type=MESH
                    )

            finish(piece, value)

        @pl.when(jnp.logical_and(n >= 4, n < normal + 4))
        def _():
            cross(n - 4)

        @pl.when(n >= 5)
        def _():
            close(n - 5)

        for e, (at, piece) in enumerate(extra_at.items()):
            for later, action in (
                (3, functools.partial(extra_sum, piece, e)),
                (4, functools.partial(extra_fold, piece, e)),
                (5, functools.partial(extra_done, piece, e)),
                (6, functools.partial(cross, piece)),
                (7, functools.partial(close, piece)),
            ):
                pl.when(n == at + later)(action)

        for step in range(len(summing)):

            @pl.when(n == normal + step - 1)
            def _():
                summing[step]()

        return carry

    lax.fori_loop(0, normal + 5, body, 0)
    slab_sent(11, 1)
    write_part().wait()

    def drain(piece, carry):
        @pl.when(jnp.logical_and(piece >= normal - slots, piece < normal))
        def _():
            for copy in one(piece) + two(piece):
                copy.wait_send()
            for j in range(others):
                shard_copy(piece, j).wait_send()

        pltpu.make_async_copy(done.at[piece], place(piece, dp), write_sem.at[piece]).wait()
        got = out.at[piece, :, pl.ds(0, width)]
        remote(got, got, send_sem.at[piece], sib_sem.at[piece], (sib, me)).wait_recv()
        sent = out.at[piece, pl.ds(0, 7 * part // 2), :]
        remote(sent, sent, send_sem.at[piece], sib_sem.at[piece], (sib, me)).wait_send()
        return carry

    lax.fori_loop(0, count, drain, 0)
    for index in range(len(lefts)):
        left_copy(index).wait_send()
    for index in range(len(rights)):
        right_copy(index).wait_send()


def reduce(groups, blocks, rel_at, lefts, saved, weights, heads, params, table):
    hidden, _, _, _, activated = lefts
    length, columns = activated.shape
    width = columns // 2
    rows = columns // groups
    part = rows // 4
    dtype = activated.dtype
    count = 12
    slots = 4
    ring = 3 if blocks == 1 else 2
    narrow = heads[2].shape
    span = table.shape[1]
    kept = pl.BlockSpec(memory_space=pl.ANY)
    inside = pl.BlockSpec(memory_space=pltpu.VMEM)
    each = pltpu.SemaphoreType.DMA((count,))
    wide = (length, columns)
    rel_shape = (groups, 2, table.shape[2] // 2, 128)
    sums = (16, columns)
    inputs = [*lefts, *saved, *weights, *heads]
    half_got = (ring, groups, part, width // 2)
    two_got = (ring, groups, 2, part, width // 2)
    return pl.pallas_call(
        functools.partial(reduce_kernel, groups, blocks, rel_at),
        out_shape=(
            jax.ShapeDtypeStruct((count, rows, columns), dtype),
            jax.ShapeDtypeStruct(sums, jnp.float32),
            jax.ShapeDtypeStruct(wide, jnp.float32),
            jax.ShapeDtypeStruct(hidden.shape, dtype),
            jax.ShapeDtypeStruct(wide, dtype),
            jax.ShapeDtypeStruct(wide, dtype),
            jax.ShapeDtypeStruct(wide, dtype),
            jax.ShapeDtypeStruct(wide, dtype),
            jax.ShapeDtypeStruct(hidden.shape, dtype),
            jax.ShapeDtypeStruct((4,) + wide, dtype),
            jax.ShapeDtypeStruct((7, length, width), dtype),
        ),
        in_specs=[kept] * len(inputs) + [inside] * 2,
        out_specs=[kept, inside] + [kept] * 9,
        scratch_shapes=[
            pltpu.VMEM((2,) + wide, dtype),
            pltpu.VMEM((2, length, width), dtype),
            pltpu.VMEM((slots, groups, 2, 2, part, width), dtype),
            pltpu.VMEM(two_got, dtype),
            pltpu.VMEM(two_got, dtype),
            pltpu.VMEM(half_got, dtype),
            pltpu.VMEM(half_got, dtype),
            pltpu.VMEM((ring, groups, part, width), dtype),
            pltpu.VMEM((count if blocks > 1 else 1, blocks, part, width), dtype),
            pltpu.VMEM((count, part, width), dtype),
            pltpu.VMEM(rel_shape, dtype),
            pltpu.VMEM(rel_shape, dtype),
            pltpu.VMEM(sums, jnp.float32),
            *([pltpu.SemaphoreType.DMA((5,))] * 2),
            *([pltpu.SemaphoreType.DMA((7,))] * 2),
            *([pltpu.SemaphoreType.DMA((1,))] * 2),
            pltpu.SemaphoreType.DMA((2 + 2 * groups,)),
            *([each] * 8),
            *([pltpu.SemaphoreType.DMA((count, groups))] * 2),
            *([pltpu.SemaphoreType.DMA((count, blocks))] * 2),
            *([each] * 6),
            *sum_scratch(groups, blocks, sums),
            pltpu.SemaphoreType.REGULAR((4,)),
            pltpu.SemaphoreType.REGULAR((groups,)),
            pltpu.VMEM(wide, jnp.float32),
            pltpu.VMEM(wide, jnp.float32),
            pltpu.VMEM(wide, jnp.float32),
            pltpu.VMEM((2, 512, columns), dtype),
            pltpu.VMEM(hidden.shape, dtype),
            pltpu.VMEM(wide, dtype),
            pltpu.VMEM(wide, dtype),
            pltpu.VMEM(wide, dtype),
            *([pltpu.VMEM(narrow, dtype)] * 3),
            pltpu.VMEM((span, narrow[1]), dtype),
            pltpu.VMEM((span, narrow[1]), dtype),
            pltpu.VMEM((2, length, length), dtype),
            pltpu.SemaphoreType.DMA((2,)),
            pltpu.SemaphoreType.DMA((14,)),
            pltpu.SemaphoreType.DMA((2,)),
            pltpu.SemaphoreType.DMA((hidden.shape[1] // 512 + 1,)),
            pltpu.VMEM((groups, 2, 2, part, width), dtype),
            pltpu.VMEM((groups - 1, 2, 2, part, width), dtype),
            pltpu.VMEM((2, 2, part, width // 2), dtype),
            pltpu.VMEM((2, 2, part, width // 2), dtype),
            pltpu.VMEM((2, part, width // 2), dtype),
            pltpu.VMEM((2, part, width // 2), dtype),
            pltpu.SemaphoreType.REGULAR((groups,)),
        ],
        compiler_params=pltpu.CompilerParams(
            collective_id=1, has_side_effects=True, vmem_limit_bytes=VMEM_LIMIT
        ),
        name="reduce",
    )(*inputs, params, table)


EPSILON = 1e-05


def normalize(values):
    centred = values - jnp.mean(values, -1, keepdims=True)
    inverse = lax.rsqrt(jnp.mean(centred * centred, -1, keepdims=True) + EPSILON)
    return (centred * inverse, inverse)


def norm_back(grad_std, standard, inverse):
    return inverse * (
        grad_std
        - jnp.mean(grad_std, -1, keepdims=True)
        - standard * jnp.mean(grad_std * standard, -1, keepdims=True)
    )


def dot_leading(left_side, right_side):
    return lax.dot_general(
        left_side, right_side, (((0,), (0,)), ((), ())), preferred_element_type=jnp.float32
    )


def dot_trailing(left_side, right_side):
    return lax.dot_general(
        left_side, right_side, (((1,), (1,)), ((), ())), preferred_element_type=jnp.float32
    )


def on_device(
    tokens,
    conv_weight,
    query_weight,
    key_weight,
    value_weight,
    out_weight,
    rel_weight,
    up_weight,
    down_weight,
    gains,
    biases,
    up_bias,
    rel_bias,
    target_table,
    clip_levels,
    window_ids,
    clip_index,
):
    groups = lax.axis_size("fsdp")
    blocks = lax.axis_size("dp") // 8
    tap_count, piece_rows, model_width = conv_weight.shape
    half_taps = tap_count // 2
    half_width = model_width // 2
    key_width = query_weight.shape[1]
    rel_rows, rel_columns = rel_weight.shape
    inputs = tokens[0].astype(jnp.float32)
    length = inputs.shape[0]
    token_total = length * lax.axis_size("dp") * lax.axis_size("fsdp")

    small_parts = [gains, biases, up_bias, rel_bias]
    small = jnp.concatenate([part.reshape(-1) for part in small_parts])
    small = jnp.pad(small, (0, -small.shape[0] % 1024)).reshape(-1, 128)
    target_row = lax.dynamic_index_in_dim(target_table, window_ids[0], 0, keepdims=True)
    levels = jnp.arange(clip_levels.shape[0], dtype=jnp.int32)
    selector = (clip_index[0][:, None] == levels[None, :]).astype(jnp.float32)
    limits = jnp.sum(selector * clip_levels[None, :], 1)[:, None]
    limits = jnp.broadcast_to(limits, (length, 128))
    (
        conv_full,
        mixed_full,
        value_full,
        out_full,
        up_full,
        down_full,
        _,
        _,
        _,
        activated,
        after_conv,
        normed_one,
        content_query,
        position_query,
        keys,
        values,
        mirrored_keys,
        probs,
        attended,
        after_attention,
        normed_two,
        hidden_pre,
        hidden,
        outputs,
        cotangent,
        tables,
        params,
    ) = gather(
        groups,
        blocks,
        [
            conv_weight,
            query_weight,
            key_weight,
            value_weight,
            out_weight,
            up_weight,
            down_weight,
            rel_weight,
        ],
        small,
        tokens[0],
        target_row,
        limits,
    )
    conv_full = conv_full.reshape(tap_count, model_width, model_width)
    mixed_full = mixed_full.reshape(model_width, -1)
    value_full = value_full.reshape(model_width, -1)
    out_full = out_full.reshape(model_width, -1)
    up_full = up_full.reshape(model_width, -1)
    down_full = down_full.reshape(-1, model_width)
    pieces, sums, part_grad, *_ = reduce(
        groups,
        blocks,
        2 * key_width - half_width,
        [hidden, normed_two, attended, normed_one, activated],
        [cotangent, hidden_pre, after_attention, after_conv, tokens[0]],
        [down_full, up_full, out_full, value_full, mixed_full, conv_full],
        [probs, values, keys, content_query, position_query, mirrored_keys],
        params,
        tables,
    )
    standard = (inputs - params[9]) * params[10]
    input_grad = part_grad - params[10] * params[0] * (
        sums[3] + standard * sums[0]
    ) / token_total
    shard = lax.axis_index("fsdp")
    by_shard = sums[:9].reshape(9, groups, -1)
    by_shard = lax.dynamic_index_in_dim(by_shard, shard, 1, keepdims=False)
    up_sums = sums[9:11].reshape(groups, -1)
    up_sums = lax.dynamic_index_in_dim(up_sums, shard, 0, keepdims=False)
    rel_sums = sums[11, : 2 * key_width].reshape(2, groups, -1)
    rel_sums = lax.dynamic_index_in_dim(rel_sums, shard, 1, keepdims=False)
    up_grad = jnp.concatenate([pieces[1], pieces[2]], 1)
    mixed_sum = pieces[5].astype(jnp.float32)
    rel_at = 2 * key_width
    return (
        outputs[None],
        input_grad.astype(jnp.bfloat16)[None],
        jnp.concatenate([pieces[6:10], pieces[11:12]], 0).astype(jnp.float32),
        mixed_sum[:, :key_width],
        mixed_sum[:, key_width:rel_at],
        pieces[4].astype(jnp.float32),
        pieces[3].astype(jnp.float32),
        mixed_sum[:rel_rows, rel_at : rel_at + rel_columns],
        up_grad.astype(jnp.float32),
        jnp.concatenate([pieces[0], pieces[10]], 0).astype(jnp.float32),
        by_shard[:3],
        by_shard[3:9],
        up_sums,
        rel_sums,
    )


def solution(mesh):
    placed = (
        P(("dp", "fsdp"), None, None),
        P(None, "fsdp", None),
        P("fsdp", None),
        P("fsdp", None),
        P("fsdp", None),
        P("fsdp", None),
        P(None, "fsdp"),
        P("fsdp", None),
        P("fsdp", None),
        P(None, "fsdp"),
        P(None, "fsdp"),
        P("fsdp"),
        P(None, "fsdp"),
        P(),
        P(),
        P(("dp", "fsdp")),
        P(("dp", "fsdp"), None),
    )
    return jax.shard_map(
        on_device,
        mesh=mesh,
        in_specs=placed,
        out_specs=(
            P(("dp", "fsdp"), None, None),
            P(("dp", "fsdp"), None, None),
            P(None, "fsdp", None),
            P("fsdp", None),
            P("fsdp", None),
            P("fsdp", None),
            P("fsdp", None),
            P(None, "fsdp"),
            P("fsdp", None),
            P("fsdp", None),
            P(None, "fsdp"),
            P(None, "fsdp"),
            P("fsdp"),
            P(None, "fsdp"),
        ),
        check_vma=False,
    )
```

```python
import functools
import math

import jax
import jax.numpy as jnp
from jax import lax
from jax.experimental import pallas as pl
from jax.experimental.pallas import tpu as pltpu
from jax.sharding import PartitionSpec as P

HEADS = 8
KEY = 64
MESH = pl.DeviceIdType.MESH
AHEAD = 2
GELU = 0.7978845608028654
VMEM_LIMIT = 62 << 20


def neighbours(dp):
    core = dp % 2
    along_x = dp // 2 % 2
    along_y = dp // 4 % 2
    return dp + 1 - 2 * core, dp + 2 - 4 * along_x, dp + 4 - 8 * along_y


def remote(src, dst, send_sem, recv_sem, device):
    return pltpu.make_async_remote_copy(
        src_ref=src,
        dst_ref=dst,
        send_sem=send_sem,
        recv_sem=recv_sem,
        device_id=device,
        device_id_type=MESH,
    )


def meet(peers):
    barrier = pltpu.get_barrier_semaphore()
    for peer in peers:
        pl.semaphore_signal(barrier, inc=1, device_id=peer, device_id_type=MESH)
    pl.semaphore_wait(barrier, len(peers))


def peers_of(groups, blocks):
    dp = lax.axis_index("dp")
    me = lax.axis_index("fsdp")
    near = [(device, me) for device in neighbours(dp)]
    shards = [(dp, (me + 1 + j) % groups) for j in range(groups - 1)]
    far = [((dp + 8 * (1 + j)) % (8 * blocks), me) for j in range(blocks - 1)]
    return near, shards, far


def sum_steps(groups, blocks, vector, total, near_got, sums, shard_got, block_got, sems):
    near_send, near_recv, shard_send, shard_recv, block_send, block_recv = sems
    me = lax.axis_index("fsdp")
    block = lax.axis_index("dp") // 8
    near, shards, far = peers_of(groups, blocks)

    def near_copy(step):
        src = vector if step == 0 else sums.at[step - 1]
        return remote(
            src, near_got.at[step], near_send.at[step], near_recv.at[step], near[step]
        )

    def fold(step):
        copy = near_copy(step)
        copy.wait()
        held = vector[...] if step == 0 else sums[step - 1]
        sums[step] = held + near_got[step]

    def shard_copy(j):
        return remote(
            sums.at[2], shard_got.at[me], shard_send.at[j], shard_recv.at[me], shards[j]
        )

    def block_copy(j):
        return remote(
            sums.at[3], block_got.at[block], block_send.at[j], block_recv.at[block], far[j]
        )

    def start():
        near_copy(0).start()

    def second():
        fold(0)
        near_copy(1).start()

    def third():
        fold(1)
        near_copy(2).start()

    def fourth():
        fold(2)
        for j in range(groups - 1):
            shard_copy(j).start()
        shard_got[me] = sums[2]

    def fifth():
        for j in range(groups - 1):
            shard_copy(j).wait_send()
            other = (me + 1 + j) % groups
            remote(
                sums.at[2], shard_got.at[other], shard_send.at[j], shard_recv.at[other], shards[j]
            ).wait_recv()
        added = shard_got[0]
        for shard in range(1, groups):
            added = added + shard_got[shard]
        sums[3] = added
        for j in range(blocks - 1):
            block_copy(j).start()
        block_got[block] = added

    def sixth():
        for j in range(blocks - 1):
            block_copy(j).wait_send()
            other = (block + 1 + j) % blocks
            remote(
                sums.at[3], block_got.at[other], block_send.at[j], block_recv.at[other], far[j]
            ).wait_recv()
        added = block_got[0]
        for other in range(1, blocks):
            added = added + block_got[other]
        total[...] = added

    return [start, second, third, fourth, fifth, sixth]


def sum_scratch(groups, blocks, shape):
    return [
        pltpu.VMEM((3,) + shape, jnp.float32),
        pltpu.VMEM((4,) + shape, jnp.float32),
        pltpu.VMEM((groups,) + shape, jnp.float32),
        pltpu.VMEM((blocks,) + shape, jnp.float32),
        pltpu.SemaphoreType.DMA((3,)),
        pltpu.SemaphoreType.DMA((3,)),
        pltpu.SemaphoreType.DMA((groups,)),
        pltpu.SemaphoreType.DMA((groups,)),
        pltpu.SemaphoreType.DMA((blocks,)),
        pltpu.SemaphoreType.DMA((blocks,)),
    ]


def gather_kernel(groups, blocks, *refs):
    weights = refs[:8]
    conv, query, key, value, out, up, down, rel = weights
    small, inputs, target, limits = refs[8:12]
    outs = refs[12:21]
    conv_out, mixed_out, value_out, out_out, up_out, down_out = outs[:6]
    rel_full, small_full, stat_total = outs[6:]
    results = list(refs[21:37])
    pre_out = results.pop(12)
    hidden_out = results.pop(12)
    results[12:12] = [
        hidden_out.at[:, pl.ds(side * conv.shape[2], conv.shape[2])] for side in range(2)
    ]
    tables, params = refs[37:39]
    refs = refs[39:]
    hold, hold_mixed, local_sem, write_sem = refs[:4]
    z_sem, x_sem, y_sem, d_sem, sib_sem, send_sem, right_send, left_send = refs[4:12]
    rel_send, rel_recv, small_send, small_recv = refs[12:16]
    near_got, sums, shard_got, block_got = refs[16:20]
    sum_sems = refs[20:26]
    weight_hold, weight_sem, result_sem = refs[26:29]
    shifted_ref, total_ref = refs[29:31]
    act_ref, norm_ref, content_ref, position_ref, key_ref, value_ref = refs[31:37]
    table_ref, probs_ref, attended_ref = refs[37:40]
    stats, loss_ref, part_sem, part_right, part_left = refs[40:45]
    dp = lax.axis_index("dp")
    me = lax.axis_index("fsdp")
    near, shards, far = peers_of(groups, blocks)
    sib, along_x, along_y = neighbours(dp)
    rows = conv.shape[1]
    part = rows // 8
    others = groups - 1
    columns = conv.shape[2]
    pieces = [conv_out.at[tap] for tap in range(5)] + [mixed_out, value_out, out_out]
    pieces += [up_out.at[:, :, pl.ds(half * columns, columns)] for half in range(2)]
    pieces += [down_out.at[:, pl.ds(half * rows, rows)] for half in range(2)]
    count = len(pieces)
    holds = [hold.at[i] for i in range(5)] + [hold_mixed] + [hold.at[i] for i in range(5, 11)]

    pending = [[] for _ in range(count)]
    started = [0]

    def load(src, dst, piece):
        copy = pltpu.make_async_copy(src, dst, local_sem.at[started[0]])
        copy.start()
        started[0] += 1
        pending[piece].append(copy)

    for tap in range(5):
        load(conv.at[tap], holds[tap], tap)
    width = query.shape[1]
    load(query, hold_mixed.at[:, pl.ds(0, width)], 5)
    load(key, hold_mixed.at[:, pl.ds(width, width)], 5)
    load(value, holds[6], 6)
    load(out, holds[7], 7)
    for half in range(2):
        load(up.at[:, pl.ds(half * columns, columns)], holds[8 + half], 8 + half)
    for half in range(2):
        load(down.at[pl.ds(half * rows, rows)], holds[10 + half], 10 + half)

    meet(near + shards + far)

    summing = sum_steps(
        groups, blocks, stats, stat_total, near_got, sums, shard_got, block_got, sum_sems
    )
    for j in range(others):
        remote(
            rel, rel_full.at[me], rel_send.at[j], rel_recv.at[me], shards[j]
        ).start()
        remote(
            small, small_full.at[me], small_send.at[j], small_recv.at[me], shards[j]
        ).start()
    rel_full[me] = rel[...]
    small_full[me] = small[...]

    def slice_of(piece, shard, owner):
        return pieces[piece].at[shard, pl.ds(pl.multiple_of(owner % 8 * part, 16), part)]

    def copy_of(piece, shard, owner, recv_sem, device):
        ref = slice_of(piece, shard, owner)
        return remote(ref, ref, send_sem.at[piece], recv_sem, (device, me))

    order = []
    for j in range(others):
        pick = 0
        for m in range(groups):
            nearest = sorted((t for t in range(groups) if t != m), key=lambda t: abs(t - m))
            pick = pick + jnp.where(me == m, nearest[j], 0)
        order.append(pick)

    def right_copy(piece, shard, src=None):
        dst = slice_of(piece, shard, dp)
        return remote(
            dst if src is None else src,
            dst,
            right_send.at[piece, shard],
            z_sem.at[piece, shard],
            (dp, (me + 1) % groups),
        )

    def left_copy(piece, shard, src=None):
        dst = slice_of(piece, shard, dp)
        return remote(
            dst if src is None else src,
            dst,
            left_send.at[piece, shard],
            z_sem.at[piece, shard],
            (dp, (me + groups - 1) % groups),
        )

    alone = count - 2
    waves = [piece for piece in range(count) if piece != alone]
    wave_count = len(waves)

    def part_copy(step, shard, device, sems, src=None):
        dst = slice_of(alone, shard, 2 * step + dp % 2)
        return remote(
            dst if src is None else src,
            dst,
            sems.at[step, shard],
            part_sem.at[step, shard],
            (dp, device),
        )

    def part_send(step):
        at = pl.ds(pl.multiple_of((2 * step + dp % 2) * part, 16), part)
        src = holds[alone].at[at]

        @pl.when(me + 1 < groups)
        def _():
            part_copy(step, me, (me + 1) % groups, part_right, src).start()

        @pl.when(me > 0)
        def _():
            part_copy(step, me, (me + groups - 1) % groups, part_left, src).start()

    def part_stage(step, shard):
        part_copy(step, shard, me, part_right).wait_recv()

        @pl.when(jnp.logical_and(shard < me, me + 1 < groups))
        def _():
            part_copy(step, shard, (me + 1) % groups, part_right).start()

        @pl.when(jnp.logical_and(shard > me, me > 0))
        def _():
            part_copy(step, shard, (me + groups - 1) % groups, part_left).start()

        ref = slice_of(alone, shard, 2 * step + dp % 2)
        remote(ref, ref, send_sem.at[alone], sib_sem.at[alone], (sib, me)).start()

    def z_send(piece):
        src = holds[piece].at[pl.ds(pl.multiple_of(dp % 8 * part, 16), part)]

        @pl.when(me + 1 < groups)
        def _():
            right_copy(piece, me, src).start()

        @pl.when(me > 0)
        def _():
            left_copy(piece, me, src).start()

    diagonal = neighbours(along_x)[2]

    def stage_a(piece, shards_now):
        for shard in shards_now:
            copy_of(piece, shard, dp, z_sem.at[piece, shard], dp).wait_recv()

            @pl.when(jnp.logical_and(shard < me, me + 1 < groups))
            def _():
                right_copy(piece, shard).start()

            @pl.when(jnp.logical_and(shard > me, me > 0))
            def _():
                left_copy(piece, shard).start()

            copy_of(piece, shard, dp, x_sem.at[piece, shard], along_x).start()
            copy_of(piece, shard, dp, y_sem.at[piece, shard], along_y).start()
            copy_of(piece, shard, dp, sib_sem.at[piece], sib).start()

    def stage_b(piece, shards_now):
        for shard in shards_now:
            route = (piece + shard) % 2
            copy_of(piece, shard, along_x, x_sem.at[piece, shard], dp).wait_recv()
            copy_of(piece, shard, along_y, y_sem.at[piece, shard], dp).wait_recv()
            owner = route * along_x + (1 - route) * along_y
            target = route * along_y + (1 - route) * along_x
            copy_of(piece, shard, owner, d_sem.at[piece, shard], target).start()
            copy_of(piece, shard, along_x, sib_sem.at[piece], sib).start()
            copy_of(piece, shard, along_y, sib_sem.at[piece], sib).start()

    def stage_c(piece, shards_now):
        for shard in shards_now:
            copy_of(piece, shard, diagonal, d_sem.at[piece, shard], dp).wait_recv()
            copy_of(piece, shard, diagonal, sib_sem.at[piece], sib).start()

    writes = []
    for piece in range(count):
        for copy in pending[piece]:
            copy.wait()
        copy = pltpu.make_async_copy(holds[piece], pieces[piece].at[me], write_sem.at[piece])
        copy.start()
        writes.append(copy)
        if piece < AHEAD:
            z_send(piece)

    def complete(piece):
        writes[piece].wait()
        got = pieces[piece].at[pl.ds(0, others), pl.ds(0, 4 * part)]
        remote(got, got, send_sem.at[piece], sib_sem.at[piece], (sib, me)).wait_recv()

    def weight_loads(piece):
        width = pieces[piece].shape[2]
        return [
            pltpu.make_async_copy(
                pieces[piece].at[shard],
                weight_hold.at[piece % 2, pl.ds(shard * rows, rows), pl.ds(0, width)],
                weight_sem.at[piece % 2, shard],
            )
            for shard in range(groups)
        ]

    def start_weight(piece):
        for copy in weight_loads(piece):
            copy.start()

    def wait_weight(piece):
        for copy in weight_loads(piece):
            copy.wait()

    def wait_smalls():
        for j in range(others):
            shard = (me + 1 + j) % groups
            remote(
                rel, rel_full.at[shard], rel_send.at[j], rel_recv.at[shard], shards[j]
            ).wait()
            remote(
                small, small_full.at[shard], small_send.at[j], small_recv.at[shard], shards[j]
            ).wait()

    length = inputs.shape[0]
    block_rows = 128
    tile = 512
    per_row = rows // 128
    token_total = length * 8 * blocks * groups

    def by_rows(fn):
        def row_body(i, carry):
            fn(pl.ds(pl.multiple_of(i * block_rows, block_rows), block_rows))
            return carry

        lax.fori_loop(0, length // block_rows, row_body, 0)

    def local_sums():
        stats[...] = jnp.zeros_like(stats)
        lanes = columns // 128

        def rows_fn(at):
            value = inputs[at, :].astype(jnp.float32)
            total = jnp.sum(value, 0, keepdims=True)
            square = jnp.sum(value * value, 0, keepdims=True)
            for j in range(lanes):
                stats[j : j + 1, :] += total[:, j * 128 : (j + 1) * 128]
                stats[lanes + j : lanes + j + 1, :] += square[:, j * 128 : (j + 1) * 128]

        by_rows(rows_fn)

    def unpack():
        for row in range(9):
            for shard in range(groups):
                for j in range(per_row):
                    at = shard * rows + j * 128
                    source = row * per_row + j
                    params[row : row + 1, at : at + 128] = small_full[
                        shard, source : source + 1, :
                    ]
        lanes = columns // 128
        for j in range(lanes):
            centre = stat_total[j : j + 1, :] / token_total
            square = stat_total[lanes + j : lanes + j + 1, :] / token_total
            params[9:10, j * 128 : (j + 1) * 128] = centre
            params[10:11, j * 128 : (j + 1) * 128] = lax.rsqrt(
                square - centre * centre + EPSILON
            )
        for shard in range(groups):
            for j in range(2 * per_row):
                source = 9 * per_row + j
                at = (shard * 2 * per_row + j) * 128
                params[13 + at // columns : 14 + at // columns, at % columns : at % columns + 128] = (
                    small_full[shard, source : source + 1, :]
                )
        taken = (9 * rows + 2 * rows) // 128
        for side in range(2):
            for shard in range(groups):
                params[11 + side : 12 + side, shard * 128 : (shard + 1) * 128] = small_full[
                    shard, taken + side : taken + side + 1, :
                ]

    def activate():
        def rows_fn(at):
            standard = (inputs[at, :].astype(jnp.float32) - params[9:10, :]) * params[10:11, :]
            act_ref[at, :] = jax.nn.gelu(standard * params[0:1, :] + params[3:4, :]).astype(
                act_ref.dtype
            )

        by_rows(rows_fn)

    result_of = [
        act_ref,
        total_ref,
        norm_ref,
        content_ref,
        position_ref,
        key_ref,
        value_ref,
        table_ref.at[1],
        probs_ref,
        attended_ref,
        total_ref,
        norm_ref,
        shifted_ref,
        act_ref,
        attended_ref,
        norm_ref,
    ]

    def write_result(index):
        return pltpu.make_async_copy(result_of[index], results[index], result_sem.at[index])

    def write_pre(half):
        at = pl.ds(half * columns, columns)
        return pltpu.make_async_copy(loss_ref, pre_out.at[:, at], result_sem.at[16 + half])

    def shift_tap(tap):
        move = tap - 2

        def column_body(i, carry):
            at = pl.ds(pl.multiple_of(i * rows, 128), rows)
            value = act_ref[:, at].astype(jnp.float32)
            value = pltpu.roll(value, -move % length, 0)
            row = lax.broadcasted_iota(jnp.int32, value.shape, 0)
            inside = row < length - move if move > 0 else row >= -move
            shifted_ref[:, at] = jnp.where(inside, value, 0.0).astype(shifted_ref.dtype)
            return carry

        lax.fori_loop(0, columns // rows, column_body, 0)

    def conv_tap(tap, i):
        at = pl.ds(pl.multiple_of(i * tile, 128), tile)
        left = act_ref if tap == 2 else shifted_ref
        value = jnp.dot(
            left[...], weight_hold[tap % 2, :, at], preferred_element_type=jnp.float32
        )
        if tap == 0:
            value = value + (inputs[:, at].astype(jnp.float32) + params[4:5, at])
        else:
            value = value + total_ref[:, at]
        total_ref[:, at] = value

    def norm_step(gain, bias):
        def rows_fn(at):
            standard, _ = normalize(total_ref[at, :])
            norm_ref[at, :] = (
                standard * params[gain : gain + 1, :] + params[bias : bias + 1, :]
            ).astype(norm_ref.dtype)

        by_rows(rows_fn)

    def query_step():
        raw = jnp.dot(
            norm_ref[...], weight_hold[1, :, 0:width], preferred_element_type=jnp.float32
        )
        raw = raw * KEY**-0.5
        content_ref[...] = (raw + params[11:12, 0:width]).astype(content_ref.dtype)
        position_ref[...] = (raw + params[12:13, 0:width]).astype(position_ref.dtype)

    def key_step():
        key_ref[...] = jnp.dot(
            norm_ref[...], weight_hold[1, :, width : 2 * width], preferred_element_type=jnp.float32
        ).astype(key_ref.dtype)

    def table_step():
        for side in range(2):
            for shard in range(groups):
                table_ref[side, :, shard * 128 : (shard + 1) * 128] = jnp.dot(
                    tables[side], rel_full[shard], preferred_element_type=jnp.float32
                ).astype(table_ref.dtype)

    def value_step(i):
        at = pl.ds(pl.multiple_of(i * tile, 128), tile)
        value_ref[:, at] = jnp.dot(
            norm_ref[...], weight_hold[0, :, at], preferred_element_type=jnp.float32
        ).astype(value_ref.dtype)

    def head_step(index, side):
        head_value = columns // HEADS
        span = tables.shape[1]
        pair = pl.ds(pl.multiple_of(index * 2 * KEY, 128), 2 * KEY)
        value_pair = pl.ds(pl.multiple_of(index * 2 * head_value, 128), 2 * head_value)
        keys = slice(side * KEY, (side + 1) * KEY)
        band = dot_trailing(position_ref[:, pair][:, keys], table_ref[0, :, pair][:, keys])
        moved = pltpu.roll(band, span - length + 1, 1, stride=1, stride_axis=0)
        scores = dot_trailing(content_ref[:, pair][:, keys], key_ref[:, pair][:, keys])
        scores = scores + moved[:, :length]
        weight = jnp.exp(scores - jnp.max(scores, -1, keepdims=True))
        probs = (weight / jnp.sum(weight, -1, keepdims=True)).astype(probs_ref.dtype)
        probs_ref[2 * index + side] = probs
        chosen = value_ref[:, value_pair][:, side * head_value : (side + 1) * head_value]
        return jnp.dot(probs, chosen, preferred_element_type=jnp.float32)

    def pair_step(index):
        both = [head_step(index, side).astype(attended_ref.dtype) for side in range(2)]
        wide = 2 * columns // HEADS
        attended_ref[:, pl.ds(pl.multiple_of(index * wide, 128), wide)] = jnp.concatenate(both, 1)

    def out_step(i):
        at = pl.ds(pl.multiple_of(i * tile, 128), tile)
        value = jnp.dot(
            attended_ref[...], weight_hold[1, :, at], preferred_element_type=jnp.float32
        )
        total_ref[:, at] = total_ref[:, at] + value + params[6:7, at]

    def make_tables():
        features = rel.shape[0]
        basis = features // 6
        span = tables.shape[1]
        row = lax.broadcasted_iota(jnp.int32, (span, features), 0)
        column = lax.broadcasted_iota(jnp.int32, (span, features), 1)
        offset = row - (length - 1)
        whole = jnp.abs(offset)
        distance = whole.astype(jnp.float32)
        order_at = column % basis
        index = order_at.astype(jnp.float32)
        ratio = index / (basis - 1)
        half_life = jnp.exp2(3.0 + (math.log2(length) - 3.0) * ratio)
        decaying = jnp.exp(-math.log(2.0) / half_life * distance)
        limit = lax.shift_left(jnp.ones_like(order_at), jnp.minimum(order_at + 1, 16)) - 1
        central = jnp.where(limit > whole, 1.0, 0.0)
        stddev = length / (2.0 * basis)
        centres = length / basis + (length - length / basis) * ratio
        shape_par = (centres / stddev) * (centres / stddev)
        rate_par = centres / (stddev * stddev)
        safe = jnp.maximum(distance, 1.0)
        score = (shape_par - 1.0) * jnp.log(safe) - rate_par * safe
        peak = jnp.max(jnp.where(whole < length, score, -jnp.inf), 0, keepdims=True)
        gamma = jnp.where(whole > 0, jnp.exp(score - peak), 0.0)
        kind = column // basis % 3
        value = jnp.where(kind == 0, decaying, jnp.where(kind == 1, central, gamma))
        value = jnp.where(whole < length, value, 0.0)
        flipped = column >= 3 * basis
        for side in range(2):
            signed = offset if side == 0 else -offset
            sign = jnp.where(signed > 0, 1.0, jnp.where(signed < 0, -1.0, 0.0))
            tables[side] = jnp.where(flipped, value * sign, value).astype(tables.dtype)

    halves = [shifted_ref, act_ref]

    def up_step(half, i):
        at = pl.ds(pl.multiple_of(i * tile, 128), tile)
        value = jnp.dot(
            norm_ref[...], weight_hold[half, :, at], preferred_element_type=jnp.float32
        )
        value = value + params[13 + half : 14 + half, at]
        loss_ref[:, at] = value
        halves[half][:, at] = jax.nn.gelu(value).astype(act_ref.dtype)

    def down_step(half, i):
        at = pl.ds(pl.multiple_of(i * tile, 128), tile)
        value = total_ref[:, at]
        for shard in range(groups):
            source = (2 * shard + half) * rows
            left = halves[source // columns][:, source % columns : source % columns + rows]
            value = value + jnp.dot(
                left,
                weight_hold[half, shard * rows : (shard + 1) * rows, at],
                preferred_element_type=jnp.float32,
            )
        if half == 0:
            total_ref[:, at] = value + params[8:9, at]
        else:
            attended_ref[:, at] = value.astype(attended_ref.dtype)
            limit = limits[:, 0:1]
            norm_ref[:, at] = jnp.clip(value - target[0:1, at], -limit, limit).astype(
                norm_ref.dtype
            )

    def over_tiles(fn):
        def tile_body(i, carry):
            fn(i)
            return carry

        lax.fori_loop(0, columns // tile, tile_body, 0)

    def over_pairs(first):
        def pair_body(i, carry):
            pair_step(i)
            return carry

        lax.fori_loop(first, first + 2, pair_body, 0)


    def compute_list(n):
        if n == 2:
            return [wait_smalls, unpack, activate, make_tables, lambda: write_result(0).start()]
        piece = n - 3
        if 0 <= piece < 5:
            work = [functools.partial(wait_weight, piece)]
            if piece != 2:
                work.append(functools.partial(shift_tap, piece))
            work += [functools.partial(over_tiles, functools.partial(conv_tap, piece))]
            return work
        if piece == 5:
            return [
                lambda: write_result(1).start(),
                functools.partial(norm_step, 1, 5),
                lambda: write_result(2).start(),
                table_step,
                lambda: write_result(7).start(),
                functools.partial(wait_weight, piece),
                query_step,
                key_step,
                lambda: [write_result(i).start() for i in (3, 4, 5)],
            ]
        if piece == 6:
            work = [functools.partial(wait_weight, piece)]
            work += [functools.partial(over_tiles, value_step)]
            return work + [lambda: write_result(6).start(), functools.partial(over_pairs, 0)]
        if piece == 7:
            work = [functools.partial(over_pairs, 2)]
            work += [lambda: [write_result(i).start() for i in (8, 9)]]
            work += [functools.partial(wait_weight, piece), lambda: write_result(1).wait()]
            work += [functools.partial(over_tiles, out_step)]
            work += [lambda: write_result(10).start(), lambda: write_result(2).wait()]
            return work + [
                functools.partial(norm_step, 2, 7),
                lambda: write_result(11).start(),
                lambda: write_result(0).wait(),
            ]
        if piece in (8, 9):
            half = piece - 8
            work = [functools.partial(wait_weight, piece)]
            if half == 1:
                work.append(lambda: write_pre(0).wait())
            work += [functools.partial(over_tiles, functools.partial(up_step, half))]
            work.append(lambda: [write_pre(half).start(), write_result(12 + half).start()])
            return work
        if piece in (10, 11):
            half = piece - 10
            work = [functools.partial(wait_weight, piece)]
            if half == 0:
                work.append(lambda: write_result(10).wait())
            else:
                work.append(lambda: [write_result(i).wait() for i in (9, 11)])
            work += [functools.partial(over_tiles, functools.partial(down_step, half))]
            if half == 1:
                work.append(lambda: [write_result(i).start() for i in (14, 15)])
            return work
        return []

    def send_list(n):
        work = []
        if n + AHEAD < wave_count:
            work.append(functools.partial(z_send, waves[n + AHEAD]))
        if n in (0, 2, 4, 6):
            work.append(functools.partial(part_send, n // 2))
        for shard in order:
            if n < wave_count:
                work.append(functools.partial(stage_a, waves[n], [shard]))
            if 1 <= n <= wave_count:
                work.append(functools.partial(stage_b, waves[n - 1], [shard]))
            if 2 <= n < wave_count + 2:
                work.append(functools.partial(stage_c, waves[n - 2], [shard]))
            if n in (2, 4, 6, 8):
                work.append(functools.partial(part_stage, n // 2 - 1, shard))
        return work

    local_sums()
    for step in summing[:4]:
        step()

    for n in range(count):
        sends = send_list(n)
        work = compute_list(n)
        if 0 <= n - 3 < wave_count - 2:
            complete(waves[n - 3])
            start_weight(waves[n - 3])
        slots = max(len(work), 1)
        for i in range(slots):
            for send in sends[len(sends) * i // slots : len(sends) * (i + 1) // slots]:
                send()
            if i < len(work):
                work[i]()
        if n < 2:
            summing[4 + n]()
    for piece in (alone - 1, alone):
        complete(piece)
        start_weight(piece)
    for work in compute_list(alone + 2) + send_list(count) + compute_list(alone + 3):
        work()
    complete(count - 1)
    start_weight(count - 1)
    for work in compute_list(count + 2):
        work()

    for index in (3, 4, 5, 6, 7, 8, 12, 13, 14, 15):
        write_result(index).wait()
    write_pre(1).wait()

    for step in range(4):
        for shard in range(groups):

            @pl.when(jnp.logical_and(shard <= me, me + 1 < groups))
            def _():
                part_copy(step, shard, (me + 1) % groups, part_right).wait_send()

            @pl.when(jnp.logical_and(shard >= me, me > 0))
            def _():
                part_copy(step, shard, (me + groups - 1) % groups, part_left).wait_send()

    sent = pieces[alone].at[pl.ds(0, others), pl.ds(0, 4 * part)]
    remote(sent, sent, send_sem.at[alone], sib_sem.at[alone], (sib, me)).wait_send()
    for piece in waves:
        for shard in range(groups):

            @pl.when(jnp.logical_and(shard <= me, me + 1 < groups))
            def _():
                right_copy(piece, shard).wait_send()

            @pl.when(jnp.logical_and(shard >= me, me > 0))
            def _():
                left_copy(piece, shard).wait_send()

        sent = pieces[piece].at[pl.ds(0, others), pl.ds(0, 7 * part)]
        remote(sent, sent, send_sem.at[piece], sib_sem.at[piece], (sib, me)).wait_send()


def gather(groups, blocks, weights, small, inputs, target, limits):
    conv, query = weights[:2]
    rel = weights[7]
    taps, rows, columns = conv.shape
    width = query.shape[1]
    length = inputs.shape[0]
    span = 2 * length
    stats_shape = (2 * columns // 128, 128)
    dtype = conv.dtype
    kept = pl.BlockSpec(memory_space=pl.ANY)
    inside = pl.BlockSpec(memory_space=pltpu.VMEM)
    full = jax.ShapeDtypeStruct((groups, rows, columns), dtype)
    count = taps + 7
    grid_sems = [pltpu.SemaphoreType.DMA((count, groups))] * 4
    wide = (length, columns)
    narrow = (length, width)
    made = [
        jax.ShapeDtypeStruct(wide, dtype),
        jax.ShapeDtypeStruct(wide, jnp.float32),
        jax.ShapeDtypeStruct(wide, dtype),
        jax.ShapeDtypeStruct(narrow, dtype),
        jax.ShapeDtypeStruct(narrow, dtype),
        jax.ShapeDtypeStruct(narrow, dtype),
        jax.ShapeDtypeStruct(wide, dtype),
        jax.ShapeDtypeStruct((span, width), dtype),
        jax.ShapeDtypeStruct((HEADS, length, length), dtype),
        jax.ShapeDtypeStruct(wide, dtype),
        jax.ShapeDtypeStruct(wide, jnp.float32),
        jax.ShapeDtypeStruct(wide, dtype),
        jax.ShapeDtypeStruct((length, 2 * columns), jnp.float32),
        jax.ShapeDtypeStruct((length, 2 * columns), dtype),
        jax.ShapeDtypeStruct(wide, dtype),
        jax.ShapeDtypeStruct(wide, dtype),
    ]
    return pl.pallas_call(
        functools.partial(gather_kernel, groups, blocks),
        out_shape=(
            jax.ShapeDtypeStruct((taps, groups, rows, columns), dtype),
            jax.ShapeDtypeStruct((groups, rows, 2 * width), dtype),
            full,
            full,
            jax.ShapeDtypeStruct((groups, rows, 2 * columns), dtype),
            jax.ShapeDtypeStruct((groups, 2 * rows, columns), dtype),
            jax.ShapeDtypeStruct((groups,) + rel.shape, dtype),
            jax.ShapeDtypeStruct((groups,) + small.shape, jnp.float32),
            jax.ShapeDtypeStruct(stats_shape, jnp.float32),
            *made,
            jax.ShapeDtypeStruct((2, span, rel.shape[0]), dtype),
            jax.ShapeDtypeStruct((16, columns), jnp.float32),
        ),
        in_specs=[kept] * 7 + [inside] * 5,
        out_specs=[kept] * 6 + [inside] * 3 + [kept] * len(made) + [inside] * 2,
        scratch_shapes=[
            pltpu.VMEM((count - 1, rows, columns), dtype),
            pltpu.VMEM((rows, 2 * width), dtype),
            pltpu.SemaphoreType.DMA((taps + 8,)),
            pltpu.SemaphoreType.DMA((count,)),
            *grid_sems,
            pltpu.SemaphoreType.DMA((count,)),
            pltpu.SemaphoreType.DMA((count,)),
            *grid_sems[:2],
            *([pltpu.SemaphoreType.DMA((groups,))] * 4),
            *sum_scratch(groups, blocks, stats_shape),
            pltpu.VMEM((2, columns, columns), dtype),
            pltpu.SemaphoreType.DMA((2, groups)),
            pltpu.SemaphoreType.DMA((len(made) + 2,)),
            pltpu.VMEM(wide, dtype),
            pltpu.VMEM(wide, jnp.float32),
            pltpu.VMEM(wide, dtype),
            pltpu.VMEM(wide, dtype),
            pltpu.VMEM(narrow, dtype),
            pltpu.VMEM(narrow, dtype),
            pltpu.VMEM(narrow, dtype),
            pltpu.VMEM(wide, dtype),
            pltpu.VMEM((2, span, width), dtype),
            pltpu.VMEM((HEADS, length, length), dtype),
            pltpu.VMEM(wide, dtype),
            pltpu.VMEM(stats_shape, jnp.float32),
            pltpu.VMEM(wide, jnp.float32),
            *([pltpu.SemaphoreType.DMA((4, groups))] * 3),
        ],
        compiler_params=pltpu.CompilerParams(
            collective_id=0, has_side_effects=True, vmem_limit_bytes=60 << 20
        ),
        name="gather",
    )(*weights, small, inputs, target, limits)


def gelu_slope(value):
    inner = GELU * (value + 0.044715 * value * value * value)
    curve = jnp.tanh(inner)
    slope = GELU * (1.0 + 3 * 0.044715 * value * value)
    return 0.5 * (1.0 + curve) + 0.5 * value * (1.0 - curve * curve) * slope


def reduce_kernel(groups, blocks, rel_at, *refs):
    lefts = refs[:5]
    cotangent, hidden_pre, after_attention, after_conv, tokens = refs[5:10]
    down_full, up_full, out_full, value_full, mixed_full, conv_full = refs[10:16]
    probs, values, keys, contents, positions, mirrored_keys = refs[16:22]
    params, table = refs[22:24]
    out, total, part_grad = refs[24:27]
    made = refs[27:32]
    hidden_got, left_got, right_got = refs[32:35]
    rights = [cotangent, *made]
    (
        left_hold,
        right_hold,
        grad,
        x_one,
        y_one,
        x_two,
        y_two,
        shard_got,
        block_got,
        done,
        rel_grad,
        rel_got,
        vector,
    ) = refs[35:48]
    left_send, left_recv, right_send, right_recv, rel_send, rel_recv = refs[48:54]
    load_sem = refs[54]
    x1s, y1s, x2s, y2s, x1r, y1r, x2r, y2r = refs[55:63]
    shard_send, shard_recv, block_send, block_recv = refs[63:67]
    write_sem, send_sem, ax, ay, ad, sib_sem = refs[67:73]
    sum_bufs = refs[73:77]
    sum_sems = refs[77:83]
    credit, shard_credit = refs[83:85]
    (
        attn_grad,
        total_ref,
        kept_ref,
        weight_hold,
        wide_hold,
        right_ref,
        value_grad_ref,
        mixed_ref,
        key_ref,
        content_ref,
        position_ref,
        table_ref,
        table_grad_ref,
        probs_ref,
    ) = refs[85:99]
    tile_sem, host_sem, probs_sem, kept_sem = refs[99:103]
    slab, slab_got, x_slab, y_slab, x_part, y_part, slab_credit = refs[103:110]

    dp = lax.axis_index("dp")
    me = lax.axis_index("fsdp")
    near, shards, far = peers_of(groups, blocks)
    sib, along_x, along_y = neighbours(dp)
    core = dp % 2
    at_x = dp // 2 % 2
    at_y = dp // 4 % 2
    block = dp // 8
    slots = grad.shape[0]
    part = grad.shape[4]
    width = grad.shape[5]
    half = width // 2
    rows = 4 * part
    count = out.shape[0]
    others = groups - 1
    first = pl.ds(0, half)
    last = pl.ds(half, half)
    taps = 5
    up_right = rights[1]
    rights[1:2] = [up_right.at[:, pl.ds(side * 2 * width, 2 * width)] for side in range(2)]
    lefts_got = [hidden_got] + [left_got.at[index] for index in range(4)]
    left_of = [0, 1, 1, 2, 3, 3, 4, 4, 4, 4, 0, 4]
    right_of = [0, 1, 2, 3, 4, 5, 6, 6, 6, 6, 0, 6]
    sequence = [0, 10, 1, 2, 3, 4, 5, 6, 11, 7, 8, 9]
    tap_of = {6: 0, 7: 1, 8: 2, 9: 3, 11: 4}
    mixed_piece = 5
    normal = 10
    extra_at = {0: 10, 6: 11}
    own_columns = pl.ds(pl.multiple_of(core * width, 128), width)
    sib_columns = pl.ds(pl.multiple_of((1 - core) * width, 128), width)

    def left_copy(index):
        return remote(
            lefts[index], lefts_got[index], left_send.at[index], left_recv.at[index], (sib, me)
        )

    def right_copy(index):
        return remote(
            rights[index].at[:, sib_columns],
            right_got.at[index],
            right_send.at[index],
            right_recv.at[index],
            (sib, me),
        )

    def rel_copy():
        return remote(rel_grad, rel_got, rel_send.at[0], rel_recv.at[0], (sib, me))

    def loads(piece):
        left = left_of[piece]
        right = right_of[piece]
        pairs = [
            (rights[right].at[:, own_columns], right_hold.at[0]),
            (right_got.at[right], right_hold.at[1]),
        ]
        if left > 0:
            pairs.append((lefts[left], left_hold.at[0]))
            pairs.append((lefts_got[left], left_hold.at[1]))
        else:
            for shard in range(groups):
                source = pl.ds((2 * shard + piece // normal) * rows, rows)
                target = pl.ds(shard * rows, rows)
                pairs.append((lefts[left].at[:, source], left_hold.at[0, :, target]))
                pairs.append((lefts_got[left].at[:, source], left_hold.at[1, :, target]))
        return [
            pltpu.make_async_copy(src, dst, load_sem.at[i]) for i, (src, dst) in enumerate(pairs)
        ]

    def start_loads(piece):
        before = sequence[: sequence.index(piece)]
        if left_of[piece] not in [left_of[other] for other in before]:
            left_copy(left_of[piece]).wait_recv()
        if right_of[piece] not in [right_of[other] for other in before]:
            right_copy(right_of[piece]).wait_recv()
        for copy in loads(piece):
            copy.start()

    def wait_loads(piece):
        for copy in loads(piece):
            copy.wait()
        if tap_of.get(piece, 2) != 2:
            shift(tap_of[piece] - taps // 2)

    meet(near + shards + far)

    for index in range(len(lefts)):
        left_copy(index).start()
        if index == 0:
            right_copy(0).start()
    start_loads(0)

    summing = sum_steps(groups, blocks, vector, total, *sum_bufs, sum_sems)

    ring = x_one.shape[0]

    def pay(piece, index, device):
        @pl.when(piece < normal - ring)
        def _():
            pl.semaphore_signal(
                credit.at[index], inc=1, device_id=(device, me), device_id_type=MESH
            )

    def claim(piece, index):
        @pl.when(piece >= ring)
        def _():
            pl.semaphore_wait(credit.at[index], 1)

    def one(piece):
        slot = piece % slots
        return (
            remote(
                grad.at[slot, :, :, 1 - at_x, :, first],
                x_one.at[piece % ring],
                x1s.at[piece],
                x1r.at[piece],
                (along_x, me),
            ),
            remote(
                grad.at[slot, :, 1 - at_y, :, :, last],
                y_one.at[piece % ring],
                y1s.at[piece],
                y1r.at[piece],
                (along_y, me),
            ),
        )

    def two(piece):
        slot = piece % slots
        return (
            remote(
                grad.at[slot, :, 1 - at_y, at_x, :, first],
                y_two.at[piece % ring],
                y2s.at[piece],
                y2r.at[piece],
                (along_y, me),
            ),
            remote(
                grad.at[slot, :, at_y, 1 - at_x, :, last],
                x_two.at[piece % ring],
                x2s.at[piece],
                x2r.at[piece],
                (along_x, me),
            ),
        )

    def shard_copy(piece, j):
        other = (me + 1 + j) % groups
        return remote(
            grad.at[piece % slots, other, at_y, at_x],
            shard_got.at[piece % ring, me],
            shard_send.at[piece, j],
            shard_recv.at[piece, me],
            (dp, other),
        )

    def shard_arrival(piece, j):
        other = (me + 1 + j) % groups
        return remote(
            grad.at[piece % slots, other, at_y, at_x],
            shard_got.at[piece % ring, other],
            shard_send.at[piece, j],
            shard_recv.at[piece, other],
            (dp, other),
        )

    def block_copy(piece, j):
        return remote(
            done.at[piece],
            block_got.at[piece, block],
            block_send.at[piece, j],
            block_recv.at[piece, block],
            far[j],
        )

    def block_arrival(piece, j):
        other = (block + 1 + j) % blocks
        return remote(
            done.at[piece],
            block_got.at[piece, other],
            block_send.at[piece, j],
            block_recv.at[piece, other],
            far[j],
        )

    def place(piece, owner):
        return out.at[
            piece,
            pl.ds(pl.multiple_of(owner % 8 // 2 * part, 16), part),
            pl.ds(pl.multiple_of(core * width, 128), width),
        ]

    def spread(piece, src, owner, recv_sem, device):
        return remote(src, place(piece, owner), send_sem.at[piece], recv_sem, (device, me))

    def forward(piece, owner, recv_sem, device):
        return spread(piece, place(piece, owner), owner, recv_sem, device)

    diagonal = neighbours(along_x)[2]

    def shift(move):
        for window in range(2):
            value = right_hold[window].astype(jnp.float32)
            value = pltpu.roll(value, move % value.shape[0], 0)
            row = lax.broadcasted_iota(jnp.int32, value.shape, 0)
            inside = row >= move if move > 0 else row < value.shape[0] + move
            value = jnp.where(inside, value, 0.0)
            right_hold[window] = value.astype(right_hold.dtype)

    def product(shard):
        at = pl.ds(pl.multiple_of(shard * rows, 128), rows)
        value = dot_leading(left_hold[0, :, at], right_hold[0])
        value = value + dot_leading(left_hold[1, :, at], right_hold[1])
        return value.astype(grad.dtype).reshape(2, 2, part, width)

    def produce(piece):
        slot = piece % slots

        def shard_body(shard, carry):
            grad[slot, shard] = product(shard)
            return carry

        lax.fori_loop(0, groups, shard_body, 0)

        @pl.when(piece == mixed_piece)
        def _():
            rel_copy().wait()

        @pl.when(jnp.logical_and(piece == mixed_piece, core == 1))
        def _():
            for shard in range(groups):
                value = rel_grad[shard].astype(jnp.float32) + rel_got[shard].astype(jnp.float32)
                grad[slot, shard, 0, :, :, pl.ds(rel_at, rel_grad.shape[3])] = value.astype(
                    grad.dtype
                )

    def slab_copy(piece, j, arriving=False):
        other = (me + 1 + j) % groups
        at = j if arriving else groups - 2 - j
        return remote(
            slab.at[other],
            slab_got.at[at],
            shard_send.at[piece, j],
            shard_recv.at[piece, at],
            (dp, other),
        )

    def slab_one(piece, e):
        return (
            remote(
                slab.at[me, :, 1 - at_x, :, first],
                x_slab.at[e],
                x1s.at[piece],
                x1r.at[piece],
                (along_x, me),
            ),
            remote(
                slab.at[me, 1 - at_y, :, :, last],
                y_slab.at[e],
                y1s.at[piece],
                y1r.at[piece],
                (along_y, me),
            ),
        )

    def slab_two(piece, e):
        return (
            remote(
                slab.at[me, 1 - at_y, at_x, :, first],
                y_part.at[e],
                y2s.at[piece],
                y2r.at[piece],
                (along_y, me),
            ),
            remote(
                slab.at[me, at_y, 1 - at_x, :, last],
                x_part.at[e],
                x2s.at[piece],
                x2r.at[piece],
                (along_x, me),
            ),
        )

    def slab_sent(piece, e):
        for j in range(others):
            slab_copy(piece, j).wait_send()
        for copy in slab_one(piece, e) + slab_two(piece, e):
            copy.wait_send()

    def extra_start(piece, e):
        start_loads(piece)
        if e > 0:
            slab_sent(piece - 1, e - 1)
        wait_loads(piece)

        def shard_body(shard, carry):
            slab[shard] = product(shard)
            return carry

        lax.fori_loop(0, groups, shard_body, 0)
        for j in range(others):
            if e > 0:
                pl.semaphore_wait(slab_credit.at[(me + 1 + j) % groups], 1)
            slab_copy(piece, j).start()

    def extra_sum(piece, e):
        for j in range(others):
            slab_copy(piece, j, True).wait_recv()
        for y in range(2):
            for x in range(2):
                value = slab[me, y, x].astype(jnp.float32)
                for j in range(others):
                    value = value + slab_got[j, y, x].astype(jnp.float32)
                slab[me, y, x] = value.astype(slab.dtype)
        if e == 0:
            for j in range(others):
                pl.semaphore_signal(
                    slab_credit.at[me], inc=1, device_id=shards[j], device_id_type=MESH
                )
        for copy in slab_one(piece, e):
            copy.start()

    def extra_fold(piece, e):
        for copy in slab_one(piece, e):
            copy.wait_recv()
        for other in range(2):
            value = slab[me, other, at_x, :, first].astype(jnp.float32)
            value = value + x_slab[e, other].astype(jnp.float32)
            slab[me, other, at_x, :, first] = value.astype(slab.dtype)
            value = slab[me, at_y, other, :, last].astype(jnp.float32)
            value = value + y_slab[e, other].astype(jnp.float32)
            slab[me, at_y, other, :, last] = value.astype(slab.dtype)
        for copy in slab_two(piece, e):
            copy.start()

    def extra_done(piece, e):
        for copy in slab_two(piece, e):
            copy.wait_recv()
        low = slab[me, at_y, at_x, :, first].astype(jnp.float32)
        high = slab[me, at_y, at_x, :, last].astype(jnp.float32)
        low = low + y_part[e].astype(jnp.float32)
        high = high + x_part[e].astype(jnp.float32)
        finish(piece, jnp.concatenate([low, high], 1))

    def finish(piece, value):
        if blocks > 1:
            done[piece] = value.astype(done.dtype)
            block_got[piece, block] = value.astype(done.dtype)
            for j in range(blocks - 1):
                block_copy(piece, j).start()
            for j in range(blocks - 1):
                block_copy(piece, j).wait_send()
                block_arrival(piece, j).wait_recv()
            value = block_got[piece, 0].astype(jnp.float32)
            for other in range(1, blocks):
                value = value + block_got[piece, other].astype(jnp.float32)
        done[piece] = value.astype(done.dtype)
        pltpu.make_async_copy(done.at[piece], place(piece, dp), write_sem.at[piece]).start()
        spread(piece, done.at[piece], dp, ax.at[piece], along_x).start()
        spread(piece, done.at[piece], dp, ay.at[piece], along_y).start()
        spread(piece, done.at[piece], dp, sib_sem.at[piece], sib).start()

    def cross(piece):
        route = piece % 2
        forward(piece, along_x, ax.at[piece], dp).wait_recv()
        forward(piece, along_y, ay.at[piece], dp).wait_recv()
        owner = route * along_x + (1 - route) * along_y
        target = route * along_y + (1 - route) * along_x
        forward(piece, owner, ad.at[piece], target).start()
        forward(piece, along_x, sib_sem.at[piece], sib).start()
        forward(piece, along_y, sib_sem.at[piece], sib).start()

    def close(piece):
        forward(piece, diagonal, ad.at[piece], dp).wait_recv()
        forward(piece, diagonal, sib_sem.at[piece], sib).start()

    def add(piece_slot, ref, columns, *index):
        ahead = grad[(piece_slot,) + index + (slice(None), columns)]
        return ahead.astype(jnp.float32) + ref.astype(jnp.float32)

    length = tokens.shape[0]
    columns = 2 * width
    tile = 512
    block_rows = 128
    head_value = columns // HEADS
    tiles = columns // tile
    hidden_tiles = hidden_pre.shape[1] // tile

    def tile_of(phase, i):
        at = pl.ds(pl.multiple_of(i * tile, tile), tile)
        if phase == 0:
            return down_full.at[at]
        if phase == 1:
            at = pl.ds(pl.multiple_of(i // 2 * tile, tile), tile)
            return up_full.at[at, pl.ds(pl.multiple_of(i % 2 * columns, columns), columns)]
        if phase == 5:
            at = pl.ds(pl.multiple_of(i % tiles * tile, tile), tile)
            return conv_full.at[i // tiles, at]
        return (out_full, mixed_full, value_full)[phase - 2].at[at]

    lengths = [hidden_tiles, 2 * tiles, tiles, tiles, tiles, taps * tiles]
    widths = [columns, columns, columns, mixed_full.shape[1], columns, columns]

    def tile_load(phase, i):
        slot = (sum(lengths[:phase]) + i) % 2
        return pltpu.make_async_copy(
            tile_of(phase, i),
            weight_hold.at[slot, :, pl.ds(0, widths[phase])],
            tile_sem.at[slot],
        )

    def next_tile(phase, i):
        tile_load(phase, i).wait()

        @pl.when(i + 1 < lengths[phase])
        def _():
            tile_load(phase, i + 1).start()

        if phase + 1 < len(lengths):

            @pl.when(i + 1 == lengths[phase])
            def _():
                tile_load(phase + 1, 0).start()

        slot = (sum(lengths[:phase]) + i) % 2
        return weight_hold[slot, :, 0 : widths[phase]]

    def over(count, fn):
        def step_body(i, carry):
            fn(i)
            return carry

        lax.fori_loop(0, count, step_body, 0)

    def columns_at(i, wide, offset=0):
        return pl.ds(pl.multiple_of(offset + i * wide, 128), wide)

    def host_load(index):
        pairs = [
            (cotangent, right_ref),
            (after_attention, kept_ref),
            (after_conv, kept_ref),
            (values, wide_hold.at[:, pl.ds(columns, columns)]),
            (keys, key_ref),
            (contents, content_ref),
            (positions, position_ref),
            (mirrored_keys, table_ref),
            (tokens, wide_hold.at[:, pl.ds(columns, columns)]),
            (wide_hold, made[0]),
            (right_ref, made[1]),
            (value_grad_ref, made[2]),
            (mixed_ref, made[3]),
            (right_ref, made[4]),
        ]
        return pltpu.make_async_copy(*pairs[index], host_sem.at[index])

    def load(*indices):
        def thunk():
            for index in indices:
                host_load(index).start()

        return thunk

    def ready(*indices):
        def thunk():
            for index in indices:
                host_load(index).wait()

        return thunk

    def send_right(*indices):
        def thunk():
            for index in indices:
                right_copy(index).start()

        return thunk

    def pre_load(i):
        return pltpu.make_async_copy(
            hidden_pre.at[:, columns_at(i, tile)],
            kept_ref.at[:, columns_at(i % 3, tile)],
            kept_sem.at[i],
        )

    def write_part():
        return pltpu.make_async_copy(attn_grad, part_grad, kept_sem.at[hidden_tiles])

    def by_rows(fn):
        def row_body(i, carry):
            fn(pl.ds(pl.multiple_of(i * block_rows, block_rows), block_rows))
            return carry

        lax.fori_loop(0, length // block_rows, row_body, 0)

    def put(row, value):
        vector[row : row + 1, :] += jnp.sum(value, 0, keepdims=True)

    def clear_total():
        def rows_fn(at):
            total_ref[at, :] = jnp.zeros((block_rows, columns), jnp.float32)

        by_rows(rows_fn)

    def begin():
        vector[...] = jnp.zeros_like(vector)
        mixed_ref[...] = jnp.zeros_like(mixed_ref)
        tile_load(0, 0).start()
        for i in range(3):
            pre_load(i).start()
        clear_total()

    def hidden_step(i):
        value = dot_trailing(right_ref[...], next_tile(0, i))
        pre_load(i).wait()
        value = value * gelu_slope(kept_ref[:, columns_at(i % 3, tile)])

        @pl.when(i + 3 < hidden_tiles)
        def _():
            pre_load(i + 3).start()

        rounded = value.astype(wide_hold.dtype)
        wide_hold[:, columns_at(i, tile)] = rounded
        sums_here = jnp.sum(rounded.astype(jnp.float32), 0, keepdims=True)
        for side in range(2):

            @pl.when(i // tiles == side)
            def _():
                vector[9 + side : 10 + side, columns_at(i % tiles, tile)] = sums_here

    def norm_two_step(i):
        left = wide_hold[:, columns_at(i % 2, columns)]
        total_ref[:, columns_at(i // 2, tile)] += dot_trailing(left, next_tile(1, i))

    def norm_two_back():
        def rows_fn(at):
            standard, inverse = normalize(kept_ref[at, :])
            value = total_ref[at, :]
            put(2, value * standard)
            put(7, value)
            cot = right_ref[at, :].astype(jnp.float32)
            put(8, cot)
            value = cot + norm_back(value * params[2:3, :], standard, inverse)
            attn_grad[at, :] = value
            rounded = value.astype(right_ref.dtype)
            right_ref[at, :] = rounded
            put(6, rounded.astype(jnp.float32))

        by_rows(rows_fn)

    def attended_step(i):
        value = dot_trailing(right_ref[...], next_tile(2, i))
        wide_hold[:, columns_at(i, tile)] = value.astype(wide_hold.dtype)

    def probs_load(head):
        return pltpu.make_async_copy(
            probs.at[head], probs_ref.at[head % 2], probs_sem.at[head % 2]
        )

    def pair_step(index):
        span = table_ref.shape[0]
        row = lax.broadcasted_iota(jnp.int32, (length, length), 0)
        column = lax.broadcasted_iota(jnp.int32, (length, length), 1)
        mirror = jnp.where(row + column == length - 1, 1.0, 0.0).astype(jnp.bfloat16)
        pair = columns_at(index, 2 * KEY)
        key_pair = columns_at(index, 2 * KEY, key_ref.shape[1])
        value_pair = columns_at(index, 2 * head_value)
        far_pair = columns_at(index, 2 * head_value, columns)
        made_here = [[], [], [], [], [], []]
        for side in range(2):
            head = 2 * index + side
            probs_load(head).wait()
            keys_at = slice(side * KEY, (side + 1) * KEY)
            values_at = slice(side * head_value, (side + 1) * head_value)
            prob = probs_ref[side]
            out_grad = wide_hold[:, value_pair][:, values_at]
            made_here[0].append(dot_leading(prob, out_grad).astype(jnp.bfloat16))
            prob_grad = dot_trailing(out_grad, wide_hold[:, far_pair][:, values_at])
            prob = prob.astype(jnp.float32)
            row_dot = jnp.sum(prob * prob_grad, -1, keepdims=True)
            rounded = (prob * (prob_grad - row_dot)).astype(jnp.bfloat16)
            content = content_ref[:, pair][:, keys_at]
            made_here[1].append(dot_leading(rounded, content).astype(jnp.bfloat16))
            content_grad = jnp.dot(
                rounded, key_ref[:, pair][:, keys_at], preferred_element_type=jnp.float32
            )
            mirrored = jnp.dot(rounded, mirror, preferred_element_type=jnp.float32)
            wide = jnp.concatenate([mirrored, jnp.zeros((length, span - length), jnp.float32)], 1)
            band = pltpu.roll(wide, 0, 1, stride=1, stride_axis=0).astype(jnp.bfloat16)
            position_grad = jnp.dot(
                band, table_ref[:, pair][:, keys_at], preferred_element_type=jnp.float32
            )
            position = position_ref[:, pair][:, keys_at]
            made_here[2].append(dot_leading(band, position).astype(jnp.bfloat16))
            made_here[3].append(((content_grad + position_grad) * KEY**-0.5).astype(jnp.bfloat16))
            made_here[4].append(jnp.sum(content_grad, 0, keepdims=True))
            made_here[5].append(jnp.sum(position_grad, 0, keepdims=True))
        value_grad_ref[:, value_pair] = jnp.concatenate(made_here[0], 1)
        mixed_ref[:, key_pair] = jnp.concatenate(made_here[1], 1)
        table_grad_ref[:, pair] = jnp.concatenate(made_here[2], 1)
        mixed_ref[:, pair] = jnp.concatenate(made_here[3], 1)
        vector[11:12, pair] = jnp.concatenate(made_here[4], 1)
        vector[11:12, key_pair] = jnp.concatenate(made_here[5], 1)

        @pl.when(index + 1 < HEADS // 2)
        def _():
            for side in range(2):
                probs_load(2 * index + 2 + side).start()

    def rel_step():
        for shard in range(groups):
            value = dot_leading(table[1], table_grad_ref[:, shard * 128 : (shard + 1) * 128])
            rel_grad[shard] = value.astype(rel_grad.dtype).reshape(rel_grad.shape[1:])
        rel_copy().start()

    def mixed_step(i):
        left = mixed_ref[:, 0 : mixed_full.shape[1]]
        total_ref[:, columns_at(i, tile)] = dot_trailing(left, next_tile(3, i))

    def value_step(i):
        total_ref[:, columns_at(i, tile)] += dot_trailing(value_grad_ref[...], next_tile(4, i))

    def norm_one_back():
        def rows_fn(at):
            standard, inverse = normalize(kept_ref[at, :])
            value = total_ref[at, :]
            put(1, value * standard)
            put(5, value)
            value = attn_grad[at, :] + norm_back(value * params[1:2, :], standard, inverse)
            attn_grad[at, :] = value
            rounded = value.astype(right_ref.dtype)
            right_ref[at, :] = rounded
            put(4, rounded.astype(jnp.float32))

        by_rows(rows_fn)

    def conv_shift(tap):
        move = tap - taps // 2

        def column_body(i, carry):
            at = columns_at(i, rows)
            value = right_ref[:, at].astype(jnp.float32)
            value = pltpu.roll(value, (move + length) % length, 0)
            row = lax.broadcasted_iota(jnp.int32, value.shape, 0) - move
            inside = jnp.logical_and(row >= 0, row < length)
            wide_hold[:, at] = jnp.where(inside, value, 0.0).astype(wide_hold.dtype)
            return carry

        lax.fori_loop(0, columns // rows, column_body, 0)

    def conv_step(i):
        left = wide_hold[:, 0:columns]
        total_ref[:, columns_at(i % tiles, tile)] += dot_trailing(left, next_tile(5, i))

    def batch_back():
        def rows_fn(at):
            value = wide_hold[at, columns : 2 * columns].astype(jnp.float32)
            standard = (value - params[9:10, :]) * params[10:11, :]
            normed = standard * params[0:1, :] + params[3:4, :]
            value = total_ref[at, :] * gelu_slope(normed)
            put(0, value * standard)
            put(3, value)
            attn_grad[at, :] += params[10:11, :] * params[0:1, :] * value

        by_rows(rows_fn)

    def start_probs():
        for head in range(2):
            probs_load(head).start()

    def step_zero():
        begin()
        ready(0)()
        over(hidden_tiles, hidden_step)
        load(9, 1)()
        ready(9)()
        send_right(1, 2)()

    def step_one():
        over(2 * tiles, norm_two_step)
        load(3)()
        ready(1)()
        norm_two_back()
        load(10, 2)()
        start_probs()

    def step_two():
        over(tiles, attended_step)
        ready(10)()
        send_right(3)()
        ready(3, 4, 5, 6, 7)()

    def step_three():
        load(11, 12, 8)()
        rel_step()
        ready(11, 12)()
        send_right(4, 5)()

    def step_four():
        over(tiles, mixed_step)
        over(tiles, value_step)
        ready(2)()
        norm_one_back()
        load(13)()
        ready(13)()
        send_right(6)()
        clear_total()

    def step_last():
        ready(8)()
        batch_back()
        write_part().start()

    pairs_each = HEADS // 4

    for copy in (0, 4, 5, 6, 7):
        host_load(copy).start()

    def host(n):
        pl.when(n == 0)(step_zero)
        pl.when(n == 1)(step_one)
        pl.when(n == 2)(step_two)

        @pl.when(jnp.logical_and(n >= 2, n < 4))
        def _():
            over(pairs_each, lambda i: pair_step((n - 2) * pairs_each + i))

        pl.when(n == 3)(step_three)
        pl.when(n == 4)(step_four)

        @pl.when(jnp.logical_and(n >= 5, n < 5 + taps))
        def _():
            conv_shift(n - 5)
            over(tiles, lambda i: conv_step((n - 5) * tiles + i))

        pl.when(n == 4 + taps)(step_last)

    def body(n, carry):
        @pl.when(n < normal)
        def _():
            @pl.when(n >= slots)
            def _():
                old = n - slots
                for copy in one(old) + two(old):
                    copy.wait_send()
                for j in range(others):
                    shard_copy(old, j).wait_send()

            for piece in range(normal):

                @pl.when(n == piece)
                def _():
                    wait_loads(piece)

            produce(n)
            claim(n, 0)
            claim(n, 1)
            for copy in one(n):
                copy.start()

        for e, (at, piece) in enumerate(extra_at.items()):

            @pl.when(n == at)
            def _():
                extra_start(piece, e)

        host(n)
        for piece in range(1, normal):

            @pl.when(n == piece - 1)
            def _():
                start_loads(piece)

        @pl.when(jnp.logical_and(n >= 1, n < normal + 1))
        def _():
            piece = n - 1
            slot = piece % slots
            for copy in one(piece):
                copy.wait_recv()

            def shard_body(shard, carry):
                for other in range(2):
                    value = add(slot, x_one[piece % ring, shard, other], first, shard, other, at_x)
                    grad[slot, shard, other, at_x, :, first] = value.astype(grad.dtype)
                    value = add(slot, y_one[piece % ring, shard, other], last, shard, at_y, other)
                    grad[slot, shard, at_y, other, :, last] = value.astype(grad.dtype)
                return carry

            lax.fori_loop(0, groups, shard_body, 0)
            pay(piece, 0, along_x)
            pay(piece, 1, along_y)
            claim(piece, 2)
            claim(piece, 3)
            for copy in two(piece):
                copy.start()

        @pl.when(jnp.logical_and(n >= 2, n < normal + 2))
        def _():
            piece = n - 2
            slot = piece % slots
            for copy in two(piece):
                copy.wait_recv()

            def shard_body(shard, carry):
                value = add(slot, y_two[piece % ring, shard], first, shard, at_y, at_x)
                grad[slot, shard, at_y, at_x, :, first] = value.astype(grad.dtype)
                value = add(slot, x_two[piece % ring, shard], last, shard, at_y, at_x)
                grad[slot, shard, at_y, at_x, :, last] = value.astype(grad.dtype)
                return carry

            lax.fori_loop(0, groups, shard_body, 0)
            pay(piece, 2, along_y)
            pay(piece, 3, along_x)
            for j in range(others):

                @pl.when(piece >= ring)
                def _():
                    pl.semaphore_wait(shard_credit.at[(me + 1 + j) % groups], 1)

                shard_copy(piece, j).start()

        @pl.when(jnp.logical_and(n >= 3, n < normal + 3))
        def _():
            piece = n - 3
            value = grad[piece % slots, me, at_y, at_x].astype(jnp.float32)
            for j in range(others):
                shard_arrival(piece, j).wait_recv()
                value = value + shard_got[piece % ring, (me + 1 + j) % groups].astype(jnp.float32)

            @pl.when(piece < normal - ring)
            def _():
                for j in range(others):
                    pl.semaphore_signal(
                        shard_credit.at[me], inc=1, device_id=shards[j], device_id_type=MESH
                    )

            finish(piece, value)

        @pl.when(jnp.logical_and(n >= 4, n < normal + 4))
        def _():
            cross(n - 4)

        @pl.when(n >= 5)
        def _():
            close(n - 5)

        for e, (at, piece) in enumerate(extra_at.items()):
            for later, action in (
                (3, functools.partial(extra_sum, piece, e)),
                (4, functools.partial(extra_fold, piece, e)),
                (5, functools.partial(extra_done, piece, e)),
                (6, functools.partial(cross, piece)),
                (7, functools.partial(close, piece)),
            ):
                pl.when(n == at + later)(action)

        for step in range(len(summing)):

            @pl.when(n == normal + step - 1)
            def _():
                summing[step]()

        return carry

    lax.fori_loop(0, normal + 5, body, 0)
    slab_sent(11, 1)
    write_part().wait()

    def drain(piece, carry):
        @pl.when(jnp.logical_and(piece >= normal - slots, piece < normal))
        def _():
            for copy in one(piece) + two(piece):
                copy.wait_send()
            for j in range(others):
                shard_copy(piece, j).wait_send()

        pltpu.make_async_copy(done.at[piece], place(piece, dp), write_sem.at[piece]).wait()
        got = out.at[piece, :, pl.ds(0, width)]
        remote(got, got, send_sem.at[piece], sib_sem.at[piece], (sib, me)).wait_recv()
        sent = out.at[piece, pl.ds(0, 7 * part // 2), :]
        remote(sent, sent, send_sem.at[piece], sib_sem.at[piece], (sib, me)).wait_send()
        return carry

    lax.fori_loop(0, count, drain, 0)
    for index in range(len(lefts)):
        left_copy(index).wait_send()
    for index in range(len(rights)):
        right_copy(index).wait_send()


def reduce(groups, blocks, rel_at, lefts, saved, weights, heads, params, table):
    hidden, _, _, _, activated = lefts
    length, columns = activated.shape
    width = columns // 2
    rows = columns // groups
    part = rows // 4
    dtype = activated.dtype
    count = 12
    slots = 4
    ring = 3 if blocks == 1 else 2
    narrow = heads[2].shape
    span = table.shape[1]
    kept = pl.BlockSpec(memory_space=pl.ANY)
    inside = pl.BlockSpec(memory_space=pltpu.VMEM)
    each = pltpu.SemaphoreType.DMA((count,))
    wide = (length, columns)
    rel_shape = (groups, 2, table.shape[2] // 2, 128)
    sums = (16, columns)
    inputs = [*lefts, *saved, *weights, *heads]
    half_got = (ring, groups, part, width // 2)
    two_got = (ring, groups, 2, part, width // 2)
    return pl.pallas_call(
        functools.partial(reduce_kernel, groups, blocks, rel_at),
        out_shape=(
            jax.ShapeDtypeStruct((count, rows, columns), dtype),
            jax.ShapeDtypeStruct(sums, jnp.float32),
            jax.ShapeDtypeStruct(wide, jnp.float32),
            jax.ShapeDtypeStruct(hidden.shape, dtype),
            jax.ShapeDtypeStruct(wide, dtype),
            jax.ShapeDtypeStruct(wide, dtype),
            jax.ShapeDtypeStruct(wide, dtype),
            jax.ShapeDtypeStruct(wide, dtype),
            jax.ShapeDtypeStruct(hidden.shape, dtype),
            jax.ShapeDtypeStruct((4,) + wide, dtype),
            jax.ShapeDtypeStruct((7, length, width), dtype),
        ),
        in_specs=[kept] * len(inputs) + [inside] * 2,
        out_specs=[kept, inside] + [kept] * 9,
        scratch_shapes=[
            pltpu.VMEM((2,) + wide, dtype),
            pltpu.VMEM((2, length, width), dtype),
            pltpu.VMEM((slots, groups, 2, 2, part, width), dtype),
            pltpu.VMEM(two_got, dtype),
            pltpu.VMEM(two_got, dtype),
            pltpu.VMEM(half_got, dtype),
            pltpu.VMEM(half_got, dtype),
            pltpu.VMEM((ring, groups, part, width), dtype),
            pltpu.VMEM((count if blocks > 1 else 1, blocks, part, width), dtype),
            pltpu.VMEM((count, part, width), dtype),
            pltpu.VMEM(rel_shape, dtype),
            pltpu.VMEM(rel_shape, dtype),
            pltpu.VMEM(sums, jnp.float32),
            *([pltpu.SemaphoreType.DMA((5,))] * 2),
            *([pltpu.SemaphoreType.DMA((7,))] * 2),
            *([pltpu.SemaphoreType.DMA((1,))] * 2),
            pltpu.SemaphoreType.DMA((2 + 2 * groups,)),
            *([each] * 8),
            *([pltpu.SemaphoreType.DMA((count, groups))] * 2),
            *([pltpu.SemaphoreType.DMA((count, blocks))] * 2),
            *([each] * 6),
            *sum_scratch(groups, blocks, sums),
            pltpu.SemaphoreType.REGULAR((4,)),
            pltpu.SemaphoreType.REGULAR((groups,)),
            pltpu.VMEM(wide, jnp.float32),
            pltpu.VMEM(wide, jnp.float32),
            pltpu.VMEM(wide, jnp.float32),
            pltpu.VMEM((2, 512, columns), dtype),
            pltpu.VMEM(hidden.shape, dtype),
            pltpu.VMEM(wide, dtype),
            pltpu.VMEM(wide, dtype),
            pltpu.VMEM(wide, dtype),
            *([pltpu.VMEM(narrow, dtype)] * 3),
            pltpu.VMEM((span, narrow[1]), dtype),
            pltpu.VMEM((span, narrow[1]), dtype),
            pltpu.VMEM((2, length, length), dtype),
            pltpu.SemaphoreType.DMA((2,)),
            pltpu.SemaphoreType.DMA((14,)),
            pltpu.SemaphoreType.DMA((2,)),
            pltpu.SemaphoreType.DMA((hidden.shape[1] // 512 + 1,)),
            pltpu.VMEM((groups, 2, 2, part, width), dtype),
            pltpu.VMEM((groups - 1, 2, 2, part, width), dtype),
            pltpu.VMEM((2, 2, part, width // 2), dtype),
            pltpu.VMEM((2, 2, part, width // 2), dtype),
            pltpu.VMEM((2, part, width // 2), dtype),
            pltpu.VMEM((2, part, width // 2), dtype),
            pltpu.SemaphoreType.REGULAR((groups,)),
        ],
        compiler_params=pltpu.CompilerParams(
            collective_id=1, has_side_effects=True, vmem_limit_bytes=VMEM_LIMIT
        ),
        name="reduce",
    )(*inputs, params, table)


EPSILON = 1e-05


def normalize(values):
    centred = values - jnp.mean(values, -1, keepdims=True)
    inverse = lax.rsqrt(jnp.mean(centred * centred, -1, keepdims=True) + EPSILON)
    return (centred * inverse, inverse)


def norm_back(grad_std, standard, inverse):
    return inverse * (
        grad_std
        - jnp.mean(grad_std, -1, keepdims=True)
        - standard * jnp.mean(grad_std * standard, -1, keepdims=True)
    )


def dot_leading(left_side, right_side):
    return lax.dot_general(
        left_side, right_side, (((0,), (0,)), ((), ())), preferred_element_type=jnp.float32
    )


def dot_trailing(left_side, right_side):
    return lax.dot_general(
        left_side, right_side, (((1,), (1,)), ((), ())), preferred_element_type=jnp.float32
    )


def on_device(
    tokens,
    conv_weight,
    query_weight,
    key_weight,
    value_weight,
    out_weight,
    rel_weight,
    up_weight,
    down_weight,
    gains,
    biases,
    up_bias,
    rel_bias,
    target_table,
    clip_levels,
    window_ids,
    clip_index,
):
    groups = lax.axis_size("fsdp")
    blocks = lax.axis_size("dp") // 8
    tap_count, piece_rows, model_width = conv_weight.shape
    half_taps = tap_count // 2
    half_width = model_width // 2
    key_width = query_weight.shape[1]
    rel_rows, rel_columns = rel_weight.shape
    inputs = tokens[0].astype(jnp.float32)
    length = inputs.shape[0]
    token_total = length * lax.axis_size("dp") * lax.axis_size("fsdp")

    small_parts = [gains, biases, up_bias, rel_bias]
    small = jnp.concatenate([part.reshape(-1) for part in small_parts])
    small = jnp.pad(small, (0, -small.shape[0] % 1024)).reshape(-1, 128)
    target_row = lax.dynamic_index_in_dim(target_table, window_ids[0], 0, keepdims=True)
    levels = jnp.arange(clip_levels.shape[0], dtype=jnp.int32)
    selector = (clip_index[0][:, None] == levels[None, :]).astype(jnp.float32)
    limits = jnp.sum(selector * clip_levels[None, :], 1)[:, None]
    limits = jnp.broadcast_to(limits, (length, 128))
    (
        conv_full,
        mixed_full,
        value_full,
        out_full,
        up_full,
        down_full,
        _,
        _,
        _,
        activated,
        after_conv,
        normed_one,
        content_query,
        position_query,
        keys,
        values,
        mirrored_keys,
        probs,
        attended,
        after_attention,
        normed_two,
        hidden_pre,
        hidden,
        outputs,
        cotangent,
        tables,
        params,
    ) = gather(
        groups,
        blocks,
        [
            conv_weight,
            query_weight,
            key_weight,
            value_weight,
            out_weight,
            up_weight,
            down_weight,
            rel_weight,
        ],
        small,
        tokens[0],
        target_row,
        limits,
    )
    conv_full = conv_full.reshape(tap_count, model_width, model_width)
    mixed_full = mixed_full.reshape(model_width, -1)
    value_full = value_full.reshape(model_width, -1)
    out_full = out_full.reshape(model_width, -1)
    up_full = up_full.reshape(model_width, -1)
    down_full = down_full.reshape(-1, model_width)
    pieces, sums, part_grad, *_ = reduce(
        groups,
        blocks,
        2 * key_width - half_width,
        [hidden, normed_two, attended, normed_one, activated],
        [cotangent, hidden_pre, after_attention, after_conv, tokens[0]],
        [down_full, up_full, out_full, value_full, mixed_full, conv_full],
        [probs, values, keys, content_query, position_query, mirrored_keys],
        params,
        tables,
    )
    standard = (inputs - params[9]) * params[10]
    input_grad = part_grad - params[10] * params[0] * (
        sums[3] + standard * sums[0]
    ) / token_total
    shard = lax.axis_index("fsdp")
    by_shard = sums[:9].reshape(9, groups, -1)
    by_shard = lax.dynamic_index_in_dim(by_shard, shard, 1, keepdims=False)
    up_sums = sums[9:11].reshape(groups, -1)
    up_sums = lax.dynamic_index_in_dim(up_sums, shard, 0, keepdims=False)
    rel_sums = sums[11, : 2 * key_width].reshape(2, groups, -1)
    rel_sums = lax.dynamic_index_in_dim(rel_sums, shard, 1, keepdims=False)
    up_grad = jnp.concatenate([pieces[1], pieces[2]], 1)
    mixed_sum = pieces[5].astype(jnp.float32)
    rel_at = 2 * key_width
    return (
        outputs[None],
        input_grad.astype(jnp.bfloat16)[None],
        jnp.concatenate([pieces[6:10], pieces[11:12]], 0).astype(jnp.float32),
        mixed_sum[:, :key_width],
        mixed_sum[:, key_width:rel_at],
        pieces[4].astype(jnp.float32),
        pieces[3].astype(jnp.float32),
        mixed_sum[:rel_rows, rel_at : rel_at + rel_columns],
        up_grad.astype(jnp.float32),
        jnp.concatenate([pieces[0], pieces[10]], 0).astype(jnp.float32),
        by_shard[:3],
        by_shard[3:9],
        up_sums,
        rel_sums,
    )


def solution(mesh):
    placed = (
        P(("dp", "fsdp"), None, None),
        P(None, "fsdp", None),
        P("fsdp", None),
        P("fsdp", None),
        P("fsdp", None),
        P("fsdp", None),
        P(None, "fsdp"),
        P("fsdp", None),
        P("fsdp", None),
        P(None, "fsdp"),
        P(None, "fsdp"),
        P("fsdp"),
        P(None, "fsdp"),
        P(),
        P(),
        P(("dp", "fsdp")),
        P(("dp", "fsdp"), None),
    )
    return jax.shard_map(
        on_device,
        mesh=mesh,
        in_specs=placed,
        out_specs=(
            P(("dp", "fsdp"), None, None),
            P(("dp", "fsdp"), None, None),
            P(None, "fsdp", None),
            P("fsdp", None),
            P("fsdp", None),
            P("fsdp", None),
            P("fsdp", None),
            P(None, "fsdp"),
            P("fsdp", None),
            P("fsdp", None),
            P(None, "fsdp"),
            P(None, "fsdp"),
            P("fsdp"),
            P(None, "fsdp"),
        ),
        check_vma=False,
    )
```
